32 devices in a mesh: tok: 8 (over y, x, core), tp: 4 (over z).
Axes of the slice: x: 2, y: 2, z: 4, core: 2. Of those that a mesh axis runs over, the one named last changes fastest.
Arguments:
- tokens: bfloat16 [6144, 2048], P('tok'), may hold values from -6 to 6
- gain_attn: float32 [2048], replicated, may hold values from 0.5 to 1.5
- w_query: bfloat16 [2048, 2048], P(None, 'tp'), may hold values from -0.125 to 0.125
- w_key: bfloat16 [2048, 512], P(None, 'tp'), may hold values from -0.125 to 0.125
- w_value: bfloat16 [2048, 512], P(None, 'tp'), may hold values from -0.125 to 0.125
- w_out: bfloat16 [2048, 2048], P('tp'), may hold values from -0.5 to 0.5
- gain_ffn: float32 [2048], replicated, may hold values from 0.5 to 1.5
- w_gate: bfloat16 [2048, 5632], P(None, 'tp'), may hold values from -0.125 to 0.125
- w_up: bfloat16 [2048, 5632], P(None, 'tp'), may hold values from -0.125 to 0.125
- w_down: bfloat16 [5632, 2048], P('tp'), may hold values from -0.078125 to 0.078125
- cotangent: bfloat16 [6144, 2048], P('tok'), may hold values from -6 to 6
- doc_lengths: int32 [6], replicated, may hold values from 128 to 2432, as said below
- keep_flags: int32 [6], replicated, may hold values from 0 to 1, as said below
Outputs:
- mixed: bfloat16 [6144, 2048], P('tok')
- token_grad: bfloat16 [6144, 2048], P('tok')
- grad_gain_attn: float32 [2048], P('tok')
- grad_query: float32 [2048, 2048], P('tok', 'tp')
- grad_key: float32 [2048, 512], P('tok', 'tp')
- grad_value: float32 [2048, 512], P('tok', 'tp')
- grad_out: float32 [2048, 2048], P('tp', 'tok')
- grad_gain_ffn: float32 [2048], P('tok')
- grad_gate: float32 [2048, 5632], P('tok', 'tp')
- grad_up: float32 [2048, 5632], P('tok', 'tp')
- grad_down: float32 [5632, 2048], P('tp', 'tok')
The draws below stay inside these ranges and needn't reach their ends.
Inputs may be any that keep to these rules, and one draw needn't show every extreme that they name: `doc_lengths`: every length is a multiple of 128 and they sum to 6144; the kept documents hold exactly half of the tokens, and one kept document has 1024 tokens or more. `keep_flags`: half of the documents are kept.
All inputs are finite; a program needn't handle non-finite values.
Results may differ from the reference program's by a relative error of at most 0.015.
Values may be sent and summed in bfloat16 or wider, within the bound.
A program may use at most 256 MiB of HBM per device.

```python
import math
import jax
import jax.numpy as jnp
from jax import lax

D = 2048
H = 16
HD = 128
KV = 4
FF = 5632
BLOCK = 128
TOK_DEV = 768
TOKENS = 6144


def document_plan(key):
    devices = TOKENS // TOK_DEV
    half_blocks = TOKENS // BLOCK // 2
    longest = half_blocks - devices // 2 - 1
    remainder = devices // 2 + 1
    key_split, key_drop, key_order = jax.random.split(key, 3)
    split_kept = jax.random.randint(key_split, (), 1, devices // 2 + 1)
    split_drop = jax.random.randint(key_drop, (), devices // 2, half_blocks - devices // 2)
    kinds = jnp.stack([jnp.asarray(longest, jnp.int32), split_kept.astype(jnp.int32), (remainder - split_kept).astype(jnp.int32), jnp.asarray(1, jnp.int32), split_drop.astype(jnp.int32), (half_blocks - 1 - split_drop).astype(jnp.int32)]) * BLOCK
    flags = jnp.array([1, 1, 1, 0, 0, 0], dtype=jnp.int32)
    order = jax.random.permutation(key_order, 6)
    return (kinds[order].astype(jnp.int32), flags[order].astype(jnp.int32))


def draw_doc_lengths(key, part):
    lengths, flags = document_plan(key)
    return lengths


def draw_keep_flags(key, part):
    lengths, flags = document_plan(key)
    return flags


def block_levels(key, shape, cuts, least, largest):
    factor_of = 1.0
    for position, blocks in cuts:
        draws = jax.random.uniform(jax.random.fold_in(jax.random.fold_in(key, 6), position), (blocks,), jnp.float32, least / len(cuts), largest / len(cuts))
        factor_of = factor_of * jnp.repeat(jnp.exp(draws), shape[position] // blocks).reshape((-1,) + (1,) * (len(shape) - 1 - position))
    return factor_of


def centred(rng, shape, spread, most, cuts=(), kind=jnp.bfloat16):
    drawn = jax.random.normal(rng, shape, jnp.float32) * spread
    if len(cuts) > 0:
        drawn = block_levels(rng, shape, cuts, -0.22, 0.18) * drawn
    return jnp.clip(drawn, min=-most, max=most).astype(kind)


def setup_inputs(seed: int = 0) -> dict:
    key_list = jax.random.split(jax.random.key(seed), 14)
    tokens = centred(key_list[0], (TOKENS, D), 1.0, 6.0, ((0, 8),))
    gain_attn = jnp.clip(1.0 + 0.1 * jax.random.normal(key_list[1], (D,), jnp.float32), 0.5, 1.5)
    w_query = centred(key_list[2], (D, H * HD), D ** -0.5, 0.125, ((1, 4),))
    w_key = centred(key_list[3], (D, KV * HD), D ** -0.5, 0.125, ((1, 4),))
    w_value = centred(key_list[4], (D, KV * HD), D ** -0.5, 0.125, ((1, 4),))
    w_out = centred(key_list[5], (H * HD, D), (H * HD // 16) ** -0.5, 0.5, ((0, 4),))
    gain_ffn = jnp.clip(1.0 + 0.1 * jax.random.normal(key_list[6], (D,), jnp.float32), 0.5, 1.5)
    w_gate = centred(key_list[7], (D, FF), D ** -0.5, 0.125, ((1, 4),))
    w_up = centred(key_list[8], (D, FF), D ** -0.5, 0.125, ((1, 4),))
    w_down = centred(key_list[9], (FF, D), FF ** -0.5, 0.078125, ((0, 4),))
    cotangent = centred(key_list[10], (TOKENS, D), 1.0, 6.0, ((0, 8),))
    doc_lengths = draw_doc_lengths(jax.random.fold_in(key_list[13], 71), 0)
    keep_flags = draw_keep_flags(jax.random.fold_in(key_list[13], 71), 0)
    return dict(tokens=tokens, gain_attn=gain_attn, w_query=w_query, w_key=w_key, w_value=w_value, w_out=w_out, gain_ffn=gain_ffn, w_gate=w_gate, w_up=w_up, w_down=w_down, cotangent=cotangent, doc_lengths=doc_lengths, keep_flags=keep_flags)


@jax.custom_vjp
def low(v):
    return lax.optimization_barrier(v.astype(jnp.bfloat16)).astype(jnp.float32)

@jax.custom_vjp
def low_back(v):
    return v

def low_keep(v):
    return (low(v), None)

def low_pass(kept, grad):
    return (grad,)

def back_keep(v):
    return (v, None)

def back_low(kept, grad):
    return (low(grad),)
low.defvjp(low_keep, low_pass)
low_back.defvjp(back_keep, back_low)
norm_eps = 1e-05
keep_scale = 2.0
highest = lax.Precision.HIGHEST

def document_tables(doc_lengths, offset, length):
    doc_ends = jnp.cumsum(doc_lengths, dtype=jnp.int32)
    doc_starts = doc_ends - doc_lengths
    places = offset + jnp.arange(length, dtype=jnp.int32)
    doc_ids = lax.optimization_barrier(jnp.sum((places[:, None] >= doc_ends[None, :]).astype(jnp.int32), axis=1, dtype=jnp.int32))
    member = (doc_ids[:, None] == jnp.arange(doc_lengths.shape[0], dtype=jnp.int32)[None, :]).astype(jnp.int32)
    positions = places - lax.optimization_barrier(jnp.sum(member * doc_starts[None, :], axis=1, dtype=jnp.int32))
    return (places, doc_ids, positions, member)

def rotary_tables(positions, head_dim):
    half_dim = head_dim // 2
    freqs = jnp.exp(jnp.arange(half_dim, dtype=jnp.float32) * (-2.0 * math.log(10000.0) / head_dim))
    angles = positions.astype(jnp.float32)[:, None] * freqs[None, :]
    return (jnp.cos(angles), jnp.sin(angles))

def rotate(values, cosine, sine):
    half_dim = values.shape[-1] // 2
    former, latter = (values[..., :half_dim], values[..., half_dim:])
    cos_b, sin_b = (cosine[:, None, :], sine[:, None, :])
    return jnp.concatenate([former * cos_b - latter * sin_b, latter * cos_b + former * sin_b], axis=-1)

def layer(x, gain_one, wq, wk, wv, wo, gain_two, wg, wu, wd, places, doc_ids, positions, rate):
    length = x.shape[0]
    score_scale = 1.0 / math.sqrt(HD)
    inv_one = lax.rsqrt(lax.optimization_barrier(jnp.mean(x * x, axis=1, keepdims=True)) + norm_eps)
    normed_one = low(x * inv_one * gain_one)
    query_pre = low_back(jnp.dot(normed_one, wq, precision=highest)).reshape(length, H, HD)
    key_pre = low_back(jnp.dot(normed_one, wk, precision=highest)).reshape(length, KV, HD)
    value_pre = low_back(jnp.dot(normed_one, wv, precision=highest)).reshape(length, KV, HD)
    cosine, sine = rotary_tables(positions, HD)
    queries = low(rotate(query_pre, cosine, sine))
    keys = low(rotate(key_pre, cosine, sine))
    values = low(value_pre)
    keys_wide = jnp.repeat(keys, H // KV, axis=1)
    values_wide = jnp.repeat(values, H // KV, axis=1)
    block_rows = min(512, length)
    blocks = length // block_rows

    def attend(pack):
        query_block, doc_block, place_block = pack
        scores = jnp.einsum('qhd,khd->hqk', query_block, keys_wide, precision=highest) * score_scale
        scores = low_back(scores)
        allowed = (doc_block[:, None] == doc_ids[None, :]) & (place_block[:, None] >= places[None, :])
        scores = jnp.where(allowed[None], scores, -1e+30)
        peak = lax.optimization_barrier(jnp.max(scores, axis=2, keepdims=True))
        weights = jnp.exp(scores - peak)
        probs = low(weights / lax.optimization_barrier(jnp.sum(weights, axis=2, keepdims=True)))
        return jnp.einsum('hqk,khd->qhd', probs, values_wide, precision=highest)
    outputs = lax.map(jax.checkpoint(attend), (queries.reshape(blocks, block_rows, H, HD), doc_ids.reshape(blocks, block_rows), places.reshape(blocks, block_rows)))
    attended = low(low_back(outputs.reshape(length, H * HD)))
    branch_attn = low_back(jnp.dot(attended, wo, precision=highest))
    hidden_res = x + branch_attn
    inv_two = lax.rsqrt(lax.optimization_barrier(jnp.mean(hidden_res * hidden_res, axis=1, keepdims=True)) + norm_eps)
    normed_two = low(hidden_res * inv_two * gain_two)
    gate = low_back(jnp.dot(normed_two, wg, precision=highest))
    upper = low_back(jnp.dot(normed_two, wu, precision=highest))
    inner = low(jax.nn.silu(gate) * upper)
    branch_ffn = low_back(jnp.dot(inner, wd, precision=highest))
    return x + rate[:, None] * (branch_attn + branch_ffn)

def reference(tokens, gain_attn, w_query, w_key, w_value, w_out, gain_ffn, w_gate, w_up, w_down, cotangent, doc_lengths, keep_flags):
    places, doc_ids, positions, member = document_tables(doc_lengths, 0, TOKENS)
    rate = keep_scale * lax.optimization_barrier(jnp.sum(member * keep_flags[None, :], axis=1, dtype=jnp.int32)).astype(jnp.float32)
    floats = (tokens.astype(jnp.float32), gain_attn, w_query.astype(jnp.float32), w_key.astype(jnp.float32), w_value.astype(jnp.float32), w_out.astype(jnp.float32), gain_ffn, w_gate.astype(jnp.float32), w_up.astype(jnp.float32), w_down.astype(jnp.float32))

    def forward(x, gain_one, wq, wk, wv, wo, gain_two, wg, wu, wd):
        return layer(x, gain_one, wq, wk, wv, wo, gain_two, wg, wu, wd, places, doc_ids, positions, rate)
    result, pullback = jax.vjp(forward, *floats)
    grads = pullback(cotangent.astype(jnp.float32))
    return (result.astype(jnp.bfloat16), grads[0].astype(jnp.bfloat16), grads[1], grads[2], grads[3], grads[4], grads[5], grads[6], grads[7], grads[8], grads[9])
```

```python
import functools
import math

import jax
import jax.numpy as jnp
from jax import lax
from jax.experimental import pallas as pl
from jax.experimental.pallas import tpu as pltpu
from jax.sharding import PartitionSpec as P

HD = 128
BLOCK = 128
SLOTS = 3
CHUNKS = 8
MESH = pl.DeviceIdType.MESH
VMEM_BYTES = 60 * 2**20

norm_eps = 1e-05
keep_scale = 2.0
F32 = jnp.float32
BF16 = jnp.bfloat16


def vmem():
    return pl.BlockSpec(memory_space=pltpu.VMEM)


def smem():
    return pl.BlockSpec(memory_space=pltpu.SMEM)


def params(collective_id):
    return pltpu.CompilerParams(
        collective_id=collective_id, has_side_effects=True, vmem_limit_bytes=VMEM_BYTES
    )


def cost(flops, moved):
    return pl.CostEstimate(flops=flops, bytes_accessed=moved, transcendentals=0)


def greet(peers):
    barrier = pltpu.get_barrier_semaphore()
    for peer in peers:
        pl.semaphore_signal(barrier, inc=1, device_id=peer, device_id_type=MESH)
    pl.semaphore_wait(barrier, len(peers))


def deal_tables(own, stages, blocks_here, lens_ref, flags_ref):
    def kept_before(place):
        total, start = jnp.int32(0), jnp.int32(0)
        for doc in range(lens_ref.shape[0]):
            blocks = lens_ref[doc] // BLOCK
            total = total + flags_ref[doc] * jnp.clip(place - start, 0, blocks)
            start = start + blocks
        return total

    def edges(stage):
        first = (own >> stage) << stage
        return (
            kept_before(first * blocks_here),
            kept_before((first + (1 << stage)) * blocks_here),
        )

    def located(stage):
        if stage == 0:
            ends = [kept_before(own * blocks_here + i + 1) for i in range(blocks_here)]

            def place(rank):
                index = jnp.int32(0)
                for end in ends:
                    index = index + (end <= rank).astype(jnp.int32)
                return index

            return place
        mine = (own >> (stage - 1)) << (stage - 1)
        low, high = edges(stage - 1)
        other = kept_before((mine ^ (1 << (stage - 1))) * blocks_here)

        def place(rank):
            inside = (rank >= low) & (rank < high)
            return jnp.where(inside, (rank - low) >> stage, SLOTS + ((rank - other) >> stage))

        return place

    keeps, sends = [], []
    for stage in range(stages):
        low, high = edges(stage)
        place = located(stage)
        period = 1 << (stage + 1)
        for table, target in ((keeps, own), (sends, own ^ (1 << stage))):
            first = low + ((target - low) & (period - 1))
            row = []
            for slot in range(SLOTS):
                rank = first + period * slot
                row.append(jnp.where(rank < high, place(rank), -1))
            table.append(row)
    place = located(stages)
    finals = [place(own + (slot << stages)) for slot in range(SLOTS)]
    return keeps, sends, finals


def choose(index, options, default=None):
    value = options[0] if default is None else default
    for number, option in enumerate(options):
        if number == 0 and default is None:
            continue
        value = jnp.where(index == number, option, value)
    return value


def deal_body(lens_ref, flags_ref, own_ref, out_ref, keep, send, recv, send_sem, recv_sem):
    stages = keep.shape[0]
    own = lax.axis_index("tok")
    plane = lax.axis_index("tp")
    blocks_here = own_ref.shape[0]
    rows = BLOCK // CHUNKS
    peers = [(own ^ (1 << stage), plane) for stage in range(stages)]
    greet(peers)
    keeps, sends, finals = deal_tables(own, stages, blocks_here, lens_ref, flags_ref)

    def copy(stage, chunk):
        return pltpu.make_async_remote_copy(
            src_ref=send.at[stage, chunk],
            dst_ref=recv.at[stage, chunk],
            send_sem=send_sem.at[stage, chunk],
            recv_sem=recv_sem.at[stage, chunk],
            device_id=peers[stage],
            device_id_type=MESH,
        )

    def held(stage, chunk):
        if stage == 0:
            span = pl.ds(pl.multiple_of(chunk * rows, rows), rows)
            return [own_ref[i, span, :] for i in range(blocks_here)]
        before = stage - 1
        return [keep[before, chunk, i] for i in range(SLOTS)] + [
            recv[before, chunk, i] for i in range(SLOTS)
        ]

    for stage in range(stages):

        def step(chunk, carry, stage=stage):
            if stage > 0:
                copy(stage - 1, chunk).wait_recv()
            options = held(stage, chunk)
            for slot in range(SLOTS):
                send[stage, chunk, slot] = choose(sends[stage][slot], options)
            copy(stage, chunk).start()
            for slot in range(SLOTS):
                keep[stage, chunk, slot] = choose(keeps[stage][slot], options)
            return carry

        lax.fori_loop(0, CHUNKS, step, 0)

    def finish(chunk, carry):
        copy(stages - 1, chunk).wait_recv()
        options = held(stages, chunk)
        span = pl.ds(pl.multiple_of(chunk * rows, rows), rows)
        for slot in range(SLOTS):
            out_ref[slot, span, :] = choose(finals[slot], options)
        return carry

    lax.fori_loop(0, CHUNKS, finish, 0)

    def drain(chunk, carry):
        for stage in range(stages):
            copy(stage, chunk).wait_send()
        return carry

    lax.fori_loop(0, CHUNKS, drain, 0)


def stages_of(axis):
    return int(math.log2(lax.axis_size(axis)))


def deal(doc_lengths, keep_flags, blocks, collective_id):
    stages = stages_of("tok")
    width = blocks.shape[2]
    rows = BLOCK // CHUNKS
    moved = (stages, CHUNKS, SLOTS, rows, width)
    return pl.pallas_call(
        deal_body,
        out_shape=jax.ShapeDtypeStruct((SLOTS, BLOCK, width), blocks.dtype),
        in_specs=[smem(), smem(), vmem()],
        out_specs=vmem(),
        scratch_shapes=[
            pltpu.VMEM(moved, blocks.dtype),
            pltpu.VMEM(moved, blocks.dtype),
            pltpu.VMEM(moved, blocks.dtype),
            pltpu.SemaphoreType.DMA((stages, CHUNKS)),
            pltpu.SemaphoreType.DMA((stages, CHUNKS)),
        ],
        compiler_params=params(collective_id),
        cost_estimate=cost(0, 40_000_000),
        name="deal",
    )(doc_lengths, keep_flags, blocks)


def undeal_body(
    lens_ref, flags_ref, kept_ref, home_ref, gains_ref, out_ref, sum_ref,
    hold, recv, gain_recv, send_sem, recv_sem, gain_send_sem, gain_recv_sem,
):
    stages = recv.shape[0]
    own = lax.axis_index("tok")
    plane = lax.axis_index("tp")
    devices = 1 << stages
    blocks_here = home_ref.shape[0]
    rows = BLOCK // CHUNKS
    share = sum_ref.shape[1]
    peers = [(own ^ (1 << stage), plane) for stage in range(stages)]
    greet([(own ^ step, plane) for step in range(1, devices)])

    def gain_copy(step):
        there = own ^ step
        return pltpu.make_async_remote_copy(
            src_ref=gains_ref.at[:, pl.ds(pl.multiple_of(there * share, share), share)]
            if share % 128 == 0
            else gains_ref,
            dst_ref=gain_recv.at[step],
            send_sem=gain_send_sem.at[step],
            recv_sem=gain_recv_sem.at[step],
            device_id=(there, plane),
            device_id_type=MESH,
        )

    for step in range(1, devices):
        gain_copy(step).start()
    keeps, sends, finals = deal_tables(own, stages, blocks_here, lens_ref, flags_ref)

    def copy(stage, chunk):
        return pltpu.make_async_remote_copy(
            src_ref=hold.at[stage, chunk, pl.ds(SLOTS, SLOTS)],
            dst_ref=recv.at[stage, chunk],
            send_sem=send_sem.at[stage, chunk],
            recv_sem=recv_sem.at[stage, chunk],
            device_id=peers[stage],
            device_id_type=MESH,
        )

    last = stages - 1

    def begin(chunk, carry):
        span = pl.ds(pl.multiple_of(chunk * rows, rows), rows)
        options = [kept_ref[slot, span, :] for slot in range(SLOTS)]
        for place in range(SLOTS, 2 * SLOTS):
            value = options[0]
            for slot in range(1, SLOTS):
                value = jnp.where(finals[slot] == place, options[slot], value)
            hold[last, chunk, place] = value
        copy(last, chunk).start()
        for place in range(SLOTS):
            value = options[0]
            for slot in range(1, SLOTS):
                value = jnp.where(finals[slot] == place, options[slot], value)
            hold[last, chunk, place] = value
        return carry

    lax.fori_loop(0, CHUNKS, begin, 0)
    for stage in range(last, -1, -1):

        def step(chunk, carry, stage=stage):
            copy(stage, chunk).wait_recv()
            options = [hold[stage, chunk, i] for i in range(SLOTS)] + [
                recv[stage, chunk, i] for i in range(SLOTS)
            ]
            places = keeps[stage] + sends[stage]

            def pick(place, value):
                for index, option in zip(places, options):
                    value = jnp.where(index == place, option, value)
                return value

            if stage == 0:
                span = pl.ds(pl.multiple_of(chunk * rows, rows), rows)
                for place in range(blocks_here):
                    out_ref[place, span, :] = pick(place, home_ref[place, span, :])
            else:
                for place in range(SLOTS, 2 * SLOTS):
                    hold[stage - 1, chunk, place] = pick(place, options[0])
                copy(stage - 1, chunk).start()
                for place in range(SLOTS):
                    hold[stage - 1, chunk, place] = pick(place, options[0])
            return carry

        lax.fori_loop(0, CHUNKS, step, 0)

    def drain(chunk, carry):
        for stage in range(stages):
            copy(stage, chunk).wait_send()
        return carry

    lax.fori_loop(0, CHUNKS, drain, 0)
    if share % 128 == 0:
        total = gains_ref[:, pl.ds(pl.multiple_of(own * share, share), share)]
    else:
        total = gains_ref[...]
    for step in range(1, devices):
        gain_copy(step).wait()
        total = total + gain_recv[step]
    sum_ref[...] = total


def undeal(doc_lengths, keep_flags, kept, home, gains, collective_id):
    stages = stages_of("tok")
    devices = 1 << stages
    width = kept.shape[2]
    rows = BLOCK // CHUNKS
    share = width // devices
    share = share if share % 128 == 0 else width
    return pl.pallas_call(
        undeal_body,
        out_shape=(
            jax.ShapeDtypeStruct(home.shape, home.dtype),
            jax.ShapeDtypeStruct((8, share), F32),
        ),
        in_specs=[smem(), smem(), vmem(), vmem(), vmem()],
        out_specs=(vmem(), vmem()),
        scratch_shapes=[
            pltpu.VMEM((stages, CHUNKS, 2 * SLOTS, rows, width), kept.dtype),
            pltpu.VMEM((stages, CHUNKS, SLOTS, rows, width), kept.dtype),
            pltpu.VMEM((devices, 8, share), F32),
            pltpu.SemaphoreType.DMA((stages, CHUNKS)),
            pltpu.SemaphoreType.DMA((stages, CHUNKS)),
            pltpu.SemaphoreType.DMA((devices,)),
            pltpu.SemaphoreType.DMA((devices,)),
        ],
        compiler_params=params(collective_id),
        cost_estimate=cost(0, 40_000_000),
        name="undeal",
    )(doc_lengths, keep_flags, kept, home, gains)


def gather_tok_body(mine_ref, out_ref, send_sem, recv_sem, relay_send_sem, relay_recv_sem):
    devices = out_ref.shape[0]
    chips = devices // 2
    own = lax.axis_index("tok")
    plane = lax.axis_index("tp")
    partner = (own ^ 1, plane)
    greet([partner] + [(own ^ (2 * step), plane) for step in range(1, chips)])

    def copy(step):
        return pltpu.make_async_remote_copy(
            src_ref=mine_ref,
            dst_ref=out_ref.at[own],
            send_sem=send_sem.at[step],
            recv_sem=recv_sem.at[step],
            device_id=(own ^ (2 * step), plane),
            device_id_type=MESH,
        )

    def relay(step):
        return pltpu.make_async_remote_copy(
            src_ref=mine_ref if step == 0 else out_ref.at[own ^ (2 * step)],
            dst_ref=out_ref.at[own ^ (2 * step)],
            send_sem=relay_send_sem.at[step],
            recv_sem=relay_recv_sem.at[step],
            device_id=partner,
            device_id_type=MESH,
        )

    for step in range(1, chips):
        copy(step).start()
    relay(0).start()
    out_ref[own] = mine_ref[...]
    for step in range(1, chips):
        copy(step).wait_recv()
        relay(step).start()
    for step in range(chips):
        relay(step).wait()
    for step in range(1, chips):
        copy(step).wait_send()


def gather_tok(mine, collective_id):
    devices = lax.axis_size("tok")
    chips = devices // 2
    return pl.pallas_call(
        gather_tok_body,
        out_shape=jax.ShapeDtypeStruct((devices,) + mine.shape, mine.dtype),
        in_specs=[vmem()],
        out_specs=vmem(),
        scratch_shapes=[pltpu.SemaphoreType.DMA((chips,))] * 4,
        compiler_params=params(collective_id),
        cost_estimate=cost(0, 10_000_000),
        name="gather_tok",
    )(mine)


def scatter_tok_body(
    part_ref, out_ref, core_recv, held, recv, core_send_sem, core_recv_sem, send_sem, recv_sem
):
    devices = part_ref.shape[0]
    chips = devices // 2
    own = lax.axis_index("tok")
    plane = lax.axis_index("tp")
    partner = (own ^ 1, plane)
    greet([partner] + [(own ^ (2 * step), plane) for step in range(1, chips)])

    def core_copy(step):
        return pltpu.make_async_remote_copy(
            src_ref=part_ref.at[own ^ (2 * step) ^ 1],
            dst_ref=core_recv.at[step],
            send_sem=core_send_sem.at[step],
            recv_sem=core_recv_sem.at[step],
            device_id=partner,
            device_id_type=MESH,
        )

    def copy(step):
        return pltpu.make_async_remote_copy(
            src_ref=held.at[step],
            dst_ref=recv.at[step],
            send_sem=send_sem.at[step],
            recv_sem=recv_sem.at[step],
            device_id=(own ^ (2 * step), plane),
            device_id_type=MESH,
        )

    order = list(range(chips - 1, -1, -1))
    for step in order:
        core_copy(step).start()
    for step in order:
        core_copy(step).wait_recv()
        total = part_ref[own ^ (2 * step)].astype(F32) + core_recv[step].astype(F32)
        if step > 0:
            held[step] = total.astype(held.dtype)
            copy(step).start()
        else:
            out_ref[...] = total
    for step in range(1, chips):
        copy(step).wait_recv()
        out_ref[...] += recv[step].astype(F32)
    for step in range(1, chips):
        copy(step).wait_send()
    for step in range(chips):
        core_copy(step).wait_send()


def scatter_tok(part, collective_id):
    devices = part.shape[0]
    chips = devices // 2
    shard = part.shape[1:]
    return pl.pallas_call(
        scatter_tok_body,
        out_shape=jax.ShapeDtypeStruct(shard, F32),
        in_specs=[vmem()],
        out_specs=vmem(),
        scratch_shapes=[
            pltpu.VMEM((chips,) + shard, part.dtype),
            pltpu.VMEM((chips,) + shard, part.dtype),
            pltpu.VMEM((chips,) + shard, part.dtype),
        ]
        + [pltpu.SemaphoreType.DMA((chips,))] * 4,
        compiler_params=params(collective_id),
        cost_estimate=cost(0, 10_000_000),
        name="scatter_tok",
    )(part)


def line_copies(own, plane, sources, targets, send_sem, recv_sem):
    def right(index):
        return pltpu.make_async_remote_copy(
            src_ref=sources.at[index],
            dst_ref=targets.at[index],
            send_sem=send_sem.at[0, index],
            recv_sem=recv_sem.at[0, index],
            device_id=(own, plane + 1),
            device_id_type=MESH,
        )

    def left(index):
        return pltpu.make_async_remote_copy(
            src_ref=sources.at[index],
            dst_ref=targets.at[index],
            send_sem=send_sem.at[1, index],
            recv_sem=recv_sem.at[1, index],
            device_id=(own, plane - 1),
            device_id_type=MESH,
        )

    return right, left


def line_greet(own, plane, planes):
    barrier = pltpu.get_barrier_semaphore()

    @pl.when(plane > 0)
    def _():
        pl.semaphore_signal(barrier, inc=1, device_id=(own, plane - 1), device_id_type=MESH)

    @pl.when(plane < planes - 1)
    def _():
        pl.semaphore_signal(barrier, inc=1, device_id=(own, plane + 1), device_id_type=MESH)

    end = (plane == 0) | (plane == planes - 1)

    @pl.when(end)
    def _():
        pl.semaphore_wait(barrier, 1)

    @pl.when(jnp.logical_not(end))
    def _():
        pl.semaphore_wait(barrier, 2)


def line_gather(own, plane, planes, out, send_sem, recv_sem):
    right, left = line_copies(own, plane, out, out, send_sem, recv_sem)
    last = planes - 1
    for step in range(1, planes + 1):
        before, after = plane - (step - 1), plane + (step - 1)

        @pl.when(before >= 0)
        def _():
            if step > 1:
                right(before).wait_recv()
            if step < planes:

                @pl.when(plane < last)
                def _():
                    right(before).start()

        @pl.when(after <= last)
        def _():
            if step > 1:
                left(after).wait_recv()
            if step < planes:

                @pl.when(plane > 0)
                def _():
                    left(after).start()

    for index in range(planes):

        @pl.when((index <= plane) & (plane < last))
        def _():
            right(index).wait_send()

        @pl.when((index >= plane) & (plane > 0))
        def _():
            left(index).wait_send()


def line_reduce(own, plane, planes, part, total, send, recv, send_sem, recv_sem):
    last = planes - 1
    right, _ = line_copies(own, plane, send.at[0], recv.at[0], send_sem, recv_sem)
    _, left = line_copies(own, plane, send.at[1], recv.at[1], send_sem, recv_sem)
    for step in range(1, planes):
        upper, lower = planes - step + plane, step - planes + plane

        @pl.when((upper <= last) & (plane < last))
        def _():
            @pl.when(plane == 0)
            def _():
                send[0, upper] = part[upper]

            @pl.when(plane > 0)
            def _():
                right(upper).wait_recv()
                send[0, upper] = (
                    part[upper].astype(F32) + recv[0, upper].astype(F32)
                ).astype(send.dtype)

            right(upper).start()

        @pl.when((lower >= 0) & (plane > 0))
        def _():
            @pl.when(plane == last)
            def _():
                send[1, lower] = part[lower]

            @pl.when(plane < last)
            def _():
                left(lower).wait_recv()
                send[1, lower] = (
                    part[lower].astype(F32) + recv[1, lower].astype(F32)
                ).astype(send.dtype)

            left(lower).start()

    total[...] = part[plane].astype(F32)

    @pl.when(plane > 0)
    def _():
        right(plane).wait_recv()
        total[...] += recv[0, plane].astype(F32)

    @pl.when(plane < last)
    def _():
        left(plane).wait_recv()
        total[...] += recv[1, plane].astype(F32)

    for index in range(planes):

        @pl.when((index > plane) & (plane < last))
        def _():
            right(index).wait_send()

        @pl.when((index < plane) & (plane > 0))
        def _():
            left(index).wait_send()


def gather_tp_body(mine_ref, out_ref, send_sem, recv_sem):
    planes = out_ref.shape[0]
    own, plane = lax.axis_index("tok"), lax.axis_index("tp")
    line_greet(own, plane, planes)
    out_ref[plane] = mine_ref[...]
    line_gather(own, plane, planes, out_ref, send_sem, recv_sem)


def gather_tp(mine, collective_id):
    planes = lax.axis_size("tp")
    return pl.pallas_call(
        gather_tp_body,
        out_shape=jax.ShapeDtypeStruct((planes,) + mine.shape, mine.dtype),
        in_specs=[vmem()],
        out_specs=vmem(),
        scratch_shapes=[
            pltpu.SemaphoreType.DMA((2, planes)),
            pltpu.SemaphoreType.DMA((2, planes)),
        ],
        compiler_params=params(collective_id),
        cost_estimate=cost(0, 30_000_000),
        name="gather_tp",
    )(mine)


def row_tiles(rows):
    tile = 16
    return [(start, tile) for start in range(0, rows, tile)]


def ffn_math(plane, total, inputs, outputs, gathered):
    hidden_ref, inv_ref, dy_ref, gain_ref = inputs
    grad_ref, gains_ref = outputs
    gains_ref[...] = jnp.zeros_like(gains_ref)

    def tile(index, carry):
        rows = pl.ds(pl.multiple_of(index * 16, 16), 16)
        dn = total[rows, :]
        hidden = hidden_ref[plane, rows, :]
        inv = inv_ref[plane, rows, :]
        weighted = gain_ref[...] * dn
        mean = jnp.mean(weighted * hidden, axis=1, keepdims=True)
        grad = (
            keep_scale * dy_ref[plane, rows, :].astype(F32)
            + inv * weighted
            - hidden * (inv * inv * inv * mean)
        )
        grad_ref[rows, :] = grad
        gathered[plane, rows, :] = grad.astype(BF16)
        gains_ref[0:1, :] += jnp.sum(dn * hidden * inv, axis=0, keepdims=True)
        return carry

    lax.fori_loop(0, total.shape[0] // 16, tile, 0)


def mixed_math(plane, total, inputs, outputs, gathered):
    hidden_ref, x_ref = inputs

    def tile(index, carry):
        rows = pl.ds(pl.multiple_of(index * 16, 16), 16)
        x = x_ref[plane, rows, :].astype(F32)
        branch = (hidden_ref[plane, rows, :] - x) + total[rows, :]
        gathered[plane, rows, :] = (x + keep_scale * branch).astype(BF16)
        return carry

    lax.fori_loop(0, total.shape[0] // 16, tile, 0)


def attn_math(plane, total, inputs, outputs, gathered):
    x_ref, inv_ref, dy_ref, grad_ref, gain_ref, ffn_gains_ref = inputs
    (gains_ref,) = outputs
    gains_ref[...] = ffn_gains_ref[...]

    def tile(index, carry):
        rows = pl.ds(pl.multiple_of(index * 16, 16), 16)
        dn = total[rows, :]
        x = x_ref[plane, rows, :].astype(F32)
        inv = inv_ref[plane, rows, :]
        weighted = gain_ref[...] * dn
        mean = jnp.mean(weighted * x, axis=1, keepdims=True)
        grad = (
            (1.0 - keep_scale) * dy_ref[plane, rows, :].astype(F32)
            + grad_ref[rows, :]
            + inv * weighted
            - x * (inv * inv * inv * mean)
        )
        gathered[plane, rows, :] = grad.astype(BF16)
        gains_ref[1:2, :] += jnp.sum(dn * x * inv, axis=0, keepdims=True)
        return carry

    lax.fori_loop(0, total.shape[0] // 16, tile, 0)


def sum_tp_body(math_rule, inputs, *refs):
    part_ref, ins = refs[0], refs[1 : 1 + inputs]
    outs, scratch = refs[1 + inputs : -7], refs[-7:]
    gathered, outs = outs[0], outs[1:]
    total, send, recv, send_sem, recv_sem, gather_send_sem, gather_recv_sem = scratch
    planes = part_ref.shape[0]
    own, plane = lax.axis_index("tok"), lax.axis_index("tp")
    line_greet(own, plane, planes)
    line_reduce(own, plane, planes, part_ref, total, send, recv, send_sem, recv_sem)
    math_rule(plane, total, ins, outs, gathered)
    line_gather(own, plane, planes, gathered, gather_send_sem, gather_recv_sem)


def sum_tp(math_rule, part, inputs, out_shapes, collective_id, name):
    planes = lax.axis_size("tp")
    rows, width = part.shape
    shard = rows // planes
    part = part.reshape(planes, shard, width)
    return pl.pallas_call(
        functools.partial(sum_tp_body, math_rule, len(inputs)),
        out_shape=[jax.ShapeDtypeStruct((planes, shard, width), BF16)] + out_shapes,
        in_specs=[vmem()] * (1 + len(inputs)),
        out_specs=[vmem()] * (1 + len(out_shapes)),
        scratch_shapes=[
            pltpu.VMEM((shard, width), F32),
            pltpu.VMEM((2, planes, shard, width), part.dtype),
            pltpu.VMEM((2, planes, shard, width), part.dtype),
        ]
        + [pltpu.SemaphoreType.DMA((2, planes))] * 4,
        compiler_params=params(collective_id),
        cost_estimate=cost(0, 60_000_000),
        name=name,
    )(part, *inputs)


def swap(values, bit):
    devices = lax.axis_size("tok")
    return lax.ppermute(values, "tok", [(i, i ^ bit) for i in range(devices)])


def pick(values, index):
    return lax.dynamic_index_in_dim(values, index, 0, keepdims=False)


def halve(values, bits, own):
    for position, bit in enumerate(bits):
        side = (own // bit) % 2
        shape = values.shape
        lead = 2 ** (len(bits) - position - 1)
        values = values.reshape((2, lead) + shape[1:])
        got = swap(pick(values, 1 - side), bit)
        summed = pick(values, side).astype(F32) + got.astype(F32)
        values = summed if position == len(bits) - 1 else summed.astype(BF16)
    return values[0]


def scatter_weights(grad):
    devices = lax.axis_size("tok")
    own = lax.axis_index("tok")
    stages = stages_of("tok")
    rows, columns = grad.shape
    share = rows // devices
    grad = grad.reshape(devices // 2, 2, share, columns)
    core = own % 2
    mine = lax.dynamic_index_in_dim(grad, core, 1, keepdims=False)
    other = lax.dynamic_index_in_dim(grad, 1 - core, 1, keepdims=False)
    both = (mine.astype(F32) + swap(other, 1).astype(F32)).astype(BF16)
    bits = [1 << stage for stage in range(stages - 1, 0, -1)]
    upper, lower = both[:, : share // 2], both[:, share // 2 :]
    sides = len(bits)
    flipped = lower.reshape((2,) * sides + lower.shape[1:])
    flipped = flipped.transpose(tuple(range(sides - 1, -1, -1)) + (sides, sides + 1))
    flipped = flipped.reshape(lower.shape)
    return jnp.concatenate([halve(upper, bits, own), halve(flipped, bits[::-1], own)], axis=0)


def document_tables(doc_lengths, places):
    doc_ends = jnp.cumsum(doc_lengths, dtype=jnp.int32)
    doc_starts = doc_ends - doc_lengths
    doc_ids = jnp.sum(
        (places[:, None] >= doc_ends[None, :]).astype(jnp.int32), axis=1, dtype=jnp.int32
    )
    member = (
        doc_ids[:, None] == jnp.arange(doc_lengths.shape[0], dtype=jnp.int32)[None, :]
    ).astype(jnp.int32)
    positions = places - jnp.sum(member * doc_starts[None, :], axis=1, dtype=jnp.int32)
    return (doc_ids, positions, member)


def rotary_tables(positions, head_dim):
    half_dim = head_dim // 2
    freqs = jnp.exp(jnp.arange(half_dim, dtype=jnp.float32) * (-2.0 * math.log(10000.0) / head_dim))
    angles = positions.astype(jnp.float32)[:, None] * freqs[None, :]
    return (jnp.cos(angles), jnp.sin(angles))


def rotate(values, cosine, sine):
    half_dim = values.shape[-1] // 2
    former, latter = (values[..., :half_dim], values[..., half_dim:])
    cos_b, sin_b = (cosine[:, None, :], sine[:, None, :])
    return jnp.concatenate(
        [former * cos_b - latter * sin_b, latter * cos_b + former * sin_b], axis=-1
    )


def unrotate(values, cosine, sine):
    half_dim = values.shape[-1] // 2
    former, latter = (values[..., :half_dim], values[..., half_dim:])
    cos_b, sin_b = (cosine[:, None, :], sine[:, None, :])
    return jnp.concatenate(
        [former * cos_b + latter * sin_b, latter * cos_b - former * sin_b], axis=-1
    )


def over_rows(left, right, kind=F32):
    return lax.dot_general(
        left, right, (((0,), (0,)), ((), ())), preferred_element_type=jnp.float32
    ).astype(kind)


def over_columns(left, right):
    return lax.dot_general(
        left, right, (((1,), (1,)), ((), ())), preferred_element_type=jnp.float32
    )


def on_device(
    tokens,
    gain_attn,
    w_query,
    w_key,
    w_value,
    w_out,
    gain_ffn,
    w_gate,
    w_up,
    w_down,
    cotangent,
    doc_lengths,
    keep_flags,
):
    length = tokens.shape[0]
    model_width = tokens.shape[1]
    devices = lax.axis_size("tok")
    planes = lax.axis_size("tp")
    own_index = lax.axis_index("tok")
    blocks_here = length // BLOCK
    kept_here = blocks_here // 2
    total_blocks = blocks_here * devices
    kept_total = kept_here * devices
    rows = kept_here * BLOCK
    token_blocks = tokens.reshape(blocks_here, BLOCK, model_width)
    grad_blocks = cotangent.reshape(blocks_here, BLOCK, model_width)

    half_columns = model_width // 2
    out_half = lax.dynamic_slice_in_dim(w_out, (own_index % 2) * half_columns, half_columns, 1)
    out_half = lax.all_gather(out_half, "tp", axis=0, tiled=True)
    out_other = swap(out_half, 1)
    first_core = own_index % 2 == 0

    rows_x = deal(doc_lengths, keep_flags, token_blocks, 0).reshape(rows, model_width)
    rows_dy = deal(doc_lengths, keep_flags, grad_blocks, 1).reshape(rows, model_width)

    block_starts = jnp.arange(total_blocks, dtype=jnp.int32) * BLOCK
    block_docs, block_pos, block_member = document_tables(doc_lengths, block_starts)
    block_kept = jnp.sum(block_member * keep_flags[None, :], axis=1, dtype=jnp.int32)
    block_rank = jnp.cumsum(block_kept, dtype=jnp.int32) - block_kept
    rank_slots = jnp.arange(kept_total, dtype=jnp.int32)
    rank_match = ((block_rank[None, :] == rank_slots[:, None]) & (block_kept[None, :] == 1)).astype(
        jnp.int32
    )
    rank_block = jnp.sum(
        rank_match * jnp.arange(total_blocks, dtype=jnp.int32)[None, :], axis=1, dtype=jnp.int32
    )
    peer_ids = jnp.arange(devices, dtype=jnp.int32)
    own_ranks = own_index + jnp.arange(kept_here, dtype=jnp.int32) * devices
    own_blocks = jnp.take(rank_block, own_ranks)
    block_offsets = jnp.arange(BLOCK, dtype=jnp.int32)
    places = (own_blocks[:, None] * BLOCK + block_offsets[None, :]).reshape(rows)
    key_ranks = (
        peer_ids[:, None] + jnp.arange(kept_here, dtype=jnp.int32)[None, :] * devices
    ).reshape(kept_total)
    key_places = (
        jnp.take(rank_block, key_ranks)[:, None] * BLOCK + block_offsets[None, :]
    ).reshape(kept_total * BLOCK)
    doc_ids, positions, member = document_tables(doc_lengths, places)
    key_docs, key_pos, key_member = document_tables(doc_lengths, key_places)
    allowed = (doc_ids[:, None] == key_docs[None, :]) & (places[:, None] >= key_places[None, :])
    cosine, sine = rotary_tables(positions, HD)
    heads_here = w_query.shape[1] // HD
    groups_here = w_key.shape[1] // HD
    sharing = heads_here // groups_here
    score_scale = 1.0 / math.sqrt(HD)

    x_full = rows_x.astype(jnp.float32)
    inv_one = lax.rsqrt(jnp.mean(x_full * x_full, axis=1, keepdims=True) + norm_eps)
    normed_one = (x_full * inv_one * gain_attn).astype(jnp.bfloat16)
    query_pre = jnp.dot(normed_one, w_query, preferred_element_type=jnp.float32).reshape(
        rows, heads_here, HD
    )
    key_pre = jnp.dot(normed_one, w_key, preferred_element_type=jnp.float32).reshape(
        rows, groups_here, HD
    )
    value_pre = jnp.dot(normed_one, w_value, preferred_element_type=jnp.float32)
    queries = rotate(query_pre, cosine, sine).astype(jnp.bfloat16)
    keys_local = rotate(key_pre, cosine, sine).astype(jnp.bfloat16).reshape(rows, groups_here * HD)
    values_local = value_pre.astype(jnp.bfloat16)
    kv_width = groups_here * HD
    key_count = kept_total * BLOCK
    both_all = gather_tok(jnp.concatenate([keys_local, values_local], axis=1), 2)
    both_all = both_all.reshape(key_count, 2, groups_here, HD)
    keys_heads, values_heads = both_all[:, 0], both_all[:, 1]
    query_heads = queries.transpose(1, 0, 2)
    slot_of_head = jnp.arange(heads_here, dtype=jnp.int32) // sharing

    def head_scores(query, slot):
        keys_one = lax.dynamic_index_in_dim(keys_heads, slot, 1, keepdims=False)
        values_one = lax.dynamic_index_in_dim(values_heads, slot, 1, keepdims=False)
        scores = (
            jnp.einsum("qd,kd->qk", query, keys_one, preferred_element_type=jnp.float32)
            * score_scale
        )
        return (jnp.where(allowed, scores, -1e30), keys_one, values_one)

    def head_forward(pack):
        query, slot = pack
        scores, keys_one, values_one = head_scores(query, slot)
        peak = jnp.max(scores, axis=1, keepdims=True)
        weights = jnp.exp(scores - peak)
        totals = jnp.sum(weights, axis=1, keepdims=True)
        probs = (weights / totals).astype(jnp.bfloat16)
        return (jnp.dot(probs, values_one, preferred_element_type=jnp.float32), peak, totals)

    head_outs, peaks, totals = lax.map(head_forward, (query_heads, slot_of_head))
    attended = head_outs.transpose(1, 0, 2).reshape(rows, heads_here * HD).astype(jnp.bfloat16)

    attended_all = gather_tp(attended, 3)
    attended_all = attended_all.transpose(1, 0, 2).reshape(rows, planes * heads_here * HD)
    mine = jnp.dot(attended_all, out_half, preferred_element_type=jnp.float32)
    other = jnp.dot(attended_all, out_other, preferred_element_type=jnp.float32)
    branch_attn = jnp.concatenate(
        [jnp.where(first_core, mine, other), jnp.where(first_core, other, mine)], axis=1
    )
    hidden_res = x_full + branch_attn
    inv_two = lax.rsqrt(jnp.mean(hidden_res * hidden_res, axis=1, keepdims=True) + norm_eps)
    normed_two = (hidden_res * inv_two * gain_ffn).astype(jnp.bfloat16)
    gate = jnp.dot(normed_two, w_gate, preferred_element_type=jnp.float32)
    upper = jnp.dot(normed_two, w_up, preferred_element_type=jnp.float32)
    sigma = jax.nn.sigmoid(gate)
    swish = gate * sigma
    inner = (swish * upper).astype(jnp.bfloat16)

    grad_m = (keep_scale * rows_dy.astype(jnp.float32)).astype(jnp.bfloat16)
    grad_inner = over_columns(grad_m, w_down)
    grad_gate_pre = (grad_inner * upper * sigma * (1.0 + gate * (1.0 - sigma))).astype(jnp.bfloat16)
    grad_up_pre = (grad_inner * swish).astype(jnp.bfloat16)
    part_two = (
        over_columns(grad_gate_pre, w_gate) + over_columns(grad_up_pre, w_up)
    ).astype(jnp.bfloat16)

    shard = rows // planes
    by_plane = lambda array: array.reshape(planes, shard, array.shape[1])
    x_planes, dy_planes = by_plane(rows_x), by_plane(rows_dy)
    hidden_planes = by_plane(hidden_res)
    grad_a, grad_hidden, gains_ffn = sum_tp(
        ffn_math,
        part_two,
        (hidden_planes, by_plane(inv_two), dy_planes, gain_ffn.reshape(1, -1)),
        [
            jax.ShapeDtypeStruct((shard, model_width), F32),
            jax.ShapeDtypeStruct((8, model_width), F32),
        ],
        4,
        "sum_ffn",
    )
    grad_a = grad_a.reshape(rows, model_width)

    grad_gate = scatter_weights(over_rows(normed_two, grad_gate_pre, BF16))
    grad_up = scatter_weights(over_rows(normed_two, grad_up_pre, BF16))
    grad_down = scatter_weights(over_rows(grad_m, inner, BF16)).T

    grad_attended = over_columns(grad_a, w_out).astype(jnp.bfloat16)
    grad_heads = grad_attended.reshape(rows, heads_here, HD).transpose(1, 0, 2)

    def head_backward(pack):
        query, grad_head, peak, total, slot = pack
        scores, keys_one, values_one = head_scores(query, slot)
        probs = jnp.exp(scores - peak) / total
        probs_low = probs.astype(jnp.bfloat16)
        grad_probs = jnp.einsum(
            "qd,kd->qk", grad_head, values_one, preferred_element_type=jnp.float32
        )
        delta = jnp.sum(probs * grad_probs, axis=1, keepdims=True)
        grad_scores = (probs * (grad_probs - delta)).astype(jnp.bfloat16)
        grad_query_head = (
            jnp.dot(grad_scores, keys_one, preferred_element_type=jnp.float32) * score_scale
        )
        grad_keys_head = over_rows(grad_scores, query) * score_scale
        grad_values_head = over_rows(probs_low, grad_head)
        return (grad_query_head, grad_keys_head, grad_values_head)

    grad_q_heads, grad_k_heads, grad_v_heads = lax.map(
        head_backward, (query_heads, grad_heads, peaks, totals, slot_of_head)
    )
    grad_k_all = (
        grad_k_heads.reshape(groups_here, sharing, key_count, HD)
        .sum(axis=1)
        .transpose(1, 0, 2)
        .reshape(key_count, kv_width)
    )
    grad_v_all = (
        grad_v_heads.reshape(groups_here, sharing, key_count, HD)
        .sum(axis=1)
        .transpose(1, 0, 2)
        .reshape(key_count, kv_width)
    )
    grad_kv = jnp.concatenate([grad_k_all, grad_v_all], axis=1).astype(BF16)
    grad_kv = scatter_tok(grad_kv.reshape(devices, rows, 2 * kv_width), 5)
    grad_k_own, grad_v_own = grad_kv[:, :kv_width], grad_kv[:, kv_width:]
    grad_query_pre = (
        unrotate(grad_q_heads.transpose(1, 0, 2), cosine, sine)
        .reshape(rows, heads_here * HD)
        .astype(jnp.bfloat16)
    )
    grad_key_pre = (
        unrotate(grad_k_own.reshape(rows, groups_here, HD), cosine, sine)
        .reshape(rows, kv_width)
        .astype(jnp.bfloat16)
    )
    grad_value_pre = grad_v_own.astype(jnp.bfloat16)
    part_one = (
        over_columns(grad_query_pre, w_query)
        + over_columns(grad_key_pre, w_key)
        + over_columns(grad_value_pre, w_value)
    ).astype(jnp.bfloat16)
    grad_rows, gains = sum_tp(
        attn_math,
        part_one,
        (x_planes, by_plane(inv_one), dy_planes, grad_hidden, gain_attn.reshape(1, -1), gains_ffn),
        [jax.ShapeDtypeStruct((8, model_width), F32)],
        6,
        "sum_attn",
    )
    gains = lax.psum(gains, "tp")

    mixed_rows = sum_tp(
        mixed_math,
        jnp.dot(inner, w_down, preferred_element_type=jnp.float32).astype(jnp.bfloat16),
        (hidden_planes, x_planes),
        [],
        7,
        "sum_mixed",
    )[0]
    mixed, _ = undeal(
        doc_lengths,
        keep_flags,
        mixed_rows.reshape(kept_here, BLOCK, model_width),
        token_blocks,
        gains_ffn,
        8,
    )
    token_grad, gain_sums = undeal(
        doc_lengths,
        keep_flags,
        grad_rows.reshape(kept_here, BLOCK, model_width),
        grad_blocks,
        gains,
        9,
    )
    own_share = model_width // devices
    if gain_sums.shape[1] != own_share:
        gain_sums = lax.dynamic_slice_in_dim(gain_sums, own_index * own_share, own_share, 1)

    attn_grads = jnp.concatenate(
        [
            over_rows(normed_one, grad_query_pre, BF16),
            over_rows(normed_one, grad_key_pre, BF16),
            over_rows(normed_one, grad_value_pre, BF16),
            over_rows(grad_a, attended, BF16),
        ],
        axis=1,
    )
    attn_grads = scatter_weights(attn_grads)
    wide, thin = w_query.shape[1], w_key.shape[1]
    grad_query = attn_grads[:, :wide]
    grad_key = attn_grads[:, wide : wide + thin]
    grad_value = attn_grads[:, wide + thin : wide + 2 * thin]
    grad_out = attn_grads[:, wide + 2 * thin :].T

    return (
        mixed.reshape(length, model_width),
        token_grad.reshape(length, model_width),
        gain_sums[1],
        grad_query,
        grad_key,
        grad_value,
        grad_out,
        gain_sums[0],
        grad_gate,
        grad_up,
        grad_down,
    )


def solution(mesh):
    placed = (
        P("tok", None),
        P(),
        P(None, "tp"),
        P(None, "tp"),
        P(None, "tp"),
        P("tp", None),
        P(),
        P(None, "tp"),
        P(None, "tp"),
        P("tp", None),
        P("tok", None),
        P(),
        P(),
    )
    return jax.shard_map(
        on_device,
        mesh=mesh,
        in_specs=placed,
        out_specs=(
            P("tok", None),
            P("tok", None),
            P("tok"),
            P("tok", "tp"),
            P("tok", "tp"),
            P("tok", "tp"),
            P("tp", "tok"),
            P("tok"),
            P("tok", "tp"),
            P("tok", "tp"),
            P("tp", "tok"),
        ),
        check_vma=False,
    )
```

```python
import functools
import math

import jax
import jax.numpy as jnp
from jax import lax
from jax.experimental import pallas as pl
from jax.experimental.pallas import tpu as pltpu
from jax.sharding import PartitionSpec as P

HD = 128
BLOCK = 128
SLOTS = 3
CHUNKS = 8
MESH = pl.DeviceIdType.MESH
VMEM_BYTES = 60 * 2**20

norm_eps = 1e-05
keep_scale = 2.0
F32 = jnp.float32
BF16 = jnp.bfloat16


def vmem():
    return pl.BlockSpec(memory_space=pltpu.VMEM)


def smem():
    return pl.BlockSpec(memory_space=pltpu.SMEM)


def params(collective_id):
    return pltpu.CompilerParams(
        collective_id=collective_id, has_side_effects=True, vmem_limit_bytes=VMEM_BYTES
    )


def cost(flops, moved):
    return pl.CostEstimate(flops=flops, bytes_accessed=moved, transcendentals=0)


def greet(peers, line=False):
    barrier = pltpu.get_barrier_semaphore()
    for peer in peers:
        pl.semaphore_signal(barrier, inc=1, device_id=peer, device_id_type=MESH)
    if not line:
        pl.semaphore_wait(barrier, len(peers))
        return
    own, plane = lax.axis_index("tok"), lax.axis_index("tp")
    last = lax.axis_size("tp") - 1

    @pl.when(plane > 0)
    def _():
        pl.semaphore_signal(barrier, inc=1, device_id=(own, plane - 1), device_id_type=MESH)

    @pl.when(plane < last)
    def _():
        pl.semaphore_signal(barrier, inc=1, device_id=(own, plane + 1), device_id_type=MESH)

    end = (plane == 0) | (plane == last)

    @pl.when(end)
    def _():
        pl.semaphore_wait(barrier, len(peers) + 1)

    @pl.when(jnp.logical_not(end))
    def _():
        pl.semaphore_wait(barrier, len(peers) + 2)


def run(*flows):
    waiting = [[next(flow), number, flow] for number, flow in enumerate(flows)]
    while waiting:
        waiting.sort(key=lambda entry: entry[:2])
        entry = waiting[0]
        try:
            entry[0] = next(entry[2])
        except StopIteration:
            waiting.pop(0)


def deal_tables(own, stages, blocks_here, lens_ref, flags_ref):
    def kept_before(place):
        total, start = jnp.int32(0), jnp.int32(0)
        for doc in range(lens_ref.shape[0]):
            blocks = lens_ref[doc] // BLOCK
            total = total + flags_ref[doc] * jnp.clip(place - start, 0, blocks)
            start = start + blocks
        return total

    def edges(stage):
        first = (own >> stage) << stage
        return (
            kept_before(first * blocks_here),
            kept_before((first + (1 << stage)) * blocks_here),
        )

    def located(stage):
        if stage == 0:
            ends = [kept_before(own * blocks_here + i + 1) for i in range(blocks_here)]

            def place(rank):
                index = jnp.int32(0)
                for end in ends:
                    index = index + (end <= rank).astype(jnp.int32)
                return index

            return place
        mine = (own >> (stage - 1)) << (stage - 1)
        low, high = edges(stage - 1)
        other = kept_before((mine ^ (1 << (stage - 1))) * blocks_here)

        def place(rank):
            inside = (rank >= low) & (rank < high)
            return jnp.where(inside, (rank - low) >> stage, SLOTS + ((rank - other) >> stage))

        return place

    keeps, sends = [], []
    for stage in range(stages):
        low, high = edges(stage)
        place = located(stage)
        period = 1 << (stage + 1)
        for table, target in ((keeps, own), (sends, own ^ (1 << stage))):
            first = low + ((target - low) & (period - 1))
            row = []
            for slot in range(SLOTS):
                rank = first + period * slot
                row.append(jnp.where(rank < high, place(rank), -1))
            table.append(row)
    place = located(stages)
    finals = [place(own + (slot << stages)) for slot in range(SLOTS)]
    return keeps, sends, finals


def choose(index, options, default=None):
    value = options[0] if default is None else default
    for number, option in enumerate(options):
        if number == 0 and default is None:
            continue
        value = jnp.where(index == number, option, value)
    return value


def bit_peers(stages):
    own, plane = lax.axis_index("tok"), lax.axis_index("tp")
    return [(own ^ (1 << stage), plane) for stage in range(stages)]


def deal_flow(lens_ref, flags_ref, own_ref, out_ref, scratch, pace=4.3):
    keep, send, recv, send_sem, recv_sem = scratch
    stages = keep.shape[0]
    own = lax.axis_index("tok")
    blocks_here = own_ref.shape[0]
    rows = BLOCK // CHUNKS
    peers = bit_peers(stages)
    keeps, sends, finals = deal_tables(own, stages, blocks_here, lens_ref, flags_ref)

    def copy(stage, chunk):
        return pltpu.make_async_remote_copy(
            src_ref=send.at[stage, chunk],
            dst_ref=recv.at[stage, chunk],
            send_sem=send_sem.at[stage, chunk],
            recv_sem=recv_sem.at[stage, chunk],
            device_id=peers[stage],
            device_id_type=MESH,
        )

    def held(stage, chunk):
        if stage == 0:
            return [own_ref[i, pl.ds(chunk * rows, rows), :] for i in range(blocks_here)]
        before = stage - 1
        return [keep[before, chunk, i] for i in range(SLOTS)] + [
            recv[before, chunk, i] for i in range(SLOTS)
        ]

    for stage in range(stages):
        for chunk in range(CHUNKS):
            yield 0.0 if stage == 0 else 1 + 0.4 * chunk + pace * (stage - 1) * (chunk + 1)
            if stage > 0:
                copy(stage - 1, chunk).wait_recv()
            options = held(stage, chunk)
            for slot in range(SLOTS):
                send[stage, chunk, slot] = choose(sends[stage][slot], options)
            copy(stage, chunk).start()
            for slot in range(SLOTS):
                keep[stage, chunk, slot] = choose(keeps[stage][slot], options)
    for chunk in range(CHUNKS):
        yield 3 + pace * (chunk + stages - 1)
        copy(stages - 1, chunk).wait_recv()
        options = held(stages, chunk)
        for slot in range(SLOTS):
            out_ref[slot, pl.ds(chunk * rows, rows), :] = choose(finals[slot], options)
    yield 1e6

    def drain(chunk, carry):
        for stage in range(stages):
            copy(stage, chunk).wait_send()
        return carry

    lax.fori_loop(0, CHUNKS, drain, 0)


def deal_scratch(stages, width, kind):
    moved = (stages, CHUNKS, SLOTS, BLOCK // CHUNKS, width)
    return [pltpu.VMEM(moved, kind)] * 3 + [pltpu.SemaphoreType.DMA((stages, CHUNKS))] * 2


def stages_of(axis):
    return int(math.log2(lax.axis_size(axis)))


def deal_body(lens_ref, flags_ref, own_ref, out_ref, *scratch):
    greet(bit_peers(scratch[0].shape[0]))
    run(deal_flow(lens_ref, flags_ref, own_ref, out_ref, scratch))


def deal(doc_lengths, keep_flags, blocks, collective_id):
    width = blocks.shape[2]
    return pl.pallas_call(
        deal_body,
        out_shape=jax.ShapeDtypeStruct((SLOTS, BLOCK, width), blocks.dtype),
        in_specs=[smem(), smem(), vmem()],
        out_specs=vmem(),
        scratch_shapes=deal_scratch(stages_of("tok"), width, blocks.dtype),
        compiler_params=params(collective_id),
        cost_estimate=cost(0, 40_000_000),
        name="deal",
    )(doc_lengths, keep_flags, blocks)


def deal_gather_body(lens_ref, flags_ref, own_ref, mine_ref, out_ref, all_ref, *scratch):
    dealing, sems = scratch[:5], scratch[5:]
    own, plane, planes = lax.axis_index("tok"), lax.axis_index("tp"), all_ref.shape[0]
    greet(bit_peers(dealing[0].shape[0]), line=True)
    all_ref[plane] = mine_ref[...]
    run(
        line_gather(own, plane, planes, [(all_ref,) + sems], 0.0, 8.5),
        deal_flow(lens_ref, flags_ref, own_ref, out_ref, dealing),
    )


def deal_gather(doc_lengths, keep_flags, blocks, mine, collective_id):
    width = blocks.shape[2]
    planes = lax.axis_size("tp")
    return pl.pallas_call(
        deal_gather_body,
        out_shape=(
            jax.ShapeDtypeStruct((SLOTS, BLOCK, width), blocks.dtype),
            jax.ShapeDtypeStruct((planes,) + mine.shape, mine.dtype),
        ),
        in_specs=[smem(), smem(), vmem(), vmem()],
        out_specs=(vmem(), vmem()),
        scratch_shapes=deal_scratch(stages_of("tok"), width, blocks.dtype) + line_sems(planes),
        compiler_params=params(collective_id),
        cost_estimate=cost(0, 40_000_000),
        name="deal_gather",
    )(doc_lengths, keep_flags, blocks, mine)


def undeal_flow(lens_ref, flags_ref, kept_ref, home_ref, out_ref, scratch, pace=4.3):
    hold, recv, send_sem, recv_sem = scratch
    stages = recv.shape[0]
    own = lax.axis_index("tok")
    blocks_here = home_ref.shape[0]
    rows = BLOCK // CHUNKS
    peers = bit_peers(stages)
    keeps, sends, finals = deal_tables(own, stages, blocks_here, lens_ref, flags_ref)

    def copy(stage, chunk):
        return pltpu.make_async_remote_copy(
            src_ref=hold.at[stage, chunk, pl.ds(SLOTS, SLOTS)],
            dst_ref=recv.at[stage, chunk],
            send_sem=send_sem.at[stage, chunk],
            recv_sem=recv_sem.at[stage, chunk],
            device_id=peers[stage],
            device_id_type=MESH,
        )

    def pick_place(places, options, place, value):
        for index, option in zip(places, options):
            value = jnp.where(index == place, option, value)
        return value

    last = stages - 1
    for stage in range(last, -2, -1):
        for chunk in range(CHUNKS):
            yield 0.0 if stage == last else 1 + pace * (chunk + last - stage - (stage < 0))
            span = pl.ds(chunk * rows, rows)
            if stage == last:
                options = [kept_ref[slot, span, :] for slot in range(SLOTS)]
                places = finals
            else:
                copy(stage + 1, chunk).wait_recv()
                options = [hold[stage + 1, chunk, i] for i in range(SLOTS)] + [
                    recv[stage + 1, chunk, i] for i in range(SLOTS)
                ]
                places = keeps[stage + 1] + sends[stage + 1]
            if stage < 0:
                for place in range(blocks_here):
                    home = home_ref[place, span, :]
                    out_ref[place, span, :] = pick_place(places, options, place, home)
            else:
                for place in range(SLOTS, 2 * SLOTS):
                    hold[stage, chunk, place] = pick_place(places, options, place, options[0])
                copy(stage, chunk).start()
                for place in range(SLOTS):
                    hold[stage, chunk, place] = pick_place(places, options, place, options[0])
    yield 1e6

    def drain(chunk, carry):
        for stage in range(stages):
            copy(stage, chunk).wait_send()
        return carry

    lax.fori_loop(0, CHUNKS, drain, 0)


def undeal_scratch(stages, width, kind):
    rows = BLOCK // CHUNKS
    return [
        pltpu.VMEM((stages, CHUNKS, 2 * SLOTS, rows, width), kind),
        pltpu.VMEM((stages, CHUNKS, SLOTS, rows, width), kind),
    ] + [pltpu.SemaphoreType.DMA((stages, CHUNKS))] * 2


def undeal_body(lens_ref, flags_ref, kept_ref, home_ref, gains_ref, out_ref, sum_ref, *scratch):
    undealing = scratch[:4]
    gain_recv, gain_send_sem, gain_recv_sem = scratch[4:]
    own, plane = lax.axis_index("tok"), lax.axis_index("tp")
    devices = gain_recv.shape[0]
    share = sum_ref.shape[1]
    greet([(own ^ step, plane) for step in range(1, devices)])

    def portion(there):
        if share % 128 == 0 and share < gains_ref.shape[1]:
            return gains_ref.at[:, pl.ds(pl.multiple_of(there * share, share), share)]
        return gains_ref

    def gain_copy(step):
        there = own ^ step
        return pltpu.make_async_remote_copy(
            src_ref=portion(there),
            dst_ref=gain_recv.at[step],
            send_sem=gain_send_sem.at[step],
            recv_sem=gain_recv_sem.at[step],
            device_id=(there, plane),
            device_id_type=MESH,
        )

    for step in range(1, devices):
        gain_copy(step).start()
    run(undeal_flow(lens_ref, flags_ref, kept_ref, home_ref, out_ref, undealing))
    total = portion(own)[...]
    for step in range(1, devices):
        gain_copy(step).wait()
        total = total + gain_recv[step]
    sum_ref[...] = total


def undeal(doc_lengths, keep_flags, kept, home, gains, collective_id):
    stages = stages_of("tok")
    devices = 1 << stages
    width = kept.shape[2]
    share = width // devices
    share = share if share % 128 == 0 else width
    return pl.pallas_call(
        undeal_body,
        out_shape=(
            jax.ShapeDtypeStruct(home.shape, home.dtype),
            jax.ShapeDtypeStruct((8, share), F32),
        ),
        in_specs=[smem(), smem(), vmem(), vmem(), vmem()],
        out_specs=(vmem(), vmem()),
        scratch_shapes=undeal_scratch(stages, width, kept.dtype)
        + [
            pltpu.VMEM((devices, 8, share), F32),
            pltpu.SemaphoreType.DMA((devices,)),
            pltpu.SemaphoreType.DMA((devices,)),
        ],
        compiler_params=params(collective_id),
        cost_estimate=cost(0, 40_000_000),
        name="undeal",
    )(doc_lengths, keep_flags, kept, home, gains)


def gather_tok_body(mine_ref, out_ref, send_sem, recv_sem, relay_send_sem, relay_recv_sem):
    devices = out_ref.shape[0]
    chips = devices // 2
    own = lax.axis_index("tok")
    plane = lax.axis_index("tp")
    partner = (own ^ 1, plane)
    greet([partner] + [(own ^ (2 * step), plane) for step in range(1, chips)])

    def copy(step):
        return pltpu.make_async_remote_copy(
            src_ref=mine_ref,
            dst_ref=out_ref.at[own],
            send_sem=send_sem.at[step],
            recv_sem=recv_sem.at[step],
            device_id=(own ^ (2 * step), plane),
            device_id_type=MESH,
        )

    def relay(step):
        return pltpu.make_async_remote_copy(
            src_ref=mine_ref if step == 0 else out_ref.at[own ^ (2 * step)],
            dst_ref=out_ref.at[own ^ (2 * step)],
            send_sem=relay_send_sem.at[step],
            recv_sem=relay_recv_sem.at[step],
            device_id=partner,
            device_id_type=MESH,
        )

    for step in range(1, chips):
        copy(step).start()
    relay(0).start()
    out_ref[own] = mine_ref[...]
    for step in range(1, chips):
        copy(step).wait_recv()
        relay(step).start()
    for step in range(chips):
        relay(step).wait()
    for step in range(1, chips):
        copy(step).wait_send()


def gather_tok(mine, collective_id):
    devices = lax.axis_size("tok")
    chips = devices // 2
    return pl.pallas_call(
        gather_tok_body,
        out_shape=jax.ShapeDtypeStruct((devices,) + mine.shape, mine.dtype),
        in_specs=[vmem()],
        out_specs=vmem(),
        scratch_shapes=[pltpu.SemaphoreType.DMA((chips,))] * 4,
        compiler_params=params(collective_id),
        cost_estimate=cost(0, 10_000_000),
        name="gather_tok",
    )(mine)


def scatter_tok_body(
    part_ref, out_ref, core_recv, held, recv, core_send_sem, core_recv_sem, send_sem, recv_sem
):
    devices = part_ref.shape[0]
    chips = devices // 2
    own = lax.axis_index("tok")
    plane = lax.axis_index("tp")
    partner = (own ^ 1, plane)
    greet([partner] + [(own ^ (2 * step), plane) for step in range(1, chips)])

    def core_copy(step):
        return pltpu.make_async_remote_copy(
            src_ref=part_ref.at[own ^ (2 * step) ^ 1],
            dst_ref=core_recv.at[step],
            send_sem=core_send_sem.at[step],
            recv_sem=core_recv_sem.at[step],
            device_id=partner,
            device_id_type=MESH,
        )

    def copy(step):
        return pltpu.make_async_remote_copy(
            src_ref=held.at[step],
            dst_ref=recv.at[step],
            send_sem=send_sem.at[step],
            recv_sem=recv_sem.at[step],
            device_id=(own ^ (2 * step), plane),
            device_id_type=MESH,
        )

    order = list(range(chips - 1, -1, -1))
    for step in order:
        core_copy(step).start()
    for step in order:
        core_copy(step).wait_recv()
        total = part_ref[own ^ (2 * step)].astype(F32) + core_recv[step].astype(F32)
        if step > 0:
            held[step] = total.astype(held.dtype)
            copy(step).start()
        else:
            out_ref[...] = total
    for step in range(1, chips):
        copy(step).wait_recv()
        out_ref[...] += recv[step].astype(F32)
    for step in range(1, chips):
        copy(step).wait_send()
    for step in range(chips):
        core_copy(step).wait_send()


def scatter_tok(part, collective_id):
    devices = part.shape[0]
    chips = devices // 2
    shard = part.shape[1:]
    return pl.pallas_call(
        scatter_tok_body,
        out_shape=jax.ShapeDtypeStruct(shard, F32),
        in_specs=[vmem()],
        out_specs=vmem(),
        scratch_shapes=[
            pltpu.VMEM((chips,) + shard, part.dtype),
            pltpu.VMEM((chips,) + shard, part.dtype),
            pltpu.VMEM((chips,) + shard, part.dtype),
        ]
        + [pltpu.SemaphoreType.DMA((chips,))] * 4,
        compiler_params=params(collective_id),
        cost_estimate=cost(0, 10_000_000),
        name="scatter_tok",
    )(part)


def line_sems(planes):
    return [pltpu.SemaphoreType.DMA((2, planes))] * 2


def line_copy(own, plane, step, source, target, send_sem, recv_sem, index):
    side = 0 if step > 0 else 1
    return pltpu.make_async_remote_copy(
        src_ref=source,
        dst_ref=target,
        send_sem=send_sem.at[side, index],
        recv_sem=recv_sem.at[side, index],
        device_id=(own, plane + step),
        device_id_type=MESH,
    )


def line_gather(own, plane, planes, arrays, start, pace):
    last = planes - 1

    def right(array, index):
        out, send_sem, recv_sem = array
        return line_copy(own, plane, 1, out.at[index], out.at[index], send_sem, recv_sem, index)

    def left(array, index):
        out, send_sem, recv_sem = array
        return line_copy(own, plane, -1, out.at[index], out.at[index], send_sem, recv_sem, index)

    for step in range(1, planes + 1):
        yield start + pace * (step - 1)
        before, after = plane - (step - 1), plane + (step - 1)

        @pl.when(before >= 0)
        def _():
            for array in arrays:
                if step > 1:
                    right(array, before).wait_recv()
                if step < planes:

                    @pl.when(plane < last)
                    def _():
                        right(array, before).start()

        @pl.when(after <= last)
        def _():
            for array in arrays:
                if step > 1:
                    left(array, after).wait_recv()
                if step < planes:

                    @pl.when(plane > 0)
                    def _():
                        left(array, after).start()

    for index in range(planes):

        @pl.when((index <= plane) & (plane < last))
        def _():
            for array in arrays:
                right(array, index).wait_send()

        @pl.when((index >= plane) & (plane > 0))
        def _():
            for array in arrays:
                left(array, index).wait_send()


def line_reduce(own, plane, planes, part, total, send, recv, send_sem, recv_sem, start, pace):
    last = planes - 1

    def right(index):
        return line_copy(
            own, plane, 1, send.at[index], recv.at[index], send_sem, recv_sem, index
        )

    def left(index):
        slot = jnp.where(index == plane - 1, planes, index)
        return line_copy(
            own, plane, -1, send.at[index], recv.at[slot], send_sem, recv_sem, index
        )

    def add(index):
        send[index] = (part[index].astype(F32) + recv[index].astype(F32)).astype(send.dtype)

    for step in range(1, planes):
        yield start + pace * (step - 1)
        upper, lower = planes - step + plane, step - planes + plane

        @pl.when((upper <= last) & (plane < last))
        def _():
            @pl.when(plane == 0)
            def _():
                send[upper] = part[upper]

            @pl.when(plane > 0)
            def _():
                right(upper).wait_recv()
                add(upper)

            right(upper).start()

        @pl.when((lower >= 0) & (plane > 0))
        def _():
            @pl.when(plane == last)
            def _():
                send[lower] = part[lower]

            @pl.when(plane < last)
            def _():
                left(lower).wait_recv()
                add(lower)

            left(lower).start()

    yield start + pace * (planes - 1)
    total[...] = part[plane].astype(F32)

    @pl.when(plane > 0)
    def _():
        right(plane).wait_recv()
        total[...] += recv[plane].astype(F32)

    @pl.when(plane < last)
    def _():
        left(plane).wait_recv()
        total[...] += recv[planes].astype(F32)

    for index in range(planes):

        @pl.when((index > plane) & (plane < last))
        def _():
            right(index).wait_send()

        @pl.when((index < plane) & (plane > 0))
        def _():
            left(index).wait_send()


def sum_flow(part_ref, gathered, scratch, math_rule, start=0.0, pace=8.7, extra=None):
    total, send, recv, send_sem, recv_sem, gather_send_sem, gather_recv_sem = scratch
    planes = part_ref.shape[0]
    own, plane = lax.axis_index("tok"), lax.axis_index("tp")
    yield from line_reduce(
        own, plane, planes, part_ref, total, send, recv, send_sem, recv_sem, start, pace
    )
    math_rule(plane, total, gathered)
    arrays = [(gathered, gather_send_sem, gather_recv_sem)] + ([] if extra is None else [extra])
    yield from line_gather(
        own, plane, planes, arrays, start + pace * (planes - 1), pace
    )


def sum_scratch(planes, shard, width, kind):
    return [
        pltpu.VMEM((shard, width), F32),
        pltpu.VMEM((planes, shard, width), kind),
        pltpu.VMEM((planes + 1, shard, width), kind),
    ] + line_sems(planes) * 2


def ffn_math(hidden_ref, inv_ref, dy_ref, gain_ref, grad_ref, gains_ref):
    def rule(plane, total, gathered):
        gains_ref[...] = jnp.zeros_like(gains_ref)

        def tile(index, carry):
            rows = pl.ds(pl.multiple_of(index * 16, 16), 16)
            dn = total[rows, :]
            hidden = hidden_ref[plane, rows, :]
            inv = inv_ref[plane, rows, :]
            weighted = gain_ref[...] * dn
            mean = jnp.mean(weighted * hidden, axis=1, keepdims=True)
            grad = (
                keep_scale * dy_ref[plane, rows, :].astype(F32)
                + inv * weighted
                - hidden * (inv * inv * inv * mean)
            )
            grad_ref[rows, :] = grad
            gathered[plane, rows, :] = grad.astype(BF16)
            gains_ref[0:1, :] += jnp.sum(dn * hidden * inv, axis=0, keepdims=True)
            return carry

        lax.fori_loop(0, total.shape[0] // 16, tile, 0)

    return rule


def mixed_math(hidden_ref, x_ref):
    def rule(plane, total, gathered):
        def tile(index, carry):
            rows = pl.ds(pl.multiple_of(index * 16, 16), 16)
            x = x_ref[plane, rows, :].astype(F32)
            branch = (hidden_ref[plane, rows, :] - x) + total[rows, :]
            gathered[plane, rows, :] = (x + keep_scale * branch).astype(BF16)
            return carry

        lax.fori_loop(0, total.shape[0] // 16, tile, 0)

    return rule


def attn_math(x_ref, inv_ref, dy_ref, grad_ref, gain_ref, ffn_gains_ref, gains_all):
    def rule(plane, total, gathered):
        gains_all[plane] = ffn_gains_ref[...]

        def tile(index, carry):
            rows = pl.ds(pl.multiple_of(index * 16, 16), 16)
            dn = total[rows, :]
            x = x_ref[plane, rows, :].astype(F32)
            inv = inv_ref[plane, rows, :]
            weighted = gain_ref[...] * dn
            mean = jnp.mean(weighted * x, axis=1, keepdims=True)
            grad = (
                (1.0 - keep_scale) * dy_ref[plane, rows, :].astype(F32)
                + grad_ref[rows, :]
                + inv * weighted
                - x * (inv * inv * inv * mean)
            )
            gathered[plane, rows, :] = grad.astype(BF16)
            gains_all[plane, 1:2, :] += jnp.sum(dn * x * inv, axis=0, keepdims=True)
            return carry

        lax.fori_loop(0, total.shape[0] // 16, tile, 0)

    return rule


def spread_flow(units, outs, scratch, pace):
    own, plane = lax.axis_index("tok"), lax.axis_index("tp")
    count = len(units)
    boxes, inboxes, core_inboxes = scratch[:count], scratch[count : 2 * count], scratch[2 * count : 3 * count]
    core_send_sem, core_recv_sem, send_sem, recv_sem = scratch[3 * count :]
    chips = boxes[0].shape[0]
    bits = [1 << i for i in range(int(math.log2(chips)))]
    orders = (bits, bits[::-1])
    stages = len(bits)

    def core_copy(unit, chip):
        return pltpu.make_async_remote_copy(
            src_ref=boxes[unit].at[chip],
            dst_ref=core_inboxes[unit].at[chip],
            send_sem=core_send_sem.at[unit, chip],
            recv_sem=core_recv_sem.at[unit, chip],
            device_id=(own ^ 1, plane),
            device_id_type=MESH,
        )

    def active(half, stage):
        gone = orders[half][:stage]
        return [chip for chip in range(chips) if all(chip & bit == 0 for bit in gone)]

    def slot(stage, half, chip):
        before = sum(chips >> (earlier + 1) for earlier in range(stage))
        return before + active(half, stage + 1).index(chip)

    def copy(unit, half, stage, chip):
        bit = orders[half][stage]
        there = slot(stage, half, chip)
        return pltpu.make_async_remote_copy(
            src_ref=boxes[unit].at[chip ^ bit, half],
            dst_ref=inboxes[unit].at[there, half],
            send_sem=send_sem.at[unit, half, there],
            recv_sem=recv_sem.at[unit, half, there],
            device_id=(own ^ (2 * bit), plane),
            device_id_type=MESH,
        )

    def offer(unit):
        def step(chip, carry):
            for half in range(2):
                term = units[unit]((own ^ (2 * chip)) ^ 1, half)
                boxes[unit][chip, half] = term.astype(BF16)
            core_copy(unit, chip).start()
            return carry

        lax.fori_loop(0, chips, step, 0)

    def collect(unit):
        def step(chip, carry):
            core_copy(unit, chip).wait()
            for half in range(2):
                term = units[unit](own ^ (2 * chip), half)
                term = term + core_inboxes[unit][chip, half].astype(F32)
                boxes[unit][chip, half] = term.astype(BF16)
            return carry

        lax.fori_loop(0, chips, step, 0)
        send(unit, 0)

    def send(unit, stage):
        for half in range(2):
            for chip in active(half, stage + 1):
                copy(unit, half, stage, chip).start()

    def take(unit, stage):
        for half in range(2):
            for chip in active(half, stage + 1):
                copy(unit, half, stage, chip).wait_recv()
                got = inboxes[unit][slot(stage, half, chip), half].astype(F32)
                total = boxes[unit][chip, half].astype(F32) + got
                if stage < stages - 1:
                    boxes[unit][chip, half] = total.astype(BF16)
                else:
                    rows = total.shape[0]
                    outs[unit][half * rows : (half + 1) * rows, :] = total
        if stage < stages - 1:
            send(unit, stage + 1)

    yield 0.1
    offer(0)
    for unit in range(count):
        if unit + 1 < count:
            yield 1.0 + 2 * unit
            offer(unit + 1)
        yield 2.0 + 2 * unit
        collect(unit)
    for stage in range(stages):
        for unit in range(count):
            yield 6.0 + pace * (unit + 1 + count * stage)
            take(unit, stage)
    for unit in range(count):
        for half in range(2):
            for stage in range(stages):
                for chip in active(half, stage + 1):
                    copy(unit, half, stage, chip).wait_send()


def spread_scratch(shapes, devices):
    chips = devices // 2
    boxes = [pltpu.VMEM((chips, 2, rows // 2, columns), BF16) for rows, columns in shapes]
    inboxes = [pltpu.VMEM((chips - 1, 2, rows // 2, columns), BF16) for rows, columns in shapes]
    return (
        boxes
        + inboxes
        + boxes
        + [pltpu.SemaphoreType.DMA((len(shapes), chips))] * 2
        + [pltpu.SemaphoreType.DMA((len(shapes), 2, chips - 1))] * 2
    )


def window(ref, number, size):
    if size % 128 == 0:
        return ref[:, pl.ds(pl.multiple_of(number * size, size), size)]
    parts = 128 // size
    tile = ref[:, pl.ds(pl.multiple_of(number // parts * 128, 128), 128)].astype(F32)
    return choose(
        number % parts, [tile[:, i * size : (i + 1) * size] for i in range(parts)]
    ).astype(ref.dtype)


def rows_by_owner(left_ref, right_ref, rows):
    def term(owner, half):
        return lax.dot_general(
            window(left_ref, owner * 2 + half, rows // 2),
            right_ref[...],
            (((0,), (0,)), ((), ())),
            preferred_element_type=F32,
        )

    return term


def columns_by_owner(left_ref, right_ref, columns):
    def term(owner, half):
        rows = left_ref.shape[1] // 2
        return lax.dot_general(
            left_ref[:, half * rows : (half + 1) * rows],
            window(right_ref, owner, columns),
            (((0,), (0,)), ((), ())),
            preferred_element_type=F32,
        )

    return term


def ffn_sums_body(
    part_ref, hidden_ref, inv_ref, dy_ref, gain_ref, normed_ref, dgate_ref, dup_ref, inner_ref, dm_ref,
    gathered, grad_ref, gains_ref, gate_out, up_out, down_out, *scratch,
):
    summing, spreading = scratch[:7], scratch[7:]
    own, plane = lax.axis_index("tok"), lax.axis_index("tp")
    devices = lax.axis_size("tok")
    share = normed_ref.shape[1] // devices
    chips = devices // 2
    greet([(own ^ 1, plane)] + [(own ^ (2 << i), plane) for i in range(stages_of("tok") - 1)], True)
    run(
        sum_flow(
            part_ref,
            gathered,
            summing,
            ffn_math(hidden_ref, inv_ref, dy_ref, gain_ref, grad_ref, gains_ref),
        ),
        spread_flow(
            [
                rows_by_owner(normed_ref, dgate_ref, share),
                rows_by_owner(normed_ref, dup_ref, share),
                columns_by_owner(inner_ref, dm_ref, share),
            ],
            [gate_out, up_out, down_out],
            spreading,
            15.6,
        ),
    )


def ffn_sums(part, hidden, inv, dy, gain, normed, dgate, dup, inner, dm, collective_id):
    planes, shard, width = part.shape
    devices = lax.axis_size("tok")
    share = width // devices
    wide = dgate.shape[1]
    shapes = [(share, wide), (share, wide), (wide, share)]
    return pl.pallas_call(
        ffn_sums_body,
        out_shape=[
            jax.ShapeDtypeStruct((planes, shard, width), BF16),
            jax.ShapeDtypeStruct((shard, width), F32),
            jax.ShapeDtypeStruct((8, width), F32),
        ]
        + [jax.ShapeDtypeStruct(shape, F32) for shape in shapes],
        in_specs=[vmem()] * 10,
        out_specs=[vmem()] * 6,
        scratch_shapes=sum_scratch(planes, shard, width, BF16) + spread_scratch(shapes, devices),
        compiler_params=params(collective_id),
        cost_estimate=cost(0, 80_000_000),
        name="ffn_sums",
    )(part, hidden, inv, dy, gain, normed, dgate, dup, inner, dm)


def attn_sums_body(
    lens_ref, flags_ref, part_ref, x_ref, inv_ref, dy_ref, grad_ref, gain_ref, ffn_gains_ref,
    kept_ref, home_ref, normed_ref, dqkv_ref, attended_ref, da_ref,
    gathered, gains_ref, mixed_ref, qkv_out, out_out, *scratch,
):
    summing, undealing, scratch = scratch[:7], scratch[7:11], scratch[11:]
    gains_all, gains_sems, spreading = scratch[0], scratch[1:3], scratch[3:]
    planes = part_ref.shape[0]
    share = normed_ref.shape[1] // lax.axis_size("tok")
    greet(bit_peers(stages_of("tok")), True)
    run(
        sum_flow(
            part_ref,
            gathered,
            summing,
            attn_math(x_ref, inv_ref, dy_ref, grad_ref, gain_ref, ffn_gains_ref, gains_all),
            extra=(gains_all,) + gains_sems,
        ),
        undeal_flow(lens_ref, flags_ref, kept_ref, home_ref, mixed_ref, undealing, 7.0),
        spread_flow(
            [
                rows_by_owner(normed_ref, dqkv_ref, share),
                columns_by_owner(attended_ref, da_ref, share),
            ],
            [qkv_out, out_out],
            spreading,
            15.0,
        ),
    )
    total = gains_all[0]
    for index in range(1, planes):
        total = total + gains_all[index]
    gains_ref[...] = total


def attn_sums(
    doc_lengths, keep_flags, part, x, inv, dy, grad, gain, ffn_gains, kept, home, normed, dqkv,
    attended, da, collective_id,
):
    planes, shard, width = part.shape
    devices = lax.axis_size("tok")
    share = width // devices
    shapes = [(share, dqkv.shape[1]), (attended.shape[1], share)]
    return pl.pallas_call(
        attn_sums_body,
        out_shape=[
            jax.ShapeDtypeStruct((planes, shard, width), BF16),
            jax.ShapeDtypeStruct((8, width), F32),
            jax.ShapeDtypeStruct(home.shape, BF16),
        ]
        + [jax.ShapeDtypeStruct(shape, F32) for shape in shapes],
        in_specs=[smem(), smem()] + [vmem()] * 13,
        out_specs=[vmem()] * 5,
        scratch_shapes=sum_scratch(planes, shard, width, BF16)
        + undeal_scratch(stages_of("tok"), width, BF16)
        + [pltpu.VMEM((planes, 8, width), F32)]
        + line_sems(planes)
        + spread_scratch(shapes, devices),
        compiler_params=params(collective_id),
        cost_estimate=cost(0, 80_000_000),
        name="attn_sums",
    )(
        doc_lengths, keep_flags, part, x, inv, dy, grad, gain, ffn_gains, kept, home, normed, dqkv,
        attended, da,
    )


def mixed_sum_body(part_ref, hidden_ref, x_ref, gathered, *scratch):
    greet([], True)
    run(sum_flow(part_ref, gathered, scratch, mixed_math(hidden_ref, x_ref)))


def mixed_sum(part, hidden, x, collective_id):
    planes, shard, width = part.shape
    return pl.pallas_call(
        mixed_sum_body,
        out_shape=jax.ShapeDtypeStruct((planes, shard, width), BF16),
        in_specs=[vmem()] * 3,
        out_specs=vmem(),
        scratch_shapes=sum_scratch(planes, shard, width, BF16),
        compiler_params=params(collective_id),
        cost_estimate=cost(0, 60_000_000),
        name="mixed_sum",
    )(part, hidden, x)


def swap(values, bit):
    devices = lax.axis_size("tok")
    return lax.ppermute(values, "tok", [(i, i ^ bit) for i in range(devices)])


def document_tables(doc_lengths, places):
    doc_ends = jnp.cumsum(doc_lengths, dtype=jnp.int32)
    doc_starts = doc_ends - doc_lengths
    doc_ids = jnp.sum(
        (places[:, None] >= doc_ends[None, :]).astype(jnp.int32), axis=1, dtype=jnp.int32
    )
    member = (
        doc_ids[:, None] == jnp.arange(doc_lengths.shape[0], dtype=jnp.int32)[None, :]
    ).astype(jnp.int32)
    positions = places - jnp.sum(member * doc_starts[None, :], axis=1, dtype=jnp.int32)
    return (doc_ids, positions, member)


def rotary_tables(positions, head_dim):
    half_dim = head_dim // 2
    freqs = jnp.exp(jnp.arange(half_dim, dtype=jnp.float32) * (-2.0 * math.log(10000.0) / head_dim))
    angles = positions.astype(jnp.float32)[:, None] * freqs[None, :]
    return (jnp.cos(angles), jnp.sin(angles))


def rotate(values, cosine, sine):
    half_dim = values.shape[-1] // 2
    former, latter = (values[..., :half_dim], values[..., half_dim:])
    cos_b, sin_b = (cosine[:, None, :], sine[:, None, :])
    return jnp.concatenate(
        [former * cos_b - latter * sin_b, latter * cos_b + former * sin_b], axis=-1
    )


def unrotate(values, cosine, sine):
    half_dim = values.shape[-1] // 2
    former, latter = (values[..., :half_dim], values[..., half_dim:])
    cos_b, sin_b = (cosine[:, None, :], sine[:, None, :])
    return jnp.concatenate(
        [former * cos_b + latter * sin_b, latter * cos_b - former * sin_b], axis=-1
    )


def over_rows(left, right):
    return lax.dot_general(
        left, right, (((0,), (0,)), ((), ())), preferred_element_type=jnp.float32
    )


def over_columns(left, right):
    return lax.dot_general(
        left, right, (((1,), (1,)), ((), ())), preferred_element_type=jnp.float32
    )


def on_device(
    tokens,
    gain_attn,
    w_query,
    w_key,
    w_value,
    w_out,
    gain_ffn,
    w_gate,
    w_up,
    w_down,
    cotangent,
    doc_lengths,
    keep_flags,
):
    length = tokens.shape[0]
    model_width = tokens.shape[1]
    devices = lax.axis_size("tok")
    planes = lax.axis_size("tp")
    own_index = lax.axis_index("tok")
    blocks_here = length // BLOCK
    kept_here = blocks_here // 2
    total_blocks = blocks_here * devices
    kept_total = kept_here * devices
    rows = kept_here * BLOCK
    token_blocks = tokens.reshape(blocks_here, BLOCK, model_width)
    grad_blocks = cotangent.reshape(blocks_here, BLOCK, model_width)

    half_columns = model_width // 2
    out_half = lax.dynamic_slice_in_dim(w_out, (own_index % 2) * half_columns, half_columns, 1)
    out_half = lax.all_gather(out_half, "tp", axis=0, tiled=True)
    out_other = swap(out_half, 1)
    first_core = own_index % 2 == 0

    rows_x = deal(doc_lengths, keep_flags, token_blocks, 0).reshape(rows, model_width)

    block_starts = jnp.arange(total_blocks, dtype=jnp.int32) * BLOCK
    block_docs, block_pos, block_member = document_tables(doc_lengths, block_starts)
    block_kept = jnp.sum(block_member * keep_flags[None, :], axis=1, dtype=jnp.int32)
    block_rank = jnp.cumsum(block_kept, dtype=jnp.int32) - block_kept
    rank_slots = jnp.arange(kept_total, dtype=jnp.int32)
    rank_match = ((block_rank[None, :] == rank_slots[:, None]) & (block_kept[None, :] == 1)).astype(
        jnp.int32
    )
    rank_block = jnp.sum(
        rank_match * jnp.arange(total_blocks, dtype=jnp.int32)[None, :], axis=1, dtype=jnp.int32
    )
    peer_ids = jnp.arange(devices, dtype=jnp.int32)
    own_ranks = own_index + jnp.arange(kept_here, dtype=jnp.int32) * devices
    own_blocks = jnp.take(rank_block, own_ranks)
    block_offsets = jnp.arange(BLOCK, dtype=jnp.int32)
    places = (own_blocks[:, None] * BLOCK + block_offsets[None, :]).reshape(rows)
    key_ranks = (
        peer_ids[:, None] + jnp.arange(kept_here, dtype=jnp.int32)[None, :] * devices
    ).reshape(kept_total)
    key_places = (
        jnp.take(rank_block, key_ranks)[:, None] * BLOCK + block_offsets[None, :]
    ).reshape(kept_total * BLOCK)
    doc_ids, positions, member = document_tables(doc_lengths, places)
    key_docs, key_pos, key_member = document_tables(doc_lengths, key_places)
    allowed = (doc_ids[:, None] == key_docs[None, :]) & (places[:, None] >= key_places[None, :])
    cosine, sine = rotary_tables(positions, HD)
    heads_here = w_query.shape[1] // HD
    groups_here = w_key.shape[1] // HD
    sharing = heads_here // groups_here
    score_scale = 1.0 / math.sqrt(HD)

    x_full = rows_x.astype(jnp.float32)
    inv_one = lax.rsqrt(jnp.mean(x_full * x_full, axis=1, keepdims=True) + norm_eps)
    normed_one = (x_full * inv_one * gain_attn).astype(jnp.bfloat16)
    query_pre = jnp.dot(normed_one, w_query, preferred_element_type=jnp.float32).reshape(
        rows, heads_here, HD
    )
    key_pre = jnp.dot(normed_one, w_key, preferred_element_type=jnp.float32).reshape(
        rows, groups_here, HD
    )
    value_pre = jnp.dot(normed_one, w_value, preferred_element_type=jnp.float32)
    queries = rotate(query_pre, cosine, sine).astype(jnp.bfloat16)
    keys_local = rotate(key_pre, cosine, sine).astype(jnp.bfloat16).reshape(rows, groups_here * HD)
    values_local = value_pre.astype(jnp.bfloat16)
    kv_width = groups_here * HD
    key_count = kept_total * BLOCK
    both_all = gather_tok(jnp.concatenate([keys_local, values_local], axis=1), 2)
    both_all = both_all.reshape(key_count, 2, groups_here, HD)
    keys_heads, values_heads = both_all[:, 0], both_all[:, 1]
    query_heads = queries.transpose(1, 0, 2)
    slot_of_head = jnp.arange(heads_here, dtype=jnp.int32) // sharing

    def head_scores(query, slot):
        keys_one = lax.dynamic_index_in_dim(keys_heads, slot, 1, keepdims=False)
        values_one = lax.dynamic_index_in_dim(values_heads, slot, 1, keepdims=False)
        scores = (
            jnp.einsum("qd,kd->qk", query, keys_one, preferred_element_type=jnp.float32)
            * score_scale
        )
        return (jnp.where(allowed, scores, -1e30), keys_one, values_one)

    def head_forward(pack):
        query, slot = pack
        scores, keys_one, values_one = head_scores(query, slot)
        peak = jnp.max(scores, axis=1, keepdims=True)
        weights = jnp.exp(scores - peak)
        totals = jnp.sum(weights, axis=1, keepdims=True)
        probs = (weights / totals).astype(jnp.bfloat16)
        return (jnp.dot(probs, values_one, preferred_element_type=jnp.float32), peak, totals)

    head_outs, peaks, totals = lax.map(head_forward, (query_heads, slot_of_head))
    attended = head_outs.transpose(1, 0, 2).reshape(rows, heads_here * HD).astype(jnp.bfloat16)

    rows_dy, attended_all = deal_gather(doc_lengths, keep_flags, grad_blocks, attended, 1)
    rows_dy = rows_dy.reshape(rows, model_width)
    attended_all = attended_all.transpose(1, 0, 2).reshape(rows, planes * heads_here * HD)
    mine = jnp.dot(attended_all, out_half, preferred_element_type=jnp.float32)
    other = jnp.dot(attended_all, out_other, preferred_element_type=jnp.float32)
    branch_attn = jnp.concatenate(
        [jnp.where(first_core, mine, other), jnp.where(first_core, other, mine)], axis=1
    )
    hidden_res = x_full + branch_attn
    inv_two = lax.rsqrt(jnp.mean(hidden_res * hidden_res, axis=1, keepdims=True) + norm_eps)
    normed_two = (hidden_res * inv_two * gain_ffn).astype(jnp.bfloat16)
    gate = jnp.dot(normed_two, w_gate, preferred_element_type=jnp.float32)
    upper = jnp.dot(normed_two, w_up, preferred_element_type=jnp.float32)
    sigma = jax.nn.sigmoid(gate)
    swish = gate * sigma
    inner = (swish * upper).astype(jnp.bfloat16)

    grad_m = (keep_scale * rows_dy.astype(jnp.float32)).astype(jnp.bfloat16)
    grad_inner = over_columns(grad_m, w_down)
    grad_gate_pre = (grad_inner * upper * sigma * (1.0 + gate * (1.0 - sigma))).astype(jnp.bfloat16)
    grad_up_pre = (grad_inner * swish).astype(jnp.bfloat16)
    part_two = (
        over_columns(grad_gate_pre, w_gate) + over_columns(grad_up_pre, w_up)
    ).astype(jnp.bfloat16)

    shard = rows // planes
    by_plane = lambda array: array.reshape(planes, shard, array.shape[1])
    x_planes, dy_planes = by_plane(rows_x), by_plane(rows_dy)
    hidden_planes = by_plane(hidden_res)
    grad_a, grad_hidden, gains_ffn, grad_gate, grad_up, grad_down = ffn_sums(
        by_plane(part_two),
        hidden_planes,
        by_plane(inv_two),
        dy_planes,
        gain_ffn.reshape(1, -1),
        normed_two,
        grad_gate_pre,
        grad_up_pre,
        inner,
        grad_m,
        4,
    )
    grad_a = grad_a.reshape(rows, model_width)

    grad_attended = over_columns(grad_a, w_out).astype(jnp.bfloat16)
    grad_heads = grad_attended.reshape(rows, heads_here, HD).transpose(1, 0, 2)

    def head_backward(pack):
        query, grad_head, peak, total, slot = pack
        scores, keys_one, values_one = head_scores(query, slot)
        probs = jnp.exp(scores - peak) / total
        probs_low = probs.astype(jnp.bfloat16)
        grad_probs = jnp.einsum(
            "qd,kd->qk", grad_head, values_one, preferred_element_type=jnp.float32
        )
        delta = jnp.sum(probs * grad_probs, axis=1, keepdims=True)
        grad_scores = (probs * (grad_probs - delta)).astype(jnp.bfloat16)
        grad_query_head = (
            jnp.dot(grad_scores, keys_one, preferred_element_type=jnp.float32) * score_scale
        )
        grad_keys_head = over_rows(grad_scores, query) * score_scale
        grad_values_head = over_rows(probs_low, grad_head)
        return (grad_query_head, grad_keys_head, grad_values_head)

    grad_q_heads, grad_k_heads, grad_v_heads = lax.map(
        head_backward, (query_heads, grad_heads, peaks, totals, slot_of_head)
    )
    grad_k_all = (
        grad_k_heads.reshape(groups_here, sharing, key_count, HD)
        .sum(axis=1)
        .transpose(1, 0, 2)
        .reshape(key_count, kv_width)
    )
    grad_v_all = (
        grad_v_heads.reshape(groups_here, sharing, key_count, HD)
        .sum(axis=1)
        .transpose(1, 0, 2)
        .reshape(key_count, kv_width)
    )
    grad_kv = jnp.concatenate([grad_k_all, grad_v_all], axis=1).astype(BF16)
    grad_kv = scatter_tok(grad_kv.reshape(devices, rows, 2 * kv_width), 5)
    grad_k_own, grad_v_own = grad_kv[:, :kv_width], grad_kv[:, kv_width:]
    grad_query_pre = (
        unrotate(grad_q_heads.transpose(1, 0, 2), cosine, sine)
        .reshape(rows, heads_here * HD)
        .astype(jnp.bfloat16)
    )
    grad_key_pre = (
        unrotate(grad_k_own.reshape(rows, groups_here, HD), cosine, sine)
        .reshape(rows, kv_width)
        .astype(jnp.bfloat16)
    )
    grad_value_pre = grad_v_own.astype(jnp.bfloat16)
    part_one = (
        over_columns(grad_query_pre, w_query)
        + over_columns(grad_key_pre, w_key)
        + over_columns(grad_value_pre, w_value)
    ).astype(jnp.bfloat16)
    mixed_rows = mixed_sum(
        by_plane(jnp.dot(inner, w_down, preferred_element_type=jnp.float32).astype(jnp.bfloat16)),
        hidden_planes,
        x_planes,
        7,
    )
    grad_rows, gains, mixed, grad_qkv, grad_out = attn_sums(
        doc_lengths,
        keep_flags,
        by_plane(part_one),
        x_planes,
        by_plane(inv_one),
        dy_planes,
        grad_hidden,
        gain_attn.reshape(1, -1),
        gains_ffn,
        mixed_rows.reshape(kept_here, BLOCK, model_width),
        token_blocks,
        normed_one,
        jnp.concatenate([grad_query_pre, grad_key_pre, grad_value_pre], axis=1),
        attended,
        grad_a,
        6,
    )
    token_grad, gain_sums = undeal(
        doc_lengths,
        keep_flags,
        grad_rows.reshape(kept_here, BLOCK, model_width),
        grad_blocks,
        gains,
        9,
    )
    own_share = model_width // devices
    if gain_sums.shape[1] != own_share:
        gain_sums = lax.dynamic_slice_in_dim(gain_sums, own_index * own_share, own_share, 1)
    wide, thin = w_query.shape[1], w_key.shape[1]
    grad_query = grad_qkv[:, :wide]
    grad_key = grad_qkv[:, wide : wide + thin]
    grad_value = grad_qkv[:, wide + thin :]

    return (
        mixed.reshape(length, model_width),
        token_grad.reshape(length, model_width),
        gain_sums[1],
        grad_query,
        grad_key,
        grad_value,
        grad_out,
        gain_sums[0],
        grad_gate,
        grad_up,
        grad_down,
    )


def solution(mesh):
    placed = (
        P("tok", None),
        P(),
        P(None, "tp"),
        P(None, "tp"),
        P(None, "tp"),
        P("tp", None),
        P(),
        P(None, "tp"),
        P(None, "tp"),
        P("tp", None),
        P("tok", None),
        P(),
        P(),
    )
    return jax.shard_map(
        on_device,
        mesh=mesh,
        in_specs=placed,
        out_specs=(
            P("tok", None),
            P("tok", None),
            P("tok"),
            P("tok", "tp"),
            P("tok", "tp"),
            P("tok", "tp"),
            P("tp", "tok"),
            P("tok"),
            P("tok", "tp"),
            P("tok", "tp"),
            P("tp", "tok"),
        ),
        check_vma=False,
    )
```

```python
import functools
import math

import jax
import jax.numpy as jnp
from jax import lax
from jax.experimental import pallas as pl
from jax.experimental.pallas import tpu as pltpu
from jax.sharding import PartitionSpec as P

HD = 128
BLOCK = 128
SLOTS = 3
CHUNKS = 8
HALVES = 2
MESH = pl.DeviceIdType.MESH
VMEM_BYTES = 60 * 2**20

norm_eps = 1e-05
keep_scale = 2.0
F32 = jnp.float32
BF16 = jnp.bfloat16


def vmem():
    return pl.BlockSpec(memory_space=pltpu.VMEM)


def smem():
    return pl.BlockSpec(memory_space=pltpu.SMEM)


def params(collective_id):
    return pltpu.CompilerParams(
        collective_id=collective_id, has_side_effects=True, vmem_limit_bytes=VMEM_BYTES
    )


def cost(flops, moved):
    return pl.CostEstimate(flops=flops, bytes_accessed=moved, transcendentals=0)


def greet(peers, line=False):
    barrier = pltpu.get_barrier_semaphore()
    for peer in peers:
        pl.semaphore_signal(barrier, inc=1, device_id=peer, device_id_type=MESH)
    if not line:
        pl.semaphore_wait(barrier, len(peers))
        return
    own, plane = lax.axis_index("tok"), lax.axis_index("tp")
    last = lax.axis_size("tp") - 1

    @pl.when(plane > 0)
    def _():
        pl.semaphore_signal(barrier, inc=1, device_id=(own, plane - 1), device_id_type=MESH)

    @pl.when(plane < last)
    def _():
        pl.semaphore_signal(barrier, inc=1, device_id=(own, plane + 1), device_id_type=MESH)

    end = (plane == 0) | (plane == last)

    @pl.when(end)
    def _():
        pl.semaphore_wait(barrier, len(peers) + 1)

    @pl.when(jnp.logical_not(end))
    def _():
        pl.semaphore_wait(barrier, len(peers) + 2)


def run(*flows):
    waiting = [[next(flow), number, flow] for number, flow in enumerate(flows)]
    while waiting:
        waiting.sort(key=lambda entry: entry[:2])
        entry = waiting[0]
        try:
            entry[0] = next(entry[2])
        except StopIteration:
            waiting.pop(0)


def deal_tables(own, stages, blocks_here, lens_ref, flags_ref):
    def kept_before(place):
        total, start = jnp.int32(0), jnp.int32(0)
        for doc in range(lens_ref.shape[0]):
            blocks = lens_ref[doc] // BLOCK
            total = total + flags_ref[doc] * jnp.clip(place - start, 0, blocks)
            start = start + blocks
        return total

    def edges(stage):
        first = (own >> stage) << stage
        return (
            kept_before(first * blocks_here),
            kept_before((first + (1 << stage)) * blocks_here),
        )

    def located(stage):
        if stage == 0:
            ends = [kept_before(own * blocks_here + i + 1) for i in range(blocks_here)]

            def place(rank):
                index = jnp.int32(0)
                for end in ends:
                    index = index + (end <= rank).astype(jnp.int32)
                return index

            return place
        mine = (own >> (stage - 1)) << (stage - 1)
        low, high = edges(stage - 1)
        other = kept_before((mine ^ (1 << (stage - 1))) * blocks_here)

        def place(rank):
            inside = (rank >= low) & (rank < high)
            return jnp.where(inside, (rank - low) >> stage, SLOTS + ((rank - other) >> stage))

        return place

    keeps, sends = [], []
    for stage in range(stages):
        low, high = edges(stage)
        place = located(stage)
        period = 1 << (stage + 1)
        for table, target in ((keeps, own), (sends, own ^ (1 << stage))):
            first = low + ((target - low) & (period - 1))
            row = []
            for slot in range(SLOTS):
                rank = first + period * slot
                row.append(jnp.where(rank < high, place(rank), -1))
            table.append(row)
    place = located(stages)
    finals = [place(own + (slot << stages)) for slot in range(SLOTS)]
    return keeps, sends, finals


def choose(index, options, default=None):
    value = options[0] if default is None else default
    for number, option in enumerate(options):
        if number == 0 and default is None:
            continue
        value = jnp.where(index == number, option, value)
    return value


def bit_peers(stages):
    own, plane = lax.axis_index("tok"), lax.axis_index("tp")
    return [(own ^ (1 << stage), plane) for stage in range(stages)]


def deal_flow(lens_ref, flags_ref, own_ref, out_ref, scratch, pace=4.3):
    keep, send, recv, send_sem, recv_sem = scratch
    stages = send.shape[0]
    own = lax.axis_index("tok")
    blocks_here = own_ref.shape[0]
    rows = BLOCK // CHUNKS
    peers = bit_peers(stages)
    keeps, sends, finals = deal_tables(own, stages, blocks_here, lens_ref, flags_ref)

    def copy(stage, chunk):
        return pltpu.make_async_remote_copy(
            src_ref=send.at[stage, chunk],
            dst_ref=recv.at[stage, chunk],
            send_sem=send_sem.at[stage, chunk],
            recv_sem=recv_sem.at[stage, chunk],
            device_id=peers[stage],
            device_id_type=MESH,
        )

    def held(stage, chunk):
        if stage == 0:
            return [own_ref[i, pl.ds(chunk * rows, rows), :] for i in range(blocks_here)]
        return [keep[chunk, i] for i in range(SLOTS)] + [
            recv[stage - 1, chunk, i] for i in range(SLOTS)
        ]

    for stage in range(stages + 1):
        for chunk in range(CHUNKS):
            yield 0.0 if stage == 0 else 1 + 0.4 * chunk + pace * (stage - 1) * (chunk + 1)
            if stage > 0:
                copy(stage - 1, chunk).wait_recv()
            options = held(stage, chunk)
            if stage == stages:
                for slot in range(SLOTS):
                    out_ref[slot, pl.ds(chunk * rows, rows), :] = choose(finals[slot], options)
            else:
                for slot in range(SLOTS):
                    send[stage, chunk, slot] = choose(sends[stage][slot], options)
                copy(stage, chunk).start()
                for slot in range(SLOTS):
                    keep[chunk, slot] = choose(keeps[stage][slot], options)
    yield 1e6

    def drain(chunk, carry):
        for stage in range(stages):
            copy(stage, chunk).wait_send()
        return carry

    lax.fori_loop(0, CHUNKS, drain, 0)


def deal_scratch(stages, width, kind):
    moved = (CHUNKS, SLOTS, BLOCK // CHUNKS, width)
    return (
        [pltpu.VMEM(moved, kind)]
        + [pltpu.VMEM((stages,) + moved, kind)] * 2
        + [pltpu.SemaphoreType.DMA((stages, CHUNKS))] * 2
    )


def stages_of(axis):
    return int(math.log2(lax.axis_size(axis)))


def deal_body(lens_ref, flags_ref, own_ref, out_ref, *scratch):
    greet(bit_peers(scratch[1].shape[0]))
    run(deal_flow(lens_ref, flags_ref, own_ref, out_ref, scratch))


def deal(doc_lengths, keep_flags, blocks, collective_id):
    width = blocks.shape[2]
    return pl.pallas_call(
        deal_body,
        out_shape=jax.ShapeDtypeStruct((SLOTS, BLOCK, width), blocks.dtype),
        in_specs=[smem(), smem(), vmem()],
        out_specs=vmem(),
        scratch_shapes=deal_scratch(stages_of("tok"), width, blocks.dtype),
        compiler_params=params(collective_id),
        cost_estimate=cost(0, 40_000_000),
        name="deal",
    )(doc_lengths, keep_flags, blocks)


def undeal_flow(lens_ref, flags_ref, kept_ref, home_ref, out_ref, scratch, pace=4.3):
    keep, send, recv, send_sem, recv_sem = scratch
    stages = recv.shape[0]
    own = lax.axis_index("tok")
    blocks_here = home_ref.shape[0]
    rows = BLOCK // CHUNKS
    peers = bit_peers(stages)
    keeps, sends, finals = deal_tables(own, stages, blocks_here, lens_ref, flags_ref)

    def copy(stage, chunk):
        return pltpu.make_async_remote_copy(
            src_ref=send.at[stage, chunk],
            dst_ref=recv.at[stage, chunk],
            send_sem=send_sem.at[stage, chunk],
            recv_sem=recv_sem.at[stage, chunk],
            device_id=peers[stage],
            device_id_type=MESH,
        )

    def pick_place(places, options, place, value):
        for index, option in zip(places, options):
            value = jnp.where(index == place, option, value)
        return value

    last = stages - 1
    for stage in range(last, -2, -1):
        for chunk in range(CHUNKS):
            yield 0.0 if stage == last else 1 + pace * (chunk + last - stage - (stage < 0))
            span = pl.ds(chunk * rows, rows)
            if stage == last:
                options = [kept_ref[slot, span, :] for slot in range(SLOTS)]
                places = finals
            else:
                copy(stage + 1, chunk).wait_recv()
                options = [keep[chunk, i] for i in range(SLOTS)] + [
                    recv[stage + 1, chunk, i] for i in range(SLOTS)
                ]
                places = keeps[stage + 1] + sends[stage + 1]
            if stage < 0:
                for place in range(blocks_here):
                    home = home_ref[place, span, :]
                    out_ref[place, span, :] = pick_place(places, options, place, home)
            else:
                for slot in range(SLOTS):
                    send[stage, chunk, slot] = pick_place(
                        places, options, SLOTS + slot, options[0]
                    )
                copy(stage, chunk).start()
                for slot in range(SLOTS):
                    keep[chunk, slot] = pick_place(places, options, slot, options[0])
    yield 1e6

    def drain(chunk, carry):
        for stage in range(stages):
            copy(stage, chunk).wait_send()
        return carry

    lax.fori_loop(0, CHUNKS, drain, 0)


def undeal_body(lens_ref, flags_ref, kept_ref, home_ref, gains_ref, out_ref, sum_ref, *scratch):
    undealing = scratch[:5]
    gain_recv, gain_send_sem, gain_recv_sem = scratch[5:]
    own, plane = lax.axis_index("tok"), lax.axis_index("tp")
    devices = gain_recv.shape[0]
    share = sum_ref.shape[1]
    greet([(own ^ step, plane) for step in range(1, devices)])

    def portion(there):
        if share % 128 == 0 and share < gains_ref.shape[1]:
            return gains_ref.at[:, pl.ds(pl.multiple_of(there * share, share), share)]
        return gains_ref

    def gain_copy(step):
        there = own ^ step
        return pltpu.make_async_remote_copy(
            src_ref=portion(there),
            dst_ref=gain_recv.at[step],
            send_sem=gain_send_sem.at[step],
            recv_sem=gain_recv_sem.at[step],
            device_id=(there, plane),
            device_id_type=MESH,
        )

    for step in range(1, devices):
        gain_copy(step).start()
    run(undeal_flow(lens_ref, flags_ref, kept_ref, home_ref, out_ref, undealing))
    total = portion(own)[...]
    for step in range(1, devices):
        gain_copy(step).wait()
        total = total + gain_recv[step]
    sum_ref[...] = total


def undeal(doc_lengths, keep_flags, kept, home, gains, collective_id):
    stages = stages_of("tok")
    devices = 1 << stages
    width = kept.shape[2]
    share = width // devices
    share = share if share % 128 == 0 else width
    return pl.pallas_call(
        undeal_body,
        out_shape=(
            jax.ShapeDtypeStruct(home.shape, home.dtype),
            jax.ShapeDtypeStruct((8, share), F32),
        ),
        in_specs=[smem(), smem(), vmem(), vmem(), vmem()],
        out_specs=(vmem(), vmem()),
        scratch_shapes=deal_scratch(stages, width, kept.dtype)
        + [
            pltpu.VMEM((devices, 8, share), F32),
            pltpu.SemaphoreType.DMA((devices,)),
            pltpu.SemaphoreType.DMA((devices,)),
        ],
        compiler_params=params(collective_id),
        cost_estimate=cost(0, 40_000_000),
        name="undeal",
    )(doc_lengths, keep_flags, kept, home, gains)


def project_body(
    x_ref, gain_ref, w_query_ref, w_key_ref, w_value_ref, cos_ref, sin_ref,
    normed_ref, inv_ref, query_ref, out_ref,
    mine_ref, send_sem, recv_sem, relay_send_sem, relay_recv_sem,
):
    devices = out_ref.shape[0]
    chips = devices // 2
    own = lax.axis_index("tok")
    plane = lax.axis_index("tp")
    partner = (own ^ 1, plane)
    rows = x_ref.shape[0]
    thin = w_key_ref.shape[1]
    greet([partner] + [(own ^ (2 * step), plane) for step in range(1, chips)])

    def copy(step):
        return pltpu.make_async_remote_copy(
            src_ref=mine_ref,
            dst_ref=out_ref.at[own],
            send_sem=send_sem.at[step],
            recv_sem=recv_sem.at[step],
            device_id=(own ^ (2 * step), plane),
            device_id_type=MESH,
        )

    def relay(step):
        return pltpu.make_async_remote_copy(
            src_ref=mine_ref if step == 0 else out_ref.at[own ^ (2 * step)],
            dst_ref=out_ref.at[own ^ (2 * step)],
            send_sem=relay_send_sem.at[step],
            recv_sem=relay_recv_sem.at[step],
            device_id=partner,
            device_id_type=MESH,
        )

    def norm(index, carry):
        span = pl.ds(pl.multiple_of(index * 16, 16), 16)
        x = x_ref[span, :].astype(F32)
        inv = lax.rsqrt(jnp.mean(x * x, axis=1, keepdims=True) + norm_eps)
        inv_ref[span, :] = inv
        normed_ref[span, :] = (x * inv * gain_ref[...]).astype(BF16)
        return carry

    lax.fori_loop(0, rows // 16, norm, 0)

    def product(w_ref):
        return lax.dot_general(
            normed_ref[...], w_ref[...], (((1,), (0,)), ((), ())), preferred_element_type=F32
        )

    keys = product(w_key_ref)
    for group in range(thin // HD):
        one = keys[:, group * HD : (group + 1) * HD]
        mine_ref[:, group * HD : (group + 1) * HD] = turn(one, cos_ref, sin_ref, -1.0).astype(BF16)
    mine_ref[:, thin:] = product(w_value_ref).astype(BF16)
    for step in range(1, chips):
        copy(step).start()
    relay(0).start()
    out_ref[own] = mine_ref[...]
    queries = product(w_query_ref)
    for head in range(w_query_ref.shape[1] // HD):
        one = queries[:, head * HD : (head + 1) * HD]
        query_ref[:, head * HD : (head + 1) * HD] = turn(one, cos_ref, sin_ref, -1.0).astype(BF16)
    for step in range(1, chips):
        copy(step).wait_recv()
        relay(step).start()
    for step in range(chips):
        relay(step).wait()
    for step in range(1, chips):
        copy(step).wait_send()


def turn(values, cos_ref, sin_ref, sign):
    return values * cos_ref[...] + pltpu.roll(values, HD // 2, 1) * (sin_ref[...] * sign)


def project(x, gain, w_query, w_key, w_value, cosine, sine, collective_id):
    devices = lax.axis_size("tok")
    chips = devices // 2
    rows = x.shape[0]
    both = w_key.shape[1] + w_value.shape[1]
    return pl.pallas_call(
        project_body,
        out_shape=(
            jax.ShapeDtypeStruct(x.shape, BF16),
            jax.ShapeDtypeStruct((rows, 1), F32),
            jax.ShapeDtypeStruct((rows, w_query.shape[1]), BF16),
            jax.ShapeDtypeStruct((devices, rows, both), BF16),
        ),
        in_specs=[vmem()] * 7,
        out_specs=(vmem(),) * 4,
        scratch_shapes=[pltpu.VMEM((rows, both), BF16)] + [pltpu.SemaphoreType.DMA((chips,))] * 4,
        compiler_params=params(collective_id),
        cost_estimate=cost(0, 30_000_000),
        name="project",
    )(x, gain, w_query, w_key, w_value, cosine, sine)


def first_rank(lens_ref, flags_ref, rank):
    first, start = jnp.int32(0), jnp.int32(0)
    for doc in range(lens_ref.shape[0]):
        blocks = flags_ref[doc] * (lens_ref[doc] // BLOCK)
        first = jnp.where((rank >= start) & (rank < start + blocks), start, first)
        start = start + blocks
    return first


def stack_heads(ref, slot):
    heads = ref.shape[1] // HD
    return jnp.concatenate(
        [ref[slot * BLOCK : (slot + 1) * BLOCK, i * HD : (i + 1) * HD] for i in range(heads)], axis=0
    )


def dot(left, right, dims):
    return lax.dot_general(left, right, ((dims[:1], dims[1:]), ((), ())), preferred_element_type=F32)


def key_block(kv_ref, rank):
    devices = kv_ref.shape[0]
    device, slot = lax.rem(rank, devices), lax.div(rank, devices)
    span = pl.ds(pl.multiple_of(slot * BLOCK, BLOCK), BLOCK)
    return device, span


def causal(scores):
    keys = lax.broadcasted_iota(jnp.int32, scores.shape, 0)
    queries = lax.rem(lax.broadcasted_iota(jnp.int32, scores.shape, 1), BLOCK)
    return jnp.where(keys <= queries, scores, -1e30)


def attend_body(lens_ref, flags_ref, own_ref, query_ref, kv_ref, out_ref, wide_ref, log_ref, total):
    devices = kv_ref.shape[0]
    scale = 1.0 / math.sqrt(HD)
    for slot in range(SLOTS):
        rank = own_ref[0] + devices * slot
        query = stack_heads(query_ref, slot)
        count = query.shape[0]
        total[...] = jnp.zeros_like(total)

        def visit(key_rank, state, masked):
            peak, weight = state
            device, span = key_block(kv_ref, key_rank)
            scores = dot(kv_ref[device, span, :HD], query, (1, 1)) * scale
            if masked:
                scores = causal(scores)
            higher = jnp.maximum(peak, jnp.max(scores, axis=0, keepdims=True))
            shrink = jnp.exp(peak - higher)
            probs = jnp.exp(scores - higher)
            weight = weight * shrink + jnp.sum(probs, axis=0, keepdims=True)
            values = kv_ref[device, span, HD:]
            total[...] = total[...] * shrink + dot(values, probs.astype(BF16), (0, 0))
            return higher, weight

        start = (jnp.full((1, count), -1e30, F32), jnp.zeros((1, count), F32))
        first = first_rank(lens_ref, flags_ref, rank)
        state = lax.fori_loop(first, rank, lambda r, s: visit(r, s, False), start)
        peak, weight = visit(rank, state, True)
        result = total[...] / weight
        wide_ref[slot] = result
        log_ref[slot] = jnp.broadcast_to(peak + jnp.log(weight), log_ref.shape[1:])
        turned = result.T.astype(BF16)
        for head in range(count // BLOCK):
            out_ref[slot * BLOCK : (slot + 1) * BLOCK, head * HD : (head + 1) * HD] = turned[
                head * BLOCK : (head + 1) * BLOCK
            ]


def attend(doc_lengths, keep_flags, own, query, kv):
    count = query.shape[1] // HD * BLOCK
    return pl.pallas_call(
        attend_body,
        out_shape=(
            jax.ShapeDtypeStruct(query.shape, BF16),
            jax.ShapeDtypeStruct((SLOTS, HD, count), F32),
            jax.ShapeDtypeStruct((SLOTS, 8, count), F32),
        ),
        in_specs=[smem()] * 3 + [vmem()] * 2,
        out_specs=(vmem(),) * 3,
        scratch_shapes=[pltpu.VMEM((HD, count), F32)],
        compiler_params=pltpu.CompilerParams(vmem_limit_bytes=VMEM_BYTES),
        cost_estimate=cost(1_000_000_000, 10_000_000),
        name="attend",
    )(doc_lengths, keep_flags, own, query, kv)


def attend_back_body(
    lens_ref, flags_ref, own_ref, query_ref, grad_ref, kv_ref, wide_ref, log_ref, cos_ref, sin_ref,
    grad_query_ref, grad_kv_ref, grad_kv, total,
):
    devices = kv_ref.shape[0]
    scale = 1.0 / math.sqrt(HD)
    grad_kv[...] = jnp.zeros_like(grad_kv)
    for slot in range(SLOTS):
        rank = own_ref[0] + devices * slot
        query = stack_heads(query_ref, slot)
        grad = stack_heads(grad_ref, slot)
        delta = jnp.sum(grad.astype(F32).T * wide_ref[slot], axis=0, keepdims=True)
        log_total = log_ref[slot, 0:1, :]
        total[...] = jnp.zeros_like(total)

        def visit(key_rank, masked):
            device, span = key_block(kv_ref, key_rank)
            keys, values = kv_ref[device, span, :HD], kv_ref[device, span, HD:]
            scores = dot(keys, query, (1, 1)) * scale
            if masked:
                scores = causal(scores)
            probs = jnp.exp(scores - log_total)
            grad_probs = dot(values, grad, (1, 1))
            grad_scores = (probs * (grad_probs - delta)).astype(BF16)
            grad_kv[device, span, HD:] += dot(probs.astype(BF16), grad, (1, 0))
            grad_kv[device, span, :HD] += dot(grad_scores, query, (1, 0)) * scale
            total[...] += dot(keys, grad_scores, (0, 0))

        def step(key_rank, carry):
            visit(key_rank, False)
            return carry

        lax.fori_loop(first_rank(lens_ref, flags_ref, rank), rank, step, 0)
        visit(rank, True)
        turned = (total[...] * scale).T
        span = pl.ds(slot * BLOCK, BLOCK)
        for head in range(turned.shape[0] // BLOCK):
            one = turned[head * BLOCK : (head + 1) * BLOCK]
            grad_query_ref[span, head * HD : (head + 1) * HD] = turn(
                one, cos_ref.at[span], sin_ref.at[span], 1.0
            ).astype(BF16)
    grad_kv_ref[...] = grad_kv[...].astype(BF16)


def attend_back(doc_lengths, keep_flags, own, query, grad, kv, wide, log_total, cosine, sine):
    count = query.shape[1] // HD * BLOCK
    return pl.pallas_call(
        attend_back_body,
        out_shape=(
            jax.ShapeDtypeStruct(query.shape, BF16),
            jax.ShapeDtypeStruct(kv.shape, BF16),
        ),
        in_specs=[smem()] * 3 + [vmem()] * 7,
        out_specs=(vmem(),) * 2,
        scratch_shapes=[pltpu.VMEM(kv.shape, F32), pltpu.VMEM((HD, count), F32)],
        compiler_params=pltpu.CompilerParams(vmem_limit_bytes=VMEM_BYTES),
        cost_estimate=cost(3_000_000_000, 20_000_000),
        name="attend_back",
    )(doc_lengths, keep_flags, own, query, grad, kv, wide, log_total, cosine, sine)


def scatter_tok_body(
    part_ref, out_ref, core_recv, held, recv, core_send_sem, core_recv_sem, send_sem, recv_sem
):
    devices = part_ref.shape[0]
    chips = devices // 2
    own = lax.axis_index("tok")
    plane = lax.axis_index("tp")
    partner = (own ^ 1, plane)
    greet([partner] + [(own ^ (2 * step), plane) for step in range(1, chips)])

    def core_copy(step):
        return pltpu.make_async_remote_copy(
            src_ref=part_ref.at[own ^ (2 * step) ^ 1],
            dst_ref=core_recv.at[step],
            send_sem=core_send_sem.at[step],
            recv_sem=core_recv_sem.at[step],
            device_id=partner,
            device_id_type=MESH,
        )

    def copy(step):
        return pltpu.make_async_remote_copy(
            src_ref=held.at[step],
            dst_ref=recv.at[step],
            send_sem=send_sem.at[step],
            recv_sem=recv_sem.at[step],
            device_id=(own ^ (2 * step), plane),
            device_id_type=MESH,
        )

    order = list(range(chips - 1, -1, -1))
    for step in order:
        core_copy(step).start()
    for step in order:
        core_copy(step).wait_recv()
        total = part_ref[own ^ (2 * step)].astype(F32) + core_recv[step].astype(F32)
        if step > 0:
            held[step] = total.astype(held.dtype)
            copy(step).start()
        else:
            out_ref[...] = total
    for step in range(1, chips):
        copy(step).wait_recv()
        out_ref[...] += recv[step].astype(F32)
    for step in range(1, chips):
        copy(step).wait_send()
    for step in range(chips):
        core_copy(step).wait_send()


def scatter_tok(part, collective_id):
    devices = part.shape[0]
    chips = devices // 2
    shard = part.shape[1:]
    return pl.pallas_call(
        scatter_tok_body,
        out_shape=jax.ShapeDtypeStruct(shard, F32),
        in_specs=[vmem()],
        out_specs=vmem(),
        scratch_shapes=[
            pltpu.VMEM((chips,) + shard, part.dtype),
            pltpu.VMEM((chips,) + shard, part.dtype),
            pltpu.VMEM((chips,) + shard, part.dtype),
        ]
        + [pltpu.SemaphoreType.DMA((chips,))] * 4,
        compiler_params=params(collective_id),
        cost_estimate=cost(0, 10_000_000),
        name="scatter_tok",
    )(part)


def line_sems(planes):
    return [pltpu.SemaphoreType.DMA((2, planes))] * 2


def line_copy(own, plane, step, source, target, send_sem, recv_sem, index):
    side = 0 if step > 0 else 1
    return pltpu.make_async_remote_copy(
        src_ref=source,
        dst_ref=target,
        send_sem=send_sem.at[side, index],
        recv_sem=recv_sem.at[side, index],
        device_id=(own, plane + step),
        device_id_type=MESH,
    )


def line_gather(own, plane, planes, arrays, start, pace):
    last = planes - 1

    def move(array, index, step):
        out, rest, send_sem, recv_sem = array
        shard = out.at[(index,) + rest]
        return line_copy(own, plane, step, shard, shard, send_sem, recv_sem, index)

    for step in range(1, planes + 1):
        yield start + pace * (step - 1)
        before, after = plane - (step - 1), plane + (step - 1)

        @pl.when(before >= 0)
        def _():
            for array in arrays:
                if step > 1:
                    move(array, before, 1).wait_recv()
                if step < planes:

                    @pl.when(plane < last)
                    def _():
                        move(array, before, 1).start()

        @pl.when(after <= last)
        def _():
            for array in arrays:
                if step > 1:
                    move(array, after, -1).wait_recv()
                if step < planes:

                    @pl.when(plane > 0)
                    def _():
                        move(array, after, -1).start()

    for index in range(planes):

        @pl.when((index <= plane) & (plane < last))
        def _():
            for array in arrays:
                move(array, index, 1).wait_send()

        @pl.when((index >= plane) & (plane > 0))
        def _():
            for array in arrays:
                move(array, index, -1).wait_send()


def line_reduce(own, plane, planes, half, part, total, send, recv, send_sem, recv_sem, start, pace):
    last = planes - 1

    def right(index):
        return line_copy(
            own, plane, 1, send.at[index, half], recv.at[index, half], send_sem, recv_sem, index
        )

    def left(index):
        slot = jnp.where(index == plane - 1, planes, index)
        return line_copy(
            own, plane, -1, send.at[index, half], recv.at[slot, half], send_sem, recv_sem, index
        )

    def add(index):
        send[index, half] = (
            part[index, half].astype(F32) + recv[index, half].astype(F32)
        ).astype(send.dtype)

    for step in range(1, planes):
        yield start + pace * (step - 1)
        upper, lower = planes - step + plane, step - planes + plane

        @pl.when((upper <= last) & (plane < last))
        def _():
            @pl.when(plane == 0)
            def _():
                send[upper, half] = part[upper, half]

            @pl.when(plane > 0)
            def _():
                right(upper).wait_recv()
                add(upper)

            right(upper).start()

        @pl.when((lower >= 0) & (plane > 0))
        def _():
            @pl.when(plane == last)
            def _():
                send[lower, half] = part[lower, half]

            @pl.when(plane < last)
            def _():
                left(lower).wait_recv()
                add(lower)

            left(lower).start()

    yield start + pace * (planes - 1)
    total[half] = part[plane, half].astype(F32)

    @pl.when(plane > 0)
    def _():
        right(plane).wait_recv()
        total[half] += recv[plane, half].astype(F32)

    @pl.when(plane < last)
    def _():
        left(plane).wait_recv()
        total[half] += recv[planes, half].astype(F32)

    yield start + pace * (2 * planes)
    for index in range(planes):

        @pl.when((index > plane) & (plane < last))
        def _():
            right(index).wait_send()

        @pl.when((index < plane) & (plane > 0))
        def _():
            left(index).wait_send()


def sum_flows(part_ref, gathered, scratch, math_rule, start=0.0, pace=8.7, extra=None):
    total, send, recv, send_sem, recv_sem, gather_send_sem, gather_recv_sem = scratch
    planes = part_ref.shape[0]
    own, plane = lax.axis_index("tok"), lax.axis_index("tp")
    lag = pace / 2

    def flow(half):
        begin = start + lag * half
        reducing = line_reduce(
            own, plane, planes, half, part_ref, total, send, recv,
            send_sem.at[half], recv_sem.at[half], begin, pace,
        )
        for number in range(planes):
            yield next(reducing)
        next(reducing)
        math_rule(plane, half, total, gathered)
        arrays = [(gathered, (half,), gather_send_sem.at[half], gather_recv_sem.at[half])]
        if extra is not None and half == HALVES - 1:
            arrays.append(extra)
        yield from line_gather(own, plane, planes, arrays, begin + pace * (planes - 1), pace)
        for _ in reducing:
            pass

    return [flow(half) for half in range(HALVES)]


def sum_scratch(planes, shard, width, kind):
    rows = shard // HALVES
    return [
        pltpu.VMEM((HALVES, rows, width), F32),
        pltpu.VMEM((planes, HALVES, rows, width), kind),
        pltpu.VMEM((planes + 1, HALVES, rows, width), kind),
    ] + [pltpu.SemaphoreType.DMA((HALVES, 2, planes))] * 4


def by_tiles(rows, step):
    lax.fori_loop(0, rows // 16, lambda i, c: (step(pl.ds(pl.multiple_of(i * 16, 16), 16)), c)[1], 0)


def norm_math(x_ref, gain_ref, hidden_ref, inv_ref):
    def rule(plane, half, total, gathered):
        def tile(rows):
            hidden = x_ref[plane, half, rows, :].astype(F32) + total[half, rows, :]
            inv = lax.rsqrt(jnp.mean(hidden * hidden, axis=1, keepdims=True) + norm_eps)
            hidden_ref[half, rows, :] = hidden
            inv_ref[half, rows, :] = inv
            gathered[plane, half, rows, :] = (hidden * inv * gain_ref[...]).astype(BF16)

        by_tiles(total.shape[1], tile)

    return rule


def ffn_math(hidden_ref, inv_ref, dy_ref, gain_ref, grad_ref, gains_ref):
    def rule(plane, half, total, gathered):
        if half == 0:
            gains_ref[...] = jnp.zeros_like(gains_ref)

        def tile(rows):
            dn = total[half, rows, :]
            hidden = hidden_ref[half, rows, :]
            inv = inv_ref[half, rows, :]
            weighted = gain_ref[...] * dn
            mean = jnp.mean(weighted * hidden, axis=1, keepdims=True)
            grad = (
                keep_scale * dy_ref[plane, half, rows, :].astype(F32)
                + inv * weighted
                - hidden * (inv * inv * inv * mean)
            )
            grad_ref[half, rows, :] = grad
            gathered[plane, half, rows, :] = grad.astype(BF16)
            gains_ref[0:1, :] += jnp.sum(dn * hidden * inv, axis=0, keepdims=True)

        by_tiles(total.shape[1], tile)

    return rule


def mixed_math(hidden_ref, x_ref):
    def rule(plane, half, total, gathered):
        def tile(rows):
            x = x_ref[plane, half, rows, :].astype(F32)
            branch = (hidden_ref[half, rows, :] - x) + total[half, rows, :]
            gathered[plane, half, rows, :] = (x + keep_scale * branch).astype(BF16)

        by_tiles(total.shape[1], tile)

    return rule


def attn_math(x_ref, inv_ref, dy_ref, grad_ref, gain_ref, ffn_gains_ref, gains_all):
    def rule(plane, half, total, gathered):
        if half == 0:
            gains_all[plane] = ffn_gains_ref[...]

        def tile(rows):
            dn = total[half, rows, :]
            x = x_ref[plane, half, rows, :].astype(F32)
            inv = inv_ref[plane, half, rows, :]
            weighted = gain_ref[...] * dn
            mean = jnp.mean(weighted * x, axis=1, keepdims=True)
            grad = (
                (1.0 - keep_scale) * dy_ref[plane, half, rows, :].astype(F32)
                + grad_ref[half, rows, :]
                + inv * weighted
                - x * (inv * inv * inv * mean)
            )
            gathered[plane, half, rows, :] = grad.astype(BF16)
            gains_all[plane, 1:2, :] += jnp.sum(dn * x * inv, axis=0, keepdims=True)

        by_tiles(total.shape[1], tile)

    return rule


def deal_sum_body(
    lens_ref, flags_ref, own_ref, part_ref, x_ref, gain_ref,
    out_ref, gathered, hidden_ref, inv_ref, *scratch,
):
    dealing, summing = scratch[:5], scratch[5:]
    greet(bit_peers(dealing[1].shape[0]), line=True)
    run(
        *sum_flows(part_ref, gathered, summing, norm_math(x_ref, gain_ref, hidden_ref, inv_ref)),
        deal_flow(lens_ref, flags_ref, own_ref, out_ref, dealing),
    )


def deal_sum(doc_lengths, keep_flags, blocks, part, x, gain, collective_id):
    planes, halves, rows, width = part.shape
    return pl.pallas_call(
        deal_sum_body,
        out_shape=(
            jax.ShapeDtypeStruct((SLOTS, BLOCK, width), blocks.dtype),
            jax.ShapeDtypeStruct(part.shape, BF16),
            jax.ShapeDtypeStruct((halves, rows, width), F32),
            jax.ShapeDtypeStruct((halves, rows, 1), F32),
        ),
        in_specs=[smem(), smem()] + [vmem()] * 4,
        out_specs=(vmem(),) * 4,
        scratch_shapes=deal_scratch(stages_of("tok"), width, blocks.dtype)
        + sum_scratch(planes, halves * rows, width, BF16),
        compiler_params=params(collective_id),
        cost_estimate=cost(0, 60_000_000),
        name="deal_sum",
    )(doc_lengths, keep_flags, blocks, part, x, gain)


def spread_flow(units, outs, scratch, pace):
    own, plane = lax.axis_index("tok"), lax.axis_index("tp")
    count = len(units)
    boxes, inboxes, core_inboxes = scratch[:count], scratch[count : 2 * count], scratch[2 * count : 3 * count]
    core_send_sem, core_recv_sem, send_sem, recv_sem = scratch[3 * count :]
    chips = boxes[0].shape[0]
    bits = [1 << i for i in range(int(math.log2(chips)))]
    orders = (bits, bits[::-1])
    stages = len(bits)

    def core_copy(unit, chip):
        return pltpu.make_async_remote_copy(
            src_ref=boxes[unit].at[chip],
            dst_ref=core_inboxes[unit].at[chip],
            send_sem=core_send_sem.at[unit, chip],
            recv_sem=core_recv_sem.at[unit, chip],
            device_id=(own ^ 1, plane),
            device_id_type=MESH,
        )

    def active(half, stage):
        gone = orders[half][:stage]
        return [chip for chip in range(chips) if all(chip & bit == 0 for bit in gone)]

    def slot(stage, half, chip):
        before = sum(chips >> (earlier + 1) for earlier in range(stage))
        return before + active(half, stage + 1).index(chip)

    def copy(unit, half, stage, chip):
        bit = orders[half][stage]
        there = slot(stage, half, chip)
        return pltpu.make_async_remote_copy(
            src_ref=boxes[unit].at[chip ^ bit, half],
            dst_ref=inboxes[unit].at[there, half],
            send_sem=send_sem.at[unit, half, there],
            recv_sem=recv_sem.at[unit, half, there],
            device_id=(own ^ (2 * bit), plane),
            device_id_type=MESH,
        )

    def offer(unit, chip):
        for half in range(2):
            term = units[unit]((own ^ (2 * chip)) ^ 1, half)
            boxes[unit][chip, half] = term.astype(BF16)
        core_copy(unit, chip).start()

    def collect(unit, chip):
        core_copy(unit, chip).wait()
        for half in range(2):
            term = units[unit](own ^ (2 * chip), half)
            term = term + core_inboxes[unit][chip, half].astype(F32)
            boxes[unit][chip, half] = term.astype(BF16)
            bit = orders[half][0]
            if chip & bit:
                copy(unit, half, 0, chip ^ bit).start()

    def take(unit, stage, half):
        for chip in active(half, stage + 1):
            copy(unit, half, stage, chip).wait_recv()
            got = inboxes[unit][slot(stage, half, chip), half].astype(F32)
            total = boxes[unit][chip, half].astype(F32) + got
            if stage < stages - 1:
                boxes[unit][chip, half] = total.astype(BF16)
                bit = orders[half][stage + 1]
                if chip & bit:
                    copy(unit, half, stage + 1, chip ^ bit).start()
            else:
                rows = total.shape[0]
                outs[unit][half * rows : (half + 1) * rows, :] = total

    chip_order = sorted(range(chips), key=lambda chip: -bin(chip).count("1"))
    for unit in range(count):
        for chip in chip_order:
            yield 0.1 + 3 * unit
            offer(unit, chip)
        for chip in chip_order:
            yield 3.2 + 3 * unit
            collect(unit, chip)
    for stage in range(stages):
        for unit in range(count):
            for half in range(2):
                yield 6.0 + pace * (unit + 1 + count * stage)
                take(unit, stage, half)
    for unit in range(count):
        for half in range(2):
            for stage in range(stages):
                for chip in active(half, stage + 1):
                    copy(unit, half, stage, chip).wait_send()


def spread_scratch(shapes, devices):
    chips = devices // 2
    boxes = [pltpu.VMEM((chips, 2, rows // 2, columns), BF16) for rows, columns in shapes]
    inboxes = [pltpu.VMEM((chips - 1, 2, rows // 2, columns), BF16) for rows, columns in shapes]
    return (
        boxes
        + inboxes
        + boxes
        + [pltpu.SemaphoreType.DMA((len(shapes), chips))] * 2
        + [pltpu.SemaphoreType.DMA((len(shapes), 2, chips - 1))] * 2
    )


def window(ref, number, size):
    if size % 128 == 0:
        return ref[:, pl.ds(pl.multiple_of(number * size, size), size)]
    parts = 128 // size
    tile = ref[:, pl.ds(pl.multiple_of(number // parts * 128, 128), 128)].astype(F32)
    return choose(
        number % parts, [tile[:, i * size : (i + 1) * size] for i in range(parts)]
    ).astype(ref.dtype)


def rows_by_owner(left_ref, right_ref, rows):
    def term(owner, half):
        return lax.dot_general(
            window(left_ref, owner * 2 + half, rows // 2),
            right_ref[...],
            (((0,), (0,)), ((), ())),
            preferred_element_type=F32,
        )

    return term


def columns_by_owner(left_ref, right_ref, columns):
    def term(owner, half):
        rows = left_ref.shape[1] // 2
        return lax.dot_general(
            left_ref[:, half * rows : (half + 1) * rows],
            window(right_ref, owner, columns),
            (((0,), (0,)), ((), ())),
            preferred_element_type=F32,
        )

    return term


def ffn_sums_body(
    part_ref, hidden_ref, inv_ref, dy_ref, gain_ref, normed_ref, dgate_ref, dup_ref, inner_ref, dm_ref,
    mixed_part_ref, x_ref,
    gathered, grad_ref, gains_ref, gate_out, up_out, down_out, mixed_gathered, *scratch,
):
    summing, mixing, spreading = scratch[:7], scratch[7:14], scratch[14:]
    own, plane = lax.axis_index("tok"), lax.axis_index("tp")
    devices = lax.axis_size("tok")
    share = normed_ref.shape[1] // devices
    chips = devices // 2
    greet([(own ^ 1, plane)] + [(own ^ (2 << i), plane) for i in range(stages_of("tok") - 1)], True)
    run(
        *sum_flows(
            part_ref,
            gathered,
            summing,
            ffn_math(hidden_ref, inv_ref, dy_ref, gain_ref, grad_ref, gains_ref),
        ),
        *sum_flows(mixed_part_ref, mixed_gathered, mixing, mixed_math(hidden_ref, x_ref), 27.0, 11.0),
        spread_flow(
            [
                rows_by_owner(normed_ref, dgate_ref, share),
                rows_by_owner(normed_ref, dup_ref, share),
                columns_by_owner(inner_ref, dm_ref, share),
            ],
            [gate_out, up_out, down_out],
            spreading,
            15.6,
        ),
    )


def ffn_sums(
    part, hidden, inv, dy, gain, normed, dgate, dup, inner, dm, mixed_part, x, collective_id
):
    planes, halves, rows, width = part.shape
    shard = halves * rows
    devices = lax.axis_size("tok")
    share = width // devices
    wide = dgate.shape[1]
    shapes = [(share, wide), (share, wide), (wide, share)]
    return pl.pallas_call(
        ffn_sums_body,
        out_shape=[
            jax.ShapeDtypeStruct(part.shape, BF16),
            jax.ShapeDtypeStruct(hidden.shape, F32),
            jax.ShapeDtypeStruct((8, width), F32),
        ]
        + [jax.ShapeDtypeStruct(shape, F32) for shape in shapes]
        + [jax.ShapeDtypeStruct(part.shape, BF16)],
        in_specs=[vmem()] * 12,
        out_specs=[vmem()] * 7,
        scratch_shapes=sum_scratch(planes, shard, width, BF16) * 2 + spread_scratch(shapes, devices),
        compiler_params=params(collective_id),
        cost_estimate=cost(0, 80_000_000),
        name="ffn_sums",
    )(part, hidden, inv, dy, gain, normed, dgate, dup, inner, dm, mixed_part, x)


def attn_sums_body(
    lens_ref, flags_ref, part_ref, x_ref, inv_ref, dy_ref, grad_ref, gain_ref, ffn_gains_ref,
    kept_ref, home_ref, normed_ref, dqkv_ref, attended_ref, da_ref,
    gathered, gains_ref, mixed_ref, qkv_out, out_out, *scratch,
):
    summing, undealing, scratch = scratch[:7], scratch[7:12], scratch[12:]
    gains_all, gains_sems, spreading = scratch[0], scratch[1:3], scratch[3:]
    planes = part_ref.shape[0]
    share = normed_ref.shape[1] // lax.axis_size("tok")
    greet(bit_peers(stages_of("tok")), True)
    run(
        *sum_flows(
            part_ref,
            gathered,
            summing,
            attn_math(x_ref, inv_ref, dy_ref, grad_ref, gain_ref, ffn_gains_ref, gains_all),
            extra=(gains_all, ()) + gains_sems,
        ),
        undeal_flow(lens_ref, flags_ref, kept_ref, home_ref, mixed_ref, undealing, 7.0),
        spread_flow(
            [
                rows_by_owner(normed_ref, dqkv_ref, share),
                columns_by_owner(attended_ref, da_ref, share),
            ],
            [qkv_out, out_out],
            spreading,
            15.0,
        ),
    )
    total = gains_all[0]
    for index in range(1, planes):
        total = total + gains_all[index]
    gains_ref[...] = total


def attn_sums(
    doc_lengths, keep_flags, part, x, inv, dy, grad, gain, ffn_gains, kept, home, normed, dqkv,
    attended, da, collective_id,
):
    planes, halves, rows, width = part.shape
    shard = halves * rows
    devices = lax.axis_size("tok")
    share = width // devices
    shapes = [(share, dqkv.shape[1]), (attended.shape[1], share)]
    return pl.pallas_call(
        attn_sums_body,
        out_shape=[
            jax.ShapeDtypeStruct(part.shape, BF16),
            jax.ShapeDtypeStruct((8, width), F32),
            jax.ShapeDtypeStruct(home.shape, BF16),
        ]
        + [jax.ShapeDtypeStruct(shape, F32) for shape in shapes],
        in_specs=[smem(), smem()] + [vmem()] * 13,
        out_specs=[vmem()] * 5,
        scratch_shapes=sum_scratch(planes, shard, width, BF16)
        + deal_scratch(stages_of("tok"), width, BF16)
        + [pltpu.VMEM((planes, 8, width), F32)]
        + line_sems(planes)
        + spread_scratch(shapes, devices),
        compiler_params=params(collective_id),
        cost_estimate=cost(0, 80_000_000),
        name="attn_sums",
    )(
        doc_lengths, keep_flags, part, x, inv, dy, grad, gain, ffn_gains, kept, home, normed, dqkv,
        attended, da,
    )


def rotary_tables(doc_lengths, keep_flags, ranks):
    blocks = keep_flags * (doc_lengths // BLOCK)
    ends = jnp.cumsum(blocks, dtype=jnp.int32)
    starts = ends - blocks
    inside = (ranks[:, None] >= starts[None, :]) & (ranks[:, None] < ends[None, :])
    first = jnp.sum(jnp.where(inside, starts[None, :], 0), axis=1, dtype=jnp.int32)
    offsets = jnp.arange(BLOCK, dtype=jnp.int32)
    positions = (((ranks - first) * BLOCK)[:, None] + offsets[None, :]).reshape(-1)
    half_dim = HD // 2
    freqs = jnp.exp(jnp.arange(half_dim, dtype=jnp.float32) * (-2.0 * math.log(10000.0) / HD))
    angles = positions.astype(jnp.float32)[:, None] * freqs[None, :]
    cosine, sine = jnp.cos(angles), jnp.sin(angles)
    return jnp.concatenate([cosine, cosine], axis=1), jnp.concatenate([sine, -sine], axis=1)


def unrotate(values, cosine, sine):
    half_dim = HD // 2
    swapped = jnp.concatenate([values[:, half_dim:], values[:, :half_dim]], axis=1)
    return values * cosine + swapped * sine


def over_columns(left, right):
    return lax.dot_general(
        left, right, (((1,), (1,)), ((), ())), preferred_element_type=jnp.float32
    )


def on_device(
    tokens,
    gain_attn,
    w_query,
    w_key,
    w_value,
    w_out,
    gain_ffn,
    w_gate,
    w_up,
    w_down,
    cotangent,
    doc_lengths,
    keep_flags,
):
    length = tokens.shape[0]
    model_width = tokens.shape[1]
    devices = lax.axis_size("tok")
    planes = lax.axis_size("tp")
    own_index = lax.axis_index("tok")
    blocks_here = length // BLOCK
    kept_here = blocks_here // 2
    total_blocks = blocks_here * devices
    kept_total = kept_here * devices
    rows = kept_here * BLOCK
    token_blocks = tokens.reshape(blocks_here, BLOCK, model_width)
    grad_blocks = cotangent.reshape(blocks_here, BLOCK, model_width)

    rows_x = deal(doc_lengths, keep_flags, token_blocks, 0).reshape(rows, model_width)

    own_ranks = own_index + jnp.arange(kept_here, dtype=jnp.int32) * devices
    cosine, sine = rotary_tables(doc_lengths, keep_flags, own_ranks)
    own = jnp.reshape(own_index, (1,)).astype(jnp.int32)
    normed_one, inv_one, queries, kv_all = project(
        rows_x, gain_attn.reshape(1, -1), w_query, w_key, w_value, cosine, sine, 2
    )
    attended, attended_wide, log_totals = attend(doc_lengths, keep_flags, own, queries, kv_all)

    shard = rows // planes

    def by_plane(array):
        return array.reshape(planes, HALVES, shard // HALVES, array.shape[1])

    x_planes = by_plane(rows_x)
    rows_dy, normed_two, hidden_res, inv_two = deal_sum(
        doc_lengths,
        keep_flags,
        grad_blocks,
        by_plane(jnp.dot(attended, w_out, preferred_element_type=jnp.float32).astype(jnp.bfloat16)),
        x_planes,
        gain_ffn.reshape(1, -1),
        1,
    )
    rows_dy = rows_dy.reshape(rows, model_width)
    normed_two = normed_two.reshape(rows, model_width)
    gate = jnp.dot(normed_two, w_gate, preferred_element_type=jnp.float32)
    upper = jnp.dot(normed_two, w_up, preferred_element_type=jnp.float32)
    sigma = jax.nn.sigmoid(gate)
    swish = gate * sigma
    inner = (swish * upper).astype(jnp.bfloat16)

    grad_m = (keep_scale * rows_dy.astype(jnp.float32)).astype(jnp.bfloat16)
    grad_inner = over_columns(grad_m, w_down)
    grad_gate_pre = (grad_inner * upper * sigma * (1.0 + gate * (1.0 - sigma))).astype(jnp.bfloat16)
    grad_up_pre = (grad_inner * swish).astype(jnp.bfloat16)
    part_two = (
        over_columns(grad_gate_pre, w_gate) + over_columns(grad_up_pre, w_up)
    ).astype(jnp.bfloat16)

    dy_planes = by_plane(rows_dy)
    grad_a, grad_hidden, gains_ffn, grad_gate, grad_up, grad_down, mixed_rows = ffn_sums(
        by_plane(part_two),
        hidden_res,
        inv_two,
        dy_planes,
        gain_ffn.reshape(1, -1),
        normed_two,
        grad_gate_pre,
        grad_up_pre,
        inner,
        grad_m,
        by_plane(jnp.dot(inner, w_down, preferred_element_type=jnp.float32).astype(jnp.bfloat16)),
        x_planes,
        4,
    )
    grad_a = grad_a.reshape(rows, model_width)

    grad_attended = over_columns(grad_a, w_out).astype(jnp.bfloat16)
    grad_query_pre, grad_kv = attend_back(
        doc_lengths,
        keep_flags,
        own,
        queries,
        grad_attended,
        kv_all,
        attended_wide,
        log_totals,
        cosine,
        sine,
    )
    grad_kv = scatter_tok(grad_kv, 5)
    grad_key_pre = unrotate(grad_kv[:, :HD], cosine, sine).astype(jnp.bfloat16)
    grad_value_pre = grad_kv[:, HD:].astype(jnp.bfloat16)
    part_one = (
        over_columns(grad_query_pre, w_query)
        + over_columns(grad_key_pre, w_key)
        + over_columns(grad_value_pre, w_value)
    ).astype(jnp.bfloat16)
    grad_rows, gains, mixed, grad_qkv, grad_out = attn_sums(
        doc_lengths,
        keep_flags,
        by_plane(part_one),
        x_planes,
        by_plane(inv_one),
        dy_planes,
        grad_hidden,
        gain_attn.reshape(1, -1),
        gains_ffn,
        mixed_rows.reshape(kept_here, BLOCK, model_width),
        token_blocks,
        normed_one,
        jnp.concatenate([grad_query_pre, grad_key_pre, grad_value_pre], axis=1),
        attended,
        grad_a,
        6,
    )
    token_grad, gain_sums = undeal(
        doc_lengths,
        keep_flags,
        grad_rows.reshape(kept_here, BLOCK, model_width),
        grad_blocks,
        gains,
        9,
    )
    own_share = model_width // devices
    if gain_sums.shape[1] != own_share:
        gain_sums = lax.dynamic_slice_in_dim(gain_sums, own_index * own_share, own_share, 1)
    wide, thin = w_query.shape[1], w_key.shape[1]
    grad_query = grad_qkv[:, :wide]
    grad_key = grad_qkv[:, wide : wide + thin]
    grad_value = grad_qkv[:, wide + thin :]

    return (
        mixed.reshape(length, model_width),
        token_grad.reshape(length, model_width),
        gain_sums[1],
        grad_query,
        grad_key,
        grad_value,
        grad_out,
        gain_sums[0],
        grad_gate,
        grad_up,
        grad_down,
    )


def solution(mesh):
    placed = (
        P("tok", None),
        P(),
        P(None, "tp"),
        P(None, "tp"),
        P(None, "tp"),
        P("tp", None),
        P(),
        P(None, "tp"),
        P(None, "tp"),
        P("tp", None),
        P("tok", None),
        P(),
        P(),
    )
    return jax.shard_map(
        on_device,
        mesh=mesh,
        in_specs=placed,
        out_specs=(
            P("tok", None),
            P("tok", None),
            P("tok"),
            P("tok", "tp"),
            P("tok", "tp"),
            P("tok", "tp"),
            P("tp", "tok"),
            P("tok"),
            P("tok", "tp"),
            P("tok", "tp"),
            P("tp", "tok"),
        ),
        check_vma=False,
    )
```

```python
import functools
import math

import jax
import jax.numpy as jnp
from jax import lax
from jax.experimental import pallas as pl
from jax.experimental.pallas import tpu as pltpu
from jax.sharding import PartitionSpec as P

HD = 128
BLOCK = 128
SLOTS = 3
CHUNKS = 8
HALVES = 2
TILE = 16
MESH = pl.DeviceIdType.MESH
VMEM_BYTES = 60 * 2**20

norm_eps = 1e-05
keep_scale = 2.0
F32 = jnp.float32
BF16 = jnp.bfloat16


def vmem():
    return pl.BlockSpec(memory_space=pltpu.VMEM)


def smem():
    return pl.BlockSpec(memory_space=pltpu.SMEM)


def params(collective_id):
    return pltpu.CompilerParams(
        collective_id=collective_id, has_side_effects=True, vmem_limit_bytes=VMEM_BYTES
    )


def cost(flops, moved):
    return pl.CostEstimate(flops=flops, bytes_accessed=moved, transcendentals=0)


def greet(peers, line=False):
    barrier = pltpu.get_barrier_semaphore()
    for peer in peers:
        pl.semaphore_signal(barrier, inc=1, device_id=peer, device_id_type=MESH)
    if not line:
        pl.semaphore_wait(barrier, len(peers))
        return
    own, plane = lax.axis_index("tok"), lax.axis_index("tp")
    last = lax.axis_size("tp") - 1

    @pl.when(plane > 0)
    def _():
        pl.semaphore_signal(barrier, inc=1, device_id=(own, plane - 1), device_id_type=MESH)

    @pl.when(plane < last)
    def _():
        pl.semaphore_signal(barrier, inc=1, device_id=(own, plane + 1), device_id_type=MESH)

    end = (plane == 0) | (plane == last)

    @pl.when(end)
    def _():
        pl.semaphore_wait(barrier, len(peers) + 1)

    @pl.when(jnp.logical_not(end))
    def _():
        pl.semaphore_wait(barrier, len(peers) + 2)


def run(*flows, done=frozenset()):
    waiting = [[next(flow), number, flow] for number, flow in enumerate(flows)]

    def order(entry):
        step = entry[0] if isinstance(entry[0], tuple) else (entry[0], None)
        return (step[1] is not None and step[1] not in done, step[0], entry[1])

    while waiting:
        waiting.sort(key=order)
        entry = waiting[0]
        assert not order(entry)[0]
        try:
            entry[0] = next(entry[2])
        except StopIteration:
            waiting.pop(0)


def deal_tables(own, stages, blocks_here, lens_ref, flags_ref):
    def kept_before(place):
        total, start = jnp.int32(0), jnp.int32(0)
        for doc in range(lens_ref.shape[0]):
            blocks = lens_ref[doc] // BLOCK
            total = total + flags_ref[doc] * jnp.clip(place - start, 0, blocks)
            start = start + blocks
        return total

    def edges(stage):
        first = (own >> stage) << stage
        return (
            kept_before(first * blocks_here),
            kept_before((first + (1 << stage)) * blocks_here),
        )

    def located(stage):
        if stage == 0:
            ends = [kept_before(own * blocks_here + i + 1) for i in range(blocks_here)]

            def place(rank):
                index = jnp.int32(0)
                for end in ends:
                    index = index + (end <= rank).astype(jnp.int32)
                return index

            return place
        mine = (own >> (stage - 1)) << (stage - 1)
        low, high = edges(stage - 1)
        other = kept_before((mine ^ (1 << (stage - 1))) * blocks_here)

        def place(rank):
            inside = (rank >= low) & (rank < high)
            return jnp.where(inside, (rank - low) >> stage, SLOTS + ((rank - other) >> stage))

        return place

    keeps, sends = [], []
    for stage in range(stages):
        low, high = edges(stage)
        place = located(stage)
        period = 1 << (stage + 1)
        for table, target in ((keeps, own), (sends, own ^ (1 << stage))):
            first = low + ((target - low) & (period - 1))
            row = []
            for slot in range(SLOTS):
                rank = first + period * slot
                row.append(jnp.where(rank < high, place(rank), -1))
            table.append(row)
    place = located(stages)
    finals = [place(own + (slot << stages)) for slot in range(SLOTS)]
    return keeps, sends, finals


def choose(index, options, default=None):
    value = options[0] if default is None else default
    for number, option in enumerate(options):
        if number == 0 and default is None:
            continue
        value = jnp.where(index == number, option, value)
    return value


def bit_peers(stages):
    own, plane = lax.axis_index("tok"), lax.axis_index("tp")
    return [(own ^ (1 << stage), plane) for stage in range(stages)]


def deal_flow(lens_ref, flags_ref, own_ref, out_ref, scratch, pace=4.3):
    keep, send, recv, send_sem, recv_sem = scratch
    stages = send.shape[0]
    own = lax.axis_index("tok")
    blocks_here = own_ref.shape[0]
    rows = BLOCK // CHUNKS
    peers = bit_peers(stages)
    keeps, sends, finals = deal_tables(own, stages, blocks_here, lens_ref, flags_ref)

    def copy(stage, chunk):
        return pltpu.make_async_remote_copy(
            src_ref=send.at[stage, chunk],
            dst_ref=recv.at[stage, chunk],
            send_sem=send_sem.at[stage, chunk],
            recv_sem=recv_sem.at[stage, chunk],
            device_id=peers[stage],
            device_id_type=MESH,
        )

    def held(stage, chunk):
        if stage == 0:
            return [own_ref[i, pl.ds(chunk * rows, rows), :] for i in range(blocks_here)]
        return [keep[chunk, i] for i in range(SLOTS)] + [
            recv[stage - 1, chunk, i] for i in range(SLOTS)
        ]

    for stage in range(stages + 1):
        for chunk in range(CHUNKS):
            yield 0.0 if stage == 0 else 1 + 0.4 * chunk + pace * (stage - 1) * (chunk + 1)
            if stage > 0:
                copy(stage - 1, chunk).wait_recv()
            options = held(stage, chunk)
            if stage == stages:
                for slot in range(SLOTS):
                    out_ref[slot, pl.ds(chunk * rows, rows), :] = choose(finals[slot], options)
            else:
                for slot in range(SLOTS):
                    send[stage, chunk, slot] = choose(sends[stage][slot], options)
                copy(stage, chunk).start()
                for slot in range(SLOTS):
                    keep[chunk, slot] = choose(keeps[stage][slot], options)
    yield 1e6

    def drain(chunk, carry):
        for stage in range(stages):
            copy(stage, chunk).wait_send()
        return carry

    lax.fori_loop(0, CHUNKS, drain, 0)


def deal_scratch(stages, width, kind):
    moved = (CHUNKS, SLOTS, BLOCK // CHUNKS, width)
    return (
        [pltpu.VMEM(moved, kind)]
        + [pltpu.VMEM((stages,) + moved, kind)] * 2
        + [pltpu.SemaphoreType.DMA((stages, CHUNKS))] * 2
    )


def stages_of(axis):
    return int(math.log2(lax.axis_size(axis)))


def deal_body(lens_ref, flags_ref, own_ref, out_ref, *scratch):
    greet(bit_peers(scratch[1].shape[0]))
    run(deal_flow(lens_ref, flags_ref, own_ref, out_ref, scratch))


def deal(doc_lengths, keep_flags, blocks, collective_id):
    width = blocks.shape[2]
    return pl.pallas_call(
        deal_body,
        out_shape=jax.ShapeDtypeStruct((SLOTS, BLOCK, width), blocks.dtype),
        in_specs=[smem(), smem(), vmem()],
        out_specs=vmem(),
        scratch_shapes=deal_scratch(stages_of("tok"), width, blocks.dtype),
        compiler_params=params(collective_id),
        cost_estimate=cost(0, 40_000_000),
        name="deal",
    )(doc_lengths, keep_flags, blocks)


def undeal_flow(
    lens_ref, flags_ref, kept_ref, out_ref, home, scratch, start=0.0, pace=4.3, key=None, lag=0.0
):
    keep, send, recv, send_sem, recv_sem = scratch
    stages = recv.shape[0]
    own = lax.axis_index("tok")
    blocks_here = out_ref.shape[0]
    planes = kept_ref.shape[2]
    rows = BLOCK // CHUNKS
    peers = bit_peers(stages)
    keeps, sends, finals = deal_tables(own, stages, blocks_here, lens_ref, flags_ref)

    def copy(stage, chunk):
        return pltpu.make_async_remote_copy(
            src_ref=send.at[stage, chunk],
            dst_ref=recv.at[stage, chunk],
            send_sem=send_sem.at[stage, chunk],
            recv_sem=recv_sem.at[stage, chunk],
            device_id=peers[stage],
            device_id_type=MESH,
        )

    def pick_place(places, options, place, value):
        for index, option in zip(places, options):
            value = jnp.where(index == place, option, value)
        return value

    last = stages - 1
    for stage in range(last, -2, -1):
        for chunk in range(CHUNKS):
            half = chunk // planes
            begin = start + lag * half
            if stage == last:
                yield (begin, None if key is None else key + (half,))
            else:
                yield begin + 1 + pace * (chunk + last - stage - (stage < 0))
            span = pl.ds(chunk * rows, rows)
            if stage == last:
                options = [kept_ref[slot, half, chunk % planes] for slot in range(SLOTS)]
                places = finals
            else:
                copy(stage + 1, chunk).wait_recv()
                options = [keep[chunk, i] for i in range(SLOTS)] + [
                    recv[stage + 1, chunk, i] for i in range(SLOTS)
                ]
                places = keeps[stage + 1] + sends[stage + 1]
            if stage < 0:
                if chunk == 0:
                    home.wait()
                for place in range(blocks_here):
                    value = out_ref[place, span, :]
                    out_ref[place, span, :] = pick_place(places, options, place, value)
            else:
                for slot in range(SLOTS):
                    send[stage, chunk, slot] = pick_place(
                        places, options, SLOTS + slot, options[0]
                    )
                copy(stage, chunk).start()
                for slot in range(SLOTS):
                    keep[chunk, slot] = pick_place(places, options, slot, options[0])
    yield 1e6

    def drain(chunk, carry):
        for stage in range(stages):
            copy(stage, chunk).wait_send()
        return carry

    lax.fori_loop(0, CHUNKS, drain, 0)


def gain_flow(gains_ref, sum_ref, scratch, start, key=None):
    gain_recv, gain_send_sem, gain_recv_sem = scratch
    own, plane = lax.axis_index("tok"), lax.axis_index("tp")
    devices = gain_recv.shape[0]
    share = sum_ref.shape[1]

    def portion(there):
        if share < gains_ref.shape[1]:
            return gains_ref.at[:, pl.ds(pl.multiple_of(there * share, share), share)]
        return gains_ref

    def copy(step):
        return pltpu.make_async_remote_copy(
            src_ref=portion(own ^ step),
            dst_ref=gain_recv.at[step],
            send_sem=gain_send_sem.at[step],
            recv_sem=gain_recv_sem.at[step],
            device_id=(own ^ step, plane),
            device_id_type=MESH,
        )

    yield (start, key)
    for step in range(1, devices):
        copy(step).start()
    yield 2e5
    total = portion(own)[...]
    for step in range(1, devices):
        copy(step).wait()
        total = total + gain_recv[step]
    sum_ref[...] = total


def gain_share(width, devices):
    share = width // devices
    return share if share % 128 == 0 else width


def gain_scratch(devices, share):
    return [pltpu.VMEM((devices, 8, share), F32)] + [pltpu.SemaphoreType.DMA((devices,))] * 2


def all_peers():
    own, plane = lax.axis_index("tok"), lax.axis_index("tp")
    return [(own ^ step, plane) for step in range(1, lax.axis_size("tok"))]


def undeal_body(lens_ref, flags_ref, kept_ref, home_ref, gains_ref, out_ref, sum_ref, home_sem, *scratch):
    home = pltpu.make_async_copy(home_ref, out_ref, home_sem)
    home.start()
    greet(all_peers())
    run(
        undeal_flow(lens_ref, flags_ref, kept_ref, out_ref, home, scratch[:5]),
        gain_flow(gains_ref, sum_ref, scratch[5:], 0.0),
    )


def undeal(doc_lengths, keep_flags, kept, home, gains, collective_id):
    stages = stages_of("tok")
    devices = 1 << stages
    width = kept.shape[-1]
    share = gain_share(width, devices)
    return pl.pallas_call(
        undeal_body,
        out_shape=(
            jax.ShapeDtypeStruct(home.shape, home.dtype),
            jax.ShapeDtypeStruct((8, share), F32),
        ),
        in_specs=[smem(), smem(), vmem(), pl.BlockSpec(memory_space=pl.ANY), vmem()],
        out_specs=(vmem(), vmem()),
        scratch_shapes=[pltpu.SemaphoreType.DMA]
        + deal_scratch(stages, width, kept.dtype)
        + gain_scratch(devices, share),
        compiler_params=params(collective_id),
        cost_estimate=cost(0, 40_000_000),
        name="undeal",
    )(doc_lengths, keep_flags, kept, home, gains)


def project_body(
    x_ref, gain_ref, w_query_ref, w_key_ref, w_value_ref, cos_ref, sin_ref,
    normed_ref, inv_ref, query_ref, out_ref,
    mine_ref, send_sem, recv_sem, relay_send_sem, relay_recv_sem,
):
    devices = out_ref.shape[0]
    chips = devices // 2
    own = lax.axis_index("tok")
    plane = lax.axis_index("tp")
    partner = (own ^ 1, plane)
    rows = x_ref.shape[0]
    thin = w_key_ref.shape[1]
    greet([partner] + [(own ^ (2 * step), plane) for step in range(1, chips)])

    def copy(step):
        return pltpu.make_async_remote_copy(
            src_ref=mine_ref,
            dst_ref=out_ref.at[own],
            send_sem=send_sem.at[step],
            recv_sem=recv_sem.at[step],
            device_id=(own ^ (2 * step), plane),
            device_id_type=MESH,
        )

    def relay(step):
        return pltpu.make_async_remote_copy(
            src_ref=mine_ref if step == 0 else out_ref.at[own ^ (2 * step)],
            dst_ref=out_ref.at[own ^ (2 * step)],
            send_sem=relay_send_sem.at[step],
            recv_sem=relay_recv_sem.at[step],
            device_id=partner,
            device_id_type=MESH,
        )

    def norm(index, carry):
        span = pl.ds(pl.multiple_of(index * 16, 16), 16)
        x = x_ref[span, :].astype(F32)
        inv = lax.rsqrt(jnp.mean(x * x, axis=1, keepdims=True) + norm_eps)
        inv_ref[span, :] = inv
        normed_ref[span, :] = (x * inv * gain_ref[...]).astype(BF16)
        return carry

    lax.fori_loop(0, rows // 16, norm, 0)

    def product(w_ref):
        return lax.dot_general(
            normed_ref[...], w_ref[...], (((1,), (0,)), ((), ())), preferred_element_type=F32
        )

    keys = product(w_key_ref)
    for group in range(thin // HD):
        one = keys[:, group * HD : (group + 1) * HD]
        mine_ref[:, group * HD : (group + 1) * HD] = turn(one, cos_ref, sin_ref, -1.0).astype(BF16)
    mine_ref[:, thin:] = product(w_value_ref).astype(BF16)
    for step in range(1, chips):
        copy(step).start()
    relay(0).start()
    out_ref[own] = mine_ref[...]
    queries = product(w_query_ref)
    for head in range(w_query_ref.shape[1] // HD):
        one = queries[:, head * HD : (head + 1) * HD]
        query_ref[:, head * HD : (head + 1) * HD] = turn(one, cos_ref, sin_ref, -1.0).astype(BF16)
    for step in range(1, chips):
        copy(step).wait_recv()
        relay(step).start()
    for step in range(chips):
        relay(step).wait()
    for step in range(1, chips):
        copy(step).wait_send()


def turn(values, cos_ref, sin_ref, sign):
    return values * cos_ref[...] + pltpu.roll(values, HD // 2, 1) * (sin_ref[...] * sign)


def project(x, gain, w_query, w_key, w_value, cosine, sine, collective_id):
    devices = lax.axis_size("tok")
    chips = devices // 2
    rows = x.shape[0]
    both = w_key.shape[1] + w_value.shape[1]
    return pl.pallas_call(
        project_body,
        out_shape=(
            jax.ShapeDtypeStruct(x.shape, BF16),
            jax.ShapeDtypeStruct((rows, 1), F32),
            jax.ShapeDtypeStruct((rows, w_query.shape[1]), BF16),
            jax.ShapeDtypeStruct((devices, rows, both), BF16),
        ),
        in_specs=[vmem()] * 7,
        out_specs=(vmem(),) * 4,
        scratch_shapes=[pltpu.VMEM((rows, both), BF16)] + [pltpu.SemaphoreType.DMA((chips,))] * 4,
        compiler_params=params(collective_id),
        cost_estimate=cost(0, 30_000_000),
        name="project",
    )(x, gain, w_query, w_key, w_value, cosine, sine)


def first_rank(lens_ref, flags_ref, rank):
    first, start = jnp.int32(0), jnp.int32(0)
    for doc in range(lens_ref.shape[0]):
        blocks = flags_ref[doc] * (lens_ref[doc] // BLOCK)
        first = jnp.where((rank >= start) & (rank < start + blocks), start, first)
        start = start + blocks
    return first


def stack_heads(ref, slot):
    heads = ref.shape[1] // HD
    return jnp.concatenate(
        [ref[slot * BLOCK : (slot + 1) * BLOCK, i * HD : (i + 1) * HD] for i in range(heads)], axis=0
    )


def dot(left, right, dims):
    return lax.dot_general(left, right, ((dims[:1], dims[1:]), ((), ())), preferred_element_type=F32)


def key_block(kv_ref, rank):
    devices = kv_ref.shape[0]
    device, slot = lax.rem(rank, devices), lax.div(rank, devices)
    span = pl.ds(pl.multiple_of(slot * BLOCK, BLOCK), BLOCK)
    return device, span


def causal(scores):
    keys = lax.broadcasted_iota(jnp.int32, scores.shape, 0)
    queries = lax.rem(lax.broadcasted_iota(jnp.int32, scores.shape, 1), BLOCK)
    return jnp.where(keys <= queries, scores, -1e30)


def attend_body(lens_ref, flags_ref, own_ref, query_ref, kv_ref, out_ref, wide_ref, log_ref, total):
    devices = kv_ref.shape[0]
    scale = 1.0 / math.sqrt(HD)
    for slot in range(SLOTS):
        rank = own_ref[0] + devices * slot
        query = stack_heads(query_ref, slot)
        count = query.shape[0]
        total[...] = jnp.zeros_like(total)

        def visit(key_rank, state, masked):
            peak, weight = state
            device, span = key_block(kv_ref, key_rank)
            scores = dot(kv_ref[device, span, :HD], query, (1, 1)) * scale
            if masked:
                scores = causal(scores)
            higher = jnp.maximum(peak, jnp.max(scores, axis=0, keepdims=True))
            shrink = jnp.exp(peak - higher)
            probs = jnp.exp(scores - higher)
            weight = weight * shrink + jnp.sum(probs, axis=0, keepdims=True)
            values = kv_ref[device, span, HD:]
            total[...] = total[...] * shrink + dot(values, probs.astype(BF16), (0, 0))
            return higher, weight

        start = (jnp.full((1, count), -1e30, F32), jnp.zeros((1, count), F32))
        first = first_rank(lens_ref, flags_ref, rank)
        state = lax.fori_loop(first, rank, lambda r, s: visit(r, s, False), start)
        peak, weight = visit(rank, state, True)
        result = total[...] / weight
        wide_ref[slot] = result
        log_ref[slot] = jnp.broadcast_to(peak + jnp.log(weight), log_ref.shape[1:])
        turned = result.T.astype(BF16)
        for head in range(count // BLOCK):
            out_ref[slot * BLOCK : (slot + 1) * BLOCK, head * HD : (head + 1) * HD] = turned[
                head * BLOCK : (head + 1) * BLOCK
            ]


def attend(doc_lengths, keep_flags, own, query, kv):
    count = query.shape[1] // HD * BLOCK
    return pl.pallas_call(
        attend_body,
        out_shape=(
            jax.ShapeDtypeStruct(query.shape, BF16),
            jax.ShapeDtypeStruct((SLOTS, HD, count), F32),
            jax.ShapeDtypeStruct((SLOTS, 8, count), F32),
        ),
        in_specs=[smem()] * 3 + [vmem()] * 2,
        out_specs=(vmem(),) * 3,
        scratch_shapes=[pltpu.VMEM((HD, count), F32)],
        compiler_params=pltpu.CompilerParams(vmem_limit_bytes=VMEM_BYTES),
        cost_estimate=cost(1_000_000_000, 10_000_000),
        name="attend",
    )(doc_lengths, keep_flags, own, query, kv)


def attend_back_body(
    lens_ref, flags_ref, own_ref, query_ref, grad_ref, kv_ref, wide_ref, log_ref, cos_ref, sin_ref,
    grad_query_ref, grad_kv_ref, grad_kv, total,
):
    devices = kv_ref.shape[0]
    scale = 1.0 / math.sqrt(HD)
    grad_kv[...] = jnp.zeros_like(grad_kv)
    for slot in range(SLOTS):
        rank = own_ref[0] + devices * slot
        query = stack_heads(query_ref, slot)
        grad = stack_heads(grad_ref, slot)
        delta = jnp.sum(grad.astype(F32).T * wide_ref[slot], axis=0, keepdims=True)
        log_total = log_ref[slot, 0:1, :]
        total[...] = jnp.zeros_like(total)

        def visit(key_rank, masked):
            device, span = key_block(kv_ref, key_rank)
            keys, values = kv_ref[device, span, :HD], kv_ref[device, span, HD:]
            scores = dot(keys, query, (1, 1)) * scale
            if masked:
                scores = causal(scores)
            probs = jnp.exp(scores - log_total)
            grad_probs = dot(values, grad, (1, 1))
            grad_scores = (probs * (grad_probs - delta)).astype(BF16)
            grad_kv[device, span, HD:] += dot(probs.astype(BF16), grad, (1, 0))
            grad_kv[device, span, :HD] += dot(grad_scores, query, (1, 0)) * scale
            total[...] += dot(keys, grad_scores, (0, 0))

        def step(key_rank, carry):
            visit(key_rank, False)
            return carry

        lax.fori_loop(first_rank(lens_ref, flags_ref, rank), rank, step, 0)
        visit(rank, True)
        turned = (total[...] * scale).T
        span = pl.ds(slot * BLOCK, BLOCK)
        for head in range(turned.shape[0] // BLOCK):
            one = turned[head * BLOCK : (head + 1) * BLOCK]
            grad_query_ref[span, head * HD : (head + 1) * HD] = turn(
                one, cos_ref.at[span], sin_ref.at[span], 1.0
            ).astype(BF16)
    grad_kv_ref[...] = grad_kv[...].astype(BF16)


def attend_back(doc_lengths, keep_flags, own, query, grad, kv, wide, log_total, cosine, sine):
    count = query.shape[1] // HD * BLOCK
    return pl.pallas_call(
        attend_back_body,
        out_shape=(
            jax.ShapeDtypeStruct(query.shape, BF16),
            jax.ShapeDtypeStruct(kv.shape, BF16),
        ),
        in_specs=[smem()] * 3 + [vmem()] * 7,
        out_specs=(vmem(),) * 2,
        scratch_shapes=[pltpu.VMEM(kv.shape, F32), pltpu.VMEM((HD, count), F32)],
        compiler_params=pltpu.CompilerParams(vmem_limit_bytes=VMEM_BYTES),
        cost_estimate=cost(3_000_000_000, 20_000_000),
        name="attend_back",
    )(doc_lengths, keep_flags, own, query, grad, kv, wide, log_total, cosine, sine)


def scatter_tok_body(
    part_ref, out_ref, core_recv, held, recv, core_send_sem, core_recv_sem, send_sem, recv_sem
):
    devices = part_ref.shape[0]
    chips = devices // 2
    own = lax.axis_index("tok")
    plane = lax.axis_index("tp")
    partner = (own ^ 1, plane)
    greet([partner] + [(own ^ (2 * step), plane) for step in range(1, chips)])

    def core_copy(step):
        return pltpu.make_async_remote_copy(
            src_ref=part_ref.at[own ^ (2 * step) ^ 1],
            dst_ref=core_recv.at[step],
            send_sem=core_send_sem.at[step],
            recv_sem=core_recv_sem.at[step],
            device_id=partner,
            device_id_type=MESH,
        )

    def copy(step):
        return pltpu.make_async_remote_copy(
            src_ref=held.at[step],
            dst_ref=recv.at[step],
            send_sem=send_sem.at[step],
            recv_sem=recv_sem.at[step],
            device_id=(own ^ (2 * step), plane),
            device_id_type=MESH,
        )

    order = list(range(chips - 1, -1, -1))
    for step in order:
        core_copy(step).start()
    for step in order:
        core_copy(step).wait_recv()
        total = part_ref[own ^ (2 * step)].astype(F32) + core_recv[step].astype(F32)
        if step > 0:
            held[step] = total.astype(held.dtype)
            copy(step).start()
        else:
            out_ref[...] = total
    for step in range(1, chips):
        copy(step).wait_recv()
        out_ref[...] += recv[step].astype(F32)
    for step in range(1, chips):
        copy(step).wait_send()
    for step in range(chips):
        core_copy(step).wait_send()


def scatter_tok(part, collective_id):
    devices = part.shape[0]
    chips = devices // 2
    shard = part.shape[1:]
    return pl.pallas_call(
        scatter_tok_body,
        out_shape=jax.ShapeDtypeStruct(shard, F32),
        in_specs=[vmem()],
        out_specs=vmem(),
        scratch_shapes=[
            pltpu.VMEM((chips,) + shard, part.dtype),
            pltpu.VMEM((chips,) + shard, part.dtype),
            pltpu.VMEM((chips,) + shard, part.dtype),
        ]
        + [pltpu.SemaphoreType.DMA((chips,))] * 4,
        compiler_params=params(collective_id),
        cost_estimate=cost(0, 10_000_000),
        name="scatter_tok",
    )(part)


def line_sems(planes):
    return [pltpu.SemaphoreType.DMA((2, planes))] * 2


def line_copy(own, plane, step, source, target, send_sem, recv_sem, index):
    side = 0 if step > 0 else 1
    return pltpu.make_async_remote_copy(
        src_ref=source,
        dst_ref=target,
        send_sem=send_sem.at[side, index],
        recv_sem=recv_sem.at[side, index],
        device_id=(own, plane + step),
        device_id_type=MESH,
    )


def line_gather(own, plane, planes, arrays, start, pace, ready=None):
    last = planes - 1

    def move(array, index, step):
        shard, send_sem, recv_sem = array
        return line_copy(own, plane, step, shard(index), shard(index), send_sem, recv_sem, index)

    for step in range(1, planes + 1):
        yield start + pace * (step - 1)
        before, after = plane - (step - 1), plane + (step - 1)

        @pl.when(before >= 0)
        def _():
            for array in arrays:
                if step > 1:
                    move(array, before, 1).wait_recv()
                if step < planes:

                    @pl.when(plane < last)
                    def _():
                        move(array, before, 1).start()

        @pl.when(after <= last)
        def _():
            for array in arrays:
                if step > 1:
                    move(array, after, -1).wait_recv()
                if step < planes:

                    @pl.when(plane > 0)
                    def _():
                        move(array, after, -1).start()

    if ready is not None:
        ready()
    yield start + pace * (planes + 1)
    for index in range(planes):

        @pl.when((index <= plane) & (plane < last))
        def _():
            for array in arrays:
                move(array, index, 1).wait_send()

        @pl.when((index >= plane) & (plane > 0))
        def _():
            for array in arrays:
                move(array, index, -1).wait_send()


def line_reduce(own, plane, planes, half, part, total, send, recv, send_sem, recv_sem, start, pace):
    last = planes - 1

    def right(index):
        return line_copy(
            own, plane, 1, send.at[index, half], recv.at[index, half], send_sem, recv_sem, index
        )

    def left(index):
        slot = jnp.where(index == plane - 1, planes, index)
        return line_copy(
            own, plane, -1, send.at[index, half], recv.at[slot, half], send_sem, recv_sem, index
        )

    def add(index):
        send[index, half] = (
            part[:, half, index].astype(F32) + recv[index, half].astype(F32)
        ).astype(send.dtype)

    for step in range(1, planes):
        yield start + pace * (step - 1)
        upper, lower = planes - step + plane, step - planes + plane

        @pl.when((upper <= last) & (plane < last))
        def _():
            @pl.when(plane == 0)
            def _():
                send[upper, half] = part[:, half, upper]

            @pl.when(plane > 0)
            def _():
                right(upper).wait_recv()
                add(upper)

            right(upper).start()

        @pl.when((lower >= 0) & (plane > 0))
        def _():
            @pl.when(plane == last)
            def _():
                send[lower, half] = part[:, half, lower]

            @pl.when(plane < last)
            def _():
                left(lower).wait_recv()
                add(lower)

            left(lower).start()

    yield start + pace * (planes - 1)
    total[half] = part[:, half, plane].astype(F32)

    @pl.when(plane > 0)
    def _():
        right(plane).wait_recv()
        total[half] += recv[plane, half].astype(F32)

    @pl.when(plane < last)
    def _():
        left(plane).wait_recv()
        total[half] += recv[planes, half].astype(F32)

    yield start + pace * (2 * planes)
    for index in range(planes):

        @pl.when((index > plane) & (plane < last))
        def _():
            right(index).wait_send()

        @pl.when((index < plane) & (plane > 0))
        def _():
            left(index).wait_send()


def gather_flows(gathered, scratch, start, pace, done=None, key=None):
    send_sem, recv_sem = scratch
    planes = gathered.shape[2]
    own, plane = lax.axis_index("tok"), lax.axis_index("tp")

    def flow(half):
        array = (lambda index: gathered.at[:, half, index], send_sem.at[half], recv_sem.at[half])
        ready = None if key is None else lambda: done.add(key + (half,))
        yield from line_gather(own, plane, planes, [array], start + pace / 2 * half, pace, ready)

    return [flow(half) for half in range(HALVES)]


def sum_flows(
    part_ref, gathered, scratch, math_rule, start=0.0, pace=8.7, extra=None, done=None, key=None
):
    total, send, recv, send_sem, recv_sem = scratch[:5]
    planes = part_ref.shape[2]
    own, plane = lax.axis_index("tok"), lax.axis_index("tp")

    def flow(half):
        begin = start + pace / 2 * half
        reducing = line_reduce(
            own, plane, planes, half, part_ref, total, send, recv,
            send_sem.at[half], recv_sem.at[half], begin, pace,
        )
        for number in range(planes):
            yield next(reducing)
        next(reducing)
        math_rule(plane, half, total)
        if gathered is not None:
            arrays = [
                (
                    lambda index: gathered.at[:, half, index],
                    scratch[5].at[half],
                    scratch[6].at[half],
                )
            ]
            if extra is not None and half == HALVES - 1:
                arrays.append(extra)
            ready = None if key is None else lambda: done.add(key + (half,))
            yield from line_gather(
                own, plane, planes, arrays, begin + pace * (planes - 1), pace, ready
            )
        for _ in reducing:
            pass

    return [flow(half) for half in range(HALVES)]


def sum_scratch(planes, width, gathers=True):
    shard = (HALVES, SLOTS, TILE, width)
    return [
        pltpu.VMEM(shard, F32),
        pltpu.VMEM((planes,) + shard, BF16),
        pltpu.VMEM((planes + 1,) + shard, BF16),
    ] + [pltpu.SemaphoreType.DMA((HALVES, 2, planes))] * (4 if gathers else 2)


def norm_math(x_ref, gain_ref, hidden_ref, inv_ref, gathered):
    def rule(plane, half, total):
        for block in range(SLOTS):
            hidden = x_ref[block, half, plane].astype(F32) + total[half, block]
            inv = lax.rsqrt(jnp.mean(hidden * hidden, axis=1, keepdims=True) + norm_eps)
            hidden_ref[half, block] = hidden
            inv_ref[half, block] = inv
            gathered[block, half, plane] = (hidden * inv * gain_ref[...]).astype(BF16)

    return rule


def ffn_math(hidden_ref, inv_ref, dy_ref, gain_ref, grad_ref, gains_ref, gathered):
    def rule(plane, half, total):
        if half == 0:
            gains_ref[...] = jnp.zeros_like(gains_ref)
        for block in range(SLOTS):
            dn = total[half, block]
            hidden = hidden_ref[half, block]
            inv = inv_ref[half, block]
            weighted = gain_ref[...] * dn
            mean = jnp.mean(weighted * hidden, axis=1, keepdims=True)
            grad = (
                keep_scale * dy_ref[block, half, plane].astype(F32)
                + inv * weighted
                - hidden * (inv * inv * inv * mean)
            )
            grad_ref[half, block] = grad
            gathered[block, half, plane] = grad.astype(BF16)
            gains_ref[0:1, :] += jnp.sum(dn * hidden * inv, axis=0, keepdims=True)

    return rule


def mixed_math(hidden_ref, x_ref, mixed_ref):
    def rule(plane, half, total):
        for block in range(SLOTS):
            x = x_ref[block, half, plane].astype(F32)
            branch = (hidden_ref[half, block] - x) + total[half, block]
            mixed_ref[half, block] = (x + keep_scale * branch).astype(BF16)

    return rule


def attn_math(x_ref, inv_ref, dy_ref, grad_ref, gain_ref, ffn_gains_ref, gains_all, gathered):
    def rule(plane, half, total):
        if half == 0:
            gains_all[plane] = ffn_gains_ref[...]
        for block in range(SLOTS):
            dn = total[half, block]
            x = x_ref[block, half, plane].astype(F32)
            inv = inv_ref[block, half, plane]
            weighted = gain_ref[...] * dn
            mean = jnp.mean(weighted * x, axis=1, keepdims=True)
            grad = (
                (1.0 - keep_scale) * dy_ref[block, half, plane].astype(F32)
                + grad_ref[half, block]
                + inv * weighted
                - x * (inv * inv * inv * mean)
            )
            gathered[block, half, plane] = grad.astype(BF16)
            gains_all[plane, 1:2, :] += jnp.sum(dn * x * inv, axis=0, keepdims=True)

    return rule


def deal_sum_body(
    lens_ref, flags_ref, own_ref, part_ref, x_ref, gain_ref,
    out_ref, gathered, hidden_ref, inv_ref, *scratch,
):
    dealing, summing = scratch[:5], scratch[5:]
    greet(bit_peers(dealing[1].shape[0]), line=True)
    rule = norm_math(x_ref, gain_ref, hidden_ref, inv_ref, gathered)
    run(
        *sum_flows(part_ref, gathered, summing, rule),
        deal_flow(lens_ref, flags_ref, own_ref, out_ref, dealing),
    )


def deal_sum(doc_lengths, keep_flags, blocks, part, x, gain, collective_id):
    planes, width = part.shape[2], part.shape[4]
    shard = (HALVES, SLOTS, TILE)
    return pl.pallas_call(
        deal_sum_body,
        out_shape=(
            jax.ShapeDtypeStruct((SLOTS, BLOCK, width), blocks.dtype),
            jax.ShapeDtypeStruct(part.shape, BF16),
            jax.ShapeDtypeStruct(shard + (width,), F32),
            jax.ShapeDtypeStruct(shard + (1,), F32),
        ),
        in_specs=[smem(), smem()] + [vmem()] * 4,
        out_specs=(vmem(),) * 4,
        scratch_shapes=deal_scratch(stages_of("tok"), width, blocks.dtype)
        + sum_scratch(planes, width),
        compiler_params=params(collective_id),
        cost_estimate=cost(0, 60_000_000),
        name="deal_sum",
    )(doc_lengths, keep_flags, blocks, part, x, gain)


def spread_flow(units, outs, scratch, pace, start=0.0):
    own, plane = lax.axis_index("tok"), lax.axis_index("tp")
    count = len(units)
    boxes, inboxes, core_inboxes = scratch[:count], scratch[count : 2 * count], scratch[2 * count : 3 * count]
    core_send_sem, core_recv_sem, send_sem, recv_sem = scratch[3 * count :]
    chips = boxes[0].shape[0]
    bits = [1 << i for i in range(int(math.log2(chips)))]
    orders = (bits, bits[::-1])
    stages = len(bits)

    def core_copy(unit, chip):
        return pltpu.make_async_remote_copy(
            src_ref=boxes[unit].at[chip],
            dst_ref=core_inboxes[unit].at[chip],
            send_sem=core_send_sem.at[unit, chip],
            recv_sem=core_recv_sem.at[unit, chip],
            device_id=(own ^ 1, plane),
            device_id_type=MESH,
        )

    def active(half, stage):
        gone = orders[half][:stage]
        return [chip for chip in range(chips) if all(chip & bit == 0 for bit in gone)]

    def slot(stage, half, chip):
        before = sum(chips >> (earlier + 1) for earlier in range(stage))
        return before + active(half, stage + 1).index(chip)

    def copy(unit, half, stage, chip):
        bit = orders[half][stage]
        there = slot(stage, half, chip)
        return pltpu.make_async_remote_copy(
            src_ref=boxes[unit].at[chip ^ bit, half],
            dst_ref=inboxes[unit].at[there, half],
            send_sem=send_sem.at[unit, half, there],
            recv_sem=recv_sem.at[unit, half, there],
            device_id=(own ^ (2 * bit), plane),
            device_id_type=MESH,
        )

    def offer(unit, chip):
        for half in range(2):
            term = units[unit]((own ^ (2 * chip)) ^ 1, half)
            boxes[unit][chip, half] = term.astype(BF16)
        core_copy(unit, chip).start()

    def collect(unit, chip):
        core_copy(unit, chip).wait()
        for half in range(2):
            term = units[unit](own ^ (2 * chip), half)
            term = term + core_inboxes[unit][chip, half].astype(F32)
            boxes[unit][chip, half] = term.astype(BF16)
            bit = orders[half][0]
            if chip & bit:
                copy(unit, half, 0, chip ^ bit).start()

    def take(unit, stage, half):
        for chip in active(half, stage + 1):
            copy(unit, half, stage, chip).wait_recv()
            got = inboxes[unit][slot(stage, half, chip), half].astype(F32)
            total = boxes[unit][chip, half].astype(F32) + got
            if stage < stages - 1:
                boxes[unit][chip, half] = total.astype(BF16)
                bit = orders[half][stage + 1]
                if chip & bit:
                    copy(unit, half, stage + 1, chip ^ bit).start()
            else:
                rows = total.shape[0]
                outs[unit][half * rows : (half + 1) * rows, :] = total

    chip_order = sorted(range(chips), key=lambda chip: -bin(chip).count("1"))
    for unit in range(count):
        for chip in chip_order:
            yield start + 0.1 + 3 * unit
            offer(unit, chip)
        for chip in chip_order:
            yield start + 3.2 + 3 * unit
            collect(unit, chip)
    for stage in range(stages):
        for unit in range(count):
            for half in range(2):
                yield start + 6.0 + pace * (unit + 1 + count * stage)
                take(unit, stage, half)
    for unit in range(count):
        for half in range(2):
            for stage in range(stages):
                for chip in active(half, stage + 1):
                    copy(unit, half, stage, chip).wait_send()


def spread_scratch(shapes, devices):
    chips = devices // 2
    boxes = [pltpu.VMEM((chips, 2, rows // 2, columns), BF16) for rows, columns in shapes]
    inboxes = [pltpu.VMEM((chips - 1, 2, rows // 2, columns), BF16) for rows, columns in shapes]
    return (
        boxes
        + inboxes
        + boxes
        + [pltpu.SemaphoreType.DMA((len(shapes), chips))] * 2
        + [pltpu.SemaphoreType.DMA((len(shapes), 2, chips - 1))] * 2
    )


def window(ref, number, size):
    if size % 128 == 0:
        return ref[:, pl.ds(pl.multiple_of(number * size, size), size)]
    parts = 128 // size
    tile = ref[:, pl.ds(pl.multiple_of(number // parts * 128, 128), 128)].astype(F32)
    return choose(
        number % parts, [tile[:, i * size : (i + 1) * size] for i in range(parts)]
    ).astype(ref.dtype)


def rows_by_owner(left_ref, right_ref, rows):
    def term(owner, half):
        return lax.dot_general(
            window(left_ref, owner * 2 + half, rows // 2),
            right_ref[...],
            (((0,), (0,)), ((), ())),
            preferred_element_type=F32,
        )

    return term


def columns_by_owner(left_ref, right_ref, columns):
    def term(owner, half):
        rows = left_ref.shape[1] // 2
        return lax.dot_general(
            left_ref[:, half * rows : (half + 1) * rows],
            window(right_ref, owner, columns),
            (((0,), (0,)), ((), ())),
            preferred_element_type=F32,
        )

    return term


def ffn_sums_body(
    part_ref, hidden_ref, inv_ref, dy_ref, gain_ref, normed_ref, dgate_ref, dup_ref, inner_ref, dm_ref,
    mixed_part_ref, x_ref,
    gathered, grad_ref, gains_ref, gate_out, up_out, down_out, mixed_ref, *scratch,
):
    summing, mixing, spreading = scratch[:7], scratch[7:12], scratch[12:]
    own, plane = lax.axis_index("tok"), lax.axis_index("tp")
    devices = lax.axis_size("tok")
    share = normed_ref.shape[1] // devices
    chips = devices // 2
    greet([(own ^ 1, plane)] + [(own ^ (2 << i), plane) for i in range(stages_of("tok") - 1)], True)
    run(
        *sum_flows(
            part_ref,
            gathered,
            summing,
            ffn_math(hidden_ref, inv_ref, dy_ref, gain_ref, grad_ref, gains_ref, gathered),
        ),
        *sum_flows(mixed_part_ref, None, mixing, mixed_math(hidden_ref, x_ref, mixed_ref), 27.0, 11.0),
        spread_flow(
            [
                rows_by_owner(normed_ref, dgate_ref, share),
                rows_by_owner(normed_ref, dup_ref, share),
                columns_by_owner(inner_ref, dm_ref, share),
            ],
            [gate_out, up_out, down_out],
            spreading,
            15.6,
        ),
    )


def ffn_sums(
    part, hidden, inv, dy, gain, normed, dgate, dup, inner, dm, mixed_part, x, collective_id
):
    planes, width = part.shape[2], part.shape[4]
    devices = lax.axis_size("tok")
    share = width // devices
    wide = dgate.shape[1]
    shapes = [(share, wide), (share, wide), (wide, share)]
    return pl.pallas_call(
        ffn_sums_body,
        out_shape=[
            jax.ShapeDtypeStruct(part.shape, BF16),
            jax.ShapeDtypeStruct(hidden.shape, F32),
            jax.ShapeDtypeStruct((8, width), F32),
        ]
        + [jax.ShapeDtypeStruct(shape, F32) for shape in shapes]
        + [jax.ShapeDtypeStruct(hidden.shape, BF16)],
        in_specs=[vmem()] * 12,
        out_specs=[vmem()] * 7,
        scratch_shapes=sum_scratch(planes, width)
        + sum_scratch(planes, width, False)
        + spread_scratch(shapes, devices),
        compiler_params=params(collective_id),
        cost_estimate=cost(0, 80_000_000),
        name="ffn_sums",
    )(part, hidden, inv, dy, gain, normed, dgate, dup, inner, dm, mixed_part, x)


def together():
    return stages_of("tok") <= 3


def attn_sums_body(
    lens_ref, flags_ref, part_ref, mixed_ref, x_ref, inv_ref, dy_ref, grad_ref, gain_ref, ffn_gains_ref,
    normed_ref, dqkv_ref, attended_ref, da_ref, home_ref, grad_home_ref, *refs,
):
    both = together()
    gathered, gains_ref, mixed_out, qkv_out, out_out = refs[:5]
    refs = refs[5:]
    if both:
        grad_out, gathered = gathered, refs[0]
        gain_sums, gains_ref = gains_ref, refs[1]
        refs = refs[2:]
    summing, undealing, refs = refs[:7], refs[7:12], refs[12:]
    mixed_all, mixed_sems, home_sems = refs[0], refs[1:3], refs[3]
    gains_all, gains_sems, refs = refs[4], refs[5:7], refs[7:]
    planes = part_ref.shape[2]
    plane = lax.axis_index("tp")
    share = normed_ref.shape[1] // lax.axis_size("tok")
    home = pltpu.make_async_copy(home_ref, mixed_out, home_sems.at[0])
    home.start()
    if both:
        grad_home = pltpu.make_async_copy(grad_home_ref, grad_out, home_sems.at[1])
        grad_home.start()
        grad_undealing, gaining, refs = refs[:5], refs[5:8], refs[8:]
    greet(all_peers() if both else bit_peers(stages_of("tok")), True)
    for half in range(HALVES):
        mixed_all[:, half, plane] = mixed_ref[half]
    done = set()

    def sum_gains():
        yield (70.0, ("grad", HALVES - 1))
        total = gains_all[0]
        for index in range(1, planes):
            total = total + gains_all[index]
        gains_ref[...] = total
        done.add(("gains",))

    flows = [
        *gather_flows(mixed_all, mixed_sems, 0.0, 8.7, done, ("mixed",)),
        *sum_flows(
            part_ref,
            gathered,
            summing,
            attn_math(
                x_ref, inv_ref, dy_ref, grad_ref, gain_ref, ffn_gains_ref, gains_all, gathered
            ),
            9.0,
            10.0,
            (lambda index: gains_all.at[index],) + gains_sems,
            done,
            ("grad",),
        ),
        spread_flow(
            [
                rows_by_owner(normed_ref, dqkv_ref, share),
                columns_by_owner(attended_ref, da_ref, share),
            ],
            [qkv_out, out_out],
            refs,
            9.0,
        ),
        undeal_flow(
            lens_ref, flags_ref, mixed_all, mixed_out, home, undealing, 28.0, 4.5, ("mixed",), 6.0
        ),
        sum_gains(),
    ]
    if both:
        flows += [
            undeal_flow(
                lens_ref, flags_ref, gathered, grad_out, grad_home, grad_undealing,
                55.0, 4.5, ("grad",), 8.0,
            ),
            gain_flow(gains_ref, gain_sums, gaining, 72.0, ("gains",)),
        ]
    run(*flows, done=done)


def attn_sums(
    doc_lengths, keep_flags, part, mixed, x, inv, dy, grad, gain, ffn_gains, normed, dqkv, attended,
    da, home, grad_home, collective_id,
):
    planes, width = part.shape[2], part.shape[4]
    devices = lax.axis_size("tok")
    share = width // devices
    shapes = [(share, dqkv.shape[1]), (attended.shape[1], share)]
    both = together()
    rows_shape = jax.ShapeDtypeStruct(part.shape, BF16)
    gains_shape = jax.ShapeDtypeStruct((8, width), F32)
    blocks_shape = jax.ShapeDtypeStruct(home.shape, BF16)
    gain_part = gain_share(width, devices)
    first = (
        [blocks_shape, jax.ShapeDtypeStruct((8, gain_part), F32)] if both else [rows_shape, gains_shape]
    )
    dealing = deal_scratch(stages_of("tok"), width, BF16)
    grads, gains, mixed_blocks, qkv, out = pl.pallas_call(
        attn_sums_body,
        out_shape=first
        + [blocks_shape]
        + [jax.ShapeDtypeStruct(shape, F32) for shape in shapes],
        in_specs=[smem(), smem()] + [vmem()] * 12 + [pl.BlockSpec(memory_space=pl.ANY)] * 2,
        out_specs=[vmem()] * 5,
        scratch_shapes=(
            [pltpu.VMEM(part.shape, BF16), pltpu.VMEM((8, width), F32)] if both else []
        )
        + sum_scratch(planes, width)
        + dealing
        + [pltpu.VMEM(part.shape, BF16)]
        + [pltpu.SemaphoreType.DMA((HALVES, 2, planes))] * 2
        + [pltpu.SemaphoreType.DMA((2,)), pltpu.VMEM((planes, 8, width), F32)]
        + line_sems(planes)
        + (dealing + gain_scratch(devices, gain_part) if both else [])
        + spread_scratch(shapes, devices),
        compiler_params=params(collective_id),
        cost_estimate=cost(0, 80_000_000),
        name="attn_sums",
    )(
        doc_lengths, keep_flags, part, mixed, x, inv, dy, grad, gain, ffn_gains, normed, dqkv, attended,
        da, home, grad_home,
    )
    if not both:
        grads, gains = undeal(doc_lengths, keep_flags, grads, grad_home, gains, collective_id + 1)
    return mixed_blocks, grads, gains, qkv, out


def rotary_tables(doc_lengths, keep_flags, ranks):
    blocks = keep_flags * (doc_lengths // BLOCK)
    ends = jnp.cumsum(blocks, dtype=jnp.int32)
    starts = ends - blocks
    inside = (ranks[:, None] >= starts[None, :]) & (ranks[:, None] < ends[None, :])
    first = jnp.sum(jnp.where(inside, starts[None, :], 0), axis=1, dtype=jnp.int32)
    offsets = jnp.arange(BLOCK, dtype=jnp.int32)
    positions = (((ranks - first) * BLOCK)[:, None] + offsets[None, :]).reshape(-1)
    half_dim = HD // 2
    freqs = jnp.exp(jnp.arange(half_dim, dtype=jnp.float32) * (-2.0 * math.log(10000.0) / HD))
    angles = positions.astype(jnp.float32)[:, None] * freqs[None, :]
    cosine, sine = jnp.cos(angles), jnp.sin(angles)
    return jnp.concatenate([cosine, cosine], axis=1), jnp.concatenate([sine, -sine], axis=1)


def unrotate(values, cosine, sine):
    half_dim = HD // 2
    swapped = jnp.concatenate([values[:, half_dim:], values[:, :half_dim]], axis=1)
    return values * cosine + swapped * sine


def over_columns(left, right):
    return lax.dot_general(
        left, right, (((1,), (1,)), ((), ())), preferred_element_type=jnp.float32
    )


def on_device(
    tokens,
    gain_attn,
    w_query,
    w_key,
    w_value,
    w_out,
    gain_ffn,
    w_gate,
    w_up,
    w_down,
    cotangent,
    doc_lengths,
    keep_flags,
):
    length = tokens.shape[0]
    model_width = tokens.shape[1]
    devices = lax.axis_size("tok")
    planes = lax.axis_size("tp")
    own_index = lax.axis_index("tok")
    blocks_here = length // BLOCK
    kept_here = blocks_here // 2
    rows = kept_here * BLOCK
    token_blocks = tokens.reshape(blocks_here, BLOCK, model_width)
    grad_blocks = cotangent.reshape(blocks_here, BLOCK, model_width)

    rows_x = deal(doc_lengths, keep_flags, token_blocks, 0).reshape(rows, model_width)

    own_ranks = own_index + jnp.arange(kept_here, dtype=jnp.int32) * devices
    cosine, sine = rotary_tables(doc_lengths, keep_flags, own_ranks)
    own = jnp.reshape(own_index, (1,)).astype(jnp.int32)
    normed_one, inv_one, queries, kv_all = project(
        rows_x, gain_attn.reshape(1, -1), w_query, w_key, w_value, cosine, sine, 2
    )
    attended, attended_wide, log_totals = attend(doc_lengths, keep_flags, own, queries, kv_all)

    def by_plane(array):
        return array.reshape(kept_here, HALVES, planes, TILE, array.shape[1])

    x_planes = by_plane(rows_x)
    rows_dy, normed_two, hidden_res, inv_two = deal_sum(
        doc_lengths,
        keep_flags,
        grad_blocks,
        by_plane(jnp.dot(attended, w_out, preferred_element_type=jnp.float32).astype(jnp.bfloat16)),
        x_planes,
        gain_ffn.reshape(1, -1),
        1,
    )
    rows_dy = rows_dy.reshape(rows, model_width)
    normed_two = normed_two.reshape(rows, model_width)
    gate = jnp.dot(normed_two, w_gate, preferred_element_type=jnp.float32)
    upper = jnp.dot(normed_two, w_up, preferred_element_type=jnp.float32)
    sigma = jax.nn.sigmoid(gate)
    swish = gate * sigma
    inner = (swish * upper).astype(jnp.bfloat16)

    grad_m = (keep_scale * rows_dy.astype(jnp.float32)).astype(jnp.bfloat16)
    grad_inner = over_columns(grad_m, w_down)
    grad_gate_pre = (grad_inner * upper * sigma * (1.0 + gate * (1.0 - sigma))).astype(jnp.bfloat16)
    grad_up_pre = (grad_inner * swish).astype(jnp.bfloat16)
    part_two = (
        over_columns(grad_gate_pre, w_gate) + over_columns(grad_up_pre, w_up)
    ).astype(jnp.bfloat16)

    dy_planes = by_plane(rows_dy)
    grad_a, grad_hidden, gains_ffn, grad_gate, grad_up, grad_down, mixed_rows = ffn_sums(
        by_plane(part_two),
        hidden_res,
        inv_two,
        dy_planes,
        gain_ffn.reshape(1, -1),
        normed_two,
        grad_gate_pre,
        grad_up_pre,
        inner,
        grad_m,
        by_plane(jnp.dot(inner, w_down, preferred_element_type=jnp.float32).astype(jnp.bfloat16)),
        x_planes,
        4,
    )
    grad_a = grad_a.reshape(rows, model_width)

    grad_attended = over_columns(grad_a, w_out).astype(jnp.bfloat16)
    grad_query_pre, grad_kv = attend_back(
        doc_lengths,
        keep_flags,
        own,
        queries,
        grad_attended,
        kv_all,
        attended_wide,
        log_totals,
        cosine,
        sine,
    )
    grad_kv = scatter_tok(grad_kv, 5)
    grad_key_pre = unrotate(grad_kv[:, :HD], cosine, sine).astype(jnp.bfloat16)
    grad_value_pre = grad_kv[:, HD:].astype(jnp.bfloat16)
    part_one = (
        over_columns(grad_query_pre, w_query)
        + over_columns(grad_key_pre, w_key)
        + over_columns(grad_value_pre, w_value)
    ).astype(jnp.bfloat16)
    mixed, token_grad, gain_sums, grad_qkv, grad_out = attn_sums(
        doc_lengths,
        keep_flags,
        by_plane(part_one),
        mixed_rows,
        x_planes,
        by_plane(inv_one),
        dy_planes,
        grad_hidden,
        gain_attn.reshape(1, -1),
        gains_ffn,
        normed_one,
        jnp.concatenate([grad_query_pre, grad_key_pre, grad_value_pre], axis=1),
        attended,
        grad_a,
        token_blocks,
        grad_blocks,
        6,
    )
    own_share = model_width // devices
    if gain_sums.shape[1] != own_share:
        gain_sums = lax.dynamic_slice_in_dim(gain_sums, own_index * own_share, own_share, 1)
    wide, thin = w_query.shape[1], w_key.shape[1]
    grad_query = grad_qkv[:, :wide]
    grad_key = grad_qkv[:, wide : wide + thin]
    grad_value = grad_qkv[:, wide + thin :]

    return (
        mixed.reshape(length, model_width),
        token_grad.reshape(length, model_width),
        gain_sums[1],
        grad_query,
        grad_key,
        grad_value,
        grad_out,
        gain_sums[0],
        grad_gate,
        grad_up,
        grad_down,
    )


def solution(mesh):
    placed = (
        P("tok", None),
        P(),
        P(None, "tp"),
        P(None, "tp"),
        P(None, "tp"),
        P("tp", None),
        P(),
        P(None, "tp"),
        P(None, "tp"),
        P("tp", None),
        P("tok", None),
        P(),
        P(),
    )
    return jax.shard_map(
        on_device,
        mesh=mesh,
        in_specs=placed,
        out_specs=(
            P("tok", None),
            P("tok", None),
            P("tok"),
            P("tok", "tp"),
            P("tok", "tp"),
            P("tok", "tp"),
            P("tp", "tok"),
            P("tok"),
            P("tok", "tp"),
            P("tok", "tp"),
            P("tp", "tok"),
        ),
        check_vma=False,
    )
```

```python
import functools
import math

import jax
import jax.numpy as jnp
from jax import lax
from jax.experimental import pallas as pl
from jax.experimental.pallas import tpu as pltpu
from jax.sharding import PartitionSpec as P

HD = 128
BLOCK = 128
SLOTS = 3
CHUNKS = 8
HALVES = 2
TILE = 16
HOP = 2.0
MESH = pl.DeviceIdType.MESH
VMEM_BYTES = 60 * 2**20

norm_eps = 1e-05
keep_scale = 2.0
F32 = jnp.float32
BF16 = jnp.bfloat16


def vmem():
    return pl.BlockSpec(memory_space=pltpu.VMEM)


def smem():
    return pl.BlockSpec(memory_space=pltpu.SMEM)


def params(collective_id):
    return pltpu.CompilerParams(
        collective_id=collective_id, has_side_effects=True, vmem_limit_bytes=VMEM_BYTES
    )


def cost(flops, moved):
    return pl.CostEstimate(flops=flops, bytes_accessed=moved, transcendentals=0)


def greet(peers, line=False):
    barrier = pltpu.get_barrier_semaphore()
    for peer in peers:
        pl.semaphore_signal(barrier, inc=1, device_id=peer, device_id_type=MESH)
    if not line:
        pl.semaphore_wait(barrier, len(peers))
        return
    own, plane = lax.axis_index("tok"), lax.axis_index("tp")
    last = lax.axis_size("tp") - 1

    @pl.when(plane > 0)
    def _():
        pl.semaphore_signal(barrier, inc=1, device_id=(own, plane - 1), device_id_type=MESH)

    @pl.when(plane < last)
    def _():
        pl.semaphore_signal(barrier, inc=1, device_id=(own, plane + 1), device_id_type=MESH)

    end = (plane == 0) | (plane == last)

    @pl.when(end)
    def _():
        pl.semaphore_wait(barrier, len(peers) + 1)

    @pl.when(jnp.logical_not(end))
    def _():
        pl.semaphore_wait(barrier, len(peers) + 2)


def run(*flows, done=frozenset()):
    waiting = [[next(flow), number, flow] for number, flow in enumerate(flows)]

    def order(entry):
        step = entry[0] if isinstance(entry[0], tuple) else (entry[0], None)
        return (step[1] is not None and step[1] not in done, step[0], entry[1])

    while waiting:
        waiting.sort(key=order)
        entry = waiting[0]
        assert not order(entry)[0]
        try:
            entry[0] = next(entry[2])
        except StopIteration:
            waiting.pop(0)


def anywhere():
    return pl.BlockSpec(memory_space=pl.ANY)


class Loaded:
    def __init__(self, source, target, sem):
        self.copy = pltpu.make_async_copy(source, target, sem)
        self.target = target
        self.here = False
        self.shape = target.shape

    def get(self):
        if not self.here:
            self.copy.wait()
            self.here = True
        return self.target


def load_all(sources, targets, sems):
    loads = [Loaded(*pair, sems.at[i]) for i, pair in enumerate(zip(sources, targets))]
    for load in loads:
        load.copy.start()
    return loads


class Stored:
    def __init__(self, target, source, sem):
        self.copy = pltpu.make_async_copy(source, target, sem)
        self.ref = source

    def send(self):
        self.copy.start()


def store_all(targets, sources, sems):
    return [Stored(*pair, sems.at[i]) for i, pair in enumerate(zip(targets, sources))]


def buffers(arrays):
    return [pltpu.VMEM(array.shape, array.dtype) for array in arrays]


def deal_tables(own, stages, blocks_here, lens_ref, flags_ref):
    def kept_before(place):
        total, start = jnp.int32(0), jnp.int32(0)
        for doc in range(lens_ref.shape[0]):
            blocks = lens_ref[doc] // BLOCK
            total = total + flags_ref[doc] * jnp.clip(place - start, 0, blocks)
            start = start + blocks
        return total

    def edges(stage):
        first = (own >> stage) << stage
        return (
            kept_before(first * blocks_here),
            kept_before((first + (1 << stage)) * blocks_here),
        )

    def located(stage):
        if stage == 0:
            ends = [kept_before(own * blocks_here + i + 1) for i in range(blocks_here)]

            def place(rank):
                index = jnp.int32(0)
                for end in ends:
                    index = index + (end <= rank).astype(jnp.int32)
                return index

            return place
        mine = (own >> (stage - 1)) << (stage - 1)
        low, high = edges(stage - 1)
        other = kept_before((mine ^ (1 << (stage - 1))) * blocks_here)

        def place(rank):
            inside = (rank >= low) & (rank < high)
            return jnp.where(inside, (rank - low) >> stage, SLOTS + ((rank - other) >> stage))

        return place

    keeps, sends = [], []
    for stage in range(stages):
        low, high = edges(stage)
        place = located(stage)
        period = 1 << (stage + 1)
        for table, target in ((keeps, own), (sends, own ^ (1 << stage))):
            first = low + ((target - low) & (period - 1))
            row = []
            for slot in range(SLOTS):
                rank = first + period * slot
                row.append(jnp.where(rank < high, place(rank), -1))
            table.append(row)
    place = located(stages)
    finals = [place(own + (slot << stages)) for slot in range(SLOTS)]
    return keeps, sends, finals


def choose(index, options):
    value = options[0]
    for number, option in enumerate(options[1:]):
        value = jnp.where(index == number + 1, option, value)
    return value


def slot_of(keep, recv, chunk, index):
    stayed = keep[chunk, jnp.clip(index, 0, SLOTS - 1)]
    arrived = recv[jnp.clip(index - SLOTS, 0, SLOTS - 1)]
    return jnp.where(index < SLOTS, stayed, arrived)


def deal_refs(scratch):
    keep, send = scratch[:2]
    stages = send.shape[0]
    recv = [scratch[2 + i * CHUNKS : 2 + (i + 1) * CHUNKS] for i in range(stages)]
    return keep, send, recv, *scratch[2 + stages * CHUNKS : 4 + stages * CHUNKS]


def bit_peers(stages):
    own, plane = lax.axis_index("tok"), lax.axis_index("tp")
    return [(own ^ (1 << stage), plane) for stage in range(stages)]


def deal_flow(lens_ref, flags_ref, blocks, finish, scratch, pace=4.3, urgent=False):
    keep, send, recv, send_sem, recv_sem = deal_refs(scratch)
    stages = send.shape[0]
    own = lax.axis_index("tok")
    blocks_here = blocks.shape[0]
    rows = BLOCK // CHUNKS
    peers = bit_peers(stages)
    keeps, sends, finals = deal_tables(own, stages, blocks_here, lens_ref, flags_ref)

    def copy(stage, chunk):
        return pltpu.make_async_remote_copy(
            src_ref=send.at[stage, chunk],
            dst_ref=recv[stage][chunk],
            send_sem=send_sem.at[stage, chunk],
            recv_sem=recv_sem.at[stage, chunk],
            device_id=peers[stage],
            device_id_type=MESH,
        )

    def held(stage, chunk, index):
        if stage == 0:
            block = jnp.clip(index, 0, blocks_here - 1)
            return blocks.get()[block, pl.ds(chunk * rows, rows), :]
        return slot_of(keep, recv[stage - 1][chunk], chunk, index)

    for stage in range(stages + 1):
        for chunk in range(CHUNKS):
            if stage < 2:
                yield 1.5 * stage + 0.3 * chunk
            else:
                slack = 4.0 if stage == stages and not urgent else 0.0
                yield 1.5 + HOP * (stage - 1) + pace * (chunk + stage - 1) + slack
            if stage > 0:
                copy(stage - 1, chunk).wait_recv()
            if stage == stages:
                finish(chunk, [held(stage, chunk, finals[slot]) for slot in range(SLOTS)])
            else:
                for slot in range(SLOTS):
                    send[stage, chunk, slot] = held(stage, chunk, sends[stage][slot])
                copy(stage, chunk).start()
                stay = [held(stage, chunk, keeps[stage][slot]) for slot in range(SLOTS)]
                for slot in range(SLOTS):
                    keep[chunk, slot] = stay[slot]
    yield 1e6

    for stage in range(stages):
        for chunk in range(CHUNKS):
            copy(stage, chunk).wait_send()


def deal_scratch(stages, width, kind):
    part = (SLOTS, BLOCK // CHUNKS, width)
    return (
        [pltpu.VMEM((CHUNKS,) + part, kind), pltpu.VMEM((stages, CHUNKS) + part, kind)]
        + [pltpu.VMEM(part, kind)] * (stages * CHUNKS)
        + [pltpu.SemaphoreType.DMA((stages, CHUNKS))] * 2
    )


def deal_count():
    return 4 + stages_of("tok") * CHUNKS


def stages_of(axis):
    return int(math.log2(lax.axis_size(axis)))


def undeal_flow(
    lens_ref, flags_ref, kept_ref, out_ref, home, scratch, start=0.0, pace=4.3, key=None, lag=0.0
):
    keep, send, recv, send_sem, recv_sem = deal_refs(scratch)
    stages = send.shape[0]
    own = lax.axis_index("tok")
    blocks_here = out_ref.shape[0]
    planes = kept_ref.shape[2]
    rows = BLOCK // CHUNKS
    peers = bit_peers(stages)
    keeps, sends, finals = deal_tables(own, stages, blocks_here, lens_ref, flags_ref)

    def copy(stage, chunk):
        return pltpu.make_async_remote_copy(
            src_ref=send.at[stage, chunk],
            dst_ref=recv[stage][chunk],
            send_sem=send_sem.at[stage, chunk],
            recv_sem=recv_sem.at[stage, chunk],
            device_id=peers[stage],
            device_id_type=MESH,
        )

    def source(places, place):
        index = jnp.int32(-1)
        for number, other in enumerate(places):
            index = jnp.where(other == place, number, index)
        return index

    last = stages - 1
    for stage in range(last, -2, -1):
        count = 2 * SLOTS if stage >= 0 else blocks_here
        places = finals if stage == last else keeps[stage + 1] + sends[stage + 1]
        sources = [source(places, place) for place in range(count)]
        for chunk in range(CHUNKS):
            half = chunk // planes
            begin = start + lag * half
            if stage == last:
                yield (begin, None if key is None else key + (half,))
                options = [kept_ref[slot, half, chunk % planes] for slot in range(SLOTS)]
            else:
                hops = last - stage
                slack = 5.0 if stage < 0 else 0.0
                yield begin + HOP * hops + pace * (chunk + hops - (stage < 0)) + slack
                copy(stage + 1, chunk).wait_recv()

            def block(place):
                if stage == last:
                    return choose(sources[place], options)
                return slot_of(keep, recv[stage + 1][chunk], chunk, sources[place])

            if stage < 0:
                if chunk == 0:
                    home.wait()
                span = pl.ds(chunk * rows, rows)
                for place in range(blocks_here):
                    value = out_ref[place, span, :]
                    out_ref[place, span, :] = jnp.where(sources[place] >= 0, block(place), value)
            else:
                for slot in range(SLOTS):
                    send[stage, chunk, slot] = block(SLOTS + slot)
                copy(stage, chunk).start()
                stay = [block(slot) for slot in range(SLOTS)]
                for slot in range(SLOTS):
                    keep[chunk, slot] = stay[slot]
    yield 1e6

    for stage in range(stages):
        for chunk in range(CHUNKS):
            copy(stage, chunk).wait_send()


def gain_flow(gains_ref, sum_ref, scratch, start, key=None):
    gain_recv, gain_send_sem, gain_recv_sem = scratch
    own, plane = lax.axis_index("tok"), lax.axis_index("tp")
    devices = gain_recv.shape[0]
    share = sum_ref.shape[1]

    def portion(there):
        if share < gains_ref.shape[1]:
            return gains_ref.at[:, pl.ds(pl.multiple_of(there * share, share), share)]
        return gains_ref

    def copy(step):
        return pltpu.make_async_remote_copy(
            src_ref=portion(own ^ step),
            dst_ref=gain_recv.at[step],
            send_sem=gain_send_sem.at[step],
            recv_sem=gain_recv_sem.at[step],
            device_id=(own ^ step, plane),
            device_id_type=MESH,
        )

    yield (start, key)
    for step in range(1, devices):
        copy(step).start()
    yield 2e5
    total = portion(own)[...]
    for step in range(1, devices):
        copy(step).wait()
        total = total + gain_recv[step]
    sum_ref[...] = total


def gain_share(width, devices):
    share = width // devices
    return share if share % 128 == 0 else width


def gain_scratch(devices, share):
    return [pltpu.VMEM((devices, 8, share), F32)] + [pltpu.SemaphoreType.DMA((devices,))] * 2


def all_peers():
    own, plane = lax.axis_index("tok"), lax.axis_index("tp")
    return [(own ^ step, plane) for step in range(1, lax.axis_size("tok"))]


def undeal_body(lens_ref, flags_ref, kept_ref, home_ref, gains_ref, out_ref, sum_ref, home_sem, *scratch):
    home = pltpu.make_async_copy(home_ref, out_ref, home_sem)
    home.start()
    greet(all_peers())
    run(
        undeal_flow(lens_ref, flags_ref, kept_ref, out_ref, home, scratch[: deal_count()]),
        gain_flow(gains_ref, sum_ref, scratch[deal_count() :], 0.0),
    )


def undeal(doc_lengths, keep_flags, kept, home, gains, collective_id):
    stages = stages_of("tok")
    devices = 1 << stages
    width = kept.shape[-1]
    share = gain_share(width, devices)
    return pl.pallas_call(
        undeal_body,
        out_shape=(
            jax.ShapeDtypeStruct(home.shape, home.dtype),
            jax.ShapeDtypeStruct((8, share), F32),
        ),
        in_specs=[smem(), smem(), vmem(), pl.BlockSpec(memory_space=pl.ANY), vmem()],
        out_specs=(vmem(), vmem()),
        scratch_shapes=[pltpu.SemaphoreType.DMA]
        + deal_scratch(stages, width, kept.dtype)
        + gain_scratch(devices, share),
        compiler_params=params(collective_id),
        cost_estimate=cost(0, 40_000_000),
        name="undeal",
    )(doc_lengths, keep_flags, kept, home, gains)


def deal_project_body(
    lens_ref, flags_ref, gain_ref, cos_ref, sin_ref, own_hbm, w_query_hbm, w_key_hbm, w_value_hbm,
    x_hbm, normed_hbm, inv_ref, query_ref, out_ref,
    own_half, w_query, w_key, w_value, x_ref, normed_ref, mine_ref, pair_send, pair_recv,
    load_sems, store_sems, pair_send_sem, pair_recv_sem,
    send_sem, recv_sem, relay_send_sem, relay_recv_sem, *dealing,
):
    devices = out_ref.shape[0]
    chips = devices // 2
    own = lax.axis_index("tok")
    plane = lax.axis_index("tp")
    partner = (own ^ 1, plane)
    width = own_half.shape[2]
    tile = BLOCK // CHUNKS
    thin = w_key.shape[1]
    columns = pl.ds(pl.multiple_of((plane % 2) * width, width), width)
    blocks, w_query, w_key, w_value = load_all(
        [own_hbm.at[:, :, columns], w_query_hbm, w_key_hbm, w_value_hbm],
        [own_half, w_query, w_key, w_value],
        load_sems,
    )
    steps = sorted({1 << i for i in range(stages_of("tok"))} | {2 * i for i in range(1, chips)})
    greet([(own ^ step, plane) for step in steps] + [(own, plane ^ 1)])

    def pair_copy(chunk):
        return pltpu.make_async_remote_copy(
            src_ref=pair_send.at[chunk],
            dst_ref=pair_recv.at[chunk],
            send_sem=pair_send_sem.at[chunk],
            recv_sem=pair_recv_sem.at[chunk],
            device_id=(own, plane ^ 1),
            device_id_type=MESH,
        )

    def finish(chunk, values):
        for slot, value in enumerate(values):
            pair_send[chunk, slot] = value
        pair_copy(chunk).start()
        for slot, value in enumerate(values):
            x_ref[slot, pl.ds(chunk * tile, tile), columns] = value

    def norms():
        for chunk in range(CHUNKS):
            yield 500.0 + chunk, (chunk,)
            other = pl.ds(pl.multiple_of((1 - plane % 2) * width, width), width)
            pair_copy(chunk).wait_recv()
            span = pl.ds(chunk * tile, tile)
            for slot in range(SLOTS):
                x_ref[slot, span, other] = pair_recv[chunk, slot]
            for slot in range(SLOTS):
                x = x_ref[slot, span, :].astype(F32)
                inv = lax.rsqrt(jnp.mean(x * x, axis=1, keepdims=True) + norm_eps)
                rows = pl.ds(slot * BLOCK + chunk * tile, tile)
                inv_ref[rows, :] = inv
                normed_ref[rows, :] = (x * inv * gain_ref[...]).astype(BF16)

    done = set()

    def mark(chunk, values):
        finish(chunk, values)
        done.add((chunk,))

    run(
        deal_flow(lens_ref, flags_ref, blocks, mark, dealing, 2.2, True),
        norms(),
        done=done,
    )
    stores = store_all([x_hbm, normed_hbm], [x_ref, normed_ref], store_sems)
    for store in stores:
        store.send()
    for chunk in range(CHUNKS):
        pair_copy(chunk).wait_send()

    def copy(step):
        return pltpu.make_async_remote_copy(
            src_ref=mine_ref,
            dst_ref=out_ref.at[own],
            send_sem=send_sem.at[step],
            recv_sem=recv_sem.at[step],
            device_id=(own ^ (2 * step), plane),
            device_id_type=MESH,
        )

    def relay(step):
        return pltpu.make_async_remote_copy(
            src_ref=mine_ref if step == 0 else out_ref.at[own ^ (2 * step)],
            dst_ref=out_ref.at[own ^ (2 * step)],
            send_sem=relay_send_sem.at[step],
            recv_sem=relay_recv_sem.at[step],
            device_id=partner,
            device_id_type=MESH,
        )

    def product(weight):
        return lax.dot_general(
            normed_ref[...], weight.get()[...], (((1,), (0,)), ((), ())), preferred_element_type=F32
        )

    keys = product(w_key)
    for group in range(thin // HD):
        one = keys[:, group * HD : (group + 1) * HD]
        mine_ref[:, group * HD : (group + 1) * HD] = turn(one, cos_ref, sin_ref, -1.0).astype(BF16)
    mine_ref[:, thin:] = product(w_value).astype(BF16)
    for step in range(1, chips):
        copy(step).start()
    relay(0).start()
    out_ref[own] = mine_ref[...]
    queries = product(w_query)
    for head in range(w_query.shape[1] // HD):
        one = queries[:, head * HD : (head + 1) * HD]
        query_ref[:, head * HD : (head + 1) * HD] = turn(one, cos_ref, sin_ref, -1.0).astype(BF16)
    for step in range(1, chips):
        copy(step).wait_recv()
        relay(step).start()
    for step in range(chips):
        relay(step).wait()
    for step in range(1, chips):
        copy(step).wait_send()
    for store in stores:
        store.copy.wait()


def turn(values, cos_ref, sin_ref, sign):
    return values * cos_ref[...] + pltpu.roll(values, HD // 2, 1) * (sin_ref[...] * sign)


def deal_project(
    doc_lengths, keep_flags, gain, cosine, sine, blocks, w_query, w_key, w_value, collective_id
):
    devices = lax.axis_size("tok")
    chips = devices // 2
    width = blocks.shape[2]
    rows = SLOTS * BLOCK
    both = w_key.shape[1] + w_value.shape[1]
    x_shape, normed_shape = (SLOTS, BLOCK, width), (rows, width)
    weights = [w_query, w_key, w_value]
    return pl.pallas_call(
        deal_project_body,
        out_shape=(
            jax.ShapeDtypeStruct(x_shape, BF16),
            jax.ShapeDtypeStruct(normed_shape, BF16),
            jax.ShapeDtypeStruct((rows, 1), F32),
            jax.ShapeDtypeStruct((rows, w_query.shape[1]), BF16),
            jax.ShapeDtypeStruct((devices, rows, both), BF16),
        ),
        in_specs=[smem()] * 2 + [vmem()] * 3 + [anywhere()] * 4,
        out_specs=(anywhere(),) * 2 + (vmem(),) * 3,
        scratch_shapes=[pltpu.VMEM(blocks.shape[:2] + (width // 2,), BF16)]
        + buffers(weights)
        + [
            pltpu.VMEM(x_shape, BF16),
            pltpu.VMEM(normed_shape, BF16),
            pltpu.VMEM((rows, both), BF16),
            pltpu.VMEM((CHUNKS, SLOTS, BLOCK // CHUNKS, width // 2), BF16),
            pltpu.VMEM((CHUNKS, SLOTS, BLOCK // CHUNKS, width // 2), BF16),
            pltpu.SemaphoreType.DMA((4,)),
            pltpu.SemaphoreType.DMA((2,)),
        ]
        + [pltpu.SemaphoreType.DMA((CHUNKS,))] * 2
        + [pltpu.SemaphoreType.DMA((chips,))] * 4
        + deal_scratch(stages_of("tok"), width // 2, BF16),
        compiler_params=params(collective_id),
        cost_estimate=cost(0, 60_000_000),
        name="deal_project",
    )(doc_lengths, keep_flags, gain, cosine, sine, blocks, *weights)


def first_rank(lens_ref, flags_ref, rank):
    first, start = jnp.int32(0), jnp.int32(0)
    for doc in range(lens_ref.shape[0]):
        blocks = flags_ref[doc] * (lens_ref[doc] // BLOCK)
        first = jnp.where((rank >= start) & (rank < start + blocks), start, first)
        start = start + blocks
    return first


def stack_heads(ref, slot):
    heads = ref.shape[1] // HD
    return jnp.concatenate(
        [ref[slot * BLOCK : (slot + 1) * BLOCK, i * HD : (i + 1) * HD] for i in range(heads)], axis=0
    )


def dot(left, right, dims):
    return lax.dot_general(left, right, ((dims[:1], dims[1:]), ((), ())), preferred_element_type=F32)


def key_block(kv_ref, rank):
    devices = kv_ref.shape[0]
    device, slot = lax.rem(rank, devices), lax.div(rank, devices)
    span = pl.ds(pl.multiple_of(slot * BLOCK, BLOCK), BLOCK)
    return device, span


def causal(scores):
    keys = lax.broadcasted_iota(jnp.int32, scores.shape, 0)
    queries = lax.rem(lax.broadcasted_iota(jnp.int32, scores.shape, 1), BLOCK)
    return jnp.where(keys <= queries, scores, -1e30)


def attend_body(lens_ref, flags_ref, own_ref, query_ref, kv_ref, out_ref, wide_ref, log_ref, total):
    devices = kv_ref.shape[0]
    scale = 1.0 / math.sqrt(HD)
    for slot in range(SLOTS):
        rank = own_ref[0] + devices * slot
        query = stack_heads(query_ref, slot)
        count = query.shape[0]
        total[...] = jnp.zeros_like(total)

        def visit(key_rank, state, masked):
            peak, weight = state
            device, span = key_block(kv_ref, key_rank)
            scores = dot(kv_ref[device, span, :HD], query, (1, 1)) * scale
            if masked:
                scores = causal(scores)
            higher = jnp.maximum(peak, jnp.max(scores, axis=0, keepdims=True))
            shrink = jnp.exp(peak - higher)
            probs = jnp.exp(scores - higher)
            weight = weight * shrink + jnp.sum(probs, axis=0, keepdims=True)
            values = kv_ref[device, span, HD:]
            total[...] = total[...] * shrink + dot(values, probs.astype(BF16), (0, 0))
            return higher, weight

        start = (jnp.full((1, count), -1e30, F32), jnp.zeros((1, count), F32))
        first = first_rank(lens_ref, flags_ref, rank)
        state = lax.fori_loop(first, rank, lambda r, s: visit(r, s, False), start)
        peak, weight = visit(rank, state, True)
        result = total[...] / weight
        wide_ref[slot] = result
        log_ref[slot] = jnp.broadcast_to(peak + jnp.log(weight), log_ref.shape[1:])
        turned = result.T.astype(BF16)
        for head in range(count // BLOCK):
            out_ref[slot * BLOCK : (slot + 1) * BLOCK, head * HD : (head + 1) * HD] = turned[
                head * BLOCK : (head + 1) * BLOCK
            ]


def attend(doc_lengths, keep_flags, own, query, kv):
    count = query.shape[1] // HD * BLOCK
    return pl.pallas_call(
        attend_body,
        out_shape=(
            jax.ShapeDtypeStruct(query.shape, BF16),
            jax.ShapeDtypeStruct((SLOTS, HD, count), F32),
            jax.ShapeDtypeStruct((SLOTS, 8, count), F32),
        ),
        in_specs=[smem()] * 3 + [vmem()] * 2,
        out_specs=(vmem(),) * 3,
        scratch_shapes=[pltpu.VMEM((HD, count), F32)],
        compiler_params=pltpu.CompilerParams(vmem_limit_bytes=VMEM_BYTES),
        cost_estimate=cost(1_000_000_000, 10_000_000),
        name="attend",
    )(doc_lengths, keep_flags, own, query, kv)


class Passed:
    def __init__(self, source, passing, targets, sems):
        self.first = pltpu.make_async_copy(source, passing, sems.at[0])
        self.rest = [pltpu.make_async_copy(part, to, sems.at[1]) for part, to in targets(passing)]
        self.first.start()

    def turn(self):
        self.first.wait()
        for copy in self.rest:
            copy.start()

    def end(self):
        for copy in self.rest:
            copy.wait()


def attend_back_body(
    lens_ref, flags_ref, own_ref, query_ref, grad_ref, kv_ref, wide_ref, log_ref, cos_ref, sin_ref,
    *refs,
):
    sources, grad_query_ref, grad_kv_ref, targets, grad_kv, total = (
        refs[:3], refs[3], refs[4], refs[5:8], refs[8], refs[9],
    )
    passing, sems = refs[10:13], refs[13]
    passes = [
        Passed(sources[i], passing[i], lambda ref, i=i: [(ref, targets[i])], sems.at[i])
        for i in range(3)
    ]
    devices = kv_ref.shape[0]
    scale = 1.0 / math.sqrt(HD)
    grad_kv[...] = jnp.zeros_like(grad_kv)
    for slot in range(SLOTS):
        if slot == 1:
            for one in passes:
                one.turn()
        rank = own_ref[0] + devices * slot
        query = stack_heads(query_ref, slot)
        grad = stack_heads(grad_ref, slot)
        delta = jnp.sum(grad.astype(F32).T * wide_ref[slot], axis=0, keepdims=True)
        log_total = log_ref[slot, 0:1, :]
        total[...] = jnp.zeros_like(total)

        def visit(key_rank, masked):
            device, span = key_block(kv_ref, key_rank)
            keys, values = kv_ref[device, span, :HD], kv_ref[device, span, HD:]
            scores = dot(keys, query, (1, 1)) * scale
            if masked:
                scores = causal(scores)
            probs = jnp.exp(scores - log_total)
            grad_probs = dot(values, grad, (1, 1))
            grad_scores = (probs * (grad_probs - delta)).astype(BF16)
            grad_kv[device, span, HD:] += dot(probs.astype(BF16), grad, (1, 0))
            grad_kv[device, span, :HD] += dot(grad_scores, query, (1, 0)) * scale
            total[...] += dot(keys, grad_scores, (0, 0))

        def step(key_rank, carry):
            visit(key_rank, False)
            return carry

        lax.fori_loop(first_rank(lens_ref, flags_ref, rank), rank, step, 0)
        visit(rank, True)
        turned = (total[...] * scale).T
        span = pl.ds(slot * BLOCK, BLOCK)
        for head in range(turned.shape[0] // BLOCK):
            one = turned[head * BLOCK : (head + 1) * BLOCK]
            grad_query_ref[span, head * HD : (head + 1) * HD] = turn(
                one, cos_ref.at[span], sin_ref.at[span], 1.0
            ).astype(BF16)
    grad_kv_ref[...] = grad_kv[...].astype(BF16)
    for one in passes:
        one.end()


def attend_back(doc_lengths, keep_flags, own, query, grad, kv, wide, log_total, cosine, sine, results):
    count = query.shape[1] // HD * BLOCK
    return pl.pallas_call(
        attend_back_body,
        out_shape=(
            jax.ShapeDtypeStruct(query.shape, BF16),
            jax.ShapeDtypeStruct(kv.shape, BF16),
        )
        + tuple(jax.ShapeDtypeStruct(result.shape, result.dtype) for result in results),
        in_specs=[smem()] * 3 + [vmem()] * 7 + [anywhere()] * 3,
        out_specs=(vmem(),) * 2 + (anywhere(),) * 3,
        scratch_shapes=[
            pltpu.VMEM(kv.shape, F32),
            pltpu.VMEM((HD, count), F32),
        ]
        + buffers(results)
        + [pltpu.SemaphoreType.DMA((3, 2))],
        compiler_params=pltpu.CompilerParams(vmem_limit_bytes=VMEM_BYTES),
        cost_estimate=cost(3_000_000_000, 20_000_000),
        name="attend_back",
    )(doc_lengths, keep_flags, own, query, grad, kv, wide, log_total, cosine, sine, *results)


def finish_body(mixed_ref, grad_ref, qkv_ref, out_ref, *refs):
    query_ref, key_ref = refs[2], refs[3]
    wide, thin = query_ref.shape[1], key_ref.shape[1]
    passing, sems = refs[6:10], refs[10]

    def parts(ref):
        yield ref.at[:, pl.ds(0, wide)], query_ref
        yield ref.at[:, pl.ds(wide, thin)], key_ref
        yield ref.at[:, pl.ds(wide + thin, thin)], refs[4]

    passes = [
        Passed(mixed_ref, passing[0], lambda ref: [(ref, refs[0])], sems.at[0]),
        Passed(grad_ref, passing[1], lambda ref: [(ref, refs[1])], sems.at[1]),
        Passed(out_ref, passing[2], lambda ref: [(ref, refs[5])], sems.at[2]),
        Passed(qkv_ref, passing[3], parts, sems.at[3]),
    ]
    for one in passes:
        one.turn()
    for one in passes:
        one.end()


def finish(mixed, grad, qkv, out, thin):
    share, wide = qkv.shape[0], qkv.shape[1] - 2 * thin
    shapes = [(mixed.shape, BF16), (grad.shape, BF16), ((share, wide), F32)]
    shapes += [((share, thin), F32)] * 2 + [(out.shape, F32)]
    return pl.pallas_call(
        finish_body,
        out_shape=[jax.ShapeDtypeStruct(*shape) for shape in shapes],
        in_specs=[anywhere()] * 4,
        out_specs=[anywhere()] * 6,
        scratch_shapes=buffers([mixed, grad, out, qkv]) + [pltpu.SemaphoreType.DMA((4, 2))],
        compiler_params=pltpu.CompilerParams(vmem_limit_bytes=VMEM_BYTES),
        cost_estimate=cost(0, 20_000_000),
        name="finish",
    )(mixed, grad, qkv, out)


def scatter_tok_body(
    part_ref, out_ref, core_recv, held, recv, core_send_sem, core_recv_sem, send_sem, recv_sem
):
    devices = part_ref.shape[0]
    chips = devices // 2
    own = lax.axis_index("tok")
    plane = lax.axis_index("tp")
    partner = (own ^ 1, plane)
    greet([partner] + [(own ^ (2 * step), plane) for step in range(1, chips)])

    def core_copy(step):
        return pltpu.make_async_remote_copy(
            src_ref=part_ref.at[own ^ (2 * step) ^ 1],
            dst_ref=core_recv.at[step],
            send_sem=core_send_sem.at[step],
            recv_sem=core_recv_sem.at[step],
            device_id=partner,
            device_id_type=MESH,
        )

    def copy(step):
        return pltpu.make_async_remote_copy(
            src_ref=held.at[step],
            dst_ref=recv.at[step],
            send_sem=send_sem.at[step],
            recv_sem=recv_sem.at[step],
            device_id=(own ^ (2 * step), plane),
            device_id_type=MESH,
        )

    order = list(range(chips - 1, -1, -1))
    for step in order:
        core_copy(step).start()
    for step in order:
        core_copy(step).wait_recv()
        total = part_ref[own ^ (2 * step)].astype(F32) + core_recv[step].astype(F32)
        if step > 0:
            held[step] = total.astype(held.dtype)
            copy(step).start()
        else:
            out_ref[...] = total
    for step in range(1, chips):
        copy(step).wait_recv()
        out_ref[...] += recv[step].astype(F32)
    for step in range(1, chips):
        copy(step).wait_send()
    for step in range(chips):
        core_copy(step).wait_send()


def scatter_tok(part, collective_id):
    devices = part.shape[0]
    chips = devices // 2
    shard = part.shape[1:]
    return pl.pallas_call(
        scatter_tok_body,
        out_shape=jax.ShapeDtypeStruct(shard, F32),
        in_specs=[vmem()],
        out_specs=vmem(),
        scratch_shapes=[
            pltpu.VMEM((chips,) + shard, part.dtype),
            pltpu.VMEM((chips,) + shard, part.dtype),
            pltpu.VMEM((chips,) + shard, part.dtype),
        ]
        + [pltpu.SemaphoreType.DMA((chips,))] * 4,
        compiler_params=params(collective_id),
        cost_estimate=cost(0, 10_000_000),
        name="scatter_tok",
    )(part)


def line_sems(planes):
    return [pltpu.SemaphoreType.DMA((2, planes))] * 2


def line_copy(own, plane, step, source, target, send_sem, recv_sem, index):
    side = 0 if step > 0 else 1
    return pltpu.make_async_remote_copy(
        src_ref=source,
        dst_ref=target,
        send_sem=send_sem.at[side, index],
        recv_sem=recv_sem.at[side, index],
        device_id=(own, plane + step),
        device_id_type=MESH,
    )


def line_gather(own, plane, planes, arrays, start, pace, ready=None):
    last = planes - 1

    def move(array, index, step):
        shard, send_sem, recv_sem = array
        return line_copy(own, plane, step, shard(index), shard(index), send_sem, recv_sem, index)

    for step in range(1, planes + 1):
        yield start + pace * (step - 1)
        before, after = plane - (step - 1), plane + (step - 1)

        @pl.when(before >= 0)
        def _():
            for array in arrays:
                if step > 1:
                    move(array, before, 1).wait_recv()
                if step < planes:

                    @pl.when(plane < last)
                    def _():
                        move(array, before, 1).start()

        @pl.when(after <= last)
        def _():
            for array in arrays:
                if step > 1:
                    move(array, after, -1).wait_recv()
                if step < planes:

                    @pl.when(plane > 0)
                    def _():
                        move(array, after, -1).start()

    if ready is not None:
        ready()
    yield start + pace * (planes + 1)
    for index in range(planes):

        @pl.when((index <= plane) & (plane < last))
        def _():
            for array in arrays:
                move(array, index, 1).wait_send()

        @pl.when((index >= plane) & (plane > 0))
        def _():
            for array in arrays:
                move(array, index, -1).wait_send()


def line_reduce(own, plane, planes, half, part, total, send, recv, send_sem, recv_sem, start, pace):
    last = planes - 1

    def right(index):
        return line_copy(
            own, plane, 1, send.at[index, half], recv.at[index, half], send_sem, recv_sem, index
        )

    def left(index):
        slot = jnp.where(index == plane - 1, planes, index)
        return line_copy(
            own, plane, -1, send.at[index, half], recv.at[slot, half], send_sem, recv_sem, index
        )

    def add(index):
        send[index, half] = (
            part[:, half, index].astype(F32) + recv[index, half].astype(F32)
        ).astype(send.dtype)

    for step in range(1, planes):
        yield start + pace * (step - 1)
        if step == 1:
            part = part.get()
        upper, lower = planes - step + plane, step - planes + plane

        @pl.when((upper <= last) & (plane < last))
        def _():
            @pl.when(plane == 0)
            def _():
                send[upper, half] = part[:, half, upper]

            @pl.when(plane > 0)
            def _():
                right(upper).wait_recv()
                add(upper)

            right(upper).start()

        @pl.when((lower >= 0) & (plane > 0))
        def _():
            @pl.when(plane == last)
            def _():
                send[lower, half] = part[:, half, lower]

            @pl.when(plane < last)
            def _():
                left(lower).wait_recv()
                add(lower)

            left(lower).start()

    yield start + pace * (planes - 1)
    total[half] = part[:, half, plane].astype(F32)

    @pl.when(plane > 0)
    def _():
        right(plane).wait_recv()
        total[half] += recv[plane, half].astype(F32)

    @pl.when(plane < last)
    def _():
        left(plane).wait_recv()
        total[half] += recv[planes, half].astype(F32)

    yield start + pace * (2 * planes)
    for index in range(planes):

        @pl.when((index > plane) & (plane < last))
        def _():
            right(index).wait_send()

        @pl.when((index < plane) & (plane > 0))
        def _():
            left(index).wait_send()


def gather_flows(gathered, scratch, start, pace, done=None, key=None):
    send_sem, recv_sem = scratch
    planes = gathered.shape[2]
    own, plane = lax.axis_index("tok"), lax.axis_index("tp")

    def flow(half):
        array = (lambda index: gathered.at[:, half, index], send_sem.at[half], recv_sem.at[half])
        ready = None if key is None else lambda: done.add(key + (half,))
        yield from line_gather(own, plane, planes, [array], start + pace / 2 * half, pace, ready)

    return [flow(half) for half in range(HALVES)]


def sum_flows(
    part_ref, gathered, scratch, math_rule, start=0.0, pace=8.7, extra=None, done=None, key=None
):
    total, send, recv, send_sem, recv_sem = scratch[:5]
    planes = part_ref.shape[2]
    own, plane = lax.axis_index("tok"), lax.axis_index("tp")

    def flow(half):
        begin = start + pace / 2 * half
        reducing = line_reduce(
            own, plane, planes, half, part_ref, total, send, recv,
            send_sem.at[half], recv_sem.at[half], begin, pace,
        )
        for number in range(planes):
            yield next(reducing)
        next(reducing)
        math_rule(plane, half, total)
        if gathered is not None:
            arrays = [
                (
                    lambda index: gathered.at[:, half, index],
                    scratch[5].at[half],
                    scratch[6].at[half],
                )
            ]
            if extra is not None and half == HALVES - 1:
                arrays.append(extra)
            ready = None if key is None else lambda: done.add(key + (half,))
            yield from line_gather(
                own, plane, planes, arrays, begin + pace * (planes - 1), pace, ready
            )
        for _ in reducing:
            pass

    return [flow(half) for half in range(HALVES)]


def sum_scratch(planes, width, gathers=True):
    shard = (HALVES, SLOTS, TILE, width)
    return [
        pltpu.VMEM(shard, F32),
        pltpu.VMEM((planes,) + shard, BF16),
        pltpu.VMEM((planes + 1,) + shard, BF16),
    ] + [pltpu.SemaphoreType.DMA((HALVES, 2, planes))] * (4 if gathers else 2)


def norm_math(x, gain_ref, hidden_ref, inv_ref, gathered):
    def rule(plane, half, total):
        x_ref = x.get()
        for block in range(SLOTS):
            hidden = x_ref[block, half, plane].astype(F32) + total[half, block]
            inv = lax.rsqrt(jnp.mean(hidden * hidden, axis=1, keepdims=True) + norm_eps)
            hidden_ref[half, block] = hidden
            inv_ref[half, block] = inv
            gathered[block, half, plane] = (hidden * inv * gain_ref[...]).astype(BF16)

    return rule


def ffn_math(hiddens, inv_ref, dy, gain_ref, grad_ref, gains_ref, gathered):
    def rule(plane, half, total):
        if half == 0:
            gains_ref[...] = jnp.zeros_like(gains_ref)
        hidden_ref, dy_ref = hiddens.get(), dy.get()
        for block in range(SLOTS):
            dn = total[half, block]
            hidden = hidden_ref[half, block]
            inv = inv_ref[half, block]
            weighted = gain_ref[...] * dn
            mean = jnp.mean(weighted * hidden, axis=1, keepdims=True)
            grad = (
                keep_scale * dy_ref[block, half, plane].astype(F32)
                + inv * weighted
                - hidden * (inv * inv * inv * mean)
            )
            grad_ref[half, block] = grad
            gathered[block, half, plane] = grad.astype(BF16)
            gains_ref[0:1, :] += jnp.sum(dn * hidden * inv, axis=0, keepdims=True)

    return rule


def mixed_math(hiddens, xs, mixed_ref):
    def rule(plane, half, total):
        hidden_ref, x_ref = hiddens.get(), xs.get()
        for block in range(SLOTS):
            x = x_ref[block, half, plane].astype(F32)
            branch = (hidden_ref[half, block] - x) + total[half, block]
            mixed_ref[half, block] = (x + keep_scale * branch).astype(BF16)

    return rule


def attn_math(xs, inv_ref, dy, grads, gain_ref, ffn_gains_ref, gains_all, gathered):
    def rule(plane, half, total):
        x_ref, dy_ref, grad_ref = xs.get(), dy.get(), grads.get()
        if half == 0:
            gains_all[plane] = ffn_gains_ref[...]
        for block in range(SLOTS):
            dn = total[half, block]
            x = x_ref[block, half, plane].astype(F32)
            inv = inv_ref[block, half, plane]
            weighted = gain_ref[...] * dn
            mean = jnp.mean(weighted * x, axis=1, keepdims=True)
            grad = (
                (1.0 - keep_scale) * dy_ref[block, half, plane].astype(F32)
                + grad_ref[half, block]
                + inv * weighted
                - x * (inv * inv * inv * mean)
            )
            gathered[block, half, plane] = grad.astype(BF16)
            gains_all[plane, 1:2, :] += jnp.sum(dn * x * inv, axis=0, keepdims=True)

    return rule


def deal_sum_body(
    lens_ref, flags_ref, gain_ref, own_hbm, part_hbm, x_hbm,
    out_hbm, gathered_hbm, hidden_ref, inv_ref,
    own_blocks, part, x, out_ref, gathered, load_sems, store_sems, *scratch,
):
    dealing, summing = scratch[: deal_count()], scratch[deal_count() :]
    part, blocks, x = load_all([part_hbm, own_hbm, x_hbm], [part, own_blocks, x], load_sems)
    out, rows = store_all([out_hbm, gathered_hbm], [out_ref, gathered], store_sems)
    greet(bit_peers(stages_of("tok")), line=True)
    tile = BLOCK // CHUNKS

    def finish(chunk, values):
        for slot, value in enumerate(values):
            out_ref[slot, pl.ds(chunk * tile, tile), :] = value
        if chunk == CHUNKS - 1:
            out.send()

    run(
        *sum_flows(part, gathered, summing, norm_math(x, gain_ref, hidden_ref, inv_ref, gathered)),
        deal_flow(lens_ref, flags_ref, blocks, finish, dealing),
    )
    rows.send()
    rows.copy.wait()
    out.copy.wait()


def deal_sum(doc_lengths, keep_flags, blocks, part, x, gain, collective_id):
    planes, width = part.shape[2], part.shape[4]
    shard = (HALVES, SLOTS, TILE)
    dealt = jax.ShapeDtypeStruct((SLOTS, BLOCK, width), blocks.dtype)
    rows = jax.ShapeDtypeStruct(part.shape, BF16)
    return pl.pallas_call(
        deal_sum_body,
        out_shape=(
            dealt,
            rows,
            jax.ShapeDtypeStruct(shard + (width,), F32),
            jax.ShapeDtypeStruct(shard + (1,), F32),
        ),
        in_specs=[smem(), smem(), vmem()] + [anywhere()] * 3,
        out_specs=(anywhere(),) * 2 + (vmem(),) * 2,
        scratch_shapes=buffers([blocks, part, x, dealt, rows])
        + [pltpu.SemaphoreType.DMA((3,)), pltpu.SemaphoreType.DMA((2,))]
        + deal_scratch(stages_of("tok"), width, blocks.dtype)
        + sum_scratch(planes, width),
        compiler_params=params(collective_id),
        cost_estimate=cost(0, 60_000_000),
        name="deal_sum",
    )(doc_lengths, keep_flags, gain, blocks, part, x)


def spread_flow(units, outs, scratch, pace, start=0.0):
    own, plane = lax.axis_index("tok"), lax.axis_index("tp")
    count = len(units)
    boxes, inboxes, core_inboxes = scratch[:count], scratch[count : 2 * count], scratch[2 * count : 3 * count]
    core_send_sem, core_recv_sem, send_sem, recv_sem = scratch[3 * count :]
    chips = boxes[0].shape[0]
    bits = [1 << i for i in range(int(math.log2(chips)))]
    orders = (bits, bits[::-1])
    stages = len(bits)

    def core_copy(unit, chip):
        return pltpu.make_async_remote_copy(
            src_ref=boxes[unit].at[chip],
            dst_ref=core_inboxes[unit].at[chip],
            send_sem=core_send_sem.at[unit, chip],
            recv_sem=core_recv_sem.at[unit, chip],
            device_id=(own ^ 1, plane),
            device_id_type=MESH,
        )

    def active(half, stage):
        gone = orders[half][:stage]
        return [chip for chip in range(chips) if all(chip & bit == 0 for bit in gone)]

    def slot(stage, half, chip):
        before = sum(chips >> (earlier + 1) for earlier in range(stage))
        return before + active(half, stage + 1).index(chip)

    def copy(unit, half, stage, chip):
        bit = orders[half][stage]
        there = slot(stage, half, chip)
        return pltpu.make_async_remote_copy(
            src_ref=boxes[unit].at[chip ^ bit, half],
            dst_ref=inboxes[unit].at[there, half],
            send_sem=send_sem.at[unit, half, there],
            recv_sem=recv_sem.at[unit, half, there],
            device_id=(own ^ (2 * bit), plane),
            device_id_type=MESH,
        )

    def offer(unit, chip):
        for half in range(2):
            term = units[unit]((own ^ (2 * chip)) ^ 1, half)
            boxes[unit][chip, half] = term.astype(BF16)
        core_copy(unit, chip).start()

    def collect(unit, chip):
        core_copy(unit, chip).wait()
        for half in range(2):
            term = units[unit](own ^ (2 * chip), half)
            term = term + core_inboxes[unit][chip, half].astype(F32)
            boxes[unit][chip, half] = term.astype(BF16)
            bit = orders[half][0]
            if chip & bit:
                copy(unit, half, 0, chip ^ bit).start()

    def take(unit, stage, half):
        for chip in active(half, stage + 1):
            copy(unit, half, stage, chip).wait_recv()
            got = inboxes[unit][slot(stage, half, chip), half].astype(F32)
            total = boxes[unit][chip, half].astype(F32) + got
            if stage < stages - 1:
                boxes[unit][chip, half] = total.astype(BF16)
                bit = orders[half][stage + 1]
                if chip & bit:
                    copy(unit, half, stage + 1, chip ^ bit).start()
            else:
                rows = total.shape[0]
                outs[unit].ref[half * rows : (half + 1) * rows, :] = total
                if half == 1:
                    outs[unit].send()

    chip_order = sorted(range(chips), key=lambda chip: -bin(chip).count("1"))
    for unit in range(count):
        for chip in chip_order:
            yield start + 0.1 + 3 * unit
            offer(unit, chip)
        for chip in chip_order:
            yield start + 3.2 + 3 * unit
            collect(unit, chip)
    for stage in range(stages):
        for unit in range(count):
            for half in range(2):
                yield start + 6.0 + pace * (unit + 1 + count * stage)
                take(unit, stage, half)
    yield 1e6
    for out in outs:
        out.copy.wait()
    for unit in range(count):
        for half in range(2):
            for stage in range(stages):
                for chip in active(half, stage + 1):
                    copy(unit, half, stage, chip).wait_send()


def spread_scratch(shapes, devices):
    chips = devices // 2
    boxes = [pltpu.VMEM((chips, 2, rows // 2, columns), BF16) for rows, columns in shapes]
    inboxes = [pltpu.VMEM((chips - 1, 2, rows // 2, columns), BF16) for rows, columns in shapes]
    return (
        boxes
        + inboxes
        + boxes
        + [pltpu.SemaphoreType.DMA((len(shapes), chips))] * 2
        + [pltpu.SemaphoreType.DMA((len(shapes), 2, chips - 1))] * 2
    )


def window(ref, number, size):
    if size % 128 == 0:
        return ref[:, pl.ds(pl.multiple_of(number * size, size), size)]
    parts = 128 // size
    tile = ref[:, pl.ds(pl.multiple_of(number // parts * 128, 128), 128)].astype(F32)
    return choose(
        number % parts, [tile[:, i * size : (i + 1) * size] for i in range(parts)]
    ).astype(ref.dtype)


def rows_by_owner(left, right, rows):
    def term(owner, half):
        return lax.dot_general(
            window(left.get(), owner * 2 + half, rows // 2),
            right.get()[...],
            (((0,), (0,)), ((), ())),
            preferred_element_type=F32,
        )

    return term


def columns_by_owner(left, right, columns):
    def term(owner, half):
        rows = left.shape[1] // 2
        return lax.dot_general(
            left.get()[:, half * rows : (half + 1) * rows],
            window(right.get(), owner, columns),
            (((0,), (0,)), ((), ())),
            preferred_element_type=F32,
        )

    return term


def ffn_sums_body(*refs):
    inv_ref, gain_ref = refs[:2]
    sources, (grad_ref, gains_ref, mixed_ref), targets = refs[2:12], refs[12:15], refs[15:19]
    loaded, stored, refs = refs[19:29], refs[29:33], refs[33:]
    load_sems, store_sems, refs = refs[0], refs[1], refs[2:]
    summing, mixing, spreading = refs[:7], refs[7:12], refs[12:]
    own, plane = lax.axis_index("tok"), lax.axis_index("tp")
    loads = load_all(sources, loaded, load_sems)
    part, normed, dgate, dup, inner, dm, hidden, dy, mixed_part, x = loads
    rows, *grads = store_all(targets, stored, store_sems)
    gathered = rows.ref
    share = normed.shape[1] // lax.axis_size("tok")
    greet([(own ^ 1, plane)] + [(own ^ (2 << i), plane) for i in range(stages_of("tok") - 1)], True)
    done = set()

    def leave():
        for half in range(HALVES):
            yield 80.0, ("rows", half)
        rows.send()

    run(
        *sum_flows(
            part,
            gathered,
            summing,
            ffn_math(hidden, inv_ref, dy, gain_ref, grad_ref, gains_ref, gathered),
            done=done,
            key=("rows",),
        ),
        *sum_flows(mixed_part, None, mixing, mixed_math(hidden, x, mixed_ref), 27.0, 11.0),
        spread_flow(
            [
                rows_by_owner(normed, dgate, share),
                rows_by_owner(normed, dup, share),
                columns_by_owner(inner, dm, share),
            ],
            grads,
            spreading,
            15.6,
        ),
        leave(),
        done=done,
    )
    rows.copy.wait()


def ffn_sums(
    part, hidden, inv, dy, gain, normed, dgate, dup, inner, dm, mixed_part, x, collective_id
):
    planes, width = part.shape[2], part.shape[4]
    devices = lax.axis_size("tok")
    share = width // devices
    wide = dgate.shape[1]
    shapes = [(share, wide), (share, wide), (wide, share)]
    rows = jax.ShapeDtypeStruct(part.shape, BF16)
    grads = [jax.ShapeDtypeStruct(shape, F32) for shape in shapes]
    sources = [part, normed, dgate, dup, inner, dm, hidden, dy, mixed_part, x]
    grad, gains, mixed, rows, gate, up, down = pl.pallas_call(
        ffn_sums_body,
        out_shape=[
            jax.ShapeDtypeStruct(hidden.shape, F32),
            jax.ShapeDtypeStruct((8, width), F32),
            jax.ShapeDtypeStruct(hidden.shape, BF16),
            rows,
        ]
        + grads,
        in_specs=[vmem()] * 2 + [anywhere()] * len(sources),
        out_specs=[vmem()] * 3 + [anywhere()] * 4,
        scratch_shapes=buffers(sources + [rows] + grads)
        + [pltpu.SemaphoreType.DMA((len(sources),)), pltpu.SemaphoreType.DMA((4,))]
        + sum_scratch(planes, width)
        + sum_scratch(planes, width, False)
        + spread_scratch(shapes, devices),
        compiler_params=params(collective_id),
        cost_estimate=cost(0, 80_000_000),
        name="ffn_sums",
    )(inv, gain, *sources)
    return rows, grad, gains, gate, up, down, mixed


def together():
    return stages_of("tok") <= 3


def attn_sums_body(lens_ref, flags_ref, *refs):
    both = together()
    mixed_ref, inv_ref, gain_ref, ffn_gains_ref = refs[:4]
    sources, home_ref, grad_home_ref, refs = refs[4:12], refs[12], refs[13], refs[14:]
    gathered, gains_ref, mixed_out = refs[:3]
    targets, refs = refs[3:5], refs[5:]
    loaded, stored, load_sems, store_sems, refs = refs[:8], refs[8:10], refs[10], refs[11], refs[12:]
    part, normed, dqkv, attended, da, x, dy, grad = load_all(sources, loaded, load_sems)
    weight_grads = store_all(targets, stored, store_sems)
    if both:
        grad_out, gathered = gathered, refs[0]
        gain_sums, gains_ref = gains_ref, refs[1]
        refs = refs[2:]
    summing, undealing, refs = refs[:7], refs[7 : 7 + deal_count()], refs[7 + deal_count() :]
    mixed_all, mixed_sems, home_sems = refs[0], refs[1:3], refs[3]
    gains_all, gains_sems, refs = refs[4], refs[5:7], refs[7:]
    planes = part.shape[2]
    plane = lax.axis_index("tp")
    share = normed.shape[1] // lax.axis_size("tok")
    home = pltpu.make_async_copy(home_ref, mixed_out, home_sems.at[0])
    home.start()
    if both:
        grad_home = pltpu.make_async_copy(grad_home_ref, grad_out, home_sems.at[1])
        grad_home.start()
        grad_undealing, refs = refs[: deal_count()], refs[deal_count() :]
        gaining, refs = refs[:3], refs[3:]
    greet(all_peers() if both else bit_peers(stages_of("tok")), True)
    for half in range(HALVES):
        mixed_all[:, half, plane] = mixed_ref[half]
    done = set()

    def sum_gains():
        yield (70.0, ("grad", HALVES - 1))
        total = gains_all[0]
        for index in range(1, planes):
            total = total + gains_all[index]
        gains_ref[...] = total
        done.add(("gains",))

    flows = [
        *gather_flows(mixed_all, mixed_sems, 0.0, 8.7, done, ("mixed",)),
        *sum_flows(
            part,
            gathered,
            summing,
            attn_math(x, inv_ref, dy, grad, gain_ref, ffn_gains_ref, gains_all, gathered),
            9.0,
            10.0,
            (lambda index: gains_all.at[index],) + gains_sems,
            done,
            ("grad",),
        ),
        spread_flow(
            [
                rows_by_owner(normed, dqkv, share),
                columns_by_owner(attended, da, share),
            ],
            weight_grads,
            refs,
            9.0,
        ),
        undeal_flow(
            lens_ref, flags_ref, mixed_all, mixed_out, home, undealing, 28.0, 4.5, ("mixed",), 6.0
        ),
        sum_gains(),
    ]
    if both:
        flows += [
            undeal_flow(
                lens_ref, flags_ref, gathered, grad_out, grad_home, grad_undealing,
                55.0, 4.5, ("grad",), 8.0,
            ),
            gain_flow(gains_ref, gain_sums, gaining, 72.0, ("gains",)),
        ]
    run(*flows, done=done)


def attn_sums(
    doc_lengths, keep_flags, part, mixed, x, inv, dy, grad, gain, ffn_gains, normed, dqkv, attended,
    da, home, grad_home, collective_id,
):
    planes, width = part.shape[2], part.shape[4]
    devices = lax.axis_size("tok")
    share = width // devices
    shapes = [(share, dqkv.shape[1]), (attended.shape[1], share)]
    both = together()
    rows_shape = jax.ShapeDtypeStruct(part.shape, BF16)
    gains_shape = jax.ShapeDtypeStruct((8, width), F32)
    blocks_shape = jax.ShapeDtypeStruct(home.shape, BF16)
    gain_part = gain_share(width, devices)
    first = (
        [blocks_shape, jax.ShapeDtypeStruct((8, gain_part), F32)] if both else [rows_shape, gains_shape]
    )
    dealing = deal_scratch(stages_of("tok"), width, BF16)
    sources = [part, normed, dqkv, attended, da, x, dy, grad]
    weight_grads = [jax.ShapeDtypeStruct(shape, F32) for shape in shapes]
    grads, gains, mixed_blocks, qkv, out = pl.pallas_call(
        attn_sums_body,
        out_shape=first
        + [blocks_shape]
        + weight_grads,
        in_specs=[smem(), smem()] + [vmem()] * 4 + [anywhere()] * 10,
        out_specs=[vmem()] * 3 + [anywhere()] * 2,
        scratch_shapes=buffers(sources + weight_grads)
        + [pltpu.SemaphoreType.DMA((8,)), pltpu.SemaphoreType.DMA((2,))]
        + (
            [pltpu.VMEM(part.shape, BF16), pltpu.VMEM((8, width), F32)] if both else []
        )
        + sum_scratch(planes, width)
        + dealing
        + [pltpu.VMEM(part.shape, BF16)]
        + [pltpu.SemaphoreType.DMA((HALVES, 2, planes))] * 2
        + [pltpu.SemaphoreType.DMA((2,)), pltpu.VMEM((planes, 8, width), F32)]
        + line_sems(planes)
        + (dealing + gain_scratch(devices, gain_part) if both else [])
        + spread_scratch(shapes, devices),
        compiler_params=params(collective_id),
        cost_estimate=cost(0, 80_000_000),
        name="attn_sums",
    )(
        doc_lengths, keep_flags, mixed, inv, gain, ffn_gains, *sources, home, grad_home
    )
    if not both:
        grads, gains = undeal(doc_lengths, keep_flags, grads, grad_home, gains, collective_id + 1)
    return mixed_blocks, grads, gains, qkv, out


def rotary_tables(doc_lengths, keep_flags, ranks):
    blocks = keep_flags * (doc_lengths // BLOCK)
    ends = jnp.cumsum(blocks, dtype=jnp.int32)
    starts = ends - blocks
    inside = (ranks[:, None] >= starts[None, :]) & (ranks[:, None] < ends[None, :])
    first = jnp.sum(jnp.where(inside, starts[None, :], 0), axis=1, dtype=jnp.int32)
    offsets = jnp.arange(BLOCK, dtype=jnp.int32)
    positions = (((ranks - first) * BLOCK)[:, None] + offsets[None, :]).reshape(-1)
    half_dim = HD // 2
    freqs = jnp.exp(jnp.arange(half_dim, dtype=jnp.float32) * (-2.0 * math.log(10000.0) / HD))
    angles = positions.astype(jnp.float32)[:, None] * freqs[None, :]
    cosine, sine = jnp.cos(angles), jnp.sin(angles)
    return jnp.concatenate([cosine, cosine], axis=1), jnp.concatenate([sine, -sine], axis=1)


def unrotate(values, cosine, sine):
    half_dim = HD // 2
    swapped = jnp.concatenate([values[:, half_dim:], values[:, :half_dim]], axis=1)
    return values * cosine + swapped * sine


def over_columns(left, right):
    return lax.dot_general(
        left, right, (((1,), (1,)), ((), ())), preferred_element_type=jnp.float32
    )


def on_device(
    tokens,
    gain_attn,
    w_query,
    w_key,
    w_value,
    w_out,
    gain_ffn,
    w_gate,
    w_up,
    w_down,
    cotangent,
    doc_lengths,
    keep_flags,
):
    length = tokens.shape[0]
    model_width = tokens.shape[1]
    devices = lax.axis_size("tok")
    planes = lax.axis_size("tp")
    own_index = lax.axis_index("tok")
    blocks_here = length // BLOCK
    kept_here = blocks_here // 2
    rows = kept_here * BLOCK
    token_blocks = tokens.reshape(blocks_here, BLOCK, model_width)
    grad_blocks = cotangent.reshape(blocks_here, BLOCK, model_width)

    own_ranks = own_index + jnp.arange(kept_here, dtype=jnp.int32) * devices
    cosine, sine = rotary_tables(doc_lengths, keep_flags, own_ranks)
    own = jnp.reshape(own_index, (1,)).astype(jnp.int32)
    rows_x, normed_one, inv_one, queries, kv_all = deal_project(
        doc_lengths,
        keep_flags,
        gain_attn.reshape(1, -1),
        cosine,
        sine,
        token_blocks,
        w_query,
        w_key,
        w_value,
        0,
    )
    rows_x = rows_x.reshape(rows, model_width)
    attended, attended_wide, log_totals = attend(doc_lengths, keep_flags, own, queries, kv_all)

    def by_plane(array):
        return array.reshape(kept_here, HALVES, planes, TILE, array.shape[1])

    x_planes = by_plane(rows_x)
    rows_dy, normed_two, hidden_res, inv_two = deal_sum(
        doc_lengths,
        keep_flags,
        grad_blocks,
        by_plane(jnp.dot(attended, w_out, preferred_element_type=jnp.float32).astype(jnp.bfloat16)),
        x_planes,
        gain_ffn.reshape(1, -1),
        1,
    )
    rows_dy = rows_dy.reshape(rows, model_width)
    normed_two = normed_two.reshape(rows, model_width)
    gate = jnp.dot(normed_two, w_gate, preferred_element_type=jnp.float32)
    upper = jnp.dot(normed_two, w_up, preferred_element_type=jnp.float32)
    sigma = jax.nn.sigmoid(gate)
    swish = gate * sigma
    inner = (swish * upper).astype(jnp.bfloat16)

    grad_m = (keep_scale * rows_dy.astype(jnp.float32)).astype(jnp.bfloat16)
    grad_inner = over_columns(grad_m, w_down)
    grad_gate_pre = (grad_inner * upper * sigma * (1.0 + gate * (1.0 - sigma))).astype(jnp.bfloat16)
    grad_up_pre = (grad_inner * swish).astype(jnp.bfloat16)
    part_two = (
        over_columns(grad_gate_pre, w_gate) + over_columns(grad_up_pre, w_up)
    ).astype(jnp.bfloat16)

    dy_planes = by_plane(rows_dy)
    grad_a, grad_hidden, gains_ffn, grad_gate, grad_up, grad_down, mixed_rows = ffn_sums(
        by_plane(part_two),
        hidden_res,
        inv_two,
        dy_planes,
        gain_ffn.reshape(1, -1),
        normed_two,
        grad_gate_pre,
        grad_up_pre,
        inner,
        grad_m,
        by_plane(jnp.dot(inner, w_down, preferred_element_type=jnp.float32).astype(jnp.bfloat16)),
        x_planes,
        4,
    )
    grad_a = grad_a.reshape(rows, model_width)

    grad_attended = over_columns(grad_a, w_out).astype(jnp.bfloat16)
    grad_query_pre, grad_kv, grad_gate, grad_up, grad_down = attend_back(
        doc_lengths,
        keep_flags,
        own,
        queries,
        grad_attended,
        kv_all,
        attended_wide,
        log_totals,
        cosine,
        sine,
        [grad_gate, grad_up, grad_down],
    )
    grad_kv = scatter_tok(grad_kv, 5)
    grad_key_pre = unrotate(grad_kv[:, :HD], cosine, sine).astype(jnp.bfloat16)
    grad_value_pre = grad_kv[:, HD:].astype(jnp.bfloat16)
    part_one = (
        over_columns(grad_query_pre, w_query)
        + over_columns(grad_key_pre, w_key)
        + over_columns(grad_value_pre, w_value)
    ).astype(jnp.bfloat16)
    mixed, token_grad, gain_sums, grad_qkv, grad_out = attn_sums(
        doc_lengths,
        keep_flags,
        by_plane(part_one),
        mixed_rows,
        x_planes,
        by_plane(inv_one),
        dy_planes,
        grad_hidden,
        gain_attn.reshape(1, -1),
        gains_ffn,
        normed_one,
        jnp.concatenate([grad_query_pre, grad_key_pre, grad_value_pre], axis=1),
        attended,
        grad_a,
        token_blocks,
        grad_blocks,
        6,
    )
    own_share = model_width // devices
    if gain_sums.shape[1] != own_share:
        gain_sums = lax.dynamic_slice_in_dim(gain_sums, own_index * own_share, own_share, 1)
    mixed, token_grad, grad_query, grad_key, grad_value, grad_out = finish(
        mixed, token_grad, grad_qkv, grad_out, w_key.shape[1]
    )

    return (
        mixed.reshape(length, model_width),
        token_grad.reshape(length, model_width),
        gain_sums[1],
        grad_query,
        grad_key,
        grad_value,
        grad_out,
        gain_sums[0],
        grad_gate,
        grad_up,
        grad_down,
    )


def solution(mesh):
    placed = (
        P("tok", None),
        P(),
        P(None, "tp"),
        P(None, "tp"),
        P(None, "tp"),
        P("tp", None),
        P(),
        P(None, "tp"),
        P(None, "tp"),
        P("tp", None),
        P("tok", None),
        P(),
        P(),
    )
    return jax.shard_map(
        on_device,
        mesh=mesh,
        in_specs=placed,
        out_specs=(
            P("tok", None),
            P("tok", None),
            P("tok"),
            P("tok", "tp"),
            P("tok", "tp"),
            P("tok", "tp"),
            P("tp", "tok"),
            P("tok"),
            P("tok", "tp"),
            P("tok", "tp"),
            P("tp", "tok"),
        ),
        check_vma=False,
    )
```

```python
import functools
import math

import jax
import jax.numpy as jnp
from jax import lax
from jax.experimental import pallas as pl
from jax.experimental.pallas import tpu as pltpu
from jax.sharding import PartitionSpec as P

HD = 128
BLOCK = 128
SLOTS = 3
CHUNKS = 8
HALVES = 2
TILE = 16
HOP = 2.0
MESH = pl.DeviceIdType.MESH
VMEM_BYTES = 60 * 2**20

norm_eps = 1e-05
keep_scale = 2.0
F32 = jnp.float32
BF16 = jnp.bfloat16


def vmem():
    return pl.BlockSpec(memory_space=pltpu.VMEM)


def smem():
    return pl.BlockSpec(memory_space=pltpu.SMEM)


def params(collective_id):
    return pltpu.CompilerParams(
        collective_id=collective_id, has_side_effects=True, vmem_limit_bytes=VMEM_BYTES
    )


def cost(flops, moved):
    return pl.CostEstimate(flops=flops, bytes_accessed=moved, transcendentals=0)


def greet(peers, line=False):
    barrier = pltpu.get_barrier_semaphore()
    for peer in peers:
        pl.semaphore_signal(barrier, inc=1, device_id=peer, device_id_type=MESH)
    if not line:
        pl.semaphore_wait(barrier, len(peers))
        return
    own, plane = lax.axis_index("tok"), lax.axis_index("tp")
    last = lax.axis_size("tp") - 1

    @pl.when(plane > 0)
    def _():
        pl.semaphore_signal(barrier, inc=1, device_id=(own, plane - 1), device_id_type=MESH)

    @pl.when(plane < last)
    def _():
        pl.semaphore_signal(barrier, inc=1, device_id=(own, plane + 1), device_id_type=MESH)

    end = (plane == 0) | (plane == last)

    @pl.when(end)
    def _():
        pl.semaphore_wait(barrier, len(peers) + 1)

    @pl.when(jnp.logical_not(end))
    def _():
        pl.semaphore_wait(barrier, len(peers) + 2)


def run(*flows, done=frozenset()):
    waiting = [[next(flow), number, flow] for number, flow in enumerate(flows)]

    def order(entry):
        step = entry[0] if isinstance(entry[0], tuple) else (entry[0], None)
        return (step[1] is not None and step[1] not in done, step[0], entry[1])

    while waiting:
        waiting.sort(key=order)
        entry = waiting[0]
        assert not order(entry)[0]
        try:
            entry[0] = next(entry[2])
        except StopIteration:
            waiting.pop(0)


def anywhere():
    return pl.BlockSpec(memory_space=pl.ANY)


class Loaded:
    def __init__(self, source, target, sem):
        self.copy = pltpu.make_async_copy(source, target, sem)
        self.target = target
        self.here = False
        self.shape = target.shape

    def get(self):
        if not self.here:
            self.copy.wait()
            self.here = True
        return self.target


def load_all(sources, targets, sems):
    loads = [Loaded(*pair, sems.at[i]) for i, pair in enumerate(zip(sources, targets))]
    for load in loads:
        load.copy.start()
    return loads


class Stored:
    def __init__(self, target, source, sem):
        self.copy = pltpu.make_async_copy(source, target, sem)
        self.ref = source

    def send(self):
        self.copy.start()


def store_all(targets, sources, sems):
    return [Stored(*pair, sems.at[i]) for i, pair in enumerate(zip(targets, sources))]


def buffers(arrays):
    return [pltpu.VMEM(array.shape, array.dtype) for array in arrays]


def deal_tables(own, stages, blocks_here, lens_ref, flags_ref):
    def kept_before(place):
        total, start = jnp.int32(0), jnp.int32(0)
        for doc in range(lens_ref.shape[0]):
            blocks = lens_ref[doc] // BLOCK
            total = total + flags_ref[doc] * jnp.clip(place - start, 0, blocks)
            start = start + blocks
        return total

    def edges(stage):
        first = (own >> stage) << stage
        return (
            kept_before(first * blocks_here),
            kept_before((first + (1 << stage)) * blocks_here),
        )

    def located(stage):
        if stage == 0:
            ends = [kept_before(own * blocks_here + i + 1) for i in range(blocks_here)]

            def place(rank):
                index = jnp.int32(0)
                for end in ends:
                    index = index + (end <= rank).astype(jnp.int32)
                return index

            return place
        mine = (own >> (stage - 1)) << (stage - 1)
        low, high = edges(stage - 1)
        other = kept_before((mine ^ (1 << (stage - 1))) * blocks_here)

        def place(rank):
            inside = (rank >= low) & (rank < high)
            return jnp.where(inside, (rank - low) >> stage, SLOTS + ((rank - other) >> stage))

        return place

    keeps, sends = [], []
    for stage in range(stages):
        low, high = edges(stage)
        place = located(stage)
        period = 1 << (stage + 1)
        for table, target in ((keeps, own), (sends, own ^ (1 << stage))):
            first = low + ((target - low) & (period - 1))
            row = []
            for slot in range(SLOTS):
                rank = first + period * slot
                row.append(jnp.where(rank < high, place(rank), -1))
            table.append(row)
    place = located(stages)
    finals = [place(own + (slot << stages)) for slot in range(SLOTS)]
    return keeps, sends, finals


def choose(index, options):
    value = options[0]
    for number, option in enumerate(options[1:]):
        value = jnp.where(index == number + 1, option, value)
    return value


def slot_of(keep, recv, chunk, index):
    stayed = keep[chunk, jnp.clip(index, 0, SLOTS - 1)]
    arrived = recv[jnp.clip(index - SLOTS, 0, SLOTS - 1)]
    return jnp.where(index < SLOTS, stayed, arrived)


def deal_refs(scratch):
    keep, send = scratch[:2]
    stages = send.shape[0]
    recv = [scratch[2 + i * CHUNKS : 2 + (i + 1) * CHUNKS] for i in range(stages)]
    return keep, send, recv, *scratch[2 + stages * CHUNKS : 4 + stages * CHUNKS]


def bit_peers(stages):
    own, plane = lax.axis_index("tok"), lax.axis_index("tp")
    return [(own ^ (1 << stage), plane) for stage in range(stages)]


def deal_flow(lens_ref, flags_ref, blocks, finish, scratch, pace=4.3, urgent=False):
    keep, send, recv, send_sem, recv_sem = deal_refs(scratch)
    stages = send.shape[0]
    own = lax.axis_index("tok")
    blocks_here = blocks.shape[0]
    rows = BLOCK // CHUNKS
    peers = bit_peers(stages)
    keeps, sends, finals = deal_tables(own, stages, blocks_here, lens_ref, flags_ref)

    def copy(stage, chunk):
        return pltpu.make_async_remote_copy(
            src_ref=send.at[stage, chunk],
            dst_ref=recv[stage][chunk],
            send_sem=send_sem.at[stage, chunk],
            recv_sem=recv_sem.at[stage, chunk],
            device_id=peers[stage],
            device_id_type=MESH,
        )

    def held(stage, chunk, index):
        if stage == 0:
            block = jnp.clip(index, 0, blocks_here - 1)
            return blocks.get()[block, pl.ds(chunk * rows, rows), :]
        return slot_of(keep, recv[stage - 1][chunk], chunk, index)

    for stage in range(stages + 1):
        for chunk in range(CHUNKS):
            if stage < 2:
                yield 1.5 * stage + 0.3 * chunk
            else:
                slack = 4.0 if stage == stages and not urgent else 0.0
                yield 1.5 + HOP * (stage - 1) + pace * (chunk + stage - 1) + slack
            if stage > 0:
                copy(stage - 1, chunk).wait_recv()
            if stage == stages:
                finish(chunk, [held(stage, chunk, finals[slot]) for slot in range(SLOTS)])
            else:
                for slot in range(SLOTS):
                    send[stage, chunk, slot] = held(stage, chunk, sends[stage][slot])
                copy(stage, chunk).start()
                stay = [held(stage, chunk, keeps[stage][slot]) for slot in range(SLOTS)]
                for slot in range(SLOTS):
                    keep[chunk, slot] = stay[slot]
    yield 1e6

    for stage in range(stages):
        for chunk in range(CHUNKS):
            copy(stage, chunk).wait_send()


def deal_scratch(stages, width, kind):
    part = (SLOTS, BLOCK // CHUNKS, width)
    return (
        [pltpu.VMEM((CHUNKS,) + part, kind), pltpu.VMEM((stages, CHUNKS) + part, kind)]
        + [pltpu.VMEM(part, kind)] * (stages * CHUNKS)
        + [pltpu.SemaphoreType.DMA((stages, CHUNKS))] * 2
    )


def deal_count():
    return 4 + stages_of("tok") * CHUNKS


def stages_of(axis):
    return int(math.log2(lax.axis_size(axis)))


def undeal_flow(
    lens_ref, flags_ref, kept_ref, out_ref, home, scratch, start=0.0, pace=4.3, key=None, lag=0.0
):
    keep, send, recv, send_sem, recv_sem = deal_refs(scratch)
    stages = send.shape[0]
    own = lax.axis_index("tok")
    blocks_here = out_ref.shape[0]
    planes = kept_ref.shape[2]
    rows = BLOCK // CHUNKS
    peers = bit_peers(stages)
    keeps, sends, finals = deal_tables(own, stages, blocks_here, lens_ref, flags_ref)

    def copy(stage, chunk):
        return pltpu.make_async_remote_copy(
            src_ref=send.at[stage, chunk],
            dst_ref=recv[stage][chunk],
            send_sem=send_sem.at[stage, chunk],
            recv_sem=recv_sem.at[stage, chunk],
            device_id=peers[stage],
            device_id_type=MESH,
        )

    def source(places, place):
        index = jnp.int32(-1)
        for number, other in enumerate(places):
            index = jnp.where(other == place, number, index)
        return index

    last = stages - 1
    for stage in range(last, -2, -1):
        count = 2 * SLOTS if stage >= 0 else blocks_here
        places = finals if stage == last else keeps[stage + 1] + sends[stage + 1]
        sources = [source(places, place) for place in range(count)]
        for chunk in range(CHUNKS):
            half = chunk // planes
            begin = start + lag * half
            if stage == last:
                yield (begin, None if key is None else key + (half,))
                options = [kept_ref[slot, half, chunk % planes] for slot in range(SLOTS)]
            else:
                hops = last - stage
                slack = 20.0 if stage < 0 else 0.0
                yield begin + HOP * hops + pace * (chunk + hops - (stage < 0)) + slack
                copy(stage + 1, chunk).wait_recv()

            def block(place):
                if stage == last:
                    return choose(sources[place], options)
                return slot_of(keep, recv[stage + 1][chunk], chunk, sources[place])

            if stage < 0:
                if chunk == 0:
                    home.wait()
                span = pl.ds(chunk * rows, rows)
                for place in range(blocks_here):
                    value = out_ref[place, span, :]
                    out_ref[place, span, :] = jnp.where(sources[place] >= 0, block(place), value)
            else:
                for slot in range(SLOTS):
                    send[stage, chunk, slot] = block(SLOTS + slot)
                copy(stage, chunk).start()
                stay = [block(slot) for slot in range(SLOTS)]
                for slot in range(SLOTS):
                    keep[chunk, slot] = stay[slot]
    yield 1e6

    for stage in range(stages):
        for chunk in range(CHUNKS):
            copy(stage, chunk).wait_send()


def gain_flow(gains_ref, sum_ref, scratch, start, key=None):
    gain_recv, gain_send_sem, gain_recv_sem = scratch
    own, plane = lax.axis_index("tok"), lax.axis_index("tp")
    devices = gain_recv.shape[0]
    share = sum_ref.shape[1]

    def portion(there):
        if share < gains_ref.shape[1]:
            return gains_ref.at[:, pl.ds(pl.multiple_of(there * share, share), share)]
        return gains_ref

    def copy(step):
        return pltpu.make_async_remote_copy(
            src_ref=portion(own ^ step),
            dst_ref=gain_recv.at[step],
            send_sem=gain_send_sem.at[step],
            recv_sem=gain_recv_sem.at[step],
            device_id=(own ^ step, plane),
            device_id_type=MESH,
        )

    yield (start, key)
    for step in range(1, devices):
        copy(step).start()
    yield 2e5
    total = portion(own)[...]
    for step in range(1, devices):
        copy(step).wait()
        total = total + gain_recv[step]
    sum_ref[...] = total


def gain_share(width, devices):
    share = width // devices
    return share if share % 128 == 0 else width


def gain_scratch(devices, share):
    return [pltpu.VMEM((devices, 8, share), F32)] + [pltpu.SemaphoreType.DMA((devices,))] * 2


def all_peers():
    own, plane = lax.axis_index("tok"), lax.axis_index("tp")
    return [(own ^ step, plane) for step in range(1, lax.axis_size("tok"))]


def undeal_body(lens_ref, flags_ref, kept_ref, home_ref, gains_ref, out_ref, sum_ref, home_sem, *scratch):
    home = pltpu.make_async_copy(home_ref, out_ref, home_sem)
    home.start()
    greet(all_peers())
    run(
        undeal_flow(lens_ref, flags_ref, kept_ref, out_ref, home, scratch[: deal_count()]),
        gain_flow(gains_ref, sum_ref, scratch[deal_count() :], 0.0),
    )


def undeal(doc_lengths, keep_flags, kept, home, gains, collective_id):
    stages = stages_of("tok")
    devices = 1 << stages
    width = kept.shape[-1]
    share = gain_share(width, devices)
    return pl.pallas_call(
        undeal_body,
        out_shape=(
            jax.ShapeDtypeStruct(home.shape, home.dtype),
            jax.ShapeDtypeStruct((8, share), F32),
        ),
        in_specs=[smem(), smem(), vmem(), pl.BlockSpec(memory_space=pl.ANY), vmem()],
        out_specs=(vmem(), vmem()),
        scratch_shapes=[pltpu.SemaphoreType.DMA]
        + deal_scratch(stages, width, kept.dtype)
        + gain_scratch(devices, share),
        compiler_params=params(collective_id),
        cost_estimate=cost(0, 40_000_000),
        name="undeal",
    )(doc_lengths, keep_flags, kept, home, gains)


def deal_project_body(
    lens_ref, flags_ref, gain_ref, cos_ref, sin_ref, own_hbm, w_query_hbm, w_key_hbm, w_value_hbm,
    x_hbm, normed_hbm, inv_ref, query_ref, out_ref,
    own_half, w_query, w_key, w_value, x_ref, normed_ref, mine_ref, pair_send, pair_recv,
    load_sems, store_sems, pair_send_sem, pair_recv_sem,
    send_sem, recv_sem, relay_send_sem, relay_recv_sem, *dealing,
):
    devices = out_ref.shape[0]
    chips = devices // 2
    own = lax.axis_index("tok")
    plane = lax.axis_index("tp")
    partner = (own ^ 1, plane)
    width = own_half.shape[2]
    tile = BLOCK // CHUNKS
    thin = w_key.shape[1]
    columns = pl.ds(pl.multiple_of((plane % 2) * width, width), width)
    blocks, w_query, w_key, w_value = load_all(
        [own_hbm.at[:, :, columns], w_query_hbm, w_key_hbm, w_value_hbm],
        [own_half, w_query, w_key, w_value],
        load_sems,
    )
    steps = sorted({1 << i for i in range(stages_of("tok"))} | {2 * i for i in range(1, chips)})
    greet([(own ^ step, plane) for step in steps] + [(own, plane ^ 1)])

    def pair_copy(chunk):
        return pltpu.make_async_remote_copy(
            src_ref=pair_send.at[chunk],
            dst_ref=pair_recv.at[chunk],
            send_sem=pair_send_sem.at[chunk],
            recv_sem=pair_recv_sem.at[chunk],
            device_id=(own, plane ^ 1),
            device_id_type=MESH,
        )

    def finish(chunk, values):
        for slot, value in enumerate(values):
            pair_send[chunk, slot] = value
        pair_copy(chunk).start()
        for slot, value in enumerate(values):
            x_ref[slot, pl.ds(chunk * tile, tile), columns] = value

    def norms():
        for chunk in range(CHUNKS):
            yield 500.0 + chunk, (chunk,)
            other = pl.ds(pl.multiple_of((1 - plane % 2) * width, width), width)
            pair_copy(chunk).wait_recv()
            span = pl.ds(chunk * tile, tile)
            for slot in range(SLOTS):
                x_ref[slot, span, other] = pair_recv[chunk, slot]
            for slot in range(SLOTS):
                x = x_ref[slot, span, :].astype(F32)
                inv = lax.rsqrt(jnp.mean(x * x, axis=1, keepdims=True) + norm_eps)
                rows = pl.ds(slot * BLOCK + chunk * tile, tile)
                inv_ref[rows, :] = inv
                normed_ref[rows, :] = (x * inv * gain_ref[...]).astype(BF16)

    done = set()

    def mark(chunk, values):
        finish(chunk, values)
        done.add((chunk,))

    run(
        deal_flow(lens_ref, flags_ref, blocks, mark, dealing, 2.2, True),
        norms(),
        done=done,
    )
    stores = store_all([x_hbm, normed_hbm], [x_ref, normed_ref], store_sems)
    for store in stores:
        store.send()
    for chunk in range(CHUNKS):
        pair_copy(chunk).wait_send()

    def copy(step):
        return pltpu.make_async_remote_copy(
            src_ref=mine_ref,
            dst_ref=out_ref.at[own],
            send_sem=send_sem.at[step],
            recv_sem=recv_sem.at[step],
            device_id=(own ^ (2 * step), plane),
            device_id_type=MESH,
        )

    def relay(step):
        return pltpu.make_async_remote_copy(
            src_ref=mine_ref if step == 0 else out_ref.at[own ^ (2 * step)],
            dst_ref=out_ref.at[own ^ (2 * step)],
            send_sem=relay_send_sem.at[step],
            recv_sem=relay_recv_sem.at[step],
            device_id=partner,
            device_id_type=MESH,
        )

    def product(weight):
        return lax.dot_general(
            normed_ref[...], weight.get()[...], (((1,), (0,)), ((), ())), preferred_element_type=F32
        )

    keys = product(w_key)
    for group in range(thin // HD):
        one = keys[:, group * HD : (group + 1) * HD]
        mine_ref[:, group * HD : (group + 1) * HD] = turn(one, cos_ref, sin_ref, -1.0).astype(BF16)
    mine_ref[:, thin:] = product(w_value).astype(BF16)
    for step in range(1, chips):
        copy(step).start()
    relay(0).start()
    out_ref[own] = mine_ref[...]
    queries = product(w_query)
    for head in range(w_query.shape[1] // HD):
        one = queries[:, head * HD : (head + 1) * HD]
        query_ref[:, head * HD : (head + 1) * HD] = turn(one, cos_ref, sin_ref, -1.0).astype(BF16)
    for step in range(1, chips):
        copy(step).wait_recv()
        relay(step).start()
    for step in range(chips):
        relay(step).wait()
    for step in range(1, chips):
        copy(step).wait_send()
    for store in stores:
        store.copy.wait()


def turn(values, cos_ref, sin_ref, sign):
    return values * cos_ref[...] + pltpu.roll(values, HD // 2, 1) * (sin_ref[...] * sign)


def deal_project(
    doc_lengths, keep_flags, gain, cosine, sine, blocks, w_query, w_key, w_value, collective_id
):
    devices = lax.axis_size("tok")
    chips = devices // 2
    width = blocks.shape[2]
    rows = SLOTS * BLOCK
    both = w_key.shape[1] + w_value.shape[1]
    x_shape, normed_shape = (SLOTS, BLOCK, width), (rows, width)
    weights = [w_query, w_key, w_value]
    return pl.pallas_call(
        deal_project_body,
        out_shape=(
            jax.ShapeDtypeStruct(x_shape, BF16),
            jax.ShapeDtypeStruct(normed_shape, BF16),
            jax.ShapeDtypeStruct((rows, 1), F32),
            jax.ShapeDtypeStruct((rows, w_query.shape[1]), BF16),
            jax.ShapeDtypeStruct((devices, rows, both), BF16),
        ),
        in_specs=[smem()] * 2 + [vmem()] * 3 + [anywhere()] * 4,
        out_specs=(anywhere(),) * 2 + (vmem(),) * 3,
        scratch_shapes=[pltpu.VMEM(blocks.shape[:2] + (width // 2,), BF16)]
        + buffers(weights)
        + [
            pltpu.VMEM(x_shape, BF16),
            pltpu.VMEM(normed_shape, BF16),
            pltpu.VMEM((rows, both), BF16),
            pltpu.VMEM((CHUNKS, SLOTS, BLOCK // CHUNKS, width // 2), BF16),
            pltpu.VMEM((CHUNKS, SLOTS, BLOCK // CHUNKS, width // 2), BF16),
            pltpu.SemaphoreType.DMA((4,)),
            pltpu.SemaphoreType.DMA((2,)),
        ]
        + [pltpu.SemaphoreType.DMA((CHUNKS,))] * 2
        + [pltpu.SemaphoreType.DMA((chips,))] * 4
        + deal_scratch(stages_of("tok"), width // 2, BF16),
        compiler_params=params(collective_id),
        cost_estimate=cost(0, 60_000_000),
        name="deal_project",
    )(doc_lengths, keep_flags, gain, cosine, sine, blocks, *weights)


def first_rank(lens_ref, flags_ref, rank):
    first, start = jnp.int32(0), jnp.int32(0)
    for doc in range(lens_ref.shape[0]):
        blocks = flags_ref[doc] * (lens_ref[doc] // BLOCK)
        first = jnp.where((rank >= start) & (rank < start + blocks), start, first)
        start = start + blocks
    return first


def stack_heads(ref, slot):
    heads = ref.shape[1] // HD
    return jnp.concatenate(
        [ref[slot * BLOCK : (slot + 1) * BLOCK, i * HD : (i + 1) * HD] for i in range(heads)], axis=0
    )


def dot(left, right, dims):
    return lax.dot_general(left, right, ((dims[:1], dims[1:]), ((), ())), preferred_element_type=F32)


def key_block(kv_ref, rank):
    devices = kv_ref.shape[0]
    device, slot = lax.rem(rank, devices), lax.div(rank, devices)
    span = pl.ds(pl.multiple_of(slot * BLOCK, BLOCK), BLOCK)
    return device, span


def causal(scores):
    keys = lax.broadcasted_iota(jnp.int32, scores.shape, 0)
    queries = lax.rem(lax.broadcasted_iota(jnp.int32, scores.shape, 1), BLOCK)
    return jnp.where(keys <= queries, scores, -1e30)


def attend_body(lens_ref, flags_ref, own_ref, query_ref, kv_ref, out_ref, wide_ref, log_ref, total):
    devices = kv_ref.shape[0]
    scale = 1.0 / math.sqrt(HD)
    for slot in range(SLOTS):
        rank = own_ref[0] + devices * slot
        query = stack_heads(query_ref, slot)
        count = query.shape[0]
        total[...] = jnp.zeros_like(total)

        def visit(key_rank, state, masked):
            peak, weight = state
            device, span = key_block(kv_ref, key_rank)
            scores = dot(kv_ref[device, span, :HD], query, (1, 1)) * scale
            if masked:
                scores = causal(scores)
            higher = jnp.maximum(peak, jnp.max(scores, axis=0, keepdims=True))
            shrink = jnp.exp(peak - higher)
            probs = jnp.exp(scores - higher)
            weight = weight * shrink + jnp.sum(probs, axis=0, keepdims=True)
            values = kv_ref[device, span, HD:]
            total[...] = total[...] * shrink + dot(values, probs.astype(BF16), (0, 0))
            return higher, weight

        start = (jnp.full((1, count), -1e30, F32), jnp.zeros((1, count), F32))
        first = first_rank(lens_ref, flags_ref, rank)
        state = lax.fori_loop(first, rank, lambda r, s: visit(r, s, False), start)
        peak, weight = visit(rank, state, True)
        result = total[...] / weight
        wide_ref[slot] = result
        log_ref[slot] = jnp.broadcast_to(peak + jnp.log(weight), log_ref.shape[1:])
        turned = result.T.astype(BF16)
        for head in range(count // BLOCK):
            out_ref[slot * BLOCK : (slot + 1) * BLOCK, head * HD : (head + 1) * HD] = turned[
                head * BLOCK : (head + 1) * BLOCK
            ]


def attend(doc_lengths, keep_flags, own, query, kv):
    count = query.shape[1] // HD * BLOCK
    return pl.pallas_call(
        attend_body,
        out_shape=(
            jax.ShapeDtypeStruct(query.shape, BF16),
            jax.ShapeDtypeStruct((SLOTS, HD, count), F32),
            jax.ShapeDtypeStruct((SLOTS, 8, count), F32),
        ),
        in_specs=[smem()] * 3 + [vmem()] * 2,
        out_specs=(vmem(),) * 3,
        scratch_shapes=[pltpu.VMEM((HD, count), F32)],
        compiler_params=pltpu.CompilerParams(vmem_limit_bytes=VMEM_BYTES),
        cost_estimate=cost(1_000_000_000, 10_000_000),
        name="attend",
    )(doc_lengths, keep_flags, own, query, kv)


class Passed:
    def __init__(self, source, passing, targets, sems):
        self.first = pltpu.make_async_copy(source, passing, sems.at[0])
        self.rest = [pltpu.make_async_copy(part, to, sems.at[1]) for part, to in targets(passing)]
        self.first.start()

    def turn(self):
        self.first.wait()
        for copy in self.rest:
            copy.start()

    def end(self):
        for copy in self.rest:
            copy.wait()


def attend_back_body(
    lens_ref, flags_ref, own_ref, query_ref, grad_ref, kv_ref, wide_ref, log_ref, cos_ref, sin_ref,
    *refs,
):
    sources, grad_query_ref, grad_kv_ref, targets, grad_kv, total = (
        refs[:3], refs[3], refs[4], refs[5:8], refs[8], refs[9],
    )
    passing, sems = refs[10:13], refs[13]
    passes = [
        Passed(sources[i], passing[i], lambda ref, i=i: [(ref, targets[i])], sems.at[i])
        for i in range(3)
    ]
    devices = kv_ref.shape[0]
    scale = 1.0 / math.sqrt(HD)
    grad_kv[...] = jnp.zeros_like(grad_kv)
    for slot in range(SLOTS):
        if slot == 1:
            for one in passes:
                one.turn()
        rank = own_ref[0] + devices * slot
        query = stack_heads(query_ref, slot)
        grad = stack_heads(grad_ref, slot)
        delta = jnp.sum(grad.astype(F32).T * wide_ref[slot], axis=0, keepdims=True)
        log_total = log_ref[slot, 0:1, :]
        total[...] = jnp.zeros_like(total)

        def visit(key_rank, masked):
            device, span = key_block(kv_ref, key_rank)
            keys, values = kv_ref[device, span, :HD], kv_ref[device, span, HD:]
            scores = dot(keys, query, (1, 1)) * scale
            if masked:
                scores = causal(scores)
            probs = jnp.exp(scores - log_total)
            grad_probs = dot(values, grad, (1, 1))
            grad_scores = (probs * (grad_probs - delta)).astype(BF16)
            grad_kv[device, span, HD:] += dot(probs.astype(BF16), grad, (1, 0))
            grad_kv[device, span, :HD] += dot(grad_scores, query, (1, 0)) * scale
            total[...] += dot(keys, grad_scores, (0, 0))

        def step(key_rank, carry):
            visit(key_rank, False)
            return carry

        lax.fori_loop(first_rank(lens_ref, flags_ref, rank), rank, step, 0)
        visit(rank, True)
        turned = (total[...] * scale).T
        span = pl.ds(slot * BLOCK, BLOCK)
        for head in range(turned.shape[0] // BLOCK):
            one = turned[head * BLOCK : (head + 1) * BLOCK]
            grad_query_ref[span, head * HD : (head + 1) * HD] = turn(
                one, cos_ref.at[span], sin_ref.at[span], 1.0
            ).astype(BF16)
    grad_kv_ref[...] = grad_kv[...].astype(BF16)
    for one in passes:
        one.end()


def attend_back(doc_lengths, keep_flags, own, query, grad, kv, wide, log_total, cosine, sine, results):
    count = query.shape[1] // HD * BLOCK
    return pl.pallas_call(
        attend_back_body,
        out_shape=(
            jax.ShapeDtypeStruct(query.shape, BF16),
            jax.ShapeDtypeStruct(kv.shape, BF16),
        )
        + tuple(jax.ShapeDtypeStruct(result.shape, result.dtype) for result in results),
        in_specs=[smem()] * 3 + [vmem()] * 7 + [anywhere()] * 3,
        out_specs=(vmem(),) * 2 + (anywhere(),) * 3,
        scratch_shapes=[
            pltpu.VMEM(kv.shape, F32),
            pltpu.VMEM((HD, count), F32),
        ]
        + buffers(results)
        + [pltpu.SemaphoreType.DMA((3, 2))],
        compiler_params=pltpu.CompilerParams(vmem_limit_bytes=VMEM_BYTES),
        cost_estimate=cost(3_000_000_000, 20_000_000),
        name="attend_back",
    )(doc_lengths, keep_flags, own, query, grad, kv, wide, log_total, cosine, sine, *results)


def finish_body(mixed_ref, grad_ref, qkv_ref, out_ref, *refs):
    query_ref, key_ref = refs[2], refs[3]
    wide, thin = query_ref.shape[1], key_ref.shape[1]
    passing, sems = refs[6:10], refs[10]

    def parts(ref):
        yield ref.at[:, pl.ds(0, wide)], query_ref
        yield ref.at[:, pl.ds(wide, thin)], key_ref
        yield ref.at[:, pl.ds(wide + thin, thin)], refs[4]

    passes = [
        Passed(mixed_ref, passing[0], lambda ref: [(ref, refs[0])], sems.at[0]),
        Passed(grad_ref, passing[1], lambda ref: [(ref, refs[1])], sems.at[1]),
        Passed(out_ref, passing[2], lambda ref: [(ref, refs[5])], sems.at[2]),
        Passed(qkv_ref, passing[3], parts, sems.at[3]),
    ]
    for one in passes:
        one.turn()
    for one in passes:
        one.end()


def finish(mixed, grad, qkv, out, thin):
    share, wide = qkv.shape[0], qkv.shape[1] - 2 * thin
    shapes = [(mixed.shape, BF16), (grad.shape, BF16), ((share, wide), F32)]
    shapes += [((share, thin), F32)] * 2 + [(out.shape, F32)]
    return pl.pallas_call(
        finish_body,
        out_shape=[jax.ShapeDtypeStruct(*shape) for shape in shapes],
        in_specs=[anywhere()] * 4,
        out_specs=[anywhere()] * 6,
        scratch_shapes=buffers([mixed, grad, out, qkv]) + [pltpu.SemaphoreType.DMA((4, 2))],
        compiler_params=pltpu.CompilerParams(vmem_limit_bytes=VMEM_BYTES),
        cost_estimate=cost(0, 20_000_000),
        name="finish",
    )(mixed, grad, qkv, out)


def scatter_back_body(
    part_ref, query_ref, cos_ref, sin_ref, w_query_hbm, w_key_hbm, w_value_hbm,
    dqkv_ref, out_ref,
    w_query, w_key, w_value, load_sems, total,
    core_recv, held, recv, core_send_sem, core_recv_sem, send_sem, recv_sem,
):
    devices = part_ref.shape[0]
    chips = devices // 2
    own = lax.axis_index("tok")
    plane = lax.axis_index("tp")
    partner = (own ^ 1, plane)
    w_query, w_key, w_value = load_all(
        [w_query_hbm, w_key_hbm, w_value_hbm], [w_query, w_key, w_value], load_sems
    )
    greet([partner] + [(own ^ (2 * step), plane) for step in range(1, chips)])

    def core_copy(step):
        return pltpu.make_async_remote_copy(
            src_ref=part_ref.at[own ^ (2 * step) ^ 1],
            dst_ref=core_recv.at[step],
            send_sem=core_send_sem.at[step],
            recv_sem=core_recv_sem.at[step],
            device_id=partner,
            device_id_type=MESH,
        )

    def copy(step):
        return pltpu.make_async_remote_copy(
            src_ref=held.at[step],
            dst_ref=recv.at[step],
            send_sem=send_sem.at[step],
            recv_sem=recv_sem.at[step],
            device_id=(own ^ (2 * step), plane),
            device_id_type=MESH,
        )

    order = list(range(chips - 1, -1, -1))
    for step in order:
        core_copy(step).start()
    for step in order:
        core_copy(step).wait_recv()
        mine = part_ref[own ^ (2 * step)].astype(F32) + core_recv[step].astype(F32)
        if step > 0:
            held[step] = mine.astype(held.dtype)
            copy(step).start()
    wide = query_ref.shape[1]
    query = query_ref[...]
    dqkv_ref[:, :wide] = query
    tiles = [pl.ds(start, 512) for start in range(0, out_ref.shape[1], 512)]
    for tile in tiles:
        total[:, tile] = dot(query, w_query.get()[tile, :], (1, 1))
    for step in range(1, chips):
        copy(step).wait_recv()
        mine = mine + recv[step].astype(F32)
    keys = turn(mine[:, :HD], cos_ref, sin_ref, 1.0).astype(BF16)
    values = mine[:, HD:].astype(BF16)
    dqkv_ref[:, wide : wide + HD] = keys
    dqkv_ref[:, wide + HD :] = values
    for tile in tiles:
        out_ref[:, tile] = (
            total[:, tile]
            + dot(keys, w_key.get()[tile, :], (1, 1))
            + dot(values, w_value.get()[tile, :], (1, 1))
        ).astype(BF16)
    for step in range(1, chips):
        copy(step).wait_send()
    for step in range(chips):
        core_copy(step).wait_send()


def scatter_back(part, query, cosine, sine, w_query, w_key, w_value, collective_id):
    devices, rows = part.shape[:2]
    chips = devices // 2
    shard = part.shape[1:]
    width = w_query.shape[0]
    weights = [w_query, w_key, w_value]
    return pl.pallas_call(
        scatter_back_body,
        out_shape=(
            jax.ShapeDtypeStruct((rows, query.shape[1] + shard[1]), BF16),
            jax.ShapeDtypeStruct((rows, width), BF16),
        ),
        in_specs=[vmem()] * 4 + [anywhere()] * 3,
        out_specs=(vmem(),) * 2,
        scratch_shapes=buffers(weights)
        + [pltpu.SemaphoreType.DMA((3,)), pltpu.VMEM((rows, width), F32)]
        + [pltpu.VMEM((chips,) + shard, part.dtype)] * 3
        + [pltpu.SemaphoreType.DMA((chips,))] * 4,
        compiler_params=params(collective_id),
        cost_estimate=cost(1_000_000_000, 10_000_000),
        name="scatter_back",
    )(part, query, cosine, sine, *weights)


def line_sems(planes):
    return [pltpu.SemaphoreType.DMA((2, planes))] * 2


def line_copy(own, plane, step, source, target, send_sem, recv_sem, index):
    side = 0 if step > 0 else 1
    return pltpu.make_async_remote_copy(
        src_ref=source,
        dst_ref=target,
        send_sem=send_sem.at[side, index],
        recv_sem=recv_sem.at[side, index],
        device_id=(own, plane + step),
        device_id_type=MESH,
    )


def line_gather(own, plane, planes, arrays, start, pace, ready=None):
    last = planes - 1

    def move(array, index, step):
        shard, send_sem, recv_sem = array
        return line_copy(own, plane, step, shard(index), shard(index), send_sem, recv_sem, index)

    for step in range(1, planes + 1):
        yield start + pace * (step - 1)
        before, after = plane - (step - 1), plane + (step - 1)

        @pl.when(before >= 0)
        def _():
            for array in arrays:
                if step > 1:
                    move(array, before, 1).wait_recv()
                if step < planes:

                    @pl.when(plane < last)
                    def _():
                        move(array, before, 1).start()

        @pl.when(after <= last)
        def _():
            for array in arrays:
                if step > 1:
                    move(array, after, -1).wait_recv()
                if step < planes:

                    @pl.when(plane > 0)
                    def _():
                        move(array, after, -1).start()

    if ready is not None:
        ready()
    yield start + pace * (planes + 1)
    for index in range(planes):

        @pl.when((index <= plane) & (plane < last))
        def _():
            for array in arrays:
                move(array, index, 1).wait_send()

        @pl.when((index >= plane) & (plane > 0))
        def _():
            for array in arrays:
                move(array, index, -1).wait_send()


def line_reduce(own, plane, planes, half, part, total, send, recv, send_sem, recv_sem, start, pace):
    last = planes - 1

    def right(index):
        return line_copy(
            own, plane, 1, send.at[index, half], recv.at[index, half], send_sem, recv_sem, index
        )

    def left(index):
        slot = jnp.where(index == plane - 1, planes, index)
        return line_copy(
            own, plane, -1, send.at[index, half], recv.at[slot, half], send_sem, recv_sem, index
        )

    def add(index):
        send[index, half] = (
            part[:, half, index].astype(F32) + recv[index, half].astype(F32)
        ).astype(send.dtype)

    for step in range(1, planes):
        yield start + pace * (step - 1)
        if step == 1:
            part = part.get()
        upper, lower = planes - step + plane, step - planes + plane

        @pl.when((upper <= last) & (plane < last))
        def _():
            @pl.when(plane == 0)
            def _():
                send[upper, half] = part[:, half, upper]

            @pl.when(plane > 0)
            def _():
                right(upper).wait_recv()
                add(upper)

            right(upper).start()

        @pl.when((lower >= 0) & (plane > 0))
        def _():
            @pl.when(plane == last)
            def _():
                send[lower, half] = part[:, half, lower]

            @pl.when(plane < last)
            def _():
                left(lower).wait_recv()
                add(lower)

            left(lower).start()

    yield start + pace * (planes - 1)
    total[half] = part[:, half, plane].astype(F32)

    @pl.when(plane > 0)
    def _():
        right(plane).wait_recv()
        total[half] += recv[plane, half].astype(F32)

    @pl.when(plane < last)
    def _():
        left(plane).wait_recv()
        total[half] += recv[planes, half].astype(F32)

    yield start + pace * (2 * planes)
    for index in range(planes):

        @pl.when((index > plane) & (plane < last))
        def _():
            right(index).wait_send()

        @pl.when((index < plane) & (plane > 0))
        def _():
            left(index).wait_send()


def gather_flows(gathered, scratch, start, pace, done=None, key=None):
    send_sem, recv_sem = scratch
    planes = gathered.shape[2]
    own, plane = lax.axis_index("tok"), lax.axis_index("tp")

    def flow(half):
        array = (lambda index: gathered.at[:, half, index], send_sem.at[half], recv_sem.at[half])
        ready = None if key is None else lambda: done.add(key + (half,))
        yield from line_gather(own, plane, planes, [array], start + pace / 2 * half, pace, ready)

    return [flow(half) for half in range(HALVES)]


def sum_flows(
    part_ref, gathered, scratch, math_rule, start=0.0, pace=8.7, extra=None, done=None, key=None
):
    total, send, recv, send_sem, recv_sem = scratch[:5]
    planes = part_ref.shape[2]
    own, plane = lax.axis_index("tok"), lax.axis_index("tp")

    def flow(half):
        begin = start + pace / 2 * half
        reducing = line_reduce(
            own, plane, planes, half, part_ref, total, send, recv,
            send_sem.at[half], recv_sem.at[half], begin, pace,
        )
        for number in range(planes):
            yield next(reducing)
        next(reducing)
        math_rule(plane, half, total)
        if gathered is not None:
            arrays = [
                (
                    lambda index: gathered.at[:, half, index],
                    scratch[5].at[half],
                    scratch[6].at[half],
                )
            ]
            if extra is not None and half == HALVES - 1:
                arrays.append(extra)
            ready = None if key is None else lambda: done.add(key + (half,))
            yield from line_gather(
                own, plane, planes, arrays, begin + pace * (planes - 1), pace, ready
            )
        for _ in reducing:
            pass

    return [flow(half) for half in range(HALVES)]


def sum_scratch(planes, width, gathers=True):
    shard = (HALVES, SLOTS, TILE, width)
    return [
        pltpu.VMEM(shard, F32),
        pltpu.VMEM((planes,) + shard, BF16),
        pltpu.VMEM((planes + 1,) + shard, BF16),
    ] + [pltpu.SemaphoreType.DMA((HALVES, 2, planes))] * (4 if gathers else 2)


def norm_math(x, gain_ref, hidden_ref, inv_ref, gathered):
    def rule(plane, half, total):
        x_ref = x.get()
        for block in range(SLOTS):
            hidden = x_ref[block, half, plane].astype(F32) + total[half, block]
            inv = lax.rsqrt(jnp.mean(hidden * hidden, axis=1, keepdims=True) + norm_eps)
            hidden_ref[half, block] = hidden
            inv_ref[half, block] = inv
            gathered[block, half, plane] = (hidden * inv * gain_ref[...]).astype(BF16)

    return rule


def ffn_math(hiddens, inv_ref, dy, gain_ref, grad_ref, gains_ref, gathered):
    def rule(plane, half, total):
        if half == 0:
            gains_ref[...] = jnp.zeros_like(gains_ref)
        hidden_ref, dy_ref = hiddens.get(), dy.get()
        for block in range(SLOTS):
            dn = total[half, block]
            hidden = hidden_ref[half, block]
            inv = inv_ref[half, block]
            weighted = gain_ref[...] * dn
            mean = jnp.mean(weighted * hidden, axis=1, keepdims=True)
            grad = (
                keep_scale * dy_ref[block, half, plane].astype(F32)
                + inv * weighted
                - hidden * (inv * inv * inv * mean)
            )
            grad_ref[half, block] = grad
            gathered[block, half, plane] = grad.astype(BF16)
            gains_ref[0:1, :] += jnp.sum(dn * hidden * inv, axis=0, keepdims=True)

    return rule


def mixed_math(hiddens, xs, mixed_ref):
    def rule(plane, half, total):
        hidden_ref, x_ref = hiddens.get(), xs.get()
        for block in range(SLOTS):
            x = x_ref[block, half, plane].astype(F32)
            branch = (hidden_ref[half, block] - x) + total[half, block]
            mixed_ref[half, block] = (x + keep_scale * branch).astype(BF16)

    return rule


def attn_math(xs, inv_ref, dy, grads, gain_ref, ffn_gains_ref, gains_all, gathered):
    def rule(plane, half, total):
        x_ref, dy_ref, grad_ref = xs.get(), dy.get(), grads.get()
        if half == 0:
            gains_all[plane] = ffn_gains_ref[...]
        for block in range(SLOTS):
            dn = total[half, block]
            x = x_ref[block, half, plane].astype(F32)
            inv = inv_ref[block, half, plane]
            weighted = gain_ref[...] * dn
            mean = jnp.mean(weighted * x, axis=1, keepdims=True)
            grad = (
                (1.0 - keep_scale) * dy_ref[block, half, plane].astype(F32)
                + grad_ref[half, block]
                + inv * weighted
                - x * (inv * inv * inv * mean)
            )
            gathered[block, half, plane] = grad.astype(BF16)
            gains_all[plane, 1:2, :] += jnp.sum(dn * x * inv, axis=0, keepdims=True)

    return rule


def deal_sum_body(
    lens_ref, flags_ref, gain_ref, own_hbm, part_hbm, x_hbm,
    out_hbm, gathered_hbm, hidden_ref, inv_ref,
    own_blocks, part, x, out_ref, gathered, load_sems, store_sems, *scratch,
):
    dealing, summing = scratch[: deal_count()], scratch[deal_count() :]
    part, blocks, x = load_all([part_hbm, own_hbm, x_hbm], [part, own_blocks, x], load_sems)
    out, rows = store_all([out_hbm, gathered_hbm], [out_ref, gathered], store_sems)
    greet(bit_peers(stages_of("tok")), line=True)
    tile = BLOCK // CHUNKS

    def finish(chunk, values):
        for slot, value in enumerate(values):
            out_ref[slot, pl.ds(chunk * tile, tile), :] = value
        if chunk == CHUNKS - 1:
            out.send()

    run(
        *sum_flows(part, gathered, summing, norm_math(x, gain_ref, hidden_ref, inv_ref, gathered)),
        deal_flow(lens_ref, flags_ref, blocks, finish, dealing),
    )
    rows.send()
    rows.copy.wait()
    out.copy.wait()


def deal_sum(doc_lengths, keep_flags, blocks, part, x, gain, collective_id):
    planes, width = part.shape[2], part.shape[4]
    shard = (HALVES, SLOTS, TILE)
    dealt = jax.ShapeDtypeStruct((SLOTS, BLOCK, width), blocks.dtype)
    rows = jax.ShapeDtypeStruct(part.shape, BF16)
    return pl.pallas_call(
        deal_sum_body,
        out_shape=(
            dealt,
            rows,
            jax.ShapeDtypeStruct(shard + (width,), F32),
            jax.ShapeDtypeStruct(shard + (1,), F32),
        ),
        in_specs=[smem(), smem(), vmem()] + [anywhere()] * 3,
        out_specs=(anywhere(),) * 2 + (vmem(),) * 2,
        scratch_shapes=buffers([blocks, part, x, dealt, rows])
        + [pltpu.SemaphoreType.DMA((3,)), pltpu.SemaphoreType.DMA((2,))]
        + deal_scratch(stages_of("tok"), width, blocks.dtype)
        + sum_scratch(planes, width),
        compiler_params=params(collective_id),
        cost_estimate=cost(0, 60_000_000),
        name="deal_sum",
    )(doc_lengths, keep_flags, gain, blocks, part, x)


def spread_flow(units, outs, scratch, pace, start=0.0):
    own, plane = lax.axis_index("tok"), lax.axis_index("tp")
    count = len(units)
    boxes, inboxes, core_inboxes = scratch[:count], scratch[count : 2 * count], scratch[2 * count : 3 * count]
    core_send_sem, core_recv_sem, send_sem, recv_sem = scratch[3 * count :]
    chips = boxes[0].shape[0]
    bits = [1 << i for i in range(int(math.log2(chips)))]
    orders = (bits, bits[::-1])
    stages = len(bits)

    def core_copy(unit, chip):
        return pltpu.make_async_remote_copy(
            src_ref=boxes[unit].at[chip],
            dst_ref=core_inboxes[unit].at[chip],
            send_sem=core_send_sem.at[unit, chip],
            recv_sem=core_recv_sem.at[unit, chip],
            device_id=(own ^ 1, plane),
            device_id_type=MESH,
        )

    def active(half, stage):
        gone = orders[half][:stage]
        return [chip for chip in range(chips) if all(chip & bit == 0 for bit in gone)]

    def slot(stage, half, chip):
        before = sum(chips >> (earlier + 1) for earlier in range(stage))
        return before + active(half, stage + 1).index(chip)

    def copy(unit, half, stage, chip):
        bit = orders[half][stage]
        there = slot(stage, half, chip)
        return pltpu.make_async_remote_copy(
            src_ref=boxes[unit].at[chip ^ bit, half],
            dst_ref=inboxes[unit].at[there, half],
            send_sem=send_sem.at[unit, half, there],
            recv_sem=recv_sem.at[unit, half, there],
            device_id=(own ^ (2 * bit), plane),
            device_id_type=MESH,
        )

    def offer(unit, chip):
        for half in range(2):
            term = units[unit]((own ^ (2 * chip)) ^ 1, half)
            boxes[unit][chip, half] = term.astype(BF16)
        core_copy(unit, chip).start()

    def collect(unit, chip):
        core_copy(unit, chip).wait()
        for half in range(2):
            term = units[unit](own ^ (2 * chip), half)
            term = term + core_inboxes[unit][chip, half].astype(F32)
            boxes[unit][chip, half] = term.astype(BF16)
            bit = orders[half][0]
            if chip & bit:
                copy(unit, half, 0, chip ^ bit).start()

    def take(unit, stage, half):
        for chip in active(half, stage + 1):
            copy(unit, half, stage, chip).wait_recv()
            got = inboxes[unit][slot(stage, half, chip), half].astype(F32)
            total = boxes[unit][chip, half].astype(F32) + got
            if stage < stages - 1:
                boxes[unit][chip, half] = total.astype(BF16)
                bit = orders[half][stage + 1]
                if chip & bit:
                    copy(unit, half, stage + 1, chip ^ bit).start()
            else:
                rows = total.shape[0]
                outs[unit].ref[half * rows : (half + 1) * rows, :] = total
                if half == 1:
                    outs[unit].send()

    chip_order = sorted(range(chips), key=lambda chip: -bin(chip).count("1"))
    for unit in range(count):
        for chip in chip_order:
            yield start + 0.1 + 3 * unit
            offer(unit, chip)
        for chip in chip_order:
            yield start + 3.2 + 3 * unit
            collect(unit, chip)
    for stage in range(stages):
        for unit in range(count):
            for half in range(2):
                yield start + 6.0 + pace * (unit + 1 + count * stage)
                take(unit, stage, half)
    yield 1e6
    for out in outs:
        out.copy.wait()
    for unit in range(count):
        for half in range(2):
            for stage in range(stages):
                for chip in active(half, stage + 1):
                    copy(unit, half, stage, chip).wait_send()


def spread_scratch(shapes, devices):
    chips = devices // 2
    boxes = [pltpu.VMEM((chips, 2, rows // 2, columns), BF16) for rows, columns in shapes]
    inboxes = [pltpu.VMEM((chips - 1, 2, rows // 2, columns), BF16) for rows, columns in shapes]
    return (
        boxes
        + inboxes
        + boxes
        + [pltpu.SemaphoreType.DMA((len(shapes), chips))] * 2
        + [pltpu.SemaphoreType.DMA((len(shapes), 2, chips - 1))] * 2
    )


def window(ref, number, size):
    if size % 128 == 0:
        return ref[:, pl.ds(pl.multiple_of(number * size, size), size)]
    parts = 128 // size
    tile = ref[:, pl.ds(pl.multiple_of(number // parts * 128, 128), 128)].astype(F32)
    return choose(
        number % parts, [tile[:, i * size : (i + 1) * size] for i in range(parts)]
    ).astype(ref.dtype)


def rows_by_owner(left, right, rows):
    def term(owner, half):
        return lax.dot_general(
            window(left.get(), owner * 2 + half, rows // 2),
            right.get()[...],
            (((0,), (0,)), ((), ())),
            preferred_element_type=F32,
        )

    return term


def columns_by_owner(left, right, columns):
    def term(owner, half):
        rows = left.shape[1] // 2
        return lax.dot_general(
            left.get()[:, half * rows : (half + 1) * rows],
            window(right.get(), owner, columns),
            (((0,), (0,)), ((), ())),
            preferred_element_type=F32,
        )

    return term


def ffn_sums_body(*refs):
    inv_ref, gain_ref = refs[:2]
    sources, (grad_ref, gains_ref, mixed_ref), targets = refs[2:12], refs[12:15], refs[15:19]
    loaded, stored, refs = refs[19:29], refs[29:33], refs[33:]
    load_sems, store_sems, refs = refs[0], refs[1], refs[2:]
    summing, mixing, spreading = refs[:7], refs[7:12], refs[12:]
    own, plane = lax.axis_index("tok"), lax.axis_index("tp")
    loads = load_all(sources, loaded, load_sems)
    part, normed, dgate, dup, inner, dm, hidden, dy, mixed_part, x = loads
    rows, *grads = store_all(targets, stored, store_sems)
    gathered = rows.ref
    share = normed.shape[1] // lax.axis_size("tok")
    greet([(own ^ 1, plane)] + [(own ^ (2 << i), plane) for i in range(stages_of("tok") - 1)], True)
    done = set()

    def leave():
        for half in range(HALVES):
            yield 80.0, ("rows", half)
        rows.send()

    run(
        *sum_flows(
            part,
            gathered,
            summing,
            ffn_math(hidden, inv_ref, dy, gain_ref, grad_ref, gains_ref, gathered),
            done=done,
            key=("rows",),
        ),
        *sum_flows(mixed_part, None, mixing, mixed_math(hidden, x, mixed_ref), 27.0, 11.0),
        spread_flow(
            [
                rows_by_owner(normed, dgate, share),
                rows_by_owner(normed, dup, share),
                columns_by_owner(inner, dm, share),
            ],
            grads,
            spreading,
            15.6,
        ),
        leave(),
        done=done,
    )
    rows.copy.wait()


def ffn_sums(
    part, hidden, inv, dy, gain, normed, dgate, dup, inner, dm, mixed_part, x, collective_id
):
    planes, width = part.shape[2], part.shape[4]
    devices = lax.axis_size("tok")
    share = width // devices
    wide = dgate.shape[1]
    shapes = [(share, wide), (share, wide), (wide, share)]
    rows = jax.ShapeDtypeStruct(part.shape, BF16)
    grads = [jax.ShapeDtypeStruct(shape, F32) for shape in shapes]
    sources = [part, normed, dgate, dup, inner, dm, hidden, dy, mixed_part, x]
    grad, gains, mixed, rows, gate, up, down = pl.pallas_call(
        ffn_sums_body,
        out_shape=[
            jax.ShapeDtypeStruct(hidden.shape, F32),
            jax.ShapeDtypeStruct((8, width), F32),
            jax.ShapeDtypeStruct(hidden.shape, BF16),
            rows,
        ]
        + grads,
        in_specs=[vmem()] * 2 + [anywhere()] * len(sources),
        out_specs=[vmem()] * 3 + [anywhere()] * 4,
        scratch_shapes=buffers(sources + [rows] + grads)
        + [pltpu.SemaphoreType.DMA((len(sources),)), pltpu.SemaphoreType.DMA((4,))]
        + sum_scratch(planes, width)
        + sum_scratch(planes, width, False)
        + spread_scratch(shapes, devices),
        compiler_params=params(collective_id),
        cost_estimate=cost(0, 80_000_000),
        name="ffn_sums",
    )(inv, gain, *sources)
    return rows, grad, gains, gate, up, down, mixed


def together():
    return stages_of("tok") <= 3


def attn_sums_body(lens_ref, flags_ref, *refs):
    both = together()
    mixed_ref, inv_ref, gain_ref, ffn_gains_ref = refs[:4]
    sources, home_ref, grad_home_ref, refs = refs[4:12], refs[12], refs[13], refs[14:]
    gathered, gains_ref, mixed_out = refs[:3]
    targets, refs = refs[3:5], refs[5:]
    loaded, stored, load_sems, store_sems, refs = refs[:8], refs[8:10], refs[10], refs[11], refs[12:]
    part, normed, dqkv, attended, da, x, dy, grad = load_all(sources, loaded, load_sems)
    weight_grads = store_all(targets, stored, store_sems)
    if both:
        grad_out, gathered = gathered, refs[0]
        gain_sums, gains_ref = gains_ref, refs[1]
        refs = refs[2:]
    summing, undealing, refs = refs[:7], refs[7 : 7 + deal_count()], refs[7 + deal_count() :]
    mixed_all, mixed_sems, home_sems = refs[0], refs[1:3], refs[3]
    gains_all, gains_sems, refs = refs[4], refs[5:7], refs[7:]
    planes = part.shape[2]
    plane = lax.axis_index("tp")
    share = normed.shape[1] // lax.axis_size("tok")
    home = pltpu.make_async_copy(home_ref, mixed_out, home_sems.at[0])
    home.start()
    if both:
        grad_home = pltpu.make_async_copy(grad_home_ref, grad_out, home_sems.at[1])
        grad_home.start()
        grad_undealing, refs = refs[: deal_count()], refs[deal_count() :]
        gaining, refs = refs[:3], refs[3:]
    greet(all_peers() if both else bit_peers(stages_of("tok")), True)
    for half in range(HALVES):
        mixed_all[:, half, plane] = mixed_ref[half]
    done = set()

    def sum_gains():
        yield (70.0, ("grad", HALVES - 1))
        total = gains_all[0]
        for index in range(1, planes):
            total = total + gains_all[index]
        gains_ref[...] = total
        done.add(("gains",))

    flows = [
        *gather_flows(mixed_all, mixed_sems, 0.0, 8.7, done, ("mixed",)),
        *sum_flows(
            part,
            gathered,
            summing,
            attn_math(x, inv_ref, dy, grad, gain_ref, ffn_gains_ref, gains_all, gathered),
            9.0,
            10.0,
            (lambda index: gains_all.at[index],) + gains_sems,
            done,
            ("grad",),
        ),
        spread_flow(
            [
                rows_by_owner(normed, dqkv, share),
                columns_by_owner(attended, da, share),
            ],
            weight_grads,
            refs,
            9.0,
        ),
        undeal_flow(
            lens_ref, flags_ref, mixed_all, mixed_out, home, undealing, 28.0, 4.5, ("mixed",), 6.0
        ),
        sum_gains(),
    ]
    if both:
        flows += [
            undeal_flow(
                lens_ref, flags_ref, gathered, grad_out, grad_home, grad_undealing,
                55.0, 4.5, ("grad",), 8.0,
            ),
            gain_flow(gains_ref, gain_sums, gaining, 72.0, ("gains",)),
        ]
    run(*flows, done=done)


def attn_sums(
    doc_lengths, keep_flags, part, mixed, x, inv, dy, grad, gain, ffn_gains, normed, dqkv, attended,
    da, home, grad_home, collective_id,
):
    planes, width = part.shape[2], part.shape[4]
    devices = lax.axis_size("tok")
    share = width // devices
    shapes = [(share, dqkv.shape[1]), (attended.shape[1], share)]
    both = together()
    rows_shape = jax.ShapeDtypeStruct(part.shape, BF16)
    gains_shape = jax.ShapeDtypeStruct((8, width), F32)
    blocks_shape = jax.ShapeDtypeStruct(home.shape, BF16)
    gain_part = gain_share(width, devices)
    first = (
        [blocks_shape, jax.ShapeDtypeStruct((8, gain_part), F32)] if both else [rows_shape, gains_shape]
    )
    dealing = deal_scratch(stages_of("tok"), width, BF16)
    sources = [part, normed, dqkv, attended, da, x, dy, grad]
    weight_grads = [jax.ShapeDtypeStruct(shape, F32) for shape in shapes]
    grads, gains, mixed_blocks, qkv, out = pl.pallas_call(
        attn_sums_body,
        out_shape=first
        + [blocks_shape]
        + weight_grads,
        in_specs=[smem(), smem()] + [vmem()] * 4 + [anywhere()] * 10,
        out_specs=[vmem()] * 3 + [anywhere()] * 2,
        scratch_shapes=buffers(sources + weight_grads)
        + [pltpu.SemaphoreType.DMA((8,)), pltpu.SemaphoreType.DMA((2,))]
        + (
            [pltpu.VMEM(part.shape, BF16), pltpu.VMEM((8, width), F32)] if both else []
        )
        + sum_scratch(planes, width)
        + dealing
        + [pltpu.VMEM(part.shape, BF16)]
        + [pltpu.SemaphoreType.DMA((HALVES, 2, planes))] * 2
        + [pltpu.SemaphoreType.DMA((2,)), pltpu.VMEM((planes, 8, width), F32)]
        + line_sems(planes)
        + (dealing + gain_scratch(devices, gain_part) if both else [])
        + spread_scratch(shapes, devices),
        compiler_params=params(collective_id),
        cost_estimate=cost(0, 80_000_000),
        name="attn_sums",
    )(
        doc_lengths, keep_flags, mixed, inv, gain, ffn_gains, *sources, home, grad_home
    )
    if not both:
        grads, gains = undeal(doc_lengths, keep_flags, grads, grad_home, gains, collective_id + 1)
    return mixed_blocks, grads, gains, qkv, out


def rotary_tables(doc_lengths, keep_flags, ranks):
    blocks = keep_flags * (doc_lengths // BLOCK)
    ends = jnp.cumsum(blocks, dtype=jnp.int32)
    starts = ends - blocks
    inside = (ranks[:, None] >= starts[None, :]) & (ranks[:, None] < ends[None, :])
    first = jnp.sum(jnp.where(inside, starts[None, :], 0), axis=1, dtype=jnp.int32)
    offsets = jnp.arange(BLOCK, dtype=jnp.int32)
    positions = (((ranks - first) * BLOCK)[:, None] + offsets[None, :]).reshape(-1)
    half_dim = HD // 2
    freqs = jnp.exp(jnp.arange(half_dim, dtype=jnp.float32) * (-2.0 * math.log(10000.0) / HD))
    angles = positions.astype(jnp.float32)[:, None] * freqs[None, :]
    cosine, sine = jnp.cos(angles), jnp.sin(angles)
    return jnp.concatenate([cosine, cosine], axis=1), jnp.concatenate([sine, -sine], axis=1)


def over_columns(left, right):
    return lax.dot_general(
        left, right, (((1,), (1,)), ((), ())), preferred_element_type=jnp.float32
    )


def on_device(
    tokens,
    gain_attn,
    w_query,
    w_key,
    w_value,
    w_out,
    gain_ffn,
    w_gate,
    w_up,
    w_down,
    cotangent,
    doc_lengths,
    keep_flags,
):
    length = tokens.shape[0]
    model_width = tokens.shape[1]
    devices = lax.axis_size("tok")
    planes = lax.axis_size("tp")
    own_index = lax.axis_index("tok")
    blocks_here = length // BLOCK
    kept_here = blocks_here // 2
    rows = kept_here * BLOCK
    token_blocks = tokens.reshape(blocks_here, BLOCK, model_width)
    grad_blocks = cotangent.reshape(blocks_here, BLOCK, model_width)

    own_ranks = own_index + jnp.arange(kept_here, dtype=jnp.int32) * devices
    cosine, sine = rotary_tables(doc_lengths, keep_flags, own_ranks)
    own = jnp.reshape(own_index, (1,)).astype(jnp.int32)
    rows_x, normed_one, inv_one, queries, kv_all = deal_project(
        doc_lengths,
        keep_flags,
        gain_attn.reshape(1, -1),
        cosine,
        sine,
        token_blocks,
        w_query,
        w_key,
        w_value,
        0,
    )
    rows_x = rows_x.reshape(rows, model_width)
    attended, attended_wide, log_totals = attend(doc_lengths, keep_flags, own, queries, kv_all)

    def by_plane(array):
        return array.reshape(kept_here, HALVES, planes, TILE, array.shape[1])

    x_planes = by_plane(rows_x)
    rows_dy, normed_two, hidden_res, inv_two = deal_sum(
        doc_lengths,
        keep_flags,
        grad_blocks,
        by_plane(jnp.dot(attended, w_out, preferred_element_type=jnp.float32).astype(jnp.bfloat16)),
        x_planes,
        gain_ffn.reshape(1, -1),
        1,
    )
    rows_dy = rows_dy.reshape(rows, model_width)
    normed_two = normed_two.reshape(rows, model_width)
    gate = jnp.dot(normed_two, w_gate, preferred_element_type=jnp.float32)
    upper = jnp.dot(normed_two, w_up, preferred_element_type=jnp.float32)
    sigma = jax.nn.sigmoid(gate)
    swish = gate * sigma
    inner = (swish * upper).astype(jnp.bfloat16)

    grad_m = (keep_scale * rows_dy.astype(jnp.float32)).astype(jnp.bfloat16)
    grad_inner = over_columns(grad_m, w_down)
    grad_gate_pre = (grad_inner * upper * sigma * (1.0 + gate * (1.0 - sigma))).astype(jnp.bfloat16)
    grad_up_pre = (grad_inner * swish).astype(jnp.bfloat16)
    part_two = (
        over_columns(grad_gate_pre, w_gate) + over_columns(grad_up_pre, w_up)
    ).astype(jnp.bfloat16)

    dy_planes = by_plane(rows_dy)
    grad_a, grad_hidden, gains_ffn, grad_gate, grad_up, grad_down, mixed_rows = ffn_sums(
        by_plane(part_two),
        hidden_res,
        inv_two,
        dy_planes,
        gain_ffn.reshape(1, -1),
        normed_two,
        grad_gate_pre,
        grad_up_pre,
        inner,
        grad_m,
        by_plane(jnp.dot(inner, w_down, preferred_element_type=jnp.float32).astype(jnp.bfloat16)),
        x_planes,
        4,
    )
    grad_a = grad_a.reshape(rows, model_width)

    grad_attended = over_columns(grad_a, w_out).astype(jnp.bfloat16)
    grad_query_pre, grad_kv, grad_gate, grad_up, grad_down = attend_back(
        doc_lengths,
        keep_flags,
        own,
        queries,
        grad_attended,
        kv_all,
        attended_wide,
        log_totals,
        cosine,
        sine,
        [grad_gate, grad_up, grad_down],
    )
    grad_qkv_pre, part_one = scatter_back(
        grad_kv, grad_query_pre, cosine, sine, w_query, w_key, w_value, 5
    )
    mixed, token_grad, gain_sums, grad_qkv, grad_out = attn_sums(
        doc_lengths,
        keep_flags,
        by_plane(part_one),
        mixed_rows,
        x_planes,
        by_plane(inv_one),
        dy_planes,
        grad_hidden,
        gain_attn.reshape(1, -1),
        gains_ffn,
        normed_one,
        grad_qkv_pre,
        attended,
        grad_a,
        token_blocks,
        grad_blocks,
        6,
    )
    own_share = model_width // devices
    if gain_sums.shape[1] != own_share:
        gain_sums = lax.dynamic_slice_in_dim(gain_sums, own_index * own_share, own_share, 1)
    mixed, token_grad, grad_query, grad_key, grad_value, grad_out = finish(
        mixed, token_grad, grad_qkv, grad_out, w_key.shape[1]
    )

    return (
        mixed.reshape(length, model_width),
        token_grad.reshape(length, model_width),
        gain_sums[1],
        grad_query,
        grad_key,
        grad_value,
        grad_out,
        gain_sums[0],
        grad_gate,
        grad_up,
        grad_down,
    )


def solution(mesh):
    placed = (
        P("tok", None),
        P(),
        P(None, "tp"),
        P(None, "tp"),
        P(None, "tp"),
        P("tp", None),
        P(),
        P(None, "tp"),
        P(None, "tp"),
        P("tp", None),
        P("tok", None),
        P(),
        P(),
    )
    return jax.shard_map(
        on_device,
        mesh=mesh,
        in_specs=placed,
        out_specs=(
            P("tok", None),
            P("tok", None),
            P("tok"),
            P("tok", "tp"),
            P("tok", "tp"),
            P("tok", "tp"),
            P("tp", "tok"),
            P("tok"),
            P("tok", "tp"),
            P("tok", "tp"),
            P("tp", "tok"),
        ),
        check_vma=False,
    )
```

```python
import functools
import math

import jax
import jax.numpy as jnp
from jax import lax
from jax.experimental import pallas as pl
from jax.experimental.pallas import tpu as pltpu
from jax.sharding import PartitionSpec as P

HD = 128
BLOCK = 128
SLOTS = 3
CHUNKS = 8
HALVES = 2
TILE = 16
HOP = 2.0
MESH = pl.DeviceIdType.MESH
VMEM_BYTES = 60 * 2**20

norm_eps = 1e-05
keep_scale = 2.0
F32 = jnp.float32
BF16 = jnp.bfloat16


def vmem():
    return pl.BlockSpec(memory_space=pltpu.VMEM)


def smem():
    return pl.BlockSpec(memory_space=pltpu.SMEM)


def params(collective_id):
    return pltpu.CompilerParams(
        collective_id=collective_id, has_side_effects=True, vmem_limit_bytes=VMEM_BYTES
    )


def cost(flops, moved):
    return pl.CostEstimate(flops=flops, bytes_accessed=moved, transcendentals=0)


def greet(peers, line=False):
    barrier = pltpu.get_barrier_semaphore()
    for peer in peers:
        pl.semaphore_signal(barrier, inc=1, device_id=peer, device_id_type=MESH)
    if not line:
        pl.semaphore_wait(barrier, len(peers))
        return
    own, plane = lax.axis_index("tok"), lax.axis_index("tp")
    last = lax.axis_size("tp") - 1

    @pl.when(plane > 0)
    def _():
        pl.semaphore_signal(barrier, inc=1, device_id=(own, plane - 1), device_id_type=MESH)

    @pl.when(plane < last)
    def _():
        pl.semaphore_signal(barrier, inc=1, device_id=(own, plane + 1), device_id_type=MESH)

    end = (plane == 0) | (plane == last)

    @pl.when(end)
    def _():
        pl.semaphore_wait(barrier, len(peers) + 1)

    @pl.when(jnp.logical_not(end))
    def _():
        pl.semaphore_wait(barrier, len(peers) + 2)


def run(*flows, done=frozenset()):
    waiting = [[next(flow), number, flow] for number, flow in enumerate(flows)]

    def order(entry):
        step = entry[0] if isinstance(entry[0], tuple) else (entry[0], None)
        return (step[1] is not None and step[1] not in done, step[0], entry[1])

    while waiting:
        waiting.sort(key=order)
        entry = waiting[0]
        assert not order(entry)[0]
        try:
            entry[0] = next(entry[2])
        except StopIteration:
            waiting.pop(0)


def anywhere():
    return pl.BlockSpec(memory_space=pl.ANY)


class Loaded:
    def __init__(self, source, target, sem):
        self.copy = pltpu.make_async_copy(source, target, sem)
        self.target = target
        self.here = False
        self.shape = target.shape

    def get(self):
        if not self.here:
            self.copy.wait()
            self.here = True
        return self.target


def load_all(sources, targets, sems):
    loads = [Loaded(*pair, sems.at[i]) for i, pair in enumerate(zip(sources, targets))]
    for load in loads:
        load.copy.start()
    return loads


class Stored:
    def __init__(self, target, source, sem):
        self.copy = pltpu.make_async_copy(source, target, sem)
        self.ref = source

    def send(self):
        self.copy.start()


def store_all(targets, sources, sems):
    return [Stored(*pair, sems.at[i]) for i, pair in enumerate(zip(targets, sources))]


def buffers(arrays):
    return [pltpu.VMEM(array.shape, array.dtype) for array in arrays]


def deal_tables(own, stages, blocks_here, lens_ref, flags_ref):
    def kept_before(place):
        total, start = jnp.int32(0), jnp.int32(0)
        for doc in range(lens_ref.shape[0]):
            blocks = lens_ref[doc] // BLOCK
            total = total + flags_ref[doc] * jnp.clip(place - start, 0, blocks)
            start = start + blocks
        return total

    def edges(stage):
        first = (own >> stage) << stage
        return (
            kept_before(first * blocks_here),
            kept_before((first + (1 << stage)) * blocks_here),
        )

    def located(stage):
        if stage == 0:
            ends = [kept_before(own * blocks_here + i + 1) for i in range(blocks_here)]

            def place(rank):
                index = jnp.int32(0)
                for end in ends:
                    index = index + (end <= rank).astype(jnp.int32)
                return index

            return place
        mine = (own >> (stage - 1)) << (stage - 1)
        low, high = edges(stage - 1)
        other = kept_before((mine ^ (1 << (stage - 1))) * blocks_here)

        def place(rank):
            inside = (rank >= low) & (rank < high)
            return jnp.where(inside, (rank - low) >> stage, SLOTS + ((rank - other) >> stage))

        return place

    keeps, sends = [], []
    for stage in range(stages):
        low, high = edges(stage)
        place = located(stage)
        period = 1 << (stage + 1)
        for table, target in ((keeps, own), (sends, own ^ (1 << stage))):
            first = low + ((target - low) & (period - 1))
            row = []
            for slot in range(SLOTS):
                rank = first + period * slot
                row.append(jnp.where(rank < high, place(rank), -1))
            table.append(row)
    place = located(stages)
    finals = [place(own + (slot << stages)) for slot in range(SLOTS)]
    return keeps, sends, finals


def choose(index, options):
    value = options[0]
    for number, option in enumerate(options[1:]):
        value = jnp.where(index == number + 1, option, value)
    return value


def slot_of(keep, recv, chunk, index):
    stayed = keep[chunk, jnp.clip(index, 0, SLOTS - 1)]
    arrived = recv[jnp.clip(index - SLOTS, 0, SLOTS - 1)]
    return jnp.where(index < SLOTS, stayed, arrived)


def deal_refs(scratch):
    keep, send = scratch[:2]
    stages = send.shape[0]
    recv = [scratch[2 + i * CHUNKS : 2 + (i + 1) * CHUNKS] for i in range(stages)]
    return keep, send, recv, *scratch[2 + stages * CHUNKS : 4 + stages * CHUNKS]


def bit_peers(stages):
    own, plane = lax.axis_index("tok"), lax.axis_index("tp")
    return [(own ^ (1 << stage), plane) for stage in range(stages)]


def deal_flow(lens_ref, flags_ref, blocks, finish, scratch, pace=4.3, urgent=False):
    keep, send, recv, send_sem, recv_sem = deal_refs(scratch)
    stages = send.shape[0]
    own = lax.axis_index("tok")
    blocks_here = blocks.shape[0]
    rows = BLOCK // CHUNKS
    peers = bit_peers(stages)
    keeps, sends, finals = deal_tables(own, stages, blocks_here, lens_ref, flags_ref)

    def copy(stage, chunk):
        return pltpu.make_async_remote_copy(
            src_ref=send.at[stage, chunk],
            dst_ref=recv[stage][chunk],
            send_sem=send_sem.at[stage, chunk],
            recv_sem=recv_sem.at[stage, chunk],
            device_id=peers[stage],
            device_id_type=MESH,
        )

    def held(stage, chunk, index):
        if stage == 0:
            block = jnp.clip(index, 0, blocks_here - 1)
            return blocks.get()[block, pl.ds(chunk * rows, rows), :]
        return slot_of(keep, recv[stage - 1][chunk], chunk, index)

    for stage in range(stages + 1):
        for chunk in range(CHUNKS):
            if stage < 2:
                yield 1.5 * stage + 0.3 * chunk
            else:
                slack = 4.0 if stage == stages and not urgent else 0.0
                yield 1.5 + HOP * (stage - 1) + pace * (chunk + stage - 1) + slack
            if stage > 0:
                copy(stage - 1, chunk).wait_recv()
            if stage == stages:
                finish(chunk, [held(stage, chunk, finals[slot]) for slot in range(SLOTS)])
            else:
                for slot in range(SLOTS):
                    send[stage, chunk, slot] = held(stage, chunk, sends[stage][slot])
                copy(stage, chunk).start()
                stay = [held(stage, chunk, keeps[stage][slot]) for slot in range(SLOTS)]
                for slot in range(SLOTS):
                    keep[chunk, slot] = stay[slot]
    yield 1e6

    for stage in range(stages):
        for chunk in range(CHUNKS):
            copy(stage, chunk).wait_send()


def deal_scratch(stages, width, kind):
    part = (SLOTS, BLOCK // CHUNKS, width)
    return (
        [pltpu.VMEM((CHUNKS,) + part, kind), pltpu.VMEM((stages, CHUNKS) + part, kind)]
        + [pltpu.VMEM(part, kind)] * (stages * CHUNKS)
        + [pltpu.SemaphoreType.DMA((stages, CHUNKS))] * 2
    )


def deal_count():
    return 4 + stages_of("tok") * CHUNKS


def stages_of(axis):
    return int(math.log2(lax.axis_size(axis)))


def undeal_flow(
    lens_ref, flags_ref, kept_ref, out_ref, home, scratch, start=0.0, pace=4.3, key=None, lag=0.0
):
    keep, send, recv, send_sem, recv_sem = deal_refs(scratch)
    stages = send.shape[0]
    own = lax.axis_index("tok")
    blocks_here = out_ref.shape[0]
    planes = kept_ref.shape[2]
    rows = BLOCK // CHUNKS
    peers = bit_peers(stages)
    keeps, sends, finals = deal_tables(own, stages, blocks_here, lens_ref, flags_ref)

    def copy(stage, chunk):
        return pltpu.make_async_remote_copy(
            src_ref=send.at[stage, chunk],
            dst_ref=recv[stage][chunk],
            send_sem=send_sem.at[stage, chunk],
            recv_sem=recv_sem.at[stage, chunk],
            device_id=peers[stage],
            device_id_type=MESH,
        )

    def source(places, place):
        index = jnp.int32(-1)
        for number, other in enumerate(places):
            index = jnp.where(other == place, number, index)
        return index

    last = stages - 1
    for stage in range(last, -2, -1):
        count = 2 * SLOTS if stage >= 0 else blocks_here
        places = finals if stage == last else keeps[stage + 1] + sends[stage + 1]
        sources = [source(places, place) for place in range(count)]
        for chunk in range(CHUNKS):
            half = chunk // planes
            begin = start + lag * half
            if stage == last:
                yield (begin, None if key is None else key + (half,))
                options = [kept_ref[slot, half, chunk % planes] for slot in range(SLOTS)]
            else:
                hops = last - stage
                slack = 20.0 if stage < 0 else 0.0
                yield begin + HOP * hops + pace * (chunk + hops - (stage < 0)) + slack
                copy(stage + 1, chunk).wait_recv()

            def block(place):
                if stage == last:
                    return choose(sources[place], options)
                return slot_of(keep, recv[stage + 1][chunk], chunk, sources[place])

            if stage < 0:
                if chunk == 0:
                    home.wait()
                span = pl.ds(chunk * rows, rows)
                for place in range(blocks_here):
                    value = out_ref[place, span, :]
                    out_ref[place, span, :] = jnp.where(sources[place] >= 0, block(place), value)
            else:
                for slot in range(SLOTS):
                    send[stage, chunk, slot] = block(SLOTS + slot)
                copy(stage, chunk).start()
                stay = [block(slot) for slot in range(SLOTS)]
                for slot in range(SLOTS):
                    keep[chunk, slot] = stay[slot]
    yield 1e6

    for stage in range(stages):
        for chunk in range(CHUNKS):
            copy(stage, chunk).wait_send()


def gain_flow(gains_ref, sum_ref, scratch, start, key=None):
    gain_recv, gain_send_sem, gain_recv_sem = scratch
    own, plane = lax.axis_index("tok"), lax.axis_index("tp")
    devices = gain_recv.shape[0]
    share = sum_ref.shape[1]

    def portion(there):
        if share < gains_ref.shape[1]:
            return gains_ref.at[:, pl.ds(pl.multiple_of(there * share, share), share)]
        return gains_ref

    def copy(step):
        return pltpu.make_async_remote_copy(
            src_ref=portion(own ^ step),
            dst_ref=gain_recv.at[step],
            send_sem=gain_send_sem.at[step],
            recv_sem=gain_recv_sem.at[step],
            device_id=(own ^ step, plane),
            device_id_type=MESH,
        )

    yield (start, key)
    for step in range(1, devices):
        copy(step).start()
    yield 2e5
    total = portion(own)[...]
    for step in range(1, devices):
        copy(step).wait()
        total = total + gain_recv[step]
    sum_ref[...] = total


def gain_share(width, devices):
    share = width // devices
    return share if share % 128 == 0 else width


def gain_scratch(devices, share):
    return [pltpu.VMEM((devices, 8, share), F32)] + [pltpu.SemaphoreType.DMA((devices,))] * 2


def all_peers():
    own, plane = lax.axis_index("tok"), lax.axis_index("tp")
    return [(own ^ step, plane) for step in range(1, lax.axis_size("tok"))]


def undeal_body(lens_ref, flags_ref, kept_ref, home_ref, gains_ref, out_ref, sum_ref, home_sem, *scratch):
    home = pltpu.make_async_copy(home_ref, out_ref, home_sem)
    home.start()
    greet(all_peers())
    run(
        undeal_flow(lens_ref, flags_ref, kept_ref, out_ref, home, scratch[: deal_count()]),
        gain_flow(gains_ref, sum_ref, scratch[deal_count() :], 0.0),
    )


def undeal(doc_lengths, keep_flags, kept, home, gains, collective_id):
    stages = stages_of("tok")
    devices = 1 << stages
    width = kept.shape[-1]
    share = gain_share(width, devices)
    return pl.pallas_call(
        undeal_body,
        out_shape=(
            jax.ShapeDtypeStruct(home.shape, home.dtype),
            jax.ShapeDtypeStruct((8, share), F32),
        ),
        in_specs=[smem(), smem(), vmem(), pl.BlockSpec(memory_space=pl.ANY), vmem()],
        out_specs=(vmem(), vmem()),
        scratch_shapes=[pltpu.SemaphoreType.DMA]
        + deal_scratch(stages, width, kept.dtype)
        + gain_scratch(devices, share),
        compiler_params=params(collective_id),
        cost_estimate=cost(0, 40_000_000),
        name="undeal",
    )(doc_lengths, keep_flags, kept, home, gains)


def deal_project_body(
    lens_ref, flags_ref, gain_ref, cos_ref, sin_ref, own_hbm, w_query_hbm, w_key_hbm, w_value_hbm,
    x_hbm, normed_hbm, inv_ref, query_ref, out_ref,
    own_half, w_query, w_key, w_value, x_ref, normed_ref, mine_ref, pair_send, pair_recv,
    load_sems, store_sems, pair_send_sem, pair_recv_sem,
    send_sem, recv_sem, relay_send_sem, relay_recv_sem, *dealing,
):
    devices = out_ref.shape[0]
    chips = devices // 2
    own = lax.axis_index("tok")
    plane = lax.axis_index("tp")
    partner = (own ^ 1, plane)
    width = own_half.shape[2]
    tile = BLOCK // CHUNKS
    thin = w_key.shape[1]
    columns = pl.ds(pl.multiple_of((plane % 2) * width, width), width)
    blocks, w_query, w_key, w_value = load_all(
        [own_hbm.at[:, :, columns], w_query_hbm, w_key_hbm, w_value_hbm],
        [own_half, w_query, w_key, w_value],
        load_sems,
    )
    steps = sorted({1 << i for i in range(stages_of("tok"))} | {2 * i for i in range(1, chips)})
    greet([(own ^ step, plane) for step in steps] + [(own, plane ^ 1)])

    def pair_copy(chunk):
        return pltpu.make_async_remote_copy(
            src_ref=pair_send.at[chunk],
            dst_ref=pair_recv.at[chunk],
            send_sem=pair_send_sem.at[chunk],
            recv_sem=pair_recv_sem.at[chunk],
            device_id=(own, plane ^ 1),
            device_id_type=MESH,
        )

    def finish(chunk, values):
        for slot, value in enumerate(values):
            pair_send[chunk, slot] = value
        pair_copy(chunk).start()
        for slot, value in enumerate(values):
            x_ref[slot, pl.ds(chunk * tile, tile), columns] = value

    def norms():
        for chunk in range(CHUNKS):
            yield 500.0 + chunk, (chunk,)
            other = pl.ds(pl.multiple_of((1 - plane % 2) * width, width), width)
            pair_copy(chunk).wait_recv()
            span = pl.ds(chunk * tile, tile)
            for slot in range(SLOTS):
                x_ref[slot, span, other] = pair_recv[chunk, slot]
            for slot in range(SLOTS):
                x = x_ref[slot, span, :].astype(F32)
                inv = lax.rsqrt(jnp.mean(x * x, axis=1, keepdims=True) + norm_eps)
                rows = pl.ds(slot * BLOCK + chunk * tile, tile)
                inv_ref[rows, :] = inv
                normed_ref[rows, :] = (x * inv * gain_ref[...]).astype(BF16)

    done = set()

    def mark(chunk, values):
        finish(chunk, values)
        done.add((chunk,))

    run(
        deal_flow(lens_ref, flags_ref, blocks, mark, dealing, 2.2, True),
        norms(),
        done=done,
    )
    stores = store_all([x_hbm, normed_hbm], [x_ref, normed_ref], store_sems)
    for store in stores:
        store.send()
    for chunk in range(CHUNKS):
        pair_copy(chunk).wait_send()

    def copy(step):
        return pltpu.make_async_remote_copy(
            src_ref=mine_ref,
            dst_ref=out_ref.at[own],
            send_sem=send_sem.at[step],
            recv_sem=recv_sem.at[step],
            device_id=(own ^ (2 * step), plane),
            device_id_type=MESH,
        )

    def relay(step):
        return pltpu.make_async_remote_copy(
            src_ref=mine_ref if step == 0 else out_ref.at[own ^ (2 * step)],
            dst_ref=out_ref.at[own ^ (2 * step)],
            send_sem=relay_send_sem.at[step],
            recv_sem=relay_recv_sem.at[step],
            device_id=partner,
            device_id_type=MESH,
        )

    def product(weight):
        return lax.dot_general(
            normed_ref[...], weight.get()[...], (((1,), (0,)), ((), ())), preferred_element_type=F32
        )

    keys = product(w_key)
    for group in range(thin // HD):
        one = keys[:, group * HD : (group + 1) * HD]
        mine_ref[:, group * HD : (group + 1) * HD] = turn(one, cos_ref, sin_ref, -1.0).astype(BF16)
    mine_ref[:, thin:] = product(w_value).astype(BF16)
    for step in range(1, chips):
        copy(step).start()
    relay(0).start()
    out_ref[own] = mine_ref[...]
    queries = product(w_query)
    for head in range(w_query.shape[1] // HD):
        one = queries[:, head * HD : (head + 1) * HD]
        query_ref[:, head * HD : (head + 1) * HD] = turn(one, cos_ref, sin_ref, -1.0).astype(BF16)
    for step in range(1, chips):
        copy(step).wait_recv()
        relay(step).start()
    for step in range(chips):
        relay(step).wait()
    for step in range(1, chips):
        copy(step).wait_send()
    for store in stores:
        store.copy.wait()


def turn(values, cos_ref, sin_ref, sign):
    return values * cos_ref[...] + pltpu.roll(values, HD // 2, 1) * (sin_ref[...] * sign)


def deal_project(
    doc_lengths, keep_flags, gain, cosine, sine, blocks, w_query, w_key, w_value, collective_id
):
    devices = lax.axis_size("tok")
    chips = devices // 2
    width = blocks.shape[2]
    rows = SLOTS * BLOCK
    both = w_key.shape[1] + w_value.shape[1]
    x_shape, normed_shape = (SLOTS, BLOCK, width), (rows, width)
    weights = [w_query, w_key, w_value]
    return pl.pallas_call(
        deal_project_body,
        out_shape=(
            jax.ShapeDtypeStruct(x_shape, BF16),
            jax.ShapeDtypeStruct(normed_shape, BF16),
            jax.ShapeDtypeStruct((rows, 1), F32),
            jax.ShapeDtypeStruct((rows, w_query.shape[1]), BF16),
            jax.ShapeDtypeStruct((devices, rows, both), BF16),
        ),
        in_specs=[smem()] * 2 + [vmem()] * 3 + [anywhere()] * 4,
        out_specs=(anywhere(),) * 2 + (vmem(),) * 3,
        scratch_shapes=[pltpu.VMEM(blocks.shape[:2] + (width // 2,), BF16)]
        + buffers(weights)
        + [
            pltpu.VMEM(x_shape, BF16),
            pltpu.VMEM(normed_shape, BF16),
            pltpu.VMEM((rows, both), BF16),
            pltpu.VMEM((CHUNKS, SLOTS, BLOCK // CHUNKS, width // 2), BF16),
            pltpu.VMEM((CHUNKS, SLOTS, BLOCK // CHUNKS, width // 2), BF16),
            pltpu.SemaphoreType.DMA((4,)),
            pltpu.SemaphoreType.DMA((2,)),
        ]
        + [pltpu.SemaphoreType.DMA((CHUNKS,))] * 2
        + [pltpu.SemaphoreType.DMA((chips,))] * 4
        + deal_scratch(stages_of("tok"), width // 2, BF16),
        compiler_params=params(collective_id),
        cost_estimate=cost(0, 60_000_000),
        name="deal_project",
    )(doc_lengths, keep_flags, gain, cosine, sine, blocks, *weights)


def first_rank(lens_ref, flags_ref, rank):
    first, start = jnp.int32(0), jnp.int32(0)
    for doc in range(lens_ref.shape[0]):
        blocks = flags_ref[doc] * (lens_ref[doc] // BLOCK)
        first = jnp.where((rank >= start) & (rank < start + blocks), start, first)
        start = start + blocks
    return first


def stack_heads(ref, slot):
    heads = ref.shape[1] // HD
    return jnp.concatenate(
        [ref[slot * BLOCK : (slot + 1) * BLOCK, i * HD : (i + 1) * HD] for i in range(heads)], axis=0
    )


def dot(left, right, dims):
    return lax.dot_general(left, right, ((dims[:1], dims[1:]), ((), ())), preferred_element_type=F32)


def key_pair(kv_ref, rank):
    devices = kv_ref.shape[0]
    both = []
    for one in (jnp.maximum(rank - 1, 0), rank):
        device, slot = lax.rem(one, devices), lax.div(one, devices)
        both.append((device, pl.ds(pl.multiple_of(slot * BLOCK, BLOCK), BLOCK)))
    return both


def read_pair(kv_ref, pair, columns):
    return jnp.concatenate([kv_ref[device, span, columns] for device, span in pair], axis=0)


KEYS, VALUES = slice(0, HD), slice(HD, 2 * HD)


def bounded(scores, alone, diagonal):
    keys = lax.broadcasted_iota(jnp.int32, scores.shape, 0)
    allowed = keys >= jnp.where(alone, BLOCK, 0)
    if diagonal:
        queries = lax.rem(lax.broadcasted_iota(jnp.int32, scores.shape, 1), BLOCK)
        allowed = allowed & (keys <= queries + BLOCK)
    return jnp.where(allowed, scores, -1e30)


def attend_body(
    lens_ref, flags_ref, own_ref, query_ref, kv_ref, w_out_hbm,
    out_ref, wide_ref, log_ref, part_ref, total, w_out, load_sems,
):
    (w_out,) = load_all([w_out_hbm], [w_out], load_sems)
    devices = kv_ref.shape[0]
    scale = 1.0 / math.sqrt(HD)
    for slot in range(SLOTS):
        rank = own_ref[0] + devices * slot
        query = stack_heads(query_ref, slot)
        count = query.shape[0]
        total[...] = jnp.zeros_like(total)

        first = first_rank(lens_ref, flags_ref, rank)

        def visit(key_rank, state, diagonal):
            peak, weight = state
            pair = key_pair(kv_ref, key_rank)
            scores = dot(read_pair(kv_ref, pair, KEYS), query, (1, 1)) * scale
            scores = bounded(scores, key_rank == first, diagonal)
            higher = jnp.maximum(peak, jnp.max(scores, axis=0, keepdims=True))
            shrink = jnp.exp(peak - higher)
            probs = jnp.exp(scores - higher)
            weight = weight * shrink + jnp.sum(probs, axis=0, keepdims=True)
            values = read_pair(kv_ref, pair, VALUES)
            total[...] = total[...] * shrink + dot(values, probs.astype(BF16), (0, 0))
            return higher, weight

        start = (jnp.full((1, count), -1e30, F32), jnp.zeros((1, count), F32))
        state = visit(rank, start, True)
        peak, weight = lax.fori_loop(
            1, lax.div(rank - first, 2) + 1, lambda i, s: visit(rank - 2 * i, s, False), state
        )
        result = total[...] / weight
        wide_ref[slot] = result
        log_ref[slot] = jnp.broadcast_to(peak + jnp.log(weight), log_ref.shape[1:])
        turned = result.T.astype(BF16)
        heads = [turned[head * BLOCK : (head + 1) * BLOCK] for head in range(count // BLOCK)]
        weights = w_out.get()
        part_ref[slot * BLOCK : (slot + 1) * BLOCK, :] = dot(
            jnp.concatenate(heads, axis=1), weights[...], (1, 0)
        ).astype(BF16)
        for head in range(count // BLOCK):
            out_ref[slot * BLOCK : (slot + 1) * BLOCK, head * HD : (head + 1) * HD] = turned[
                head * BLOCK : (head + 1) * BLOCK
            ]


def attend(doc_lengths, keep_flags, own, query, kv, w_out):
    count = query.shape[1] // HD * BLOCK
    return pl.pallas_call(
        attend_body,
        out_shape=(
            jax.ShapeDtypeStruct(query.shape, BF16),
            jax.ShapeDtypeStruct((SLOTS, HD, count), F32),
            jax.ShapeDtypeStruct((SLOTS, 8, count), F32),
            jax.ShapeDtypeStruct((query.shape[0], w_out.shape[1]), BF16),
        ),
        in_specs=[smem()] * 3 + [vmem()] * 2 + [anywhere()],
        out_specs=(vmem(),) * 4,
        scratch_shapes=[pltpu.VMEM((HD, count), F32)]
        + buffers([w_out])
        + [pltpu.SemaphoreType.DMA((1,))],
        compiler_params=pltpu.CompilerParams(vmem_limit_bytes=VMEM_BYTES),
        cost_estimate=cost(1_000_000_000, 10_000_000),
        name="attend",
    )(doc_lengths, keep_flags, own, query, kv, w_out)


class Passed:
    def __init__(self, source, passing, targets, sems):
        self.first = pltpu.make_async_copy(source, passing, sems.at[0])
        self.rest = [pltpu.make_async_copy(part, to, sems.at[1]) for part, to in targets(passing)]
        self.first.start()

    def turn(self):
        self.first.wait()
        for copy in self.rest:
            copy.start()

    def end(self):
        for copy in self.rest:
            copy.wait()


def attend_back_body(
    lens_ref, flags_ref, own_ref, query_ref, rows_ref, w_out_ref, kv_ref, wide_ref, log_ref, cos_ref, sin_ref,
    *refs,
):
    sources, grad_query_ref, grad_kv_ref, targets, grad_kv, total = (
        refs[:3], refs[3], refs[4], refs[5:8], refs[8], refs[9],
    )
    passing, sems = refs[10:13], refs[13]
    passes = [
        Passed(sources[i], passing[i], lambda ref, i=i: [(ref, targets[i])], sems.at[i])
        for i in range(3)
    ]
    devices = kv_ref.shape[0]
    scale = 1.0 / math.sqrt(HD)
    grad_kv[...] = jnp.zeros_like(grad_kv)
    for slot in range(SLOTS):
        if slot == 1:
            for one in passes:
                one.turn()
        rank = own_ref[0] + devices * slot
        query = stack_heads(query_ref, slot)
        grad = dot(rows_ref[slot * BLOCK : (slot + 1) * BLOCK, :], w_out_ref[...], (1, 1)).astype(BF16)
        grad = jnp.concatenate(
            [grad[:, i * HD : (i + 1) * HD] for i in range(grad.shape[1] // HD)], axis=0
        )
        delta = jnp.sum(grad.astype(F32).T * wide_ref[slot], axis=0, keepdims=True)
        log_total = log_ref[slot, 0:1, :]
        total[...] = jnp.zeros_like(total)

        first = first_rank(lens_ref, flags_ref, rank)

        def visit(key_rank, diagonal):
            pair = key_pair(kv_ref, key_rank)
            keys, values = read_pair(kv_ref, pair, KEYS), read_pair(kv_ref, pair, VALUES)
            scores = dot(keys, query, (1, 1)) * scale
            scores = bounded(scores, key_rank == first, diagonal)
            probs = jnp.exp(scores - log_total)
            grad_probs = dot(values, grad, (1, 1))
            grad_scores = (probs * (grad_probs - delta)).astype(BF16)
            grad_values = dot(probs.astype(BF16), grad, (1, 0))
            grad_keys = dot(grad_scores, query, (1, 0)) * scale
            for half, (device, span) in enumerate(pair):
                rows = slice(half * BLOCK, (half + 1) * BLOCK)
                grad_kv[device, span, HD:] += grad_values[rows]
                grad_kv[device, span, :HD] += grad_keys[rows]
            total[...] += dot(keys, grad_scores, (0, 0))

        def step(index, carry):
            visit(rank - 2 * index, False)
            return carry

        visit(rank, True)
        lax.fori_loop(1, lax.div(rank - first, 2) + 1, step, 0)
        turned = (total[...] * scale).T
        span = pl.ds(slot * BLOCK, BLOCK)
        for head in range(turned.shape[0] // BLOCK):
            one = turned[head * BLOCK : (head + 1) * BLOCK]
            grad_query_ref[span, head * HD : (head + 1) * HD] = turn(
                one, cos_ref.at[span], sin_ref.at[span], 1.0
            ).astype(BF16)
    grad_kv_ref[...] = grad_kv[...].astype(BF16)
    for one in passes:
        one.end()


def attend_back(
    doc_lengths, keep_flags, own, query, rows, w_out, kv, wide, log_total, cosine, sine, results
):
    count = query.shape[1] // HD * BLOCK
    return pl.pallas_call(
        attend_back_body,
        out_shape=(
            jax.ShapeDtypeStruct(query.shape, BF16),
            jax.ShapeDtypeStruct(kv.shape, BF16),
        )
        + tuple(jax.ShapeDtypeStruct(result.shape, result.dtype) for result in results),
        in_specs=[smem()] * 3 + [vmem()] * 8 + [anywhere()] * 3,
        out_specs=(vmem(),) * 2 + (anywhere(),) * 3,
        scratch_shapes=[
            pltpu.VMEM(kv.shape, F32),
            pltpu.VMEM((HD, count), F32),
        ]
        + buffers(results)
        + [pltpu.SemaphoreType.DMA((3, 2))],
        compiler_params=pltpu.CompilerParams(vmem_limit_bytes=VMEM_BYTES),
        cost_estimate=cost(3_000_000_000, 20_000_000),
        name="attend_back",
    )(
        doc_lengths, keep_flags, own, query, rows, w_out, kv, wide, log_total, cosine, sine, *results
    )


def finish_body(mixed_ref, grad_ref, qkv_ref, out_ref, *refs):
    query_ref, key_ref = refs[2], refs[3]
    wide, thin = query_ref.shape[1], key_ref.shape[1]
    passing, sems = refs[6:10], refs[10]

    def parts(ref):
        yield ref.at[:, pl.ds(0, wide)], query_ref
        yield ref.at[:, pl.ds(wide, thin)], key_ref
        yield ref.at[:, pl.ds(wide + thin, thin)], refs[4]

    passes = [
        Passed(mixed_ref, passing[0], lambda ref: [(ref, refs[0])], sems.at[0]),
        Passed(grad_ref, passing[1], lambda ref: [(ref, refs[1])], sems.at[1]),
        Passed(out_ref, passing[2], lambda ref: [(ref, refs[5])], sems.at[2]),
        Passed(qkv_ref, passing[3], parts, sems.at[3]),
    ]
    for one in passes:
        one.turn()
    for one in passes:
        one.end()


def finish(mixed, grad, qkv, out, thin):
    share, wide = qkv.shape[0], qkv.shape[1] - 2 * thin
    shapes = [(mixed.shape, BF16), (grad.shape, BF16), ((share, wide), F32)]
    shapes += [((share, thin), F32)] * 2 + [(out.shape, F32)]
    return pl.pallas_call(
        finish_body,
        out_shape=[jax.ShapeDtypeStruct(*shape) for shape in shapes],
        in_specs=[anywhere()] * 4,
        out_specs=[anywhere()] * 6,
        scratch_shapes=buffers([mixed, grad, out, qkv]) + [pltpu.SemaphoreType.DMA((4, 2))],
        compiler_params=pltpu.CompilerParams(vmem_limit_bytes=VMEM_BYTES),
        cost_estimate=cost(0, 20_000_000),
        name="finish",
    )(mixed, grad, qkv, out)


def scatter_back_body(
    part_ref, query_ref, cos_ref, sin_ref, w_query_hbm, w_key_hbm, w_value_hbm,
    dqkv_ref, out_ref,
    w_query, w_key, w_value, load_sems, total,
    core_recv, held, recv, core_send_sem, core_recv_sem, send_sem, recv_sem,
):
    devices = part_ref.shape[0]
    chips = devices // 2
    own = lax.axis_index("tok")
    plane = lax.axis_index("tp")
    partner = (own ^ 1, plane)
    w_query, w_key, w_value = load_all(
        [w_query_hbm, w_key_hbm, w_value_hbm], [w_query, w_key, w_value], load_sems
    )
    greet([partner] + [(own ^ (2 * step), plane) for step in range(1, chips)])

    def core_copy(step):
        return pltpu.make_async_remote_copy(
            src_ref=part_ref.at[own ^ (2 * step) ^ 1],
            dst_ref=core_recv.at[step],
            send_sem=core_send_sem.at[step],
            recv_sem=core_recv_sem.at[step],
            device_id=partner,
            device_id_type=MESH,
        )

    def copy(step):
        return pltpu.make_async_remote_copy(
            src_ref=held.at[step],
            dst_ref=recv.at[step],
            send_sem=send_sem.at[step],
            recv_sem=recv_sem.at[step],
            device_id=(own ^ (2 * step), plane),
            device_id_type=MESH,
        )

    order = list(range(chips - 1, -1, -1))
    for step in order:
        core_copy(step).start()
    for step in order:
        core_copy(step).wait_recv()
        mine = part_ref[own ^ (2 * step)].astype(F32) + core_recv[step].astype(F32)
        if step > 0:
            held[step] = mine.astype(held.dtype)
            copy(step).start()
    wide = query_ref.shape[1]
    query = query_ref[...]
    dqkv_ref[:, :wide] = query
    tiles = [pl.ds(start, 512) for start in range(0, out_ref.shape[1], 512)]
    for tile in tiles:
        total[:, tile] = dot(query, w_query.get()[tile, :], (1, 1))
    for step in range(1, chips):
        copy(step).wait_recv()
        mine = mine + recv[step].astype(F32)
    keys = turn(mine[:, :HD], cos_ref, sin_ref, 1.0).astype(BF16)
    values = mine[:, HD:].astype(BF16)
    dqkv_ref[:, wide : wide + HD] = keys
    dqkv_ref[:, wide + HD :] = values
    for tile in tiles:
        out_ref[:, tile] = (
            total[:, tile]
            + dot(keys, w_key.get()[tile, :], (1, 1))
            + dot(values, w_value.get()[tile, :], (1, 1))
        ).astype(BF16)
    for step in range(1, chips):
        copy(step).wait_send()
    for step in range(chips):
        core_copy(step).wait_send()


def scatter_back(part, query, cosine, sine, w_query, w_key, w_value, collective_id):
    devices, rows = part.shape[:2]
    chips = devices // 2
    shard = part.shape[1:]
    width = w_query.shape[0]
    weights = [w_query, w_key, w_value]
    return pl.pallas_call(
        scatter_back_body,
        out_shape=(
            jax.ShapeDtypeStruct((rows, query.shape[1] + shard[1]), BF16),
            jax.ShapeDtypeStruct((rows, width), BF16),
        ),
        in_specs=[vmem()] * 4 + [anywhere()] * 3,
        out_specs=(vmem(),) * 2,
        scratch_shapes=buffers(weights)
        + [pltpu.SemaphoreType.DMA((3,)), pltpu.VMEM((rows, width), F32)]
        + [pltpu.VMEM((chips,) + shard, part.dtype)] * 3
        + [pltpu.SemaphoreType.DMA((chips,))] * 4,
        compiler_params=params(collective_id),
        cost_estimate=cost(1_000_000_000, 10_000_000),
        name="scatter_back",
    )(part, query, cosine, sine, *weights)


def line_sems(planes):
    return [pltpu.SemaphoreType.DMA((2, planes))] * 2


def line_copy(own, plane, step, source, target, send_sem, recv_sem, index):
    side = 0 if step > 0 else 1
    return pltpu.make_async_remote_copy(
        src_ref=source,
        dst_ref=target,
        send_sem=send_sem.at[side, index],
        recv_sem=recv_sem.at[side, index],
        device_id=(own, plane + step),
        device_id_type=MESH,
    )


def line_gather(own, plane, planes, arrays, start, pace, ready=None):
    last = planes - 1

    def move(array, index, step):
        shard, send_sem, recv_sem = array
        return line_copy(own, plane, step, shard(index), shard(index), send_sem, recv_sem, index)

    for step in range(1, planes + 1):
        yield start + pace * (step - 1)
        before, after = plane - (step - 1), plane + (step - 1)

        @pl.when(before >= 0)
        def _():
            for array in arrays:
                if step > 1:
                    move(array, before, 1).wait_recv()
                if step < planes:

                    @pl.when(plane < last)
                    def _():
                        move(array, before, 1).start()

        @pl.when(after <= last)
        def _():
            for array in arrays:
                if step > 1:
                    move(array, after, -1).wait_recv()
                if step < planes:

                    @pl.when(plane > 0)
                    def _():
                        move(array, after, -1).start()

    if ready is not None:
        ready()
    yield start + pace * (planes + 1)
    for index in range(planes):

        @pl.when((index <= plane) & (plane < last))
        def _():
            for array in arrays:
                move(array, index, 1).wait_send()

        @pl.when((index >= plane) & (plane > 0))
        def _():
            for array in arrays:
                move(array, index, -1).wait_send()


def line_reduce(own, plane, planes, half, part, total, send, recv, send_sem, recv_sem, start, pace):
    last = planes - 1

    def right(index):
        return line_copy(
            own, plane, 1, send.at[index, half], recv.at[index, half], send_sem, recv_sem, index
        )

    def left(index):
        slot = jnp.where(index == plane - 1, planes, index)
        return line_copy(
            own, plane, -1, send.at[index, half], recv.at[slot, half], send_sem, recv_sem, index
        )

    def add(index):
        send[index, half] = (
            part[:, half, index].astype(F32) + recv[index, half].astype(F32)
        ).astype(send.dtype)

    for step in range(1, planes):
        yield start + pace * (step - 1)
        if step == 1:
            part = part.get()
        upper, lower = planes - step + plane, step - planes + plane

        @pl.when((upper <= last) & (plane < last))
        def _():
            @pl.when(plane == 0)
            def _():
                send[upper, half] = part[:, half, upper]

            @pl.when(plane > 0)
            def _():
                right(upper).wait_recv()
                add(upper)

            right(upper).start()

        @pl.when((lower >= 0) & (plane > 0))
        def _():
            @pl.when(plane == last)
            def _():
                send[lower, half] = part[:, half, lower]

            @pl.when(plane < last)
            def _():
                left(lower).wait_recv()
                add(lower)

            left(lower).start()

    yield start + pace * (planes - 1)
    total[half] = part[:, half, plane].astype(F32)

    @pl.when(plane > 0)
    def _():
        right(plane).wait_recv()
        total[half] += recv[plane, half].astype(F32)

    @pl.when(plane < last)
    def _():
        left(plane).wait_recv()
        total[half] += recv[planes, half].astype(F32)

    yield start + pace * (2 * planes)
    for index in range(planes):

        @pl.when((index > plane) & (plane < last))
        def _():
            right(index).wait_send()

        @pl.when((index < plane) & (plane > 0))
        def _():
            left(index).wait_send()


def gather_flows(gathered, scratch, start, pace, done=None, key=None):
    send_sem, recv_sem = scratch
    planes = gathered.shape[2]
    own, plane = lax.axis_index("tok"), lax.axis_index("tp")

    def flow(half):
        array = (lambda index: gathered.at[:, half, index], send_sem.at[half], recv_sem.at[half])
        ready = None if key is None else lambda: done.add(key + (half,))
        yield from line_gather(own, plane, planes, [array], start + pace / 2 * half, pace, ready)

    return [flow(half) for half in range(HALVES)]


def sum_flows(
    part_ref, gathered, scratch, math_rule, start=0.0, pace=8.7, extra=None, done=None, key=None
):
    total, send, recv, send_sem, recv_sem = scratch[:5]
    planes = part_ref.shape[2]
    own, plane = lax.axis_index("tok"), lax.axis_index("tp")

    def flow(half):
        begin = start + pace / 2 * half
        reducing = line_reduce(
            own, plane, planes, half, part_ref, total, send, recv,
            send_sem.at[half], recv_sem.at[half], begin, pace,
        )
        for number in range(planes):
            yield next(reducing)
        next(reducing)
        math_rule(plane, half, total)
        if gathered is not None:
            arrays = [
                (
                    lambda index: gathered.at[:, half, index],
                    scratch[5].at[half],
                    scratch[6].at[half],
                )
            ]
            if extra is not None and half == HALVES - 1:
                arrays.append(extra)
            ready = None if key is None else lambda: done.add(key + (half,))
            yield from line_gather(
                own, plane, planes, arrays, begin + pace * (planes - 1), pace, ready
            )
        for _ in reducing:
            pass

    return [flow(half) for half in range(HALVES)]


def sum_scratch(planes, width, gathers=True):
    shard = (HALVES, SLOTS, TILE, width)
    return [
        pltpu.VMEM(shard, F32),
        pltpu.VMEM((planes,) + shard, BF16),
        pltpu.VMEM((planes + 1,) + shard, BF16),
    ] + [pltpu.SemaphoreType.DMA((HALVES, 2, planes))] * (4 if gathers else 2)


def norm_math(x, gain_ref, hidden_ref, inv_ref, gathered):
    def rule(plane, half, total):
        x_ref = x.get()
        for block in range(SLOTS):
            hidden = x_ref[block, half, plane].astype(F32) + total[half, block]
            inv = lax.rsqrt(jnp.mean(hidden * hidden, axis=1, keepdims=True) + norm_eps)
            hidden_ref[half, block] = hidden
            inv_ref[half, block] = inv
            gathered[block, half, plane] = (hidden * inv * gain_ref[...]).astype(BF16)

    return rule


def ffn_math(hiddens, inv_ref, dy, gain_ref, grad_ref, gains_ref, gathered):
    def rule(plane, half, total):
        if half == 0:
            gains_ref[...] = jnp.zeros_like(gains_ref)
        hidden_ref, dy_ref = hiddens.get(), dy.get()
        for block in range(SLOTS):
            dn = total[half, block]
            hidden = hidden_ref[half, block]
            inv = inv_ref[half, block]
            weighted = gain_ref[...] * dn
            mean = jnp.mean(weighted * hidden, axis=1, keepdims=True)
            grad = (
                keep_scale * dy_ref[block, half, plane].astype(F32)
                + inv * weighted
                - hidden * (inv * inv * inv * mean)
            )
            grad_ref[half, block] = grad
            gathered[block, half, plane] = grad.astype(BF16)
            gains_ref[0:1, :] += jnp.sum(dn * hidden * inv, axis=0, keepdims=True)

    return rule


def mixed_math(hiddens, xs, mixed_ref):
    def rule(plane, half, total):
        hidden_ref, x_ref = hiddens.get(), xs.get()
        for block in range(SLOTS):
            x = x_ref[block, half, plane].astype(F32)
            branch = (hidden_ref[half, block] - x) + total[half, block]
            mixed_ref[half, block] = (x + keep_scale * branch).astype(BF16)

    return rule


def attn_math(xs, inv_ref, dy, grads, gain_ref, ffn_gains_ref, gains_all, gathered):
    def rule(plane, half, total):
        x_ref, dy_ref, grad_ref = xs.get(), dy.get(), grads.get()
        if half == 0:
            gains_all[plane] = ffn_gains_ref[...]
        for block in range(SLOTS):
            dn = total[half, block]
            x = x_ref[block, half, plane].astype(F32)
            inv = inv_ref[block, half, plane]
            weighted = gain_ref[...] * dn
            mean = jnp.mean(weighted * x, axis=1, keepdims=True)
            grad = (
                (1.0 - keep_scale) * dy_ref[block, half, plane].astype(F32)
                + grad_ref[half, block]
                + inv * weighted
                - x * (inv * inv * inv * mean)
            )
            gathered[block, half, plane] = grad.astype(BF16)
            gains_all[plane, 1:2, :] += jnp.sum(dn * x * inv, axis=0, keepdims=True)

    return rule


def deal_sum_body(
    lens_ref, flags_ref, gain_ref, own_hbm, part_hbm, x_hbm,
    out_hbm, gathered_hbm, hidden_ref, inv_ref,
    own_blocks, part, x, out_ref, gathered, load_sems, store_sems, *scratch,
):
    dealing, summing = scratch[: deal_count()], scratch[deal_count() :]
    part, blocks, x = load_all([part_hbm, own_hbm, x_hbm], [part, own_blocks, x], load_sems)
    out, rows = store_all([out_hbm, gathered_hbm], [out_ref, gathered], store_sems)
    greet(bit_peers(stages_of("tok")), line=True)
    tile = BLOCK // CHUNKS

    def finish(chunk, values):
        for slot, value in enumerate(values):
            out_ref[slot, pl.ds(chunk * tile, tile), :] = value
        if chunk == CHUNKS - 1:
            out.send()

    run(
        *sum_flows(part, gathered, summing, norm_math(x, gain_ref, hidden_ref, inv_ref, gathered)),
        deal_flow(lens_ref, flags_ref, blocks, finish, dealing, 5.0),
    )
    rows.send()
    rows.copy.wait()
    out.copy.wait()


def deal_sum(doc_lengths, keep_flags, blocks, part, x, gain, collective_id):
    planes, width = part.shape[2], part.shape[4]
    shard = (HALVES, SLOTS, TILE)
    dealt = jax.ShapeDtypeStruct((SLOTS, BLOCK, width), blocks.dtype)
    rows = jax.ShapeDtypeStruct(part.shape, BF16)
    return pl.pallas_call(
        deal_sum_body,
        out_shape=(
            dealt,
            rows,
            jax.ShapeDtypeStruct(shard + (width,), F32),
            jax.ShapeDtypeStruct(shard + (1,), F32),
        ),
        in_specs=[smem(), smem(), vmem()] + [anywhere()] * 3,
        out_specs=(anywhere(),) * 2 + (vmem(),) * 2,
        scratch_shapes=buffers([blocks, part, x, dealt, rows])
        + [pltpu.SemaphoreType.DMA((3,)), pltpu.SemaphoreType.DMA((2,))]
        + deal_scratch(stages_of("tok"), width, blocks.dtype)
        + sum_scratch(planes, width),
        compiler_params=params(collective_id),
        cost_estimate=cost(0, 60_000_000),
        name="deal_sum",
    )(doc_lengths, keep_flags, gain, blocks, part, x)


def spread_flow(units, outs, scratch, pace, start=0.0):
    own, plane = lax.axis_index("tok"), lax.axis_index("tp")
    count = len(units)
    boxes, inboxes, core_inboxes = scratch[:count], scratch[count : 2 * count], scratch[2 * count : 3 * count]
    core_send_sem, core_recv_sem, send_sem, recv_sem = scratch[3 * count :]
    chips = boxes[0].shape[0]
    bits = [1 << i for i in range(int(math.log2(chips)))]
    orders = (bits, bits[::-1])
    stages = len(bits)

    def core_copy(unit, chip):
        return pltpu.make_async_remote_copy(
            src_ref=boxes[unit].at[chip],
            dst_ref=core_inboxes[unit].at[chip],
            send_sem=core_send_sem.at[unit, chip],
            recv_sem=core_recv_sem.at[unit, chip],
            device_id=(own ^ 1, plane),
            device_id_type=MESH,
        )

    def active(half, stage):
        gone = orders[half][:stage]
        return [chip for chip in range(chips) if all(chip & bit == 0 for bit in gone)]

    def slot(stage, half, chip):
        before = sum(chips >> (earlier + 1) for earlier in range(stage))
        return before + active(half, stage + 1).index(chip)

    def copy(unit, half, stage, chip):
        bit = orders[half][stage]
        there = slot(stage, half, chip)
        return pltpu.make_async_remote_copy(
            src_ref=boxes[unit].at[chip ^ bit, half],
            dst_ref=inboxes[unit].at[there, half],
            send_sem=send_sem.at[unit, half, there],
            recv_sem=recv_sem.at[unit, half, there],
            device_id=(own ^ (2 * bit), plane),
            device_id_type=MESH,
        )

    def offer(unit, chip):
        for half in range(2):
            term = units[unit]((own ^ (2 * chip)) ^ 1, half)
            boxes[unit][chip, half] = term.astype(BF16)
        core_copy(unit, chip).start()

    def collect(unit, chip):
        core_copy(unit, chip).wait()
        for half in range(2):
            term = units[unit](own ^ (2 * chip), half)
            term = term + core_inboxes[unit][chip, half].astype(F32)
            boxes[unit][chip, half] = term.astype(BF16)
            bit = orders[half][0]
            if chip & bit:
                copy(unit, half, 0, chip ^ bit).start()

    def take(unit, stage, half):
        for chip in active(half, stage + 1):
            copy(unit, half, stage, chip).wait_recv()
            got = inboxes[unit][slot(stage, half, chip), half].astype(F32)
            total = boxes[unit][chip, half].astype(F32) + got
            if stage < stages - 1:
                boxes[unit][chip, half] = total.astype(BF16)
                bit = orders[half][stage + 1]
                if chip & bit:
                    copy(unit, half, stage + 1, chip ^ bit).start()
            else:
                rows = total.shape[0]
                outs[unit].ref[half * rows : (half + 1) * rows, :] = total
                if half == 1:
                    outs[unit].send()

    chip_order = sorted(range(chips), key=lambda chip: -bin(chip).count("1"))
    for unit in range(count):
        for chip in chip_order:
            yield start + 0.1 + 3 * unit
            offer(unit, chip)
        for chip in chip_order:
            yield start + 3.2 + 3 * unit
            collect(unit, chip)
    for stage in range(stages):
        for unit in range(count):
            for half in range(2):
                yield start + 6.0 + pace * (unit + 1 + count * stage)
                take(unit, stage, half)
    yield 1e6
    for out in outs:
        out.copy.wait()
    for unit in range(count):
        for half in range(2):
            for stage in range(stages):
                for chip in active(half, stage + 1):
                    copy(unit, half, stage, chip).wait_send()


def spread_scratch(shapes, devices):
    chips = devices // 2
    boxes = [pltpu.VMEM((chips, 2, rows // 2, columns), BF16) for rows, columns in shapes]
    inboxes = [pltpu.VMEM((chips - 1, 2, rows // 2, columns), BF16) for rows, columns in shapes]
    return (
        boxes
        + inboxes
        + boxes
        + [pltpu.SemaphoreType.DMA((len(shapes), chips))] * 2
        + [pltpu.SemaphoreType.DMA((len(shapes), 2, chips - 1))] * 2
    )


def window(ref, number, size):
    if size % 128 == 0:
        return ref[:, pl.ds(pl.multiple_of(number * size, size), size)]
    parts = 128 // size
    tile = ref[:, pl.ds(pl.multiple_of(number // parts * 128, 128), 128)].astype(F32)
    return choose(
        number % parts, [tile[:, i * size : (i + 1) * size] for i in range(parts)]
    ).astype(ref.dtype)


def rows_by_owner(left, right, rows):
    def term(owner, half):
        return lax.dot_general(
            window(left.get(), owner * 2 + half, rows // 2),
            right.get()[...],
            (((0,), (0,)), ((), ())),
            preferred_element_type=F32,
        )

    return term


def columns_by_owner(left, right, columns):
    def term(owner, half):
        rows = left.shape[1] // 2
        return lax.dot_general(
            left.get()[:, half * rows : (half + 1) * rows],
            window(right.get(), owner, columns),
            (((0,), (0,)), ((), ())),
            preferred_element_type=F32,
        )

    return term


def ffn_sums_body(*refs):
    inv_ref, gain_ref = refs[:2]
    sources, (grad_ref, gains_ref, mixed_ref), targets = refs[2:12], refs[12:15], refs[15:19]
    loaded, stored, refs = refs[19:29], refs[29:33], refs[33:]
    load_sems, store_sems, refs = refs[0], refs[1], refs[2:]
    summing, mixing, spreading = refs[:7], refs[7:12], refs[12:]
    own, plane = lax.axis_index("tok"), lax.axis_index("tp")
    loads = load_all(sources, loaded, load_sems)
    part, normed, dgate, dup, inner, dm, hidden, dy, mixed_part, x = loads
    rows, *grads = store_all(targets, stored, store_sems)
    gathered = rows.ref
    share = normed.shape[1] // lax.axis_size("tok")
    greet([(own ^ 1, plane)] + [(own ^ (2 << i), plane) for i in range(stages_of("tok") - 1)], True)
    done = set()

    def leave():
        for half in range(HALVES):
            yield 80.0, ("rows", half)
        rows.send()

    run(
        *sum_flows(
            part,
            gathered,
            summing,
            ffn_math(hidden, inv_ref, dy, gain_ref, grad_ref, gains_ref, gathered),
            done=done,
            key=("rows",),
        ),
        *sum_flows(mixed_part, None, mixing, mixed_math(hidden, x, mixed_ref), 27.0, 11.0),
        spread_flow(
            [
                rows_by_owner(normed, dgate, share),
                rows_by_owner(normed, dup, share),
                columns_by_owner(inner, dm, share),
            ],
            grads,
            spreading,
            15.6,
        ),
        leave(),
        done=done,
    )
    rows.copy.wait()


def ffn_sums(
    part, hidden, inv, dy, gain, normed, dgate, dup, inner, dm, mixed_part, x, collective_id
):
    planes, width = part.shape[2], part.shape[4]
    devices = lax.axis_size("tok")
    share = width // devices
    wide = dgate.shape[1]
    shapes = [(share, wide), (share, wide), (wide, share)]
    rows = jax.ShapeDtypeStruct(part.shape, BF16)
    grads = [jax.ShapeDtypeStruct(shape, F32) for shape in shapes]
    sources = [part, normed, dgate, dup, inner, dm, hidden, dy, mixed_part, x]
    grad, gains, mixed, rows, gate, up, down = pl.pallas_call(
        ffn_sums_body,
        out_shape=[
            jax.ShapeDtypeStruct(hidden.shape, F32),
            jax.ShapeDtypeStruct((8, width), F32),
            jax.ShapeDtypeStruct(hidden.shape, BF16),
            rows,
        ]
        + grads,
        in_specs=[vmem()] * 2 + [anywhere()] * len(sources),
        out_specs=[vmem()] * 3 + [anywhere()] * 4,
        scratch_shapes=buffers(sources + [rows] + grads)
        + [pltpu.SemaphoreType.DMA((len(sources),)), pltpu.SemaphoreType.DMA((4,))]
        + sum_scratch(planes, width)
        + sum_scratch(planes, width, False)
        + spread_scratch(shapes, devices),
        compiler_params=params(collective_id),
        cost_estimate=cost(0, 80_000_000),
        name="ffn_sums",
    )(inv, gain, *sources)
    return rows, grad, gains, gate, up, down, mixed


def together():
    return stages_of("tok") <= 3


def attn_sums_body(lens_ref, flags_ref, *refs):
    both = together()
    mixed_ref, inv_ref, gain_ref, ffn_gains_ref = refs[:4]
    sources, home_ref, grad_home_ref, refs = refs[4:12], refs[12], refs[13], refs[14:]
    gathered, gains_ref, mixed_out = refs[:3]
    targets, refs = refs[3:5], refs[5:]
    loaded, stored, load_sems, store_sems, refs = refs[:8], refs[8:10], refs[10], refs[11], refs[12:]
    part, normed, dqkv, attended, da, x, dy, grad = load_all(sources, loaded, load_sems)
    weight_grads = store_all(targets, stored, store_sems)
    if both:
        grad_out, gathered = gathered, refs[0]
        gain_sums, gains_ref = gains_ref, refs[1]
        refs = refs[2:]
    summing, undealing, refs = refs[:7], refs[7 : 7 + deal_count()], refs[7 + deal_count() :]
    mixed_all, mixed_sems, home_sems = refs[0], refs[1:3], refs[3]
    gains_all, gains_sems, refs = refs[4], refs[5:7], refs[7:]
    planes = part.shape[2]
    plane = lax.axis_index("tp")
    share = normed.shape[1] // lax.axis_size("tok")
    home = pltpu.make_async_copy(home_ref, mixed_out, home_sems.at[0])
    home.start()
    if both:
        grad_home = pltpu.make_async_copy(grad_home_ref, grad_out, home_sems.at[1])
        grad_home.start()
        grad_undealing, refs = refs[: deal_count()], refs[deal_count() :]
        gaining, refs = refs[:3], refs[3:]
    greet(all_peers() if both else bit_peers(stages_of("tok")), True)
    for half in range(HALVES):
        mixed_all[:, half, plane] = mixed_ref[half]
    done = set()

    def sum_gains():
        yield (70.0, ("grad", HALVES - 1))
        total = gains_all[0]
        for index in range(1, planes):
            total = total + gains_all[index]
        gains_ref[...] = total
        done.add(("gains",))

    flows = [
        *gather_flows(mixed_all, mixed_sems, 0.0, 8.7, done, ("mixed",)),
        *sum_flows(
            part,
            gathered,
            summing,
            attn_math(x, inv_ref, dy, grad, gain_ref, ffn_gains_ref, gains_all, gathered),
            9.0,
            10.0,
            (lambda index: gains_all.at[index],) + gains_sems,
            done,
            ("grad",),
        ),
        spread_flow(
            [
                rows_by_owner(normed, dqkv, share),
                columns_by_owner(attended, da, share),
            ],
            weight_grads,
            refs,
            9.0,
        ),
        undeal_flow(
            lens_ref, flags_ref, mixed_all, mixed_out, home, undealing, 28.0, 4.5, ("mixed",), 6.0
        ),
        sum_gains(),
    ]
    if both:
        flows += [
            undeal_flow(
                lens_ref, flags_ref, gathered, grad_out, grad_home, grad_undealing,
                55.0, 4.5, ("grad",), 8.0,
            ),
            gain_flow(gains_ref, gain_sums, gaining, 72.0, ("gains",)),
        ]
    run(*flows, done=done)


def attn_sums(
    doc_lengths, keep_flags, part, mixed, x, inv, dy, grad, gain, ffn_gains, normed, dqkv, attended,
    da, home, grad_home, collective_id,
):
    planes, width = part.shape[2], part.shape[4]
    devices = lax.axis_size("tok")
    share = width // devices
    shapes = [(share, dqkv.shape[1]), (attended.shape[1], share)]
    both = together()
    rows_shape = jax.ShapeDtypeStruct(part.shape, BF16)
    gains_shape = jax.ShapeDtypeStruct((8, width), F32)
    blocks_shape = jax.ShapeDtypeStruct(home.shape, BF16)
    gain_part = gain_share(width, devices)
    first = (
        [blocks_shape, jax.ShapeDtypeStruct((8, gain_part), F32)] if both else [rows_shape, gains_shape]
    )
    dealing = deal_scratch(stages_of("tok"), width, BF16)
    sources = [part, normed, dqkv, attended, da, x, dy, grad]
    weight_grads = [jax.ShapeDtypeStruct(shape, F32) for shape in shapes]
    grads, gains, mixed_blocks, qkv, out = pl.pallas_call(
        attn_sums_body,
        out_shape=first
        + [blocks_shape]
        + weight_grads,
        in_specs=[smem(), smem()] + [vmem()] * 4 + [anywhere()] * 10,
        out_specs=[vmem()] * 3 + [anywhere()] * 2,
        scratch_shapes=buffers(sources + weight_grads)
        + [pltpu.SemaphoreType.DMA((8,)), pltpu.SemaphoreType.DMA((2,))]
        + (
            [pltpu.VMEM(part.shape, BF16), pltpu.VMEM((8, width), F32)] if both else []
        )
        + sum_scratch(planes, width)
        + dealing
        + [pltpu.VMEM(part.shape, BF16)]
        + [pltpu.SemaphoreType.DMA((HALVES, 2, planes))] * 2
        + [pltpu.SemaphoreType.DMA((2,)), pltpu.VMEM((planes, 8, width), F32)]
        + line_sems(planes)
        + (dealing + gain_scratch(devices, gain_part) if both else [])
        + spread_scratch(shapes, devices),
        compiler_params=params(collective_id),
        cost_estimate=cost(0, 80_000_000),
        name="attn_sums",
    )(
        doc_lengths, keep_flags, mixed, inv, gain, ffn_gains, *sources, home, grad_home
    )
    if not both:
        grads, gains = undeal(doc_lengths, keep_flags, grads, grad_home, gains, collective_id + 1)
    return mixed_blocks, grads, gains, qkv, out


def rotary_tables(doc_lengths, keep_flags, ranks):
    blocks = keep_flags * (doc_lengths // BLOCK)
    ends = jnp.cumsum(blocks, dtype=jnp.int32)
    starts = ends - blocks
    inside = (ranks[:, None] >= starts[None, :]) & (ranks[:, None] < ends[None, :])
    first = jnp.sum(jnp.where(inside, starts[None, :], 0), axis=1, dtype=jnp.int32)
    offsets = jnp.arange(BLOCK, dtype=jnp.int32)
    positions = (((ranks - first) * BLOCK)[:, None] + offsets[None, :]).reshape(-1)
    half_dim = HD // 2
    freqs = jnp.exp(jnp.arange(half_dim, dtype=jnp.float32) * (-2.0 * math.log(10000.0) / HD))
    angles = positions.astype(jnp.float32)[:, None] * freqs[None, :]
    cosine, sine = jnp.cos(angles), jnp.sin(angles)
    return jnp.concatenate([cosine, cosine], axis=1), jnp.concatenate([sine, -sine], axis=1)


def over_columns(left, right):
    return lax.dot_general(
        left, right, (((1,), (1,)), ((), ())), preferred_element_type=jnp.float32
    )


def on_device(
    tokens,
    gain_attn,
    w_query,
    w_key,
    w_value,
    w_out,
    gain_ffn,
    w_gate,
    w_up,
    w_down,
    cotangent,
    doc_lengths,
    keep_flags,
):
    length = tokens.shape[0]
    model_width = tokens.shape[1]
    devices = lax.axis_size("tok")
    planes = lax.axis_size("tp")
    own_index = lax.axis_index("tok")
    blocks_here = length // BLOCK
    kept_here = blocks_here // 2
    rows = kept_here * BLOCK
    token_blocks = tokens.reshape(blocks_here, BLOCK, model_width)
    grad_blocks = cotangent.reshape(blocks_here, BLOCK, model_width)

    own_ranks = own_index + jnp.arange(kept_here, dtype=jnp.int32) * devices
    cosine, sine = rotary_tables(doc_lengths, keep_flags, own_ranks)
    own = jnp.reshape(own_index, (1,)).astype(jnp.int32)
    rows_x, normed_one, inv_one, queries, kv_all = deal_project(
        doc_lengths,
        keep_flags,
        gain_attn.reshape(1, -1),
        cosine,
        sine,
        token_blocks,
        w_query,
        w_key,
        w_value,
        0,
    )
    rows_x = rows_x.reshape(rows, model_width)
    attended, attended_wide, log_totals, part_out = attend(
        doc_lengths, keep_flags, own, queries, kv_all, w_out
    )

    def by_plane(array):
        return array.reshape(kept_here, HALVES, planes, TILE, array.shape[1])

    x_planes = by_plane(rows_x)
    rows_dy, normed_two, hidden_res, inv_two = deal_sum(
        doc_lengths,
        keep_flags,
        grad_blocks,
        by_plane(part_out),
        x_planes,
        gain_ffn.reshape(1, -1),
        1,
    )
    rows_dy = rows_dy.reshape(rows, model_width)
    normed_two = normed_two.reshape(rows, model_width)
    gate = jnp.dot(normed_two, w_gate, preferred_element_type=jnp.float32)
    upper = jnp.dot(normed_two, w_up, preferred_element_type=jnp.float32)
    sigma = jax.nn.sigmoid(gate)
    swish = gate * sigma
    inner = (swish * upper).astype(jnp.bfloat16)

    grad_m = (keep_scale * rows_dy.astype(jnp.float32)).astype(jnp.bfloat16)
    grad_inner = over_columns(grad_m, w_down)
    grad_gate_pre = (grad_inner * upper * sigma * (1.0 + gate * (1.0 - sigma))).astype(jnp.bfloat16)
    grad_up_pre = (grad_inner * swish).astype(jnp.bfloat16)
    part_two = (
        over_columns(grad_gate_pre, w_gate) + over_columns(grad_up_pre, w_up)
    ).astype(jnp.bfloat16)

    dy_planes = by_plane(rows_dy)
    grad_a, grad_hidden, gains_ffn, grad_gate, grad_up, grad_down, mixed_rows = ffn_sums(
        by_plane(part_two),
        hidden_res,
        inv_two,
        dy_planes,
        gain_ffn.reshape(1, -1),
        normed_two,
        grad_gate_pre,
        grad_up_pre,
        inner,
        grad_m,
        by_plane(jnp.dot(inner, w_down, preferred_element_type=jnp.float32).astype(jnp.bfloat16)),
        x_planes,
        4,
    )
    grad_a = grad_a.reshape(rows, model_width)

    grad_query_pre, grad_kv, grad_gate, grad_up, grad_down = attend_back(
        doc_lengths,
        keep_flags,
        own,
        queries,
        grad_a,
        w_out,
        kv_all,
        attended_wide,
        log_totals,
        cosine,
        sine,
        [grad_gate, grad_up, grad_down],
    )
    grad_qkv_pre, part_one = scatter_back(
        grad_kv, grad_query_pre, cosine, sine, w_query, w_key, w_value, 5
    )
    mixed, token_grad, gain_sums, grad_qkv, grad_out = attn_sums(
        doc_lengths,
        keep_flags,
        by_plane(part_one),
        mixed_rows,
        x_planes,
        by_plane(inv_one),
        dy_planes,
        grad_hidden,
        gain_attn.reshape(1, -1),
        gains_ffn,
        normed_one,
        grad_qkv_pre,
        attended,
        grad_a,
        token_blocks,
        grad_blocks,
        6,
    )
    own_share = model_width // devices
    if gain_sums.shape[1] != own_share:
        gain_sums = lax.dynamic_slice_in_dim(gain_sums, own_index * own_share, own_share, 1)
    mixed, token_grad, grad_query, grad_key, grad_value, grad_out = finish(
        mixed, token_grad, grad_qkv, grad_out, w_key.shape[1]
    )

    return (
        mixed.reshape(length, model_width),
        token_grad.reshape(length, model_width),
        gain_sums[1],
        grad_query,
        grad_key,
        grad_value,
        grad_out,
        gain_sums[0],
        grad_gate,
        grad_up,
        grad_down,
    )


def solution(mesh):
    placed = (
        P("tok", None),
        P(),
        P(None, "tp"),
        P(None, "tp"),
        P(None, "tp"),
        P("tp", None),
        P(),
        P(None, "tp"),
        P(None, "tp"),
        P("tp", None),
        P("tok", None),
        P(),
        P(),
    )
    return jax.shard_map(
        on_device,
        mesh=mesh,
        in_specs=placed,
        out_specs=(
            P("tok", None),
            P("tok", None),
            P("tok"),
            P("tok", "tp"),
            P("tok", "tp"),
            P("tok", "tp"),
            P("tp", "tok"),
            P("tok"),
            P("tok", "tp"),
            P("tok", "tp"),
            P("tp", "tok"),
        ),
        check_vma=False,
    )
```

```python
import functools
import math

import jax
import jax.numpy as jnp
from jax import lax
from jax.experimental import pallas as pl
from jax.experimental.pallas import tpu as pltpu
from jax.sharding import PartitionSpec as P

HD = 128
BLOCK = 128
SLOTS = 3
CHUNKS = 8
HALVES = 2
TILE = 16
HOP = 2.0
MESH = pl.DeviceIdType.MESH
VMEM_BYTES = 60 * 2**20

norm_eps = 1e-05
keep_scale = 2.0
F32 = jnp.float32
BF16 = jnp.bfloat16


def vmem():
    return pl.BlockSpec(memory_space=pltpu.VMEM)


def smem():
    return pl.BlockSpec(memory_space=pltpu.SMEM)


def params(collective_id):
    return pltpu.CompilerParams(
        collective_id=collective_id, has_side_effects=True, vmem_limit_bytes=VMEM_BYTES
    )


def cost(flops, moved):
    return pl.CostEstimate(flops=flops, bytes_accessed=moved, transcendentals=0)


def greet(peers, line=False):
    barrier = pltpu.get_barrier_semaphore()
    for peer in peers:
        pl.semaphore_signal(barrier, inc=1, device_id=peer, device_id_type=MESH)
    if not line:
        pl.semaphore_wait(barrier, len(peers))
        return
    own, plane = lax.axis_index("tok"), lax.axis_index("tp")
    last = lax.axis_size("tp") - 1

    @pl.when(plane > 0)
    def _():
        pl.semaphore_signal(barrier, inc=1, device_id=(own, plane - 1), device_id_type=MESH)

    @pl.when(plane < last)
    def _():
        pl.semaphore_signal(barrier, inc=1, device_id=(own, plane + 1), device_id_type=MESH)

    end = (plane == 0) | (plane == last)

    @pl.when(end)
    def _():
        pl.semaphore_wait(barrier, len(peers) + 1)

    @pl.when(jnp.logical_not(end))
    def _():
        pl.semaphore_wait(barrier, len(peers) + 2)


def run(*flows, done=frozenset()):
    waiting = [[next(flow), number, flow] for number, flow in enumerate(flows)]

    def order(entry):
        step = entry[0] if isinstance(entry[0], tuple) else (entry[0], None)
        return (step[1] is not None and step[1] not in done, step[0], entry[1])

    while waiting:
        waiting.sort(key=order)
        entry = waiting[0]
        assert not order(entry)[0]
        try:
            entry[0] = next(entry[2])
        except StopIteration:
            waiting.pop(0)


def anywhere():
    return pl.BlockSpec(memory_space=pl.ANY)


class Loaded:
    def __init__(self, source, target, sem):
        self.copy = pltpu.make_async_copy(source, target, sem)
        self.target = target
        self.here = False
        self.shape = target.shape

    def get(self):
        if not self.here:
            self.copy.wait()
            self.here = True
        return self.target


def load_all(sources, targets, sems):
    loads = [Loaded(*pair, sems.at[i]) for i, pair in enumerate(zip(sources, targets))]
    for load in loads:
        load.copy.start()
    return loads


class Stored:
    def __init__(self, target, source, sem):
        self.copy = pltpu.make_async_copy(source, target, sem)
        self.ref = source

    def send(self):
        self.copy.start()


def store_all(targets, sources, sems):
    return [Stored(*pair, sems.at[i]) for i, pair in enumerate(zip(targets, sources))]


def buffers(arrays):
    return [pltpu.VMEM(array.shape, array.dtype) for array in arrays]


def deal_tables(own, stages, blocks_here, lens_ref, flags_ref):
    def kept_before(place):
        total, start = jnp.int32(0), jnp.int32(0)
        for doc in range(lens_ref.shape[0]):
            blocks = lens_ref[doc] // BLOCK
            total = total + flags_ref[doc] * jnp.clip(place - start, 0, blocks)
            start = start + blocks
        return total

    def edges(stage):
        first = (own >> stage) << stage
        return (
            kept_before(first * blocks_here),
            kept_before((first + (1 << stage)) * blocks_here),
        )

    def located(stage):
        if stage == 0:
            ends = [kept_before(own * blocks_here + i + 1) for i in range(blocks_here)]

            def place(rank):
                index = jnp.int32(0)
                for end in ends:
                    index = index + (end <= rank).astype(jnp.int32)
                return index

            return place
        mine = (own >> (stage - 1)) << (stage - 1)
        low, high = edges(stage - 1)
        other = kept_before((mine ^ (1 << (stage - 1))) * blocks_here)

        def place(rank):
            inside = (rank >= low) & (rank < high)
            return jnp.where(inside, (rank - low) >> stage, SLOTS + ((rank - other) >> stage))

        return place

    keeps, sends = [], []
    for stage in range(stages):
        low, high = edges(stage)
        place = located(stage)
        period = 1 << (stage + 1)
        for table, target in ((keeps, own), (sends, own ^ (1 << stage))):
            first = low + ((target - low) & (period - 1))
            row = []
            for slot in range(SLOTS):
                rank = first + period * slot
                row.append(jnp.where(rank < high, place(rank), -1))
            table.append(row)
    place = located(stages)
    finals = [place(own + (slot << stages)) for slot in range(SLOTS)]
    return keeps, sends, finals


def choose(index, options):
    value = options[0]
    for number, option in enumerate(options[1:]):
        value = jnp.where(index == number + 1, option, value)
    return value


def slot_of(keep, recv, chunk, index):
    stayed = keep[chunk, jnp.clip(index, 0, SLOTS - 1)]
    arrived = recv[jnp.clip(index - SLOTS, 0, SLOTS - 1)]
    return jnp.where(index < SLOTS, stayed, arrived)


def deal_refs(scratch):
    keep, send = scratch[:2]
    stages = send.shape[0]
    recv = [scratch[2 + i * CHUNKS : 2 + (i + 1) * CHUNKS] for i in range(stages)]
    return keep, send, recv, *scratch[2 + stages * CHUNKS : 4 + stages * CHUNKS]


def bit_peers(stages):
    own, plane = lax.axis_index("tok"), lax.axis_index("tp")
    return [(own ^ (1 << stage), plane) for stage in range(stages)]


def deal_flow(lens_ref, flags_ref, blocks, finish, scratch, pace=4.3, urgent=False):
    keep, send, recv, send_sem, recv_sem = deal_refs(scratch)
    stages = send.shape[0]
    own = lax.axis_index("tok")
    blocks_here = blocks.shape[0]
    rows = BLOCK // CHUNKS
    peers = bit_peers(stages)
    keeps, sends, finals = deal_tables(own, stages, blocks_here, lens_ref, flags_ref)

    def copy(stage, chunk):
        return pltpu.make_async_remote_copy(
            src_ref=send.at[stage, chunk],
            dst_ref=recv[stage][chunk],
            send_sem=send_sem.at[stage, chunk],
            recv_sem=recv_sem.at[stage, chunk],
            device_id=peers[stage],
            device_id_type=MESH,
        )

    def held(stage, chunk, index):
        if stage == 0:
            block = jnp.clip(index, 0, blocks_here - 1)
            return blocks.get()[block, pl.ds(chunk * rows, rows), :]
        return slot_of(keep, recv[stage - 1][chunk], chunk, index)

    for stage in range(stages + 1):
        for chunk in range(CHUNKS):
            if stage < 2:
                yield 1.5 * stage + 0.3 * chunk
            else:
                slack = 4.0 if stage == stages and not urgent else 0.0
                yield 1.5 + HOP * (stage - 1) + pace * (chunk + stage - 1) + slack
            if stage > 0:
                copy(stage - 1, chunk).wait_recv()
            if stage == stages:
                finish(chunk, [held(stage, chunk, finals[slot]) for slot in range(SLOTS)])
            else:
                for slot in range(SLOTS):
                    send[stage, chunk, slot] = held(stage, chunk, sends[stage][slot])
                copy(stage, chunk).start()
                stay = [held(stage, chunk, keeps[stage][slot]) for slot in range(SLOTS)]
                for slot in range(SLOTS):
                    keep[chunk, slot] = stay[slot]
    yield 1e6

    for stage in range(stages):
        for chunk in range(CHUNKS):
            copy(stage, chunk).wait_send()


def deal_scratch(stages, width, kind):
    part = (SLOTS, BLOCK // CHUNKS, width)
    return (
        [pltpu.VMEM((CHUNKS,) + part, kind), pltpu.VMEM((stages, CHUNKS) + part, kind)]
        + [pltpu.VMEM(part, kind)] * (stages * CHUNKS)
        + [pltpu.SemaphoreType.DMA((stages, CHUNKS))] * 2
    )


def deal_count():
    return 4 + stages_of("tok") * CHUNKS


def stages_of(axis):
    return int(math.log2(lax.axis_size(axis)))


def undeal_flow(
    lens_ref, flags_ref, kept_ref, out_ref, home, scratch, start=0.0, pace=4.3, key=None, lag=0.0
):
    keep, send, recv, send_sem, recv_sem = deal_refs(scratch)
    stages = send.shape[0]
    own = lax.axis_index("tok")
    blocks_here = out_ref.shape[0]
    planes = kept_ref.shape[2]
    rows = BLOCK // CHUNKS
    peers = bit_peers(stages)
    keeps, sends, finals = deal_tables(own, stages, blocks_here, lens_ref, flags_ref)

    def copy(stage, chunk):
        return pltpu.make_async_remote_copy(
            src_ref=send.at[stage, chunk],
            dst_ref=recv[stage][chunk],
            send_sem=send_sem.at[stage, chunk],
            recv_sem=recv_sem.at[stage, chunk],
            device_id=peers[stage],
            device_id_type=MESH,
        )

    def source(places, place):
        index = jnp.int32(-1)
        for number, other in enumerate(places):
            index = jnp.where(other == place, number, index)
        return index

    last = stages - 1
    for stage in range(last, -2, -1):
        count = 2 * SLOTS if stage >= 0 else blocks_here
        places = finals if stage == last else keeps[stage + 1] + sends[stage + 1]
        sources = [source(places, place) for place in range(count)]
        for chunk in range(CHUNKS):
            half = chunk // planes
            begin = start + lag * half
            if stage == last:
                yield (begin, None if key is None else key + (half,))
                options = [kept_ref[slot, half, chunk % planes] for slot in range(SLOTS)]
            else:
                hops = last - stage
                slack = 20.0 if stage < 0 else 0.0
                yield begin + HOP * hops + pace * (chunk + hops - (stage < 0)) + slack
                copy(stage + 1, chunk).wait_recv()

            def block(place):
                if stage == last:
                    return choose(sources[place], options)
                return slot_of(keep, recv[stage + 1][chunk], chunk, sources[place])

            if stage < 0:
                if chunk == 0:
                    home.wait()
                span = pl.ds(chunk * rows, rows)
                for place in range(blocks_here):
                    value = out_ref[place, span, :]
                    out_ref[place, span, :] = jnp.where(sources[place] >= 0, block(place), value)
            else:
                for slot in range(SLOTS):
                    send[stage, chunk, slot] = block(SLOTS + slot)
                copy(stage, chunk).start()
                stay = [block(slot) for slot in range(SLOTS)]
                for slot in range(SLOTS):
                    keep[chunk, slot] = stay[slot]
    yield 1e6

    for stage in range(stages):
        for chunk in range(CHUNKS):
            copy(stage, chunk).wait_send()


def gain_flow(gains_ref, sum_ref, scratch, start, key=None):
    gain_recv, gain_send_sem, gain_recv_sem = scratch
    own, plane = lax.axis_index("tok"), lax.axis_index("tp")
    devices = gain_recv.shape[0]
    share = sum_ref.shape[1]

    def portion(there):
        if share < gains_ref.shape[1]:
            return gains_ref.at[:, pl.ds(pl.multiple_of(there * share, share), share)]
        return gains_ref

    def copy(step):
        return pltpu.make_async_remote_copy(
            src_ref=portion(own ^ step),
            dst_ref=gain_recv.at[step],
            send_sem=gain_send_sem.at[step],
            recv_sem=gain_recv_sem.at[step],
            device_id=(own ^ step, plane),
            device_id_type=MESH,
        )

    yield (start, key)
    for step in range(1, devices):
        copy(step).start()
    yield 2e5
    total = portion(own)[...]
    for step in range(1, devices):
        copy(step).wait()
        total = total + gain_recv[step]
    sum_ref[...] = total


def gain_share(width, devices):
    share = width // devices
    return share if share % 128 == 0 else width


def gain_scratch(devices, share):
    return [pltpu.VMEM((devices, 8, share), F32)] + [pltpu.SemaphoreType.DMA((devices,))] * 2


def all_peers():
    own, plane = lax.axis_index("tok"), lax.axis_index("tp")
    return [(own ^ step, plane) for step in range(1, lax.axis_size("tok"))]


def undeal_body(lens_ref, flags_ref, kept_ref, home_ref, gains_ref, out_ref, sum_ref, home_sem, *scratch):
    home = pltpu.make_async_copy(home_ref, out_ref, home_sem)
    home.start()
    greet(all_peers())
    run(
        undeal_flow(lens_ref, flags_ref, kept_ref, out_ref, home, scratch[: deal_count()]),
        gain_flow(gains_ref, sum_ref, scratch[deal_count() :], 0.0),
    )


def undeal(doc_lengths, keep_flags, kept, home, gains, collective_id):
    stages = stages_of("tok")
    devices = 1 << stages
    width = kept.shape[-1]
    share = gain_share(width, devices)
    return pl.pallas_call(
        undeal_body,
        out_shape=(
            jax.ShapeDtypeStruct(home.shape, home.dtype),
            jax.ShapeDtypeStruct((8, share), F32),
        ),
        in_specs=[smem(), smem(), vmem(), pl.BlockSpec(memory_space=pl.ANY), vmem()],
        out_specs=(vmem(), vmem()),
        scratch_shapes=[pltpu.SemaphoreType.DMA]
        + deal_scratch(stages, width, kept.dtype)
        + gain_scratch(devices, share),
        compiler_params=params(collective_id),
        cost_estimate=cost(0, 40_000_000),
        name="undeal",
    )(doc_lengths, keep_flags, kept, home, gains)


def deal_project_body(
    lens_ref, flags_ref, gain_ref, cos_ref, sin_ref, own_hbm, w_query_hbm, w_key_hbm, w_value_hbm,
    x_hbm, normed_hbm, inv_ref, query_ref, out_ref,
    own_half, w_query, w_key, w_value, x_ref, normed_ref, mine_ref, pair_send, pair_recv,
    load_sems, store_sems, pair_send_sem, pair_recv_sem,
    send_sem, recv_sem, relay_send_sem, relay_recv_sem, *dealing,
):
    devices = out_ref.shape[0]
    chips = devices // 2
    own = lax.axis_index("tok")
    plane = lax.axis_index("tp")
    partner = (own ^ 1, plane)
    width = own_half.shape[2]
    tile = BLOCK // CHUNKS
    thin = w_key.shape[1]
    columns = pl.ds(pl.multiple_of((plane % 2) * width, width), width)
    blocks, w_query, w_key, w_value = load_all(
        [own_hbm.at[:, :, columns], w_query_hbm, w_key_hbm, w_value_hbm],
        [own_half, w_query, w_key, w_value],
        load_sems,
    )
    steps = sorted({1 << i for i in range(stages_of("tok"))} | {2 * i for i in range(1, chips)})
    greet([(own ^ step, plane) for step in steps] + [(own, plane ^ 1)])

    def pair_copy(chunk):
        return pltpu.make_async_remote_copy(
            src_ref=pair_send.at[chunk],
            dst_ref=pair_recv.at[chunk],
            send_sem=pair_send_sem.at[chunk],
            recv_sem=pair_recv_sem.at[chunk],
            device_id=(own, plane ^ 1),
            device_id_type=MESH,
        )

    def finish(chunk, values):
        for slot, value in enumerate(values):
            pair_send[chunk, slot] = value
        pair_copy(chunk).start()
        for slot, value in enumerate(values):
            x_ref[slot, pl.ds(chunk * tile, tile), columns] = value

    def norms():
        for chunk in range(CHUNKS):
            yield 500.0 + chunk, (chunk,)
            other = pl.ds(pl.multiple_of((1 - plane % 2) * width, width), width)
            pair_copy(chunk).wait_recv()
            span = pl.ds(chunk * tile, tile)
            for slot in range(SLOTS):
                x_ref[slot, span, other] = pair_recv[chunk, slot]
            for slot in range(SLOTS):
                x = x_ref[slot, span, :].astype(F32)
                inv = lax.rsqrt(jnp.mean(x * x, axis=1, keepdims=True) + norm_eps)
                rows = pl.ds(slot * BLOCK + chunk * tile, tile)
                inv_ref[rows, :] = inv
                normed_ref[rows, :] = (x * inv * gain_ref[...]).astype(BF16)

    done = set()

    def mark(chunk, values):
        finish(chunk, values)
        done.add((chunk,))

    run(
        deal_flow(lens_ref, flags_ref, blocks, mark, dealing, 2.8, True),
        norms(),
        done=done,
    )
    stores = store_all([x_hbm, normed_hbm], [x_ref, normed_ref], store_sems)
    for store in stores:
        store.send()
    for chunk in range(CHUNKS):
        pair_copy(chunk).wait_send()

    def copy(step):
        return pltpu.make_async_remote_copy(
            src_ref=mine_ref,
            dst_ref=out_ref.at[own],
            send_sem=send_sem.at[step],
            recv_sem=recv_sem.at[step],
            device_id=(own ^ (2 * step), plane),
            device_id_type=MESH,
        )

    def relay(step):
        return pltpu.make_async_remote_copy(
            src_ref=mine_ref if step == 0 else out_ref.at[own ^ (2 * step)],
            dst_ref=out_ref.at[own ^ (2 * step)],
            send_sem=relay_send_sem.at[step],
            recv_sem=relay_recv_sem.at[step],
            device_id=partner,
            device_id_type=MESH,
        )

    def product(weight):
        return lax.dot_general(
            normed_ref[...], weight.get()[...], (((1,), (0,)), ((), ())), preferred_element_type=F32
        )

    keys = product(w_key)
    for group in range(thin // HD):
        one = keys[:, group * HD : (group + 1) * HD]
        mine_ref[:, group * HD : (group + 1) * HD] = turn(one, cos_ref, sin_ref, -1.0).astype(BF16)
    mine_ref[:, thin:] = product(w_value).astype(BF16)
    for step in range(1, chips):
        copy(step).start()
    relay(0).start()
    out_ref[own] = mine_ref[...]
    queries = product(w_query)
    for head in range(w_query.shape[1] // HD):
        one = queries[:, head * HD : (head + 1) * HD]
        query_ref[:, head * HD : (head + 1) * HD] = turn(one, cos_ref, sin_ref, -1.0).astype(BF16)
    for step in range(1, chips):
        copy(step).wait_recv()
        relay(step).start()
    for step in range(chips):
        relay(step).wait()
    for step in range(1, chips):
        copy(step).wait_send()
    for store in stores:
        store.copy.wait()


def turn(values, cos_ref, sin_ref, sign):
    return values * cos_ref[...] + pltpu.roll(values, HD // 2, 1) * (sin_ref[...] * sign)


def deal_project(
    doc_lengths, keep_flags, gain, cosine, sine, blocks, w_query, w_key, w_value, collective_id
):
    devices = lax.axis_size("tok")
    chips = devices // 2
    width = blocks.shape[2]
    rows = SLOTS * BLOCK
    both = w_key.shape[1] + w_value.shape[1]
    x_shape, normed_shape = (SLOTS, BLOCK, width), (rows, width)
    weights = [w_query, w_key, w_value]
    return pl.pallas_call(
        deal_project_body,
        out_shape=(
            jax.ShapeDtypeStruct(x_shape, BF16),
            jax.ShapeDtypeStruct(normed_shape, BF16),
            jax.ShapeDtypeStruct((rows, 1), F32),
            jax.ShapeDtypeStruct((rows, w_query.shape[1]), BF16),
            jax.ShapeDtypeStruct((devices, rows, both), BF16),
        ),
        in_specs=[smem()] * 2 + [vmem()] * 3 + [anywhere()] * 4,
        out_specs=(anywhere(),) * 2 + (vmem(),) * 3,
        scratch_shapes=[pltpu.VMEM(blocks.shape[:2] + (width // 2,), BF16)]
        + buffers(weights)
        + [
            pltpu.VMEM(x_shape, BF16),
            pltpu.VMEM(normed_shape, BF16),
            pltpu.VMEM((rows, both), BF16),
            pltpu.VMEM((CHUNKS, SLOTS, BLOCK // CHUNKS, width // 2), BF16),
            pltpu.VMEM((CHUNKS, SLOTS, BLOCK // CHUNKS, width // 2), BF16),
            pltpu.SemaphoreType.DMA((4,)),
            pltpu.SemaphoreType.DMA((2,)),
        ]
        + [pltpu.SemaphoreType.DMA((CHUNKS,))] * 2
        + [pltpu.SemaphoreType.DMA((chips,))] * 4
        + deal_scratch(stages_of("tok"), width // 2, BF16),
        compiler_params=params(collective_id),
        cost_estimate=cost(0, 60_000_000),
        name="deal_project",
    )(doc_lengths, keep_flags, gain, cosine, sine, blocks, *weights)


def first_rank(lens_ref, flags_ref, rank):
    first, start = jnp.int32(0), jnp.int32(0)
    for doc in range(lens_ref.shape[0]):
        blocks = flags_ref[doc] * (lens_ref[doc] // BLOCK)
        first = jnp.where((rank >= start) & (rank < start + blocks), start, first)
        start = start + blocks
    return first


def stack_heads(ref, slot):
    heads = ref.shape[1] // HD
    return jnp.concatenate(
        [ref[slot * BLOCK : (slot + 1) * BLOCK, i * HD : (i + 1) * HD] for i in range(heads)], axis=0
    )


def dot(left, right, dims):
    return lax.dot_general(left, right, ((dims[:1], dims[1:]), ((), ())), preferred_element_type=F32)


def key_pair(kv_ref, rank):
    devices = kv_ref.shape[0]
    both = []
    for one in (jnp.maximum(rank - 1, 0), rank):
        device, slot = lax.rem(one, devices), lax.div(one, devices)
        both.append((device, pl.ds(pl.multiple_of(slot * BLOCK, BLOCK), BLOCK)))
    return both


def read_pair(kv_ref, pair, columns):
    return jnp.concatenate([kv_ref[device, span, columns] for device, span in pair], axis=0)


KEYS, VALUES = slice(0, HD), slice(HD, 2 * HD)


def bounded(scores, alone, diagonal):
    keys = lax.broadcasted_iota(jnp.int32, scores.shape, 0)
    allowed = keys >= jnp.where(alone, BLOCK, 0)
    if diagonal:
        queries = lax.rem(lax.broadcasted_iota(jnp.int32, scores.shape, 1), BLOCK)
        allowed = allowed & (keys <= queries + BLOCK)
    return jnp.where(allowed, scores, -1e30)


def attend_body(
    lens_ref, flags_ref, own_ref, query_ref, kv_ref, w_out_hbm,
    out_ref, wide_ref, log_ref, part_ref, total, w_out, load_sems,
):
    (w_out,) = load_all([w_out_hbm], [w_out], load_sems)
    devices = kv_ref.shape[0]
    scale = 1.0 / math.sqrt(HD)
    for slot in range(SLOTS):
        rank = own_ref[0] + devices * slot
        query = stack_heads(query_ref, slot)
        count = query.shape[0]
        total[...] = jnp.zeros_like(total)

        first = first_rank(lens_ref, flags_ref, rank)

        def visit(key_rank, state, diagonal):
            peak, weight = state
            pair = key_pair(kv_ref, key_rank)
            scores = dot(read_pair(kv_ref, pair, KEYS), query, (1, 1)) * scale
            scores = bounded(scores, key_rank == first, diagonal)
            higher = jnp.maximum(peak, jnp.max(scores, axis=0, keepdims=True))
            shrink = jnp.exp(peak - higher)
            probs = jnp.exp(scores - higher)
            weight = weight * shrink + jnp.sum(probs, axis=0, keepdims=True)
            values = read_pair(kv_ref, pair, VALUES)
            total[...] = total[...] * shrink + dot(values, probs.astype(BF16), (0, 0))
            return higher, weight

        start = (jnp.full((1, count), -1e30, F32), jnp.zeros((1, count), F32))
        state = visit(rank, start, True)
        peak, weight = lax.fori_loop(
            1, lax.div(rank - first, 2) + 1, lambda i, s: visit(rank - 2 * i, s, False), state
        )
        result = total[...] / weight
        wide_ref[slot] = result
        log_ref[slot] = jnp.broadcast_to(peak + jnp.log(weight), log_ref.shape[1:])
        turned = result.T.astype(BF16)
        heads = [turned[head * BLOCK : (head + 1) * BLOCK] for head in range(count // BLOCK)]
        weights = w_out.get()
        part_ref[slot * BLOCK : (slot + 1) * BLOCK, :] = dot(
            jnp.concatenate(heads, axis=1), weights[...], (1, 0)
        ).astype(BF16)
        for head in range(count // BLOCK):
            out_ref[slot * BLOCK : (slot + 1) * BLOCK, head * HD : (head + 1) * HD] = turned[
                head * BLOCK : (head + 1) * BLOCK
            ]


def attend(doc_lengths, keep_flags, own, query, kv, w_out):
    count = query.shape[1] // HD * BLOCK
    return pl.pallas_call(
        attend_body,
        out_shape=(
            jax.ShapeDtypeStruct(query.shape, BF16),
            jax.ShapeDtypeStruct((SLOTS, HD, count), F32),
            jax.ShapeDtypeStruct((SLOTS, 8, count), F32),
            jax.ShapeDtypeStruct((query.shape[0], w_out.shape[1]), BF16),
        ),
        in_specs=[smem()] * 3 + [vmem()] * 2 + [anywhere()],
        out_specs=(vmem(),) * 4,
        scratch_shapes=[pltpu.VMEM((HD, count), F32)]
        + buffers([w_out])
        + [pltpu.SemaphoreType.DMA((1,))],
        compiler_params=pltpu.CompilerParams(vmem_limit_bytes=VMEM_BYTES),
        cost_estimate=cost(1_000_000_000, 10_000_000),
        name="attend",
    )(doc_lengths, keep_flags, own, query, kv, w_out)


class Passed:
    def __init__(self, source, passing, targets, sems):
        self.first = pltpu.make_async_copy(source, passing, sems.at[0])
        self.rest = [pltpu.make_async_copy(part, to, sems.at[1]) for part, to in targets(passing)]
        self.first.start()

    def turn(self):
        self.first.wait()
        for copy in self.rest:
            copy.start()

    def end(self):
        for copy in self.rest:
            copy.wait()


def attend_back_body(
    lens_ref, flags_ref, own_ref, query_ref, rows_ref, w_out_ref, kv_ref, wide_ref, log_ref, cos_ref, sin_ref,
    *refs,
):
    sources, grad_query_ref, grad_kv_ref, targets, grad_kv, total = (
        refs[:3], refs[3], refs[4], refs[5:8], refs[8], refs[9],
    )
    passing, sems = refs[10:13], refs[13]
    passes = [
        Passed(sources[i], passing[i], lambda ref, i=i: [(ref, targets[i])], sems.at[i])
        for i in range(3)
    ]
    devices = kv_ref.shape[0]
    scale = 1.0 / math.sqrt(HD)
    grad_kv[...] = jnp.zeros_like(grad_kv)
    for slot in range(SLOTS):
        if slot == 1:
            for one in passes:
                one.turn()
        rank = own_ref[0] + devices * slot
        query = stack_heads(query_ref, slot)
        grad = dot(rows_ref[slot * BLOCK : (slot + 1) * BLOCK, :], w_out_ref[...], (1, 1)).astype(BF16)
        grad = jnp.concatenate(
            [grad[:, i * HD : (i + 1) * HD] for i in range(grad.shape[1] // HD)], axis=0
        )
        delta = jnp.sum(grad.astype(F32).T * wide_ref[slot], axis=0, keepdims=True)
        log_total = log_ref[slot, 0:1, :]
        total[...] = jnp.zeros_like(total)

        first = first_rank(lens_ref, flags_ref, rank)

        def visit(key_rank, diagonal):
            pair = key_pair(kv_ref, key_rank)
            keys, values = read_pair(kv_ref, pair, KEYS), read_pair(kv_ref, pair, VALUES)
            scores = dot(keys, query, (1, 1)) * scale
            scores = bounded(scores, key_rank == first, diagonal)
            probs = jnp.exp(scores - log_total)
            grad_probs = dot(values, grad, (1, 1))
            grad_scores = (probs * (grad_probs - delta)).astype(BF16)
            grad_values = dot(probs.astype(BF16), grad, (1, 0))
            grad_keys = dot(grad_scores, query, (1, 0)) * scale
            for half, (device, span) in enumerate(pair):
                rows = slice(half * BLOCK, (half + 1) * BLOCK)
                grad_kv[device, span, HD:] += grad_values[rows]
                grad_kv[device, span, :HD] += grad_keys[rows]
            total[...] += dot(keys, grad_scores, (0, 0))

        def step(index, carry):
            visit(rank - 2 * index, False)
            return carry

        visit(rank, True)
        lax.fori_loop(1, lax.div(rank - first, 2) + 1, step, 0)
        turned = (total[...] * scale).T
        span = pl.ds(slot * BLOCK, BLOCK)
        for head in range(turned.shape[0] // BLOCK):
            one = turned[head * BLOCK : (head + 1) * BLOCK]
            grad_query_ref[span, head * HD : (head + 1) * HD] = turn(
                one, cos_ref.at[span], sin_ref.at[span], 1.0
            ).astype(BF16)
    grad_kv_ref[...] = grad_kv[...].astype(BF16)
    for one in passes:
        one.end()


def attend_back(
    doc_lengths, keep_flags, own, query, rows, w_out, kv, wide, log_total, cosine, sine, results
):
    count = query.shape[1] // HD * BLOCK
    return pl.pallas_call(
        attend_back_body,
        out_shape=(
            jax.ShapeDtypeStruct(query.shape, BF16),
            jax.ShapeDtypeStruct(kv.shape, BF16),
        )
        + tuple(jax.ShapeDtypeStruct(result.shape, result.dtype) for result in results),
        in_specs=[smem()] * 3 + [vmem()] * 8 + [anywhere()] * 3,
        out_specs=(vmem(),) * 2 + (anywhere(),) * 3,
        scratch_shapes=[
            pltpu.VMEM(kv.shape, F32),
            pltpu.VMEM((HD, count), F32),
        ]
        + buffers(results)
        + [pltpu.SemaphoreType.DMA((3, 2))],
        compiler_params=pltpu.CompilerParams(vmem_limit_bytes=VMEM_BYTES),
        cost_estimate=cost(3_000_000_000, 20_000_000),
        name="attend_back",
    )(
        doc_lengths, keep_flags, own, query, rows, w_out, kv, wide, log_total, cosine, sine, *results
    )


def finish_body(mixed_ref, grad_ref, qkv_ref, out_ref, *refs):
    query_ref, key_ref = refs[2], refs[3]
    wide, thin = query_ref.shape[1], key_ref.shape[1]
    passing, sems = refs[6:10], refs[10]

    def parts(ref):
        yield ref.at[:, pl.ds(0, wide)], query_ref
        yield ref.at[:, pl.ds(wide, thin)], key_ref
        yield ref.at[:, pl.ds(wide + thin, thin)], refs[4]

    passes = [
        Passed(mixed_ref, passing[0], lambda ref: [(ref, refs[0])], sems.at[0]),
        Passed(grad_ref, passing[1], lambda ref: [(ref, refs[1])], sems.at[1]),
        Passed(out_ref, passing[2], lambda ref: [(ref, refs[5])], sems.at[2]),
        Passed(qkv_ref, passing[3], parts, sems.at[3]),
    ]
    for one in passes:
        one.turn()
    for one in passes:
        one.end()


def finish(mixed, grad, qkv, out, thin):
    share, wide = qkv.shape[0], qkv.shape[1] - 2 * thin
    shapes = [(mixed.shape, BF16), (grad.shape, BF16), ((share, wide), F32)]
    shapes += [((share, thin), F32)] * 2 + [(out.shape, F32)]
    return pl.pallas_call(
        finish_body,
        out_shape=[jax.ShapeDtypeStruct(*shape) for shape in shapes],
        in_specs=[anywhere()] * 4,
        out_specs=[anywhere()] * 6,
        scratch_shapes=buffers([mixed, grad, out, qkv]) + [pltpu.SemaphoreType.DMA((4, 2))],
        compiler_params=pltpu.CompilerParams(vmem_limit_bytes=VMEM_BYTES),
        cost_estimate=cost(0, 20_000_000),
        name="finish",
    )(mixed, grad, qkv, out)


def scatter_back_body(
    part_ref, query_ref, cos_ref, sin_ref, w_query_hbm, w_key_hbm, w_value_hbm,
    dqkv_ref, out_ref,
    w_query, w_key, w_value, load_sems, total,
    core_recv, held, recv, core_send_sem, core_recv_sem, send_sem, recv_sem,
):
    devices = part_ref.shape[0]
    chips = devices // 2
    own = lax.axis_index("tok")
    plane = lax.axis_index("tp")
    partner = (own ^ 1, plane)
    w_query, w_key, w_value = load_all(
        [w_query_hbm, w_key_hbm, w_value_hbm], [w_query, w_key, w_value], load_sems
    )
    greet([partner] + [(own ^ (2 * step), plane) for step in range(1, chips)])

    def core_copy(step):
        return pltpu.make_async_remote_copy(
            src_ref=part_ref.at[own ^ (2 * step) ^ 1],
            dst_ref=core_recv.at[step],
            send_sem=core_send_sem.at[step],
            recv_sem=core_recv_sem.at[step],
            device_id=partner,
            device_id_type=MESH,
        )

    def copy(step):
        return pltpu.make_async_remote_copy(
            src_ref=held.at[step],
            dst_ref=recv.at[step],
            send_sem=send_sem.at[step],
            recv_sem=recv_sem.at[step],
            device_id=(own ^ (2 * step), plane),
            device_id_type=MESH,
        )

    order = list(range(chips - 1, -1, -1))
    for step in order:
        core_copy(step).start()
    for step in order:
        core_copy(step).wait_recv()
        mine = part_ref[own ^ (2 * step)].astype(F32) + core_recv[step].astype(F32)
        if step > 0:
            held[step] = mine.astype(held.dtype)
            copy(step).start()
    wide = query_ref.shape[1]
    query = query_ref[...]
    dqkv_ref[:, :wide] = query
    tiles = [pl.ds(start, 512) for start in range(0, out_ref.shape[1], 512)]
    for tile in tiles:
        total[:, tile] = dot(query, w_query.get()[tile, :], (1, 1))
    for step in range(1, chips):
        copy(step).wait_recv()
        mine = mine + recv[step].astype(F32)
    keys = turn(mine[:, :HD], cos_ref, sin_ref, 1.0).astype(BF16)
    values = mine[:, HD:].astype(BF16)
    dqkv_ref[:, wide : wide + HD] = keys
    dqkv_ref[:, wide + HD :] = values
    for tile in tiles:
        out_ref[:, tile] = (
            total[:, tile]
            + dot(keys, w_key.get()[tile, :], (1, 1))
            + dot(values, w_value.get()[tile, :], (1, 1))
        ).astype(BF16)
    for step in range(1, chips):
        copy(step).wait_send()
    for step in range(chips):
        core_copy(step).wait_send()


def scatter_back(part, query, cosine, sine, w_query, w_key, w_value, collective_id):
    devices, rows = part.shape[:2]
    chips = devices // 2
    shard = part.shape[1:]
    width = w_query.shape[0]
    weights = [w_query, w_key, w_value]
    return pl.pallas_call(
        scatter_back_body,
        out_shape=(
            jax.ShapeDtypeStruct((rows, query.shape[1] + shard[1]), BF16),
            jax.ShapeDtypeStruct((rows, width), BF16),
        ),
        in_specs=[vmem()] * 4 + [anywhere()] * 3,
        out_specs=(vmem(),) * 2,
        scratch_shapes=buffers(weights)
        + [pltpu.SemaphoreType.DMA((3,)), pltpu.VMEM((rows, width), F32)]
        + [pltpu.VMEM((chips,) + shard, part.dtype)] * 3
        + [pltpu.SemaphoreType.DMA((chips,))] * 4,
        compiler_params=params(collective_id),
        cost_estimate=cost(1_000_000_000, 10_000_000),
        name="scatter_back",
    )(part, query, cosine, sine, *weights)


def line_sems(planes):
    return [pltpu.SemaphoreType.DMA((2, planes))] * 2


def line_copy(own, plane, step, source, target, send_sem, recv_sem, index):
    side = 0 if step > 0 else 1
    return pltpu.make_async_remote_copy(
        src_ref=source,
        dst_ref=target,
        send_sem=send_sem.at[side, index],
        recv_sem=recv_sem.at[side, index],
        device_id=(own, plane + step),
        device_id_type=MESH,
    )


def line_gather(own, plane, planes, arrays, start, pace, ready=None):
    last = planes - 1

    def move(array, index, step):
        shard, send_sem, recv_sem = array
        return line_copy(own, plane, step, shard(index), shard(index), send_sem, recv_sem, index)

    for step in range(1, planes + 1):
        yield start + pace * (step - 1)
        before, after = plane - (step - 1), plane + (step - 1)

        @pl.when(before >= 0)
        def _():
            for array in arrays:
                if step > 1:
                    move(array, before, 1).wait_recv()
                if step < planes:

                    @pl.when(plane < last)
                    def _():
                        move(array, before, 1).start()

        @pl.when(after <= last)
        def _():
            for array in arrays:
                if step > 1:
                    move(array, after, -1).wait_recv()
                if step < planes:

                    @pl.when(plane > 0)
                    def _():
                        move(array, after, -1).start()

    if ready is not None:
        ready()
    yield start + pace * (planes + 1)
    for index in range(planes):

        @pl.when((index <= plane) & (plane < last))
        def _():
            for array in arrays:
                move(array, index, 1).wait_send()

        @pl.when((index >= plane) & (plane > 0))
        def _():
            for array in arrays:
                move(array, index, -1).wait_send()


def line_reduce(own, plane, planes, half, part, total, send, recv, send_sem, recv_sem, start, pace):
    last = planes - 1

    def right(index):
        return line_copy(
            own, plane, 1, send.at[index, half], recv.at[index, half], send_sem, recv_sem, index
        )

    def left(index):
        slot = jnp.where(index == plane - 1, planes, index)
        return line_copy(
            own, plane, -1, send.at[index, half], recv.at[slot, half], send_sem, recv_sem, index
        )

    def add(index):
        send[index, half] = (
            part[:, half, index].astype(F32) + recv[index, half].astype(F32)
        ).astype(send.dtype)

    for step in range(1, planes):
        yield start + pace * (step - 1)
        if step == 1:
            part = part.get()
        upper, lower = planes - step + plane, step - planes + plane

        @pl.when((upper <= last) & (plane < last))
        def _():
            @pl.when(plane == 0)
            def _():
                send[upper, half] = part[:, half, upper]

            @pl.when(plane > 0)
            def _():
                right(upper).wait_recv()
                add(upper)

            right(upper).start()

        @pl.when((lower >= 0) & (plane > 0))
        def _():
            @pl.when(plane == last)
            def _():
                send[lower, half] = part[:, half, lower]

            @pl.when(plane < last)
            def _():
                left(lower).wait_recv()
                add(lower)

            left(lower).start()

    yield start + pace * (planes - 1)
    total[half] = part[:, half, plane].astype(F32)

    @pl.when(plane > 0)
    def _():
        right(plane).wait_recv()
        total[half] += recv[plane, half].astype(F32)

    @pl.when(plane < last)
    def _():
        left(plane).wait_recv()
        total[half] += recv[planes, half].astype(F32)

    yield start + pace * (2 * planes)
    for index in range(planes):

        @pl.when((index > plane) & (plane < last))
        def _():
            right(index).wait_send()

        @pl.when((index < plane) & (plane > 0))
        def _():
            left(index).wait_send()


def gather_flows(gathered, scratch, start, pace, done=None, key=None):
    send_sem, recv_sem = scratch
    planes = gathered.shape[2]
    own, plane = lax.axis_index("tok"), lax.axis_index("tp")

    def flow(half):
        array = (lambda index: gathered.at[:, half, index], send_sem.at[half], recv_sem.at[half])
        ready = None if key is None else lambda: done.add(key + (half,))
        yield from line_gather(own, plane, planes, [array], start + pace / 2 * half, pace, ready)

    return [flow(half) for half in range(HALVES)]


def sum_flows(
    part_ref, gathered, scratch, math_rule, start=0.0, pace=8.7, extra=None, done=None, key=None
):
    total, send, recv, send_sem, recv_sem = scratch[:5]
    planes = part_ref.shape[2]
    own, plane = lax.axis_index("tok"), lax.axis_index("tp")

    def flow(half):
        begin = start + pace / 2 * half
        reducing = line_reduce(
            own, plane, planes, half, part_ref, total, send, recv,
            send_sem.at[half], recv_sem.at[half], begin, pace,
        )
        for number in range(planes):
            yield next(reducing)
        next(reducing)
        math_rule(plane, half, total)
        if gathered is not None:
            arrays = [
                (
                    lambda index: gathered.at[:, half, index],
                    scratch[5].at[half],
                    scratch[6].at[half],
                )
            ]
            if extra is not None and half == HALVES - 1:
                arrays.append(extra)
            ready = None if key is None else lambda: done.add(key + (half,))
            yield from line_gather(
                own, plane, planes, arrays, begin + pace * (planes - 1), pace, ready
            )
        for _ in reducing:
            pass

    return [flow(half) for half in range(HALVES)]


def sum_scratch(planes, width, gathers=True):
    shard = (HALVES, SLOTS, TILE, width)
    return [
        pltpu.VMEM(shard, F32),
        pltpu.VMEM((planes,) + shard, BF16),
        pltpu.VMEM((planes + 1,) + shard, BF16),
    ] + [pltpu.SemaphoreType.DMA((HALVES, 2, planes))] * (4 if gathers else 2)


def norm_math(x, gain_ref, hidden_ref, inv_ref, gathered):
    def rule(plane, half, total):
        x_ref = x.get()
        for block in range(SLOTS):
            hidden = x_ref[block, half, plane].astype(F32) + total[half, block]
            inv = lax.rsqrt(jnp.mean(hidden * hidden, axis=1, keepdims=True) + norm_eps)
            hidden_ref[half, block] = hidden
            inv_ref[half, block] = inv
            gathered[block, half, plane] = (hidden * inv * gain_ref[...]).astype(BF16)

    return rule


def ffn_math(hiddens, inv_ref, dy, gain_ref, grad_ref, gains_ref, gathered):
    def rule(plane, half, total):
        if half == 0:
            gains_ref[...] = jnp.zeros_like(gains_ref)
        hidden_ref, dy_ref = hiddens.get(), dy.get()
        for block in range(SLOTS):
            dn = total[half, block]
            hidden = hidden_ref[half, block]
            inv = inv_ref[half, block]
            weighted = gain_ref[...] * dn
            mean = jnp.mean(weighted * hidden, axis=1, keepdims=True)
            grad = (
                keep_scale * dy_ref[block, half, plane].astype(F32)
                + inv * weighted
                - hidden * (inv * inv * inv * mean)
            )
            grad_ref[half, block] = grad
            gathered[block, half, plane] = grad.astype(BF16)
            gains_ref[0:1, :] += jnp.sum(dn * hidden * inv, axis=0, keepdims=True)

    return rule


def mixed_math(hiddens, xs, mixed_ref):
    def rule(plane, half, total):
        hidden_ref, x_ref = hiddens.get(), xs.get()
        for block in range(SLOTS):
            x = x_ref[block, half, plane].astype(F32)
            branch = (hidden_ref[half, block] - x) + total[half, block]
            mixed_ref[half, block] = (x + keep_scale * branch).astype(BF16)

    return rule


def attn_math(xs, inv_ref, dy, grads, gain_ref, ffn_gains_ref, gains_all, gathered):
    def rule(plane, half, total):
        x_ref, dy_ref, grad_ref = xs.get(), dy.get(), grads.get()
        if half == 0:
            gains_all[plane] = ffn_gains_ref[...]
        for block in range(SLOTS):
            dn = total[half, block]
            x = x_ref[block, half, plane].astype(F32)
            inv = inv_ref[block, half, plane]
            weighted = gain_ref[...] * dn
            mean = jnp.mean(weighted * x, axis=1, keepdims=True)
            grad = (
                (1.0 - keep_scale) * dy_ref[block, half, plane].astype(F32)
                + grad_ref[half, block]
                + inv * weighted
                - x * (inv * inv * inv * mean)
            )
            gathered[block, half, plane] = grad.astype(BF16)
            gains_all[plane, 1:2, :] += jnp.sum(dn * x * inv, axis=0, keepdims=True)

    return rule


def deal_sum_body(
    lens_ref, flags_ref, gain_ref, own_hbm, part_hbm, x_hbm,
    out_hbm, gathered_hbm, hidden_ref, inv_ref,
    own_blocks, part, x, out_ref, gathered, load_sems, store_sems, *scratch,
):
    dealing, summing = scratch[: deal_count()], scratch[deal_count() :]
    part, blocks, x = load_all([part_hbm, own_hbm, x_hbm], [part, own_blocks, x], load_sems)
    out, rows = store_all([out_hbm, gathered_hbm], [out_ref, gathered], store_sems)
    greet(bit_peers(stages_of("tok")), line=True)
    tile = BLOCK // CHUNKS

    def finish(chunk, values):
        for slot, value in enumerate(values):
            out_ref[slot, pl.ds(chunk * tile, tile), :] = value
        if chunk == CHUNKS - 1:
            out.send()

    run(
        *sum_flows(part, gathered, summing, norm_math(x, gain_ref, hidden_ref, inv_ref, gathered)),
        deal_flow(lens_ref, flags_ref, blocks, finish, dealing, 5.0),
    )
    rows.send()
    rows.copy.wait()
    out.copy.wait()


def deal_sum(doc_lengths, keep_flags, blocks, part, x, gain, collective_id):
    planes, width = part.shape[2], part.shape[4]
    shard = (HALVES, SLOTS, TILE)
    dealt = jax.ShapeDtypeStruct((SLOTS, BLOCK, width), blocks.dtype)
    rows = jax.ShapeDtypeStruct(part.shape, BF16)
    return pl.pallas_call(
        deal_sum_body,
        out_shape=(
            dealt,
            rows,
            jax.ShapeDtypeStruct(shard + (width,), F32),
            jax.ShapeDtypeStruct(shard + (1,), F32),
        ),
        in_specs=[smem(), smem(), vmem()] + [anywhere()] * 3,
        out_specs=(anywhere(),) * 2 + (vmem(),) * 2,
        scratch_shapes=buffers([blocks, part, x, dealt, rows])
        + [pltpu.SemaphoreType.DMA((3,)), pltpu.SemaphoreType.DMA((2,))]
        + deal_scratch(stages_of("tok"), width, blocks.dtype)
        + sum_scratch(planes, width),
        compiler_params=params(collective_id),
        cost_estimate=cost(0, 60_000_000),
        name="deal_sum",
    )(doc_lengths, keep_flags, gain, blocks, part, x)


def spread_flow(units, outs, scratch, pace, start=0.0):
    own, plane = lax.axis_index("tok"), lax.axis_index("tp")
    count = len(units)
    boxes, inboxes, core_inboxes = scratch[:count], scratch[count : 2 * count], scratch[2 * count : 3 * count]
    core_send_sem, core_recv_sem, send_sem, recv_sem = scratch[3 * count :]
    chips = boxes[0].shape[0]
    bits = [1 << i for i in range(int(math.log2(chips)))]
    orders = (bits, bits[::-1])
    stages = len(bits)

    def core_copy(unit, chip):
        return pltpu.make_async_remote_copy(
            src_ref=boxes[unit].at[chip],
            dst_ref=core_inboxes[unit].at[chip],
            send_sem=core_send_sem.at[unit, chip],
            recv_sem=core_recv_sem.at[unit, chip],
            device_id=(own ^ 1, plane),
            device_id_type=MESH,
        )

    def active(half, stage):
        gone = orders[half][:stage]
        return [chip for chip in range(chips) if all(chip & bit == 0 for bit in gone)]

    def slot(stage, half, chip):
        before = sum(chips >> (earlier + 1) for earlier in range(stage))
        return before + active(half, stage + 1).index(chip)

    def copy(unit, half, stage, chip):
        bit = orders[half][stage]
        there = slot(stage, half, chip)
        return pltpu.make_async_remote_copy(
            src_ref=boxes[unit].at[chip ^ bit, half],
            dst_ref=inboxes[unit].at[there, half],
            send_sem=send_sem.at[unit, half, there],
            recv_sem=recv_sem.at[unit, half, there],
            device_id=(own ^ (2 * bit), plane),
            device_id_type=MESH,
        )

    def offer(unit, chip):
        for half in range(2):
            term = units[unit]((own ^ (2 * chip)) ^ 1, half)
            boxes[unit][chip, half] = term.astype(BF16)
        core_copy(unit, chip).start()

    def collect(unit, chip):
        core_copy(unit, chip).wait()
        for half in range(2):
            term = units[unit](own ^ (2 * chip), half)
            term = term + core_inboxes[unit][chip, half].astype(F32)
            boxes[unit][chip, half] = term.astype(BF16)
            bit = orders[half][0]
            if chip & bit:
                copy(unit, half, 0, chip ^ bit).start()

    def take(unit, stage, half):
        for chip in active(half, stage + 1):
            copy(unit, half, stage, chip).wait_recv()
            got = inboxes[unit][slot(stage, half, chip), half].astype(F32)
            total = boxes[unit][chip, half].astype(F32) + got
            if stage < stages - 1:
                boxes[unit][chip, half] = total.astype(BF16)
                bit = orders[half][stage + 1]
                if chip & bit:
                    copy(unit, half, stage + 1, chip ^ bit).start()
            else:
                rows = total.shape[0]
                outs[unit].ref[half * rows : (half + 1) * rows, :] = total
                if half == 1:
                    outs[unit].send()

    chip_order = sorted(range(chips), key=lambda chip: -bin(chip).count("1"))
    for unit in range(count):
        for chip in chip_order:
            yield start + 0.1 + 3 * unit
            offer(unit, chip)
        for chip in chip_order:
            yield start + 3.2 + 3 * unit
            collect(unit, chip)
    for stage in range(stages):
        for unit in range(count):
            for half in range(2):
                yield start + 6.0 + pace * (unit + 1 + count * stage)
                take(unit, stage, half)
    yield 1e6
    for out in outs:
        out.copy.wait()
    for unit in range(count):
        for half in range(2):
            for stage in range(stages):
                for chip in active(half, stage + 1):
                    copy(unit, half, stage, chip).wait_send()


def spread_scratch(shapes, devices):
    chips = devices // 2
    boxes = [pltpu.VMEM((chips, 2, rows // 2, columns), BF16) for rows, columns in shapes]
    inboxes = [pltpu.VMEM((chips - 1, 2, rows // 2, columns), BF16) for rows, columns in shapes]
    return (
        boxes
        + inboxes
        + boxes
        + [pltpu.SemaphoreType.DMA((len(shapes), chips))] * 2
        + [pltpu.SemaphoreType.DMA((len(shapes), 2, chips - 1))] * 2
    )


def window(ref, number, size):
    if size % 128 == 0:
        return ref[:, pl.ds(pl.multiple_of(number * size, size), size)]
    parts = 128 // size
    tile = ref[:, pl.ds(pl.multiple_of(number // parts * 128, 128), 128)].astype(F32)
    return choose(
        number % parts, [tile[:, i * size : (i + 1) * size] for i in range(parts)]
    ).astype(ref.dtype)


def rows_by_owner(left, right, rows):
    def term(owner, half):
        return lax.dot_general(
            window(left.get(), owner * 2 + half, rows // 2),
            right.get()[...],
            (((0,), (0,)), ((), ())),
            preferred_element_type=F32,
        )

    return term


def columns_by_owner(left, right, columns):
    def term(owner, half):
        rows = left.shape[1] // 2
        return lax.dot_general(
            left.get()[:, half * rows : (half + 1) * rows],
            window(right.get(), owner, columns),
            (((0,), (0,)), ((), ())),
            preferred_element_type=F32,
        )

    return term


def ffn_sums_body(*refs):
    inv_ref, gain_ref = refs[:2]
    sources, (grad_ref, gains_ref, mixed_ref), targets = refs[2:12], refs[12:15], refs[15:19]
    loaded, stored, refs = refs[19:29], refs[29:33], refs[33:]
    load_sems, store_sems, refs = refs[0], refs[1], refs[2:]
    summing, mixing, spreading = refs[:7], refs[7:12], refs[12:]
    own, plane = lax.axis_index("tok"), lax.axis_index("tp")
    loads = load_all(sources, loaded, load_sems)
    part, normed, dgate, dup, inner, dm, hidden, dy, mixed_part, x = loads
    rows, *grads = store_all(targets, stored, store_sems)
    gathered = rows.ref
    share = normed.shape[1] // lax.axis_size("tok")
    greet([(own ^ 1, plane)] + [(own ^ (2 << i), plane) for i in range(stages_of("tok") - 1)], True)
    done = set()

    def leave():
        for half in range(HALVES):
            yield 80.0, ("rows", half)
        rows.send()

    run(
        *sum_flows(
            part,
            gathered,
            summing,
            ffn_math(hidden, inv_ref, dy, gain_ref, grad_ref, gains_ref, gathered),
            done=done,
            key=("rows",),
        ),
        *sum_flows(mixed_part, None, mixing, mixed_math(hidden, x, mixed_ref), 27.0, 11.0),
        spread_flow(
            [
                rows_by_owner(normed, dgate, share),
                rows_by_owner(normed, dup, share),
                columns_by_owner(inner, dm, share),
            ],
            grads,
            spreading,
            15.6,
        ),
        leave(),
        done=done,
    )
    rows.copy.wait()


def ffn_sums(
    part, hidden, inv, dy, gain, normed, dgate, dup, inner, dm, mixed_part, x, collective_id
):
    planes, width = part.shape[2], part.shape[4]
    devices = lax.axis_size("tok")
    share = width // devices
    wide = dgate.shape[1]
    shapes = [(share, wide), (share, wide), (wide, share)]
    rows = jax.ShapeDtypeStruct(part.shape, BF16)
    grads = [jax.ShapeDtypeStruct(shape, F32) for shape in shapes]
    sources = [part, normed, dgate, dup, inner, dm, hidden, dy, mixed_part, x]
    grad, gains, mixed, rows, gate, up, down = pl.pallas_call(
        ffn_sums_body,
        out_shape=[
            jax.ShapeDtypeStruct(hidden.shape, F32),
            jax.ShapeDtypeStruct((8, width), F32),
            jax.ShapeDtypeStruct(hidden.shape, BF16),
            rows,
        ]
        + grads,
        in_specs=[vmem()] * 2 + [anywhere()] * len(sources),
        out_specs=[vmem()] * 3 + [anywhere()] * 4,
        scratch_shapes=buffers(sources + [rows] + grads)
        + [pltpu.SemaphoreType.DMA((len(sources),)), pltpu.SemaphoreType.DMA((4,))]
        + sum_scratch(planes, width)
        + sum_scratch(planes, width, False)
        + spread_scratch(shapes, devices),
        compiler_params=params(collective_id),
        cost_estimate=cost(0, 80_000_000),
        name="ffn_sums",
    )(inv, gain, *sources)
    return rows, grad, gains, gate, up, down, mixed


def together():
    return stages_of("tok") <= 3


def attn_sums_body(lens_ref, flags_ref, *refs):
    both = together()
    mixed_ref, inv_ref, gain_ref, ffn_gains_ref = refs[:4]
    sources, home_ref, grad_home_ref, refs = refs[4:12], refs[12], refs[13], refs[14:]
    gathered, gains_ref, mixed_out = refs[:3]
    targets, refs = refs[3:5], refs[5:]
    loaded, stored, load_sems, store_sems, refs = refs[:8], refs[8:10], refs[10], refs[11], refs[12:]
    part, normed, dqkv, attended, da, x, dy, grad = load_all(sources, loaded, load_sems)
    weight_grads = store_all(targets, stored, store_sems)
    if both:
        grad_out, gathered = gathered, refs[0]
        gain_sums, gains_ref = gains_ref, refs[1]
        refs = refs[2:]
    summing, undealing, refs = refs[:7], refs[7 : 7 + deal_count()], refs[7 + deal_count() :]
    mixed_all, mixed_sems, home_sems = refs[0], refs[1:3], refs[3]
    gains_all, gains_sems, refs = refs[4], refs[5:7], refs[7:]
    planes = part.shape[2]
    plane = lax.axis_index("tp")
    share = normed.shape[1] // lax.axis_size("tok")
    home = pltpu.make_async_copy(home_ref, mixed_out, home_sems.at[0])
    home.start()
    if both:
        grad_home = pltpu.make_async_copy(grad_home_ref, grad_out, home_sems.at[1])
        grad_home.start()
        grad_undealing, refs = refs[: deal_count()], refs[deal_count() :]
        gaining, refs = refs[:3], refs[3:]
    greet(all_peers() if both else bit_peers(stages_of("tok")), True)
    for half in range(HALVES):
        mixed_all[:, half, plane] = mixed_ref[half]
    done = set()

    def sum_gains():
        yield (70.0, ("grad", HALVES - 1))
        total = gains_all[0]
        for index in range(1, planes):
            total = total + gains_all[index]
        gains_ref[...] = total
        done.add(("gains",))

    flows = [
        *gather_flows(mixed_all, mixed_sems, 0.0, 8.7, done, ("mixed",)),
        *sum_flows(
            part,
            gathered,
            summing,
            attn_math(x, inv_ref, dy, grad, gain_ref, ffn_gains_ref, gains_all, gathered),
            9.0,
            10.0,
            (lambda index: gains_all.at[index],) + gains_sems,
            done,
            ("grad",),
        ),
        spread_flow(
            [
                rows_by_owner(normed, dqkv, share),
                columns_by_owner(attended, da, share),
            ],
            weight_grads,
            refs,
            9.0,
        ),
        undeal_flow(
            lens_ref, flags_ref, mixed_all, mixed_out, home, undealing, 28.0, 4.5, ("mixed",), 6.0
        ),
        sum_gains(),
    ]
    if both:
        flows += [
            undeal_flow(
                lens_ref, flags_ref, gathered, grad_out, grad_home, grad_undealing,
                55.0, 5.2, ("grad",), 8.0,
            ),
            gain_flow(gains_ref, gain_sums, gaining, 72.0, ("gains",)),
        ]
    run(*flows, done=done)


def attn_sums(
    doc_lengths, keep_flags, part, mixed, x, inv, dy, grad, gain, ffn_gains, normed, dqkv, attended,
    da, home, grad_home, collective_id,
):
    planes, width = part.shape[2], part.shape[4]
    devices = lax.axis_size("tok")
    share = width // devices
    shapes = [(share, dqkv.shape[1]), (attended.shape[1], share)]
    both = together()
    rows_shape = jax.ShapeDtypeStruct(part.shape, BF16)
    gains_shape = jax.ShapeDtypeStruct((8, width), F32)
    blocks_shape = jax.ShapeDtypeStruct(home.shape, BF16)
    gain_part = gain_share(width, devices)
    first = (
        [blocks_shape, jax.ShapeDtypeStruct((8, gain_part), F32)] if both else [rows_shape, gains_shape]
    )
    dealing = deal_scratch(stages_of("tok"), width, BF16)
    sources = [part, normed, dqkv, attended, da, x, dy, grad]
    weight_grads = [jax.ShapeDtypeStruct(shape, F32) for shape in shapes]
    grads, gains, mixed_blocks, qkv, out = pl.pallas_call(
        attn_sums_body,
        out_shape=first
        + [blocks_shape]
        + weight_grads,
        in_specs=[smem(), smem()] + [vmem()] * 4 + [anywhere()] * 10,
        out_specs=[vmem()] * 3 + [anywhere()] * 2,
        scratch_shapes=buffers(sources + weight_grads)
        + [pltpu.SemaphoreType.DMA((8,)), pltpu.SemaphoreType.DMA((2,))]
        + (
            [pltpu.VMEM(part.shape, BF16), pltpu.VMEM((8, width), F32)] if both else []
        )
        + sum_scratch(planes, width)
        + dealing
        + [pltpu.VMEM(part.shape, BF16)]
        + [pltpu.SemaphoreType.DMA((HALVES, 2, planes))] * 2
        + [pltpu.SemaphoreType.DMA((2,)), pltpu.VMEM((planes, 8, width), F32)]
        + line_sems(planes)
        + (dealing + gain_scratch(devices, gain_part) if both else [])
        + spread_scratch(shapes, devices),
        compiler_params=params(collective_id),
        cost_estimate=cost(0, 80_000_000),
        name="attn_sums",
    )(
        doc_lengths, keep_flags, mixed, inv, gain, ffn_gains, *sources, home, grad_home
    )
    if not both:
        grads, gains = undeal(doc_lengths, keep_flags, grads, grad_home, gains, collective_id + 1)
    return mixed_blocks, grads, gains, qkv, out


def rotary_tables(doc_lengths, keep_flags, ranks):
    blocks = keep_flags * (doc_lengths // BLOCK)
    ends = jnp.cumsum(blocks, dtype=jnp.int32)
    starts = ends - blocks
    inside = (ranks[:, None] >= starts[None, :]) & (ranks[:, None] < ends[None, :])
    first = jnp.sum(jnp.where(inside, starts[None, :], 0), axis=1, dtype=jnp.int32)
    offsets = jnp.arange(BLOCK, dtype=jnp.int32)
    positions = (((ranks - first) * BLOCK)[:, None] + offsets[None, :]).reshape(-1)
    half_dim = HD // 2
    freqs = jnp.exp(jnp.arange(half_dim, dtype=jnp.float32) * (-2.0 * math.log(10000.0) / HD))
    angles = positions.astype(jnp.float32)[:, None] * freqs[None, :]
    cosine, sine = jnp.cos(angles), jnp.sin(angles)
    return jnp.concatenate([cosine, cosine], axis=1), jnp.concatenate([sine, -sine], axis=1)


def over_columns(left, right):
    return lax.dot_general(
        left, right, (((1,), (1,)), ((), ())), preferred_element_type=jnp.float32
    )


def on_device(
    tokens,
    gain_attn,
    w_query,
    w_key,
    w_value,
    w_out,
    gain_ffn,
    w_gate,
    w_up,
    w_down,
    cotangent,
    doc_lengths,
    keep_flags,
):
    length = tokens.shape[0]
    model_width = tokens.shape[1]
    devices = lax.axis_size("tok")
    planes = lax.axis_size("tp")
    own_index = lax.axis_index("tok")
    blocks_here = length // BLOCK
    kept_here = blocks_here // 2
    rows = kept_here * BLOCK
    token_blocks = tokens.reshape(blocks_here, BLOCK, model_width)
    grad_blocks = cotangent.reshape(blocks_here, BLOCK, model_width)

    own_ranks = own_index + jnp.arange(kept_here, dtype=jnp.int32) * devices
    cosine, sine = rotary_tables(doc_lengths, keep_flags, own_ranks)
    own = jnp.reshape(own_index, (1,)).astype(jnp.int32)
    rows_x, normed_one, inv_one, queries, kv_all = deal_project(
        doc_lengths,
        keep_flags,
        gain_attn.reshape(1, -1),
        cosine,
        sine,
        token_blocks,
        w_query,
        w_key,
        w_value,
        0,
    )
    rows_x = rows_x.reshape(rows, model_width)
    attended, attended_wide, log_totals, part_out = attend(
        doc_lengths, keep_flags, own, queries, kv_all, w_out
    )

    def by_plane(array):
        return array.reshape(kept_here, HALVES, planes, TILE, array.shape[1])

    x_planes = by_plane(rows_x)
    rows_dy, normed_two, hidden_res, inv_two = deal_sum(
        doc_lengths,
        keep_flags,
        grad_blocks,
        by_plane(part_out),
        x_planes,
        gain_ffn.reshape(1, -1),
        1,
    )
    rows_dy = rows_dy.reshape(rows, model_width)
    normed_two = normed_two.reshape(rows, model_width)
    gate = jnp.dot(normed_two, w_gate, preferred_element_type=jnp.float32)
    upper = jnp.dot(normed_two, w_up, preferred_element_type=jnp.float32)
    sigma = jax.nn.sigmoid(gate)
    swish = gate * sigma
    inner = (swish * upper).astype(jnp.bfloat16)

    grad_m = (keep_scale * rows_dy.astype(jnp.float32)).astype(jnp.bfloat16)
    grad_inner = over_columns(grad_m, w_down)
    grad_gate_pre = (grad_inner * upper * sigma * (1.0 + gate * (1.0 - sigma))).astype(jnp.bfloat16)
    grad_up_pre = (grad_inner * swish).astype(jnp.bfloat16)
    part_two = (
        over_columns(grad_gate_pre, w_gate) + over_columns(grad_up_pre, w_up)
    ).astype(jnp.bfloat16)

    dy_planes = by_plane(rows_dy)
    grad_a, grad_hidden, gains_ffn, grad_gate, grad_up, grad_down, mixed_rows = ffn_sums(
        by_plane(part_two),
        hidden_res,
        inv_two,
        dy_planes,
        gain_ffn.reshape(1, -1),
        normed_two,
        grad_gate_pre,
        grad_up_pre,
        inner,
        grad_m,
        by_plane(jnp.dot(inner, w_down, preferred_element_type=jnp.float32).astype(jnp.bfloat16)),
        x_planes,
        4,
    )
    grad_a = grad_a.reshape(rows, model_width)

    grad_query_pre, grad_kv, grad_gate, grad_up, grad_down = attend_back(
        doc_lengths,
        keep_flags,
        own,
        queries,
        grad_a,
        w_out,
        kv_all,
        attended_wide,
        log_totals,
        cosine,
        sine,
        [grad_gate, grad_up, grad_down],
    )
    grad_qkv_pre, part_one = scatter_back(
        grad_kv, grad_query_pre, cosine, sine, w_query, w_key, w_value, 5
    )
    mixed, token_grad, gain_sums, grad_qkv, grad_out = attn_sums(
        doc_lengths,
        keep_flags,
        by_plane(part_one),
        mixed_rows,
        x_planes,
        by_plane(inv_one),
        dy_planes,
        grad_hidden,
        gain_attn.reshape(1, -1),
        gains_ffn,
        normed_one,
        grad_qkv_pre,
        attended,
        grad_a,
        token_blocks,
        grad_blocks,
        6,
    )
    own_share = model_width // devices
    if gain_sums.shape[1] != own_share:
        gain_sums = lax.dynamic_slice_in_dim(gain_sums, own_index * own_share, own_share, 1)
    mixed, token_grad, grad_query, grad_key, grad_value, grad_out = finish(
        mixed, token_grad, grad_qkv, grad_out, w_key.shape[1]
    )

    return (
        mixed.reshape(length, model_width),
        token_grad.reshape(length, model_width),
        gain_sums[1],
        grad_query,
        grad_key,
        grad_value,
        grad_out,
        gain_sums[0],
        grad_gate,
        grad_up,
        grad_down,
    )


def solution(mesh):
    placed = (
        P("tok", None),
        P(),
        P(None, "tp"),
        P(None, "tp"),
        P(None, "tp"),
        P("tp", None),
        P(),
        P(None, "tp"),
        P(None, "tp"),
        P("tp", None),
        P("tok", None),
        P(),
        P(),
    )
    return jax.shard_map(
        on_device,
        mesh=mesh,
        in_specs=placed,
        out_specs=(
            P("tok", None),
            P("tok", None),
            P("tok"),
            P("tok", "tp"),
            P("tok", "tp"),
            P("tok", "tp"),
            P("tp", "tok"),
            P("tok"),
            P("tok", "tp"),
            P("tok", "tp"),
            P("tp", "tok"),
        ),
        check_vma=False,
    )
```
